32 devices in a mesh: stream: 2 (over x), dp: 4 (over z), tensor: 4 (over y, core).
Axes of the slice: x: 2, y: 2, z: 4, core: 2. Of those that a mesh axis runs over, the one named last changes fastest.
Arguments:
- text_in: bfloat16 [16384, 768], P(('stream', 'dp', 'tensor')), may hold values from -6 to 6
- image_in: bfloat16 [4736, 1024], P(('stream', 'dp', 'tensor')), may hold values from -6 to 6
- lengths: int32 [128], P(('stream', 'dp')), may hold values from 8 to 128, as said below
- text_cot: bfloat16 [16384, 768], P(('stream', 'dp', 'tensor')), may hold values from -6 to 6
- image_cot: bfloat16 [4736, 1024], P(('stream', 'dp', 'tensor')), may hold values from -6 to 6
- text_cross_q: bfloat16 [1, 768, 1024], P(None, None, 'tensor'), may hold values from -0.21875 to 0.21875
- text_cross_kv: bfloat16 [1, 1024, 2, 1024], P(None, None, None, 'tensor'), may hold values from -0.1875 to 0.1875
- text_cross_out: bfloat16 [1, 1024, 768], P(None, 'tensor'), may hold values from -0.5 to 0.5
- text_up: bfloat16 [1, 768, 3072], P(None, None, 'tensor'), may hold values from -0.21875 to 0.21875
- text_down: bfloat16 [1, 3072, 768], P(None, 'tensor'), may hold values from -0.21875 to 0.21875
- text_self_qkv: bfloat16 [1, 768, 3, 768], P(None, None, None, 'tensor'), may hold values from -0.21875 to 0.21875
- text_self_out: bfloat16 [1, 768, 768], P(None, 'tensor'), may hold values from -0.625 to 0.625
- text_gain: bfloat16 [1, 3, 768], replicated, may hold values from 0.099609375 to 1.8984375
- text_bias: bfloat16 [1, 3, 768], replicated, may hold values from -1.5 to 1.5
- image_cross_q: bfloat16 [1, 1024, 1024], P(None, None, 'tensor'), may hold values from -0.1875 to 0.1875
- image_cross_kv: bfloat16 [1, 768, 2, 1024], P(None, None, None, 'tensor'), may hold values from -0.21875 to 0.21875
- image_cross_out: bfloat16 [1, 1024, 1024], P(None, 'tensor'), may hold values from -0.5 to 0.5
- image_up: bfloat16 [1, 1024, 1024], P(None, None, 'tensor'), may hold values from -0.1875 to 0.1875
- image_down: bfloat16 [1, 1024, 1024], P(None, 'tensor'), may hold values from -0.375 to 0.375
- image_self_qkv: bfloat16 [1, 1024, 3, 1024], P(None, None, None, 'tensor'), may hold values from -0.1875 to 0.1875
- image_self_out: bfloat16 [1, 1024, 1024], P(None, 'tensor'), may hold values from -0.5 to 0.5
- image_gain: bfloat16 [1, 3, 1024], replicated, may hold values from 0.099609375 to 1.8984375
- image_bias: bfloat16 [1, 3, 1024], replicated, may hold values from -1.5 to 1.5
Outputs:
- text_out: float32 [16384, 768], P(('stream', 'dp', 'tensor'))
- image_out: float32 [4736, 1024], P(('stream', 'dp', 'tensor'))
- text_grad: float32 [16384, 768], P(('stream', 'dp', 'tensor'))
- image_grad: float32 [4736, 1024], P(('stream', 'dp', 'tensor'))
- grad_text_cross_q: float32 [1, 768, 1024], P(None, ('stream', 'dp'), 'tensor')
- grad_text_cross_kv: float32 [1, 1024, 2, 1024], P(None, ('stream', 'dp'), None, 'tensor')
- grad_text_cross_out: float32 [1, 1024, 768], P(None, 'tensor', ('stream', 'dp'))
- grad_text_up: float32 [1, 768, 3072], P(None, ('stream', 'dp'), 'tensor')
- grad_text_down: float32 [1, 3072, 768], P(None, 'tensor', ('stream', 'dp'))
- grad_text_self_qkv: float32 [1, 768, 3, 768], P(None, ('stream', 'dp'), None, 'tensor')
- grad_text_self_out: float32 [1, 768, 768], P(None, 'tensor', ('stream', 'dp'))
- grad_text_gain: float32 [1, 3, 768], P(None, None, ('stream', 'dp'))
- grad_text_bias: float32 [1, 3, 768], P(None, None, ('stream', 'dp'))
- grad_image_cross_q: float32 [1, 1024, 1024], P(None, ('stream', 'dp'), 'tensor')
- grad_image_cross_kv: float32 [1, 768, 2, 1024], P(None, ('stream', 'dp'), None, 'tensor')
- grad_image_cross_out: float32 [1, 1024, 1024], P(None, 'tensor', ('stream', 'dp'))
- grad_image_up: float32 [1, 1024, 1024], P(None, ('stream', 'dp'), 'tensor')
- grad_image_down: float32 [1, 1024, 1024], P(None, 'tensor', ('stream', 'dp'))
- grad_image_self_qkv: float32 [1, 1024, 3, 1024], P(None, ('stream', 'dp'), None, 'tensor')
- grad_image_self_out: float32 [1, 1024, 1024], P(None, 'tensor', ('stream', 'dp'))
- grad_image_gain: float32 [1, 3, 1024], P(None, None, ('stream', 'dp'))
- grad_image_bias: float32 [1, 3, 1024], P(None, None, ('stream', 'dp'))
The draws below stay inside these ranges and needn't reach their ends.
Inputs may be any that keep to these rules, and one draw needn't show every extreme that they name: `lengths`: every caption has at least 8 tokens; some caption has all 128.
All inputs are finite; a program needn't handle non-finite values.
Results may differ from the reference program's by a relative error of at most 0.03.
Values may be sent and summed in bfloat16 or wider, within the bound.
A program may use at most 192 MiB of HBM per device.

```python
import math
import jax
import jax.numpy as jnp
from jax import lax

DT = 768
DV = 1024
DC = 1024
HC = 8
HT = 12
HV = 8
FT = 3072
FV = 1024
SLOTS = 128
REGIONS = 37
MIN_LEN = 8
LAYERS = 1
PAIRS = 128


def draw_lengths(key, part):
    key = jax.random.fold_in(key, 5)
    draw_key, pick_key = jax.random.split(key)
    lengths_drawn = jax.random.randint(draw_key, (PAIRS,), MIN_LEN, SLOTS + 1)
    longest = jax.random.randint(pick_key, (), 0, PAIRS)
    return jnp.where(jnp.arange(PAIRS) == longest, SLOTS, lengths_drawn).astype(jnp.int32)


def strengthened(entries, key, source, target, shards_of, factor):
    def block_of(axis_at):
        return (jnp.arange(entries.shape[axis_at]) // (entries.shape[axis_at] // shards_of)).reshape((-1,) + (1,) * (entries.ndim - 1 - axis_at))

    one_side = jax.random.permutation(key, shards_of)[block_of(target)]
    far = (block_of(target) + shards_of // 2) % shards_of
    return jnp.where((block_of(source) == one_side) | (block_of(source) == far), factor * entries, entries)


def block_scale(stream_key, extent, cuts, least, high):
    def one(position, parts):
        steps = jax.random.uniform(jax.random.fold_in(jax.random.fold_in(stream_key, 6), position), (parts,), jnp.float32, least / len(cuts), high / len(cuts))
        return jnp.repeat(jnp.exp(steps), extent[position] // parts).reshape((-1,) + (1,) * (len(extent) - position - 1))

    level = one(*cuts[0])
    for cut in cuts[1:]:
        level = level * one(*cut)
    return level


def noise(stream_key, shape, deviation, reach, pieces=(), kind=jnp.bfloat16):
    result = deviation * jax.random.normal(stream_key, shape, jnp.float32)
    if pieces:
        result = result * block_scale(stream_key, shape, pieces, -0.22, 0.18)
    return jnp.clip(result, -reach, reach).astype(kind)


def heavy_noise(own_key, extent, spread, bound, cuts, heavy, held_as=jnp.bfloat16):
    result = spread * jax.random.normal(own_key, extent, jnp.float32)
    if cuts:
        result = result * block_scale(own_key, extent, cuts, -0.22, 0.18)
    return jnp.clip(strengthened(result, jax.random.fold_in(own_key, 3), *heavy), -bound, bound).astype(held_as)


def setup_inputs(seed: int = 0) -> dict:
    keys = jax.random.split(jax.random.key(seed), 24)
    return {
        "text_in": noise(keys[0], (PAIRS * SLOTS, DT), 1.0, 6.0, ((0, 32),)),
        "image_in": noise(keys[1], (PAIRS * REGIONS, DV), 1.0, 6.0, ((0, 32),)),
        "lengths": draw_lengths(jax.random.fold_in(keys[23], 71), 0),
        "text_cot": heavy_noise(keys[3], (PAIRS * SLOTS, DT), 1.0, 6.0, ((0, 32),), (0, 1, 32, 2.75)),
        "image_cot": heavy_noise(keys[4], (PAIRS * REGIONS, DV), 1.0, 6.0, ((0, 32),), (0, 1, 32, 2.75)),
        "text_cross_q": noise(keys[5], (LAYERS, DT, DC), DT ** -0.5, 0.21875, ((2, 4),)),
        "text_cross_kv": noise(keys[6], (LAYERS, DV, 2, DC), DV ** -0.5, 0.1875, ((3, 4),)),
        "text_cross_out": noise(keys[7], (LAYERS, DC, DT), (DC // 8) ** -0.5, 0.5, ((1, 4),)),
        "text_up": noise(keys[8], (LAYERS, DT, FT), DT ** -0.5, 0.21875, ((2, 4),)),
        "text_down": noise(keys[9], (LAYERS, FT, DT), (FT // 4) ** -0.5, 0.21875, ((1, 4),)),
        "text_self_qkv": noise(keys[10], (LAYERS, DT, 3, DT), DT ** -0.5, 0.21875, ((3, 4),)),
        "text_self_out": noise(keys[11], (LAYERS, DT, DT), (DT // 8) ** -0.5, 0.625, ((1, 4),)),
        "text_gain": jnp.clip(1.0 + 0.18 * jax.random.normal(keys[12], (LAYERS, 3, DT), jnp.float32), 0.099609375, 1.8984375).astype(jnp.bfloat16),
        "text_bias": noise(keys[13], (LAYERS, 3, DT), 0.3, 1.5),
        "image_cross_q": noise(keys[14], (LAYERS, DV, DC), DV ** -0.5, 0.1875, ((2, 4),)),
        "image_cross_kv": noise(keys[15], (LAYERS, DT, 2, DC), DT ** -0.5, 0.21875, ((3, 4),)),
        "image_cross_out": noise(keys[16], (LAYERS, DC, DV), (DC // 8) ** -0.5, 0.5, ((1, 4),)),
        "image_up": noise(keys[17], (LAYERS, DV, FV), DV ** -0.5, 0.1875, ((2, 4),)),
        "image_down": noise(keys[18], (LAYERS, FV, DV), (FV // 4) ** -0.5, 0.375, ((1, 4),)),
        "image_self_qkv": noise(keys[19], (LAYERS, DV, 3, DV), DV ** -0.5, 0.1875, ((3, 4),)),
        "image_self_out": noise(keys[20], (LAYERS, DV, DV), (DV // 8) ** -0.5, 0.5, ((1, 4),)),
        "image_gain": jnp.clip(1.0 + 0.18 * jax.random.normal(keys[21], (LAYERS, 3, DV), jnp.float32), 0.099609375, 1.8984375).astype(jnp.bfloat16),
        "image_bias": noise(keys[22], (LAYERS, 3, DV), 0.3, 1.5),
    }


@jax.custom_vjp
def low(v):
    return lax.optimization_barrier(v.astype(jnp.bfloat16)).astype(jnp.float32)

@jax.custom_vjp
def low_back(v):
    return v

def low_keep(v):
    return (low(v), None)

def low_pass(kept, grad):
    return (grad,)

def back_keep(v):
    return (v, None)

def back_low(kept, grad):
    return (low(grad),)
low.defvjp(low_keep, low_pass)
low_back.defvjp(back_keep, back_low)
highest = lax.Precision.HIGHEST
norm_eps = 1e-05
masked_score = -1e+30

def project(inputs, weight):
    return low_back(jnp.tensordot(inputs, weight, axes=1, precision=highest))

def layer_norm(inputs, gain_row, bias_row):
    centered = inputs - lax.optimization_barrier(jnp.mean(inputs, axis=-1, keepdims=True))
    variance = lax.optimization_barrier(jnp.mean(centered * centered, axis=-1, keepdims=True))
    return centered * lax.rsqrt(variance + norm_eps) * gain_row + bias_row

def smooth_gate(inputs):
    return jax.nn.gelu(inputs, approximate=False)

def attend(blocks):
    queries, keys_in, values, key_mask = blocks
    scaling = queries.shape[-1] ** (-0.5)
    scores = jnp.einsum('gqhd,gkhd->ghqk', queries, keys_in, precision=highest) * scaling
    scores = low_back(jnp.where(key_mask[:, None, None, :], scores, masked_score))
    attn_probs = jax.nn.softmax(scores, axis=-1)
    context = jnp.einsum('ghqk,gkhd->gqhd', low(attn_probs), values, precision=highest)
    return low_back(low(context))

def attention(queries, keys_in, values, key_mask, head_size):
    pair_total = queries.shape[0]
    group_size = math.gcd(pair_total, 32)

    def blocked(full_array):
        return full_array.reshape((pair_total // group_size, group_size) + full_array.shape[1:])

    def heads_of(member):
        return blocked(member.reshape(member.shape[:2] + (member.shape[2] // head_size, head_size)))
    context = lax.map(jax.checkpoint(attend), (heads_of(queries), heads_of(keys_in), heads_of(values), blocked(key_mask)))
    return context.reshape(queries.shape)

def cross_block(own, own_low, other_low, other_mask, query_w, pair_w, out_w, gain_row, bias_row):
    queries = low(project(own_low, query_w))
    pair_proj = low(project(other_low, pair_w))
    context = attention(queries, pair_proj[:, :, 0], pair_proj[:, :, 1], other_mask, DC // HC)
    return layer_norm(own + project(context, out_w), gain_row, bias_row)

def mlp_block(own, up_w, down_w, gain_row, bias_row):
    hidden = project(low(own), up_w)
    return layer_norm(own + project(low(smooth_gate(hidden)), down_w), gain_row, bias_row)

def self_block(own, key_mask, qkv_w, out_w, head_size, gain_row, bias_row):
    triple = low(project(low(own), qkv_w))
    context = attention(triple[:, :, 0], triple[:, :, 1], triple[:, :, 2], key_mask, head_size)
    return layer_norm(own + project(context, out_w), gain_row, bias_row)

def one_layer(text_run, image_run, text_mask, weights):
    tq, tkv, tout, tup, tdown, tqkv, tsout, tgain, tbias, iq, ikv, iout, iup, idown, iqkv, isout, igain, ibias = weights
    text_low = low(text_run)
    image_low = low(image_run)
    other_image = jnp.roll(image_low, PAIRS // 2, axis=0)
    other_text = jnp.roll(text_low, PAIRS // 2, axis=0)
    other_mask = jnp.roll(text_mask, PAIRS // 2, axis=0)
    image_mask = jnp.ones((PAIRS, REGIONS), dtype=jnp.bool_)
    text_one = cross_block(text_run, text_low, other_image, image_mask, tq, tkv, tout, tgain[0], tbias[0])
    image_one = cross_block(image_run, image_low, other_text, other_mask, iq, ikv, iout, igain[0], ibias[0])
    text_two = mlp_block(text_one, tup, tdown, tgain[1], tbias[1])
    image_two = mlp_block(image_one, iup, idown, igain[1], ibias[1])
    text_three = self_block(text_two, text_mask, tqkv, tsout, DT // HT, tgain[2], tbias[2])
    image_three = self_block(image_two, image_mask, iqkv, isout, DV // HV, igain[2], ibias[2])
    return (text_three, image_three)

def reference(text_in, image_in, lengths, text_cot, image_cot, text_cross_q, text_cross_kv, text_cross_out, text_up, text_down, text_self_qkv, text_self_out, text_gain, text_bias, image_cross_q, image_cross_kv, image_cross_out, image_up, image_down, image_self_qkv, image_self_out, image_gain, image_bias):
    slot_ids = lax.broadcasted_iota(jnp.int32, (PAIRS, SLOTS), 1)
    text_mask = slot_ids < lengths.astype(jnp.int32)[:, None]
    weight_list = (text_cross_q, text_cross_kv, text_cross_out, text_up, text_down, text_self_qkv, text_self_out, text_gain, text_bias, image_cross_q, image_cross_kv, image_cross_out, image_up, image_down, image_self_qkv, image_self_out, image_gain, image_bias)
    weights_wide = tuple((member.astype(jnp.float32) for member in weight_list))

    def forward(text_wide, image_wide, *layer_weights):
        text_run = text_wide.reshape(PAIRS, SLOTS, DT)
        image_run = image_wide.reshape(PAIRS, REGIONS, DV)
        for layer_idx in range(LAYERS):
            picked = tuple((member[layer_idx] for member in layer_weights))
            text_run, image_run = one_layer(text_run, image_run, text_mask, picked)
        return (text_run.reshape(PAIRS * SLOTS, DT), image_run.reshape(PAIRS * REGIONS, DV))
    outputs, pullback = jax.vjp(forward, text_in.astype(jnp.float32), image_in.astype(jnp.float32), *weights_wide)
    grads = pullback((text_cot.astype(jnp.float32), image_cot.astype(jnp.float32)))
    return (outputs[0], outputs[1], grads[0], grads[1], grads[2], grads[3], grads[4], grads[5], grads[6], grads[7], grads[8], grads[9], grads[10], grads[11], grads[12], grads[13], grads[14], grads[15], grads[16], grads[17], grads[18], grads[19])
```

```python
import functools

import jax
import jax.numpy as jnp
from jax import lax
from jax.experimental import pallas as pl
from jax.experimental.pallas import tpu as pltpu
from jax.sharding import PartitionSpec as P

DT = 768
DV = 1024
HEAD = 128
SELF_HEAD = 64
SLOTS = 128
REGIONS = 37
PADDED = 48
QUARTERS = 4
BLOCK = 256

norm_eps = 1e-05
masked_score = -1e30

BF = jnp.bfloat16
F32 = jnp.float32
FORWARD = (0, 1, 2, 3)
BACKWARD = (1, 3, 0, 2)


def nn(left, right):
    return lax.dot_general(left, right, (((1,), (0,)), ((), ())), preferred_element_type=F32)


def nt(left, right):
    return lax.dot_general(left, right, (((1,), (1,)), ((), ())), preferred_element_type=F32)


def tn(left, right):
    return lax.dot_general(left, right, (((0,), (0,)), ((), ())), preferred_element_type=F32)


def low(value):
    return value.astype(BF)


def normed(inputs):
    centered = inputs - jnp.mean(inputs, axis=-1, keepdims=True)
    scale = lax.rsqrt(jnp.mean(centered * centered, axis=-1, keepdims=True) + norm_eps)
    return centered * scale, scale


def layer_norm(inputs, affine):
    return normed(inputs)[0] * affine[0:1] + affine[1:2]


def norm_back(inputs, affine, grad):
    unit, scale = normed(inputs)
    gain_grad = jnp.sum(grad * unit, axis=0, keepdims=True)
    bias_grad = jnp.sum(grad, axis=0, keepdims=True)
    inner = grad * affine[0:1]
    shift = jnp.mean(inner, axis=-1, keepdims=True)
    slope = jnp.mean(inner * unit, axis=-1, keepdims=True)
    return scale * (inner - shift - unit * slope), gain_grad, bias_grad


def softmax_all(scores):
    tops = [jnp.max(s, axis=-1, keepdims=True) for s in scores]
    powers = [jnp.exp(s - t) for s, t in zip(scores, tops)]
    sums = [jnp.sum(e, axis=-1, keepdims=True) for e in powers]
    return [low(e / total) for e, total in zip(powers, sums)]


def attend(queries, keys, values, scale, masks):
    scores = [nt(q, k) * scale for q, k in zip(queries, keys)]
    scores = [s if m is None else jnp.where(m, s, masked_score) for s, m in zip(scores, masks)]
    probs = softmax_all(scores)
    return probs, [nn(p, v) for p, v in zip(probs, values)]


def attend_back(queries, keys, values, probs, grads, scale):
    grad_probs = [nt(g, v) for g, v in zip(grads, values)]
    grad_values = [low(tn(p, g)) for p, g in zip(probs, grads)]
    wide = [p.astype(F32) for p in probs]
    inner = [jnp.sum(p * g, axis=-1, keepdims=True) for p, g in zip(wide, grad_probs)]
    grad_scores = [low(p * (g - i)) for p, g, i in zip(wide, grad_probs, inner)]
    grad_queries = [low(nn(g, k) * scale) for g, k in zip(grad_scores, keys)]
    grad_keys = [low(tn(g, q) * scale) for g, q in zip(grad_scores, queries)]
    return grad_queries, grad_keys, grad_values


def side(ref, row, width, count):
    return jnp.concatenate([ref[row + b * width : row + (b + 1) * width, :] for b in range(count)], axis=1)


def fetch(step, order, parts, buffer, sems):
    copies = [
        (order.index(quarter), pltpu.make_async_copy(ref, buffer.at[order.index(quarter), pl.ds(row, ref.shape[0])], sems.at[i]))
        for i, (quarter, row, ref) in enumerate(parts)
    ]
    copies.sort(key=lambda entry: entry[0])

    @pl.when(step == 0)
    def begin():
        for unused, copy in copies:
            copy.start()

    for at in range(QUARTERS):

        @pl.when(step == at)
        def arrive():
            for slot, copy in copies:
                if slot == at:
                    copy.wait()


def store_grad(step, buffer, send, keep, sems):
    copies = [
        pltpu.make_async_copy(buffer.at[at], (send if at < 2 else keep).at[at % 2], sems.at[at]) for at in range(QUARTERS)
    ]
    for at in range(QUARTERS):

        @pl.when(step == at)
        def leave():
            copies[at].start()

    @pl.when(step == QUARTERS - 1)
    def finish():
        for copy in copies:
            copy.wait()


def put(buffer, step, x_at, first, value, depth, padded):
    dp = buffer.shape[2]
    for half in range(2):
        place = lax.bitwise_xor(x_at, half)
        for z in range(dp):
            start = (half * dp + z) * depth
            for b in range(value.shape[1] // BLOCK):
                buffer[step, place, z, pl.ds(first + b * padded, depth), :] = low(
                    value[start : start + depth, b * BLOCK : (b + 1) * BLOCK]
                )


def flip(ref, scratch):
    scratch[...] = ref.T


CROSS_ROWS = 7168
MLP_ROWS = 6656
SELF_ROWS = 6400


def rows_of(pair, size):
    return slice(pair * size, (pair + 1) * size)


def cross_forward(pairs, lens, text, image, text_affine, image_affine, *refs):
    parts, (text_pre, text_one, image_pre, image_one, text_kept, image_kept, text_probs, image_probs), scratch = (
        refs[:6],
        refs[6:14],
        refs[14:],
    )
    weights, text_sum, image_sum, sems = scratch
    step = pl.program_id(0)
    fetch(step, FORWARD, gathered(parts), weights, sems)

    @pl.when(step == 0)
    def begin():
        text_sum[...] = text[...].astype(F32)
        image_sum[...] = image[...].astype(F32)

    w = weights.at[step]
    text_low = text[...]
    image_low = image[...]
    text_kept[0, :, 0:256] = low(nn(text_low, w[0:768, :]))
    text_kept[0, :, 256:512] = low(nn(text_low, w[768:1536, :]))
    text_kept[0, :, 512:768] = low(nn(text_low, w[1536:2304, :]))
    image_kept[0, :, 0:256] = low(nn(image_low, w[2304:3328, :]))
    image_kept[0, :, 256:512] = low(nn(image_low, w[3328:4352, :]))
    image_kept[0, :, 512:768] = low(nn(image_low, w[4352:5376, :]))

    image_mask = lax.broadcasted_iota(jnp.int32, (SLOTS, PADDED), 1) < REGIONS
    slots = lax.broadcasted_iota(jnp.int32, (PADDED, SLOTS), 1)
    units = [(p, h) for p in range(pairs) for h in range(2)]

    def text_part(at):
        return [text_kept[0, rows_of(p, SLOTS), at + h * HEAD : at + (h + 1) * HEAD] for p, h in units]

    def image_part(at):
        return [image_kept[0, rows_of(p, PADDED), at + h * HEAD : at + (h + 1) * HEAD] for p, h in units]

    scale = HEAD**-0.5
    probs, context = attend(text_part(0), image_part(0), image_part(256), scale, [image_mask] * len(units))
    for i, (p, h) in enumerate(units):
        text_probs[0, i] = probs[i]
        text_kept[0, rows_of(p, SLOTS), 768 + h * HEAD : 768 + (h + 1) * HEAD] = low(context[i])
    masks = [slots < lens[p] for p, h in units]
    probs, context = attend(image_part(512), text_part(256), text_part(512), scale, masks)
    for i, (p, h) in enumerate(units):
        image_probs[0, i] = probs[i]
        image_kept[0, rows_of(p, PADDED), 768 + h * HEAD : 768 + (h + 1) * HEAD] = low(context[i])

    text_sum[...] += nn(text_kept[0, :, 768:1024], side(w, 5376, 256, 3))
    image_sum[...] += nn(image_kept[0, :, 768:1024], side(w, 6144, 256, 4))

    @pl.when(step == QUARTERS - 1)
    def finish():
        text_pre[...] = text_sum[...]
        text_one[...] = layer_norm(text_sum[...], text_affine)
        image_pre[...] = image_sum[...]
        image_one[...] = layer_norm(image_sum[...], image_affine)


def gate(hidden):
    half = 0.5 * (1.0 + lax.erf(hidden * (2.0**-0.5)))
    density = jnp.exp(-0.5 * hidden * hidden) * 0.3989422804014327
    return hidden * half, half + hidden * density


def mlp_forward(pairs, text, image, text_affine, image_affine, *refs):
    parts, (text_pre, text_two, image_pre, image_two, text_activ, text_slope, image_activ, image_slope), scratch = (
        refs[:6],
        refs[6:14],
        refs[14:],
    )
    weights, text_sum, image_sum, text_low, image_low, sems = scratch
    step = pl.program_id(0)
    fetch(step, FORWARD, gathered(parts), weights, sems)

    @pl.when(step == 0)
    def begin():
        text_sum[...] = text[...]
        image_sum[...] = image[...]
        text_low[...] = low(text[...])
        image_low[...] = low(image[...])

    w = weights.at[step]
    for b in range(3):
        activ, slope = gate(nn(text_low[...], w[b * 768 : (b + 1) * 768, :]))
        text_activ[0, :, b * 256 : (b + 1) * 256] = low(activ)
        text_slope[0, :, b * 256 : (b + 1) * 256] = low(slope)
    activ, slope = gate(nn(image_low[...], w[4608:5632, :]))
    image_activ[0] = low(activ)
    image_slope[0] = low(slope)
    text_sum[...] += nn(text_activ[0], side(w, 2304, 768, 3))
    image_sum[...] += nn(image_activ[0], side(w, 5632, 256, 4))

    @pl.when(step == QUARTERS - 1)
    def finish():
        text_pre[...] = text_sum[...]
        text_two[...] = layer_norm(text_sum[...], text_affine)
        image_pre[...] = image_sum[...]
        image_two[...] = layer_norm(image_sum[...], image_affine)


def lane_masks():
    lane = lax.broadcasted_iota(jnp.int32, (1, 2 * SELF_HEAD), 1)
    left = (lane < SELF_HEAD).astype(F32)
    return low(left), low(1.0 - left), lane < SELF_HEAD


def both_heads(tile, masks):
    return jnp.concatenate([tile * masks[0], tile * masks[1]], axis=0)


def one_tile(stacked, masks):
    return jnp.where(masks[2], stacked[:SLOTS], stacked[SLOTS:])


def self_forward(pairs, lens, text, image, text_affine, image_affine, text_cot, image_cot, *refs):
    parts = refs[:6]
    (
        text_out,
        image_out,
        text_grad,
        image_grad,
        text_vec,
        image_vec,
        text_q,
        text_k,
        text_v,
        text_c,
        text_probs,
        image_kept,
        image_probs,
    ) = refs[6:19]
    weights, text_sum, image_sum, text_low, image_low, sems = refs[19:]
    step = pl.program_id(0)
    fetch(step, FORWARD, gathered(parts), weights, sems)

    @pl.when(step == 0)
    def begin():
        text_sum[...] = text[...]
        image_sum[...] = image[...]
        text_low[...] = low(text[...])
        image_low[...] = low(image[...])

    w = weights.at[step]
    for n, out in enumerate((text_q, text_k, text_v)):
        wide = jnp.concatenate([w[b * 576 + n * 192 : b * 576 + (n + 1) * 192, :] for b in range(3)], axis=1)
        out[0] = low(nt(text_low[...], wide))
    for n in range(3):
        image_kept[0, :, n * 256 : (n + 1) * 256] = low(nn(image_low[...], w[2304 + n * 1024 : 3328 + n * 1024, :]))

    masks = lane_masks()
    slots = lax.broadcasted_iota(jnp.int32, (1, SLOTS), 1)
    valid = [slots < lens[p] for p in range(pairs)]
    first, last = slice(0, 128), slice(128, 192)
    queries, keys, values, limits = [], [], [], []
    for p in range(pairs):
        rows = rows_of(p, SLOTS)
        queries += [both_heads(text_q[0, rows, first], masks), text_q[0, rows, last]]
        keys += [text_k[0, rows, first], text_k[0, rows, last]]
        values += [text_v[0, rows, first], text_v[0, rows, last]]
        limits += [valid[p], valid[p]]
    probs, context = attend(queries, keys, values, SELF_HEAD**-0.5, limits)
    for p in range(pairs):
        rows = rows_of(p, SLOTS)
        text_probs[0, p, 0:256, :] = probs[2 * p]
        text_probs[0, p, 256:384, :] = probs[2 * p + 1]
        text_c[0, rows, first] = low(one_tile(context[2 * p], masks))
        text_c[0, rows, last] = low(context[2 * p + 1])

    image_mask = lax.broadcasted_iota(jnp.int32, (PADDED, PADDED), 1) < REGIONS
    units = [(p, h) for p in range(pairs) for h in range(2)]

    def image_part(at):
        return [image_kept[0, rows_of(p, PADDED), at + h * HEAD : at + (h + 1) * HEAD] for p, h in units]

    probs, context = attend(image_part(0), image_part(256), image_part(512), HEAD**-0.5, [image_mask] * len(units))
    for i, (p, h) in enumerate(units):
        image_probs[0, i] = probs[i]
        image_kept[0, rows_of(p, PADDED), 768 + h * HEAD : 768 + (h + 1) * HEAD] = low(context[i])

    text_sum[...] += nn(text_c[0], side(w, 1728, 192, 3))
    image_sum[...] += nn(image_kept[0, :, 768:1024], side(w, 5376, 256, 4))

    @pl.when(step == QUARTERS - 1)
    def finish():
        for total, affine, cot, out, grad, vec in (
            (text_sum, text_affine, text_cot, text_out, text_grad, text_vec),
            (image_sum, image_affine, image_cot, image_out, image_grad, image_vec),
        ):
            out[...] = layer_norm(total[...], affine).astype(out.dtype)
            back, gain_grad, bias_grad = norm_back(total[...], affine, cot[...].astype(F32))
            grad[...] = back
            vec[0:1] = gain_grad
            vec[1:2] = bias_grad


def self_back(pairs, x_at, text_g, image_g, text_two, image_two, text_pre, image_pre, text_affine, image_affine, *refs):
    text_q, text_k, text_v, text_c, text_probs, image_kept, image_probs = refs[:7]
    parts = refs[7:13]
    text_n, image_n, text_vec, image_vec, send, keep = refs[13:19]
    (
        weights,
        grads,
        text_sum,
        image_sum,
        text_g_low,
        image_g_low,
        text_g_flip,
        image_g_flip,
        text_flip,
        image_flip,
        text_d,
        image_d,
        sems,
        out_sems,
    ) = refs[19:]
    step = pl.program_id(0)
    fetch(step, BACKWARD, gathered(parts), weights, sems)

    @pl.when(step == 0)
    def begin():
        text_sum[...] = text_g[...]
        image_sum[...] = image_g[...]
        text_g_low[...] = low(text_g[...])
        image_g_low[...] = low(image_g[...])
        text_g_flip[...] = text_g_low[...].T
        image_g_flip[...] = image_g_low[...].T
        text_flip[...] = low(text_two[...]).T
        image_flip[...] = low(image_two[...]).T

    w = weights.at[step]
    x = x_at[0]
    masks = lane_masks()
    first, last = slice(0, 128), slice(128, 192)
    text_dc = low(nt(text_g_low[...], side(w, 1728, 192, 3)))
    queries, keys, values, probs, outer = [], [], [], [], []
    for p in range(pairs):
        rows = rows_of(p, SLOTS)
        queries += [both_heads(text_q[0, rows, first], masks), text_q[0, rows, last]]
        keys += [text_k[0, rows, first], text_k[0, rows, last]]
        values += [text_v[0, rows, first], text_v[0, rows, last]]
        probs += [text_probs[0, p, 0:256, :], text_probs[0, p, 256:384, :]]
        outer += [both_heads(text_dc[rows, first], masks), text_dc[rows, last]]
    grad_q, grad_k, grad_v = attend_back(queries, keys, values, probs, outer, SELF_HEAD**-0.5)
    for p in range(pairs):
        rows = rows_of(p, SLOTS)
        text_d[0, rows, first] = one_tile(grad_q[2 * p], masks)
        text_d[0, rows, last] = grad_q[2 * p + 1]
        for n, grad in ((1, grad_k), (2, grad_v)):
            text_d[n, rows, first] = grad[2 * p]
            text_d[n, rows, last] = grad[2 * p + 1]

    image_dc = low(nt(image_g_low[...], side(w, 5376, 256, 4)))
    units = [(p, h) for p in range(pairs) for h in range(2)]

    def image_part(at):
        return [image_kept[0, rows_of(p, PADDED), at + h * HEAD : at + (h + 1) * HEAD] for p, h in units]

    outer = [image_dc[rows_of(p, PADDED), h * HEAD : (h + 1) * HEAD] for p, h in units]
    found = attend_back(
        image_part(0), image_part(256), image_part(512), [image_probs[0, i] for i in range(len(units))], outer, HEAD**-0.5
    )
    for n in range(3):
        for i, (p, h) in enumerate(units):
            image_d[rows_of(p, PADDED), n * 256 + h * HEAD : n * 256 + (h + 1) * HEAD] = found[n][i]

    gained = text_sum[...]
    for n in range(3):
        wide = jnp.concatenate([w[b * 576 + n * 192 : b * 576 + (n + 1) * 192, :] for b in range(3)], axis=1)
        gained = gained + nn(text_d[n], wide)
    text_sum[...] = gained
    image_sum[...] += nt(image_d[...], side(w, 2304, 1024, 3))

    text_depth, image_depth, text_padded = depths(grads)
    text_w = jnp.concatenate(
        [nn(text_flip[...], text_d[n]) for n in range(3)] + [nn(text_g_flip[...], text_c[0])], axis=1
    )
    put(grads, step, x, 0, text_w, text_depth, text_padded)
    put(grads, step, x, 3 * text_padded, nn(image_flip[...], image_d[...]), image_depth, image_depth)
    put(
        grads,
        step,
        x,
        3 * text_padded + 3 * image_depth,
        nn(image_g_flip[...], image_kept[0, :, 768:1024]),
        image_depth,
        image_depth,
    )
    store_grad(step, grads, send, keep, out_sems)
    leave_norm(step, text_sum, image_sum, text_pre, image_pre, text_affine, image_affine, text_n, image_n, text_vec, image_vec)


def leave_norm(step, text_sum, image_sum, text_pre, image_pre, text_affine, image_affine, text_n, image_n, text_vec, image_vec):
    @pl.when(step == QUARTERS - 1)
    def finish():
        for total, pre, affine, out, vec in (
            (text_sum, text_pre, text_affine, text_n, text_vec),
            (image_sum, image_pre, image_affine, image_n, image_vec),
        ):
            back, gain_grad, bias_grad = norm_back(pre[...], affine, total[...])
            out[...] = back
            vec[0:1] = gain_grad
            vec[1:2] = bias_grad


def depths(grads):
    places = 2 * grads.shape[2]
    text_depth = DT // places
    return text_depth, DV // places, -(-text_depth // 16) * 16


def mlp_back(pairs, x_at, text_g, image_g, text_one, image_one, text_pre, image_pre, text_affine, image_affine, *refs):
    text_activ, text_slope, image_activ, image_slope = refs[:4]
    parts = refs[4:10]
    text_n, image_n, text_vec, image_vec, send, keep = refs[10:16]
    (
        weights,
        grads,
        text_sum,
        image_sum,
        text_g_low,
        image_g_low,
        text_g_flip,
        image_g_flip,
        text_flip,
        image_flip,
        text_d,
        sems,
        out_sems,
    ) = refs[16:]
    step = pl.program_id(0)
    fetch(step, BACKWARD, gathered(parts), weights, sems)

    @pl.when(step == 0)
    def begin():
        text_sum[...] = text_g[...]
        image_sum[...] = image_g[...]
        text_g_low[...] = low(text_g[...])
        image_g_low[...] = low(image_g[...])
        text_g_flip[...] = text_g_low[...].T
        image_g_flip[...] = image_g_low[...].T
        text_flip[...] = low(text_one[...]).T
        image_flip[...] = low(image_one[...]).T

    w = weights.at[step]
    x = x_at[0]
    text_depth, image_depth, text_padded = depths(grads)
    wide = side(w, 2304, 768, 3)
    for b in range(3):
        columns = slice(b * 256, (b + 1) * 256)
        back = nt(text_g_low[...], wide[columns])
        text_d[:, columns] = low(back * text_slope[0, :, columns].astype(F32))
    text_sum[...] += nt(text_d[...], side(w, 0, 768, 3))
    put(grads, step, x, 0, nn(text_flip[...], text_d[...]), text_depth, text_padded)
    put(grads, step, x, 3 * text_padded, nn(text_g_flip[...], text_activ[0]), text_depth, text_padded)
    image_d = low(nt(image_g_low[...], side(w, 5632, 256, 4)) * image_slope[0].astype(F32))
    image_sum[...] += nt(image_d, w[4608:5632, :])
    put(grads, step, x, 6 * text_padded, nn(image_flip[...], image_d), image_depth, image_depth)
    put(grads, step, x, 6 * text_padded + image_depth, nn(image_g_flip[...], image_activ[0]), image_depth, image_depth)
    store_grad(step, grads, send, keep, out_sems)
    leave_norm(step, text_sum, image_sum, text_pre, image_pre, text_affine, image_affine, text_n, image_n, text_vec, image_vec)


def cross_back(pairs, x_at, text_g, image_g, text, image, *refs):
    text_kept, image_kept, text_probs, image_probs = refs[:4]
    parts = refs[4:10]
    text_grad, image_grad, send, keep = refs[10:14]
    (
        weights,
        grads,
        text_sum,
        image_sum,
        text_g_low,
        image_g_low,
        text_g_flip,
        image_g_flip,
        text_flip,
        image_flip,
        text_d,
        image_d,
        sems,
        out_sems,
    ) = refs[14:]
    step = pl.program_id(0)
    fetch(step, BACKWARD, gathered(parts), weights, sems)

    @pl.when(step == 0)
    def begin():
        text_sum[...] = text_g[...]
        image_sum[...] = image_g[...]
        text_g_low[...] = low(text_g[...])
        image_g_low[...] = low(image_g[...])
        text_g_flip[...] = text_g_low[...].T
        image_g_flip[...] = image_g_low[...].T
        text_flip[...] = text[...].T
        image_flip[...] = image[...].T

    w = weights.at[step]
    x = x_at[0]
    text_depth, image_depth, text_padded = depths(grads)
    text_dc = low(nt(text_g_low[...], side(w, 5376, 256, 3)))
    image_dc = low(nt(image_g_low[...], side(w, 6144, 256, 4)))
    units = [(p, h) for p in range(pairs) for h in range(2)]

    def text_part(at):
        return [text_kept[0, rows_of(p, SLOTS), at + h * HEAD : at + (h + 1) * HEAD] for p, h in units]

    def image_part(at):
        return [image_kept[0, rows_of(p, PADDED), at + h * HEAD : at + (h + 1) * HEAD] for p, h in units]

    scale = HEAD**-0.5
    outer = [text_dc[rows_of(p, SLOTS), h * HEAD : (h + 1) * HEAD] for p, h in units]
    probs = [text_probs[0, i] for i in range(len(units))]
    found = attend_back(text_part(0), image_part(0), image_part(256), probs, outer, scale)
    for i, (p, h) in enumerate(units):
        text_d[rows_of(p, SLOTS), h * HEAD : (h + 1) * HEAD] = found[0][i]
        image_d[rows_of(p, PADDED), h * HEAD : (h + 1) * HEAD] = found[1][i]
        image_d[rows_of(p, PADDED), 256 + h * HEAD : 256 + (h + 1) * HEAD] = found[2][i]
    outer = [image_dc[rows_of(p, PADDED), h * HEAD : (h + 1) * HEAD] for p, h in units]
    probs = [image_probs[0, i] for i in range(len(units))]
    found = attend_back(image_part(512), text_part(256), text_part(512), probs, outer, scale)
    for i, (p, h) in enumerate(units):
        image_d[rows_of(p, PADDED), 512 + h * HEAD : 512 + (h + 1) * HEAD] = found[0][i]
        text_d[rows_of(p, SLOTS), 256 + h * HEAD : 256 + (h + 1) * HEAD] = found[1][i]
        text_d[rows_of(p, SLOTS), 512 + h * HEAD : 512 + (h + 1) * HEAD] = found[2][i]

    text_sum[...] += nt(text_d[...], side(w, 0, 768, 3))
    image_sum[...] += nt(image_d[...], side(w, 2304, 1024, 3))
    put(grads, step, x, 0, nn(text_flip[...], text_d[...]), text_depth, text_padded)
    put(grads, step, x, 3 * text_padded, nn(text_g_flip[...], text_kept[0, :, 768:1024]), text_depth, text_padded)
    put(grads, step, x, 4 * text_padded, nn(image_flip[...], image_d[...]), image_depth, image_depth)
    put(
        grads,
        step,
        x,
        4 * text_padded + 3 * image_depth,
        nn(image_g_flip[...], image_kept[0, :, 768:1024]),
        image_depth,
        image_depth,
    )
    store_grad(step, grads, send, keep, out_sems)

    @pl.when(step == QUARTERS - 1)
    def finish():
        text_grad[...] = text_sum[...]
        image_grad[...] = image_sum[...].astype(image_grad.dtype)


def gathered(parts):
    own, near, far, far_rest, corner, corner_rest = parts
    cut = far.shape[0]
    return ((0, 0, own), (1, 0, near), (2, 0, far), (2, cut, far_rest), (3, 0, corner), (3, cut, corner_rest))


ANY = pl.BlockSpec(memory_space=pl.ANY)
SCALARS = pl.BlockSpec(memory_space=pltpu.SMEM)


def whole(array):
    zeros = (0,) * len(array.shape)
    return pl.BlockSpec(array.shape, lambda s: zeros)


def quarter(array, order):
    tail = (0,) * (len(array.shape) - 1)
    if order is FORWARD:
        return pl.BlockSpec((1,) + array.shape[1:], lambda s: (s,) + tail)
    return pl.BlockSpec((1,) + array.shape[1:], lambda s: (lax.rem(2 * s + 1 - lax.div(s, 2), 4),) + tail)


def shape(*dims, of=BF):
    return jax.ShapeDtypeStruct(dims, of)


def run(kernel, pairs, order, operands, outs, scratch, flops):
    def spec(kind, array):
        return {"s": lambda: SCALARS, "w": lambda: whole(array), "q": lambda: quarter(array, order), "a": lambda: ANY}[kind]()

    moved = sum(a.size * a.dtype.itemsize for k, a in operands + outs)
    return pl.pallas_call(
        functools.partial(kernel, pairs),
        grid=(QUARTERS,),
        in_specs=[spec(*entry) for entry in operands],
        out_specs=[spec(*entry) for entry in outs],
        out_shape=[array for unused, array in outs],
        scratch_shapes=scratch,
        compiler_params=pltpu.CompilerParams(dimension_semantics=("arbitrary",), vmem_limit_bytes=60 * 2**20),
        cost_estimate=pl.CostEstimate(flops=flops, bytes_accessed=moved, transcendentals=0),
    )(*[array for unused, array in operands])


def swap(value, axis, apart):
    return lax.ppermute(value, axis, [(i, i ^ apart) for i in range(lax.axis_size(axis))])


def spread(own, place, places, rest):
    cut = own.shape[0] - rest
    near = swap(own, "tensor", 1)
    far = swap(own[:cut], "tensor", 2)
    share = rest // places
    mine = lax.dynamic_slice_in_dim(own, cut + place * share, share, 0)
    far_rest = lax.all_gather(swap(mine, "tensor", 2), ("stream", "dp"), axis=0, tiled=True)
    return own, near, far, far_rest, swap(far, "tensor", 1), swap(far_rest, "tensor", 1)


def fold(send, keep):
    got = swap(send, "tensor", 1)
    depth = send.shape[3]
    half = depth // 32 * 16

    def both(*index):
        return low(keep[index].astype(F32) + got[index].astype(F32))

    def add(left, right):
        return low(left.astype(F32) + right.astype(F32))

    every = slice(None)
    top, bottom = slice(0, half), slice(half, depth)
    by_y = swap(both(1, every, every, top), "tensor", 2)
    by_x = swap(both(every, 1, every, bottom), "stream", 1)
    own_top = both(0, every, every, top)
    own_bottom = both(every, 0, every, bottom)
    then_x = swap(add(own_top[1], by_y[1]), "stream", 1)
    then_y = swap(add(own_bottom[1], by_x[1]), "tensor", 2)

    def three(own, first, second):
        return low(own.astype(F32) + first.astype(F32) + second.astype(F32))

    total = jnp.concatenate([three(own_top[0], by_y[0], then_x), three(own_bottom[0], by_x[0], then_y)], axis=1)
    return lax.psum_scatter(total, "dp", scatter_dimension=0, tiled=True)[0]


def stacked(*pieces):
    return jnp.concatenate(pieces, axis=0)


def column_blocks(matrix):
    return [matrix[:, b * BLOCK : (b + 1) * BLOCK] for b in range(matrix.shape[1] // BLOCK)]


def local(
    text_in,
    image_in,
    lengths,
    text_cot,
    image_cot,
    text_cross_q,
    text_cross_kv,
    text_cross_out,
    text_up,
    text_down,
    text_self_qkv,
    text_self_out,
    text_gain,
    text_bias,
    image_cross_q,
    image_cross_kv,
    image_cross_out,
    image_up,
    image_down,
    image_self_qkv,
    image_self_out,
    image_gain,
    image_bias,
):
    dp = lax.axis_size("dp")
    places = 2 * dp
    x_at = lax.axis_index("stream")
    t_at = lax.axis_index("tensor")
    place = x_at * dp + lax.axis_index("dp")
    text_rows = text_in.shape[0]
    pairs = text_rows // SLOTS
    image_rows = pairs * PADDED
    lens = lax.dynamic_slice_in_dim(lengths, t_at * pairs, pairs, 0)
    x_ref = x_at.astype(jnp.int32).reshape(1)

    def arrive(rows):
        moved = swap(rows, "stream", 1).reshape(pairs, REGIONS, DV)
        return jnp.pad(moved, ((0, 0), (0, PADDED - REGIONS), (0, 0))).reshape(image_rows, DV)

    def leave(rows):
        return swap(rows.reshape(pairs, PADDED, DV)[:, :REGIONS].reshape(pairs * REGIONS, DV), "stream", 1)

    cross_own = stacked(
        text_cross_q[0],
        image_cross_kv[0, :, 0],
        image_cross_kv[0, :, 1],
        text_cross_kv[0, :, 0],
        text_cross_kv[0, :, 1],
        image_cross_q[0],
        *column_blocks(text_cross_out[0]),
        *column_blocks(image_cross_out[0]),
    )
    mlp_own = stacked(
        *column_blocks(text_up[0]), *column_blocks(text_down[0]), image_up[0], *column_blocks(image_down[0])
    )
    self_own = stacked(
        *column_blocks(text_self_qkv[0].transpose(1, 2, 0).reshape(-1, DT)),
        *column_blocks(text_self_out[0]),
        *[image_self_qkv[0, :, n] for n in range(3)],
        *column_blocks(image_self_out[0]),
    )
    image = arrive(image_in)
    cross_w = spread(cross_own, place, places, 3584)
    mlp_w = spread(mlp_own, place, places, 3584)
    self_w = spread(self_own, place, places, 3584)
    image_cot_here = arrive(image_cot)

    def affine(gain, bias, norm):
        return jnp.stack([gain[0, norm], bias[0, norm]]).astype(F32)

    text_affine = [affine(text_gain, text_bias, n) for n in range(3)]
    image_affine = [affine(image_gain, image_bias, n) for n in range(3)]

    def parts(weights):
        return [("a", w) for w in weights]

    def s(value):
        return ("s", value)

    def w(value):
        return ("w", value)

    def q(value):
        return ("q", value)

    def buffer(weights):
        return pltpu.VMEM((QUARTERS, weights[0].shape[0], BLOCK), BF)

    text_wide, image_wide = shape(text_rows, DT, of=F32), shape(image_rows, DV, of=F32)
    text_f32, image_f32 = pltpu.VMEM((text_rows, DT), F32), pltpu.VMEM((image_rows, DV), F32)
    text_bf, image_bf = pltpu.VMEM((text_rows, DT), BF), pltpu.VMEM((image_rows, DV), BF)
    text_tr, image_tr = pltpu.VMEM((DT, text_rows), BF), pltpu.VMEM((DV, image_rows), BF)
    in_sems, out_sems = pltpu.SemaphoreType.DMA((6,)), pltpu.SemaphoreType.DMA((QUARTERS,))
    units = 2 * pairs

    def flops(weights):
        return 2 * QUARTERS * weights[0].size * (text_rows + image_rows) // 2

    text_pre1, text_one, image_pre1, image_one, text_kept, image_kept, text_probs, image_probs = run(
        cross_forward,
        pairs,
        FORWARD,
        [s(lens), w(text_in), w(image), w(text_affine[0]), w(image_affine[0])] + parts(cross_w),
        [
            w(text_wide),
            w(text_wide),
            w(image_wide),
            w(image_wide),
            q(shape(QUARTERS, text_rows, 1024)),
            q(shape(QUARTERS, image_rows, 1024)),
            q(shape(QUARTERS, units, SLOTS, PADDED)),
            q(shape(QUARTERS, units, PADDED, SLOTS)),
        ],
        [buffer(cross_w), text_f32, image_f32, in_sems],
        flops(cross_w),
    )
    text_pre2, text_two, image_pre2, image_two, text_activ, text_slope, image_activ, image_slope = run(
        mlp_forward,
        pairs,
        FORWARD,
        [w(text_one), w(image_one), w(text_affine[1]), w(image_affine[1])] + parts(mlp_w),
        [
            w(text_wide),
            w(text_wide),
            w(image_wide),
            w(image_wide),
            q(shape(QUARTERS, text_rows, 768)),
            q(shape(QUARTERS, text_rows, 768)),
            q(shape(QUARTERS, image_rows, 256)),
            q(shape(QUARTERS, image_rows, 256)),
        ],
        [buffer(mlp_w), text_f32, image_f32, text_bf, image_bf, in_sems],
        flops(mlp_w),
    )
    (
        text_out,
        image_out,
        text_n3,
        image_n3,
        text_vec3,
        image_vec3,
        self_q,
        self_k,
        self_v,
        self_c,
        self_probs,
        self_kept,
        self_image_probs,
    ) = run(
        self_forward,
        pairs,
        FORWARD,
        [
            s(lens),
            w(text_two),
            w(image_two),
            w(text_affine[2]),
            w(image_affine[2]),
            w(text_cot),
            w(image_cot_here),
        ]
        + parts(self_w),
        [
            w(text_wide),
            w(shape(image_rows, DV)),
            w(text_wide),
            w(image_wide),
            w(shape(2, DT, of=F32)),
            w(shape(2, DV, of=F32)),
            q(shape(QUARTERS, text_rows, 192)),
            q(shape(QUARTERS, text_rows, 192)),
            q(shape(QUARTERS, text_rows, 192)),
            q(shape(QUARTERS, text_rows, 192)),
            q(shape(QUARTERS, pairs, 384, SLOTS)),
            q(shape(QUARTERS, image_rows, 1024)),
            q(shape(QUARTERS, units, PADDED, PADDED)),
        ],
        [buffer(self_w), text_f32, image_f32, text_bf, image_bf, in_sems],
        flops(self_w),
    )

    text_depth, image_depth = DT // places, DV // places
    text_padded = -(-text_depth // 16) * 16

    def grad_outs(depth):
        return [("a", shape(2, 2, dp, depth, BLOCK))] * 2

    def back_scratch(weights, depth):
        return [
            buffer(weights),
            pltpu.VMEM((QUARTERS, 2, dp, depth, BLOCK), BF),
            text_f32,
            image_f32,
            text_bf,
            image_bf,
            text_tr,
            image_tr,
            text_tr,
            image_tr,
        ]

    image_out = leave(image_out).astype(F32)
    self_depth = 3 * text_padded + 4 * image_depth
    text_n2, image_n2, text_vec2, image_vec2, send, keep = run(
        self_back,
        pairs,
        BACKWARD,
        [
            s(x_ref),
            w(text_n3),
            w(image_n3),
            w(text_two),
            w(image_two),
            w(text_pre2),
            w(image_pre2),
            w(text_affine[1]),
            w(image_affine[1]),
            q(self_q),
            q(self_k),
            q(self_v),
            q(self_c),
            q(self_probs),
            q(self_kept),
            q(self_image_probs),
        ]
        + parts(self_w),
        [w(text_wide), w(image_wide), w(shape(2, DT, of=F32)), w(shape(2, DV, of=F32))] + grad_outs(self_depth),
        back_scratch(self_w, self_depth)
        + [pltpu.VMEM((3, text_rows, 192), BF), pltpu.VMEM((image_rows, 768), BF), in_sems, out_sems],
        2 * flops(self_w),
    )
    self_grads = fold(send, keep)
    mlp_depth = 6 * text_padded + 2 * image_depth
    text_n1, image_n1, text_vec1, image_vec1, send, keep = run(
        mlp_back,
        pairs,
        BACKWARD,
        [
            s(x_ref),
            w(text_n2),
            w(image_n2),
            w(text_one),
            w(image_one),
            w(text_pre1),
            w(image_pre1),
            w(text_affine[0]),
            w(image_affine[0]),
            q(text_activ),
            q(text_slope),
            q(image_activ),
            q(image_slope),
        ]
        + parts(mlp_w),
        [w(text_wide), w(image_wide), w(shape(2, DT, of=F32)), w(shape(2, DV, of=F32))] + grad_outs(mlp_depth),
        back_scratch(mlp_w, mlp_depth) + [text_bf, in_sems, out_sems],
        2 * flops(mlp_w),
    )
    mlp_grads = fold(send, keep)
    cross_depth = 4 * text_padded + 4 * image_depth
    text_grad, image_grad, send, keep = run(
        cross_back,
        pairs,
        BACKWARD,
        [
            s(x_ref),
            w(text_n1),
            w(image_n1),
            w(text_in),
            w(image),
            q(text_kept),
            q(image_kept),
            q(text_probs),
            q(image_probs),
        ]
        + parts(cross_w),
        [w(text_wide), w(shape(image_rows, DV))] + grad_outs(cross_depth),
        back_scratch(cross_w, cross_depth)
        + [pltpu.VMEM((text_rows, 768), BF), pltpu.VMEM((image_rows, 768), BF), in_sems, out_sems],
        2 * flops(cross_w),
    )
    image_grad = leave(image_grad).astype(F32)
    cross_grads = fold(send, keep)

    def pick(packed, first, count, depth, padded):
        rows = [packed[first + b * padded : first + b * padded + depth] for b in range(count)]
        return jnp.concatenate(rows, axis=1).astype(F32)

    def text_pick(packed, at, count):
        return pick(packed, at * text_padded, count, text_depth, text_padded)

    def image_pick(packed, text_blocks, at, count):
        return pick(packed, text_blocks * text_padded + at * image_depth, count, image_depth, image_depth)

    vec_rows = jnp.concatenate([text_vec1, text_vec2, text_vec3], axis=0).reshape(6, places, text_depth)
    vec_rows = jnp.pad(vec_rows, ((0, 0), (0, 0), (0, image_depth - text_depth)))
    vec_image = jnp.concatenate([image_vec1, image_vec2, image_vec3], axis=0).reshape(6, places, image_depth)
    vectors = lax.psum(jnp.concatenate([vec_rows, vec_image], axis=0).transpose(1, 0, 2), "tensor")
    vectors = lax.psum_scatter(vectors, ("stream", "dp"), scatter_dimension=0, tiled=True)[0]
    text_vectors, image_vectors = vectors[:6, :text_depth], vectors[6:]

    self_text = text_pick(self_grads, 0, 3)
    return (
        text_out,
        image_out,
        text_grad,
        image_grad,
        text_pick(cross_grads, 0, 1)[None],
        image_pick(cross_grads, 4, 0, 2).reshape(1, image_depth, 2, 256),
        text_pick(cross_grads, 3, 1).T[None],
        text_pick(mlp_grads, 0, 3)[None],
        text_pick(mlp_grads, 3, 3).T[None],
        self_text[:, :576].reshape(1, text_depth, 3, 192),
        self_text[:, 576:].T[None],
        text_vectors[0::2][None],
        text_vectors[1::2][None],
        image_pick(cross_grads, 4, 2, 1)[None],
        text_pick(cross_grads, 1, 2).reshape(1, text_depth, 2, 256),
        image_pick(cross_grads, 4, 3, 1).T[None],
        image_pick(mlp_grads, 6, 0, 1)[None],
        image_pick(mlp_grads, 6, 1, 1).T[None],
        image_pick(self_grads, 3, 0, 3).reshape(1, image_depth, 3, 256),
        image_pick(self_grads, 3, 3, 1).T[None],
        image_vectors[0::2][None],
        image_vectors[1::2][None],
    )


def solution(mesh):
    rows = P(("stream", "dp", "tensor"), None)
    wide_in = P(None, None, "tensor")
    group_in = P(None, None, None, "tensor")
    wide_out = P(None, "tensor", None)
    grad_in = P(None, ("stream", "dp"), "tensor")
    grad_group = P(None, ("stream", "dp"), None, "tensor")
    grad_out = P(None, "tensor", ("stream", "dp"))
    vector = P(None, None, ("stream", "dp"))
    weights = (wide_in, group_in, wide_out, wide_in, wide_out, group_in, wide_out, P(), P())
    grads = (grad_in, grad_group, grad_out, grad_in, grad_out, grad_group, grad_out, vector, vector)
    return jax.shard_map(
        local,
        mesh=mesh,
        in_specs=(rows, rows, P(("stream", "dp")), rows, rows) + weights + weights,
        out_specs=(rows, rows, rows, rows) + grads + grads,
        check_vma=False,
    )
```

```python
import functools

import jax
import jax.numpy as jnp
from jax import lax
from jax.experimental import pallas as pl
from jax.experimental.pallas import tpu as pltpu
from jax.sharding import PartitionSpec as P

DT = 768
DV = 1024
HEAD = 128
SELF_HEAD = 64
SLOTS = 128
REGIONS = 37
PADDED = 48
QUARTERS = 4
BLOCK = 256

norm_eps = 1e-05
masked_score = -1e30

BF = jnp.bfloat16
F32 = jnp.float32
FORWARD = (0, 1, 2, 3)
BACKWARD = (1, 3, 0, 2)


def nn(left, right):
    return lax.dot_general(left, right, (((1,), (0,)), ((), ())), preferred_element_type=F32)


def nt(left, right):
    return lax.dot_general(left, right, (((1,), (1,)), ((), ())), preferred_element_type=F32)


def tn(left, right):
    return lax.dot_general(left, right, (((0,), (0,)), ((), ())), preferred_element_type=F32)


def low(value):
    return value.astype(BF)


def normed(inputs):
    centered = inputs - jnp.mean(inputs, axis=-1, keepdims=True)
    scale = lax.rsqrt(jnp.mean(centered * centered, axis=-1, keepdims=True) + norm_eps)
    return centered * scale, scale


def norm_back(unit, scale, gain, grad, vec):
    vec[0:1] = jnp.sum(grad * unit, axis=0, keepdims=True)
    vec[1:2] = jnp.sum(grad, axis=0, keepdims=True)
    inner = grad * gain
    shift = jnp.mean(inner, axis=-1, keepdims=True)
    slope = jnp.mean(inner * unit, axis=-1, keepdims=True)
    return scale * (inner - shift - unit * slope)


def softmax_all(scores):
    tops = [jnp.max(s, axis=-1, keepdims=True) for s in scores]
    powers = [jnp.exp(s - t) for s, t in zip(scores, tops)]
    sums = [jnp.sum(e, axis=-1, keepdims=True) for e in powers]
    return [low(e / total) for e, total in zip(powers, sums)]


def attend(queries, keys, values, scale, masks):
    scores = [nt(q, k) * scale for q, k in zip(queries, keys)]
    scores = [s if m is None else jnp.where(m, s, masked_score) for s, m in zip(scores, masks)]
    probs = softmax_all(scores)
    return probs, [nn(p, v) for p, v in zip(probs, values)]


def attend_back(queries, keys, values, probs, grads, scale):
    grad_probs = [nt(g, v) for g, v in zip(grads, values)]
    grad_values = [low(tn(p, g)) for p, g in zip(probs, grads)]
    wide = [p.astype(F32) for p in probs]
    inner = [jnp.sum(p * g, axis=-1, keepdims=True) for p, g in zip(wide, grad_probs)]
    grad_scores = [low(p * (g - i)) for p, g, i in zip(wide, grad_probs, inner)]
    grad_queries = [low(nn(g, k) * scale) for g, k in zip(grad_scores, keys)]
    grad_keys = [low(tn(g, q) * scale) for g, q in zip(grad_scores, queries)]
    return grad_queries, grad_keys, grad_values


def side(ref, row, width, count):
    return jnp.concatenate([ref[row + b * width : row + (b + 1) * width, :] for b in range(count)], axis=1)


def rows_of(pair, size):
    return slice(pair * size, (pair + 1) * size)


def fetch(step, order, parts, buffer, sems):
    copies = [
        (order.index(quarter), pltpu.make_async_copy(ref, buffer.at[order.index(quarter), pl.ds(row, ref.shape[0])], sems.at[i]))
        for i, (quarter, row, ref) in enumerate(parts)
    ]
    copies.sort(key=lambda entry: entry[0])

    @pl.when(step == 0)
    def begin():
        for unused, copy in copies:
            copy.start()

    for at in range(QUARTERS):

        @pl.when(step == at)
        def arrive():
            for slot, copy in copies:
                if slot == at:
                    copy.wait()


def leave_quarter(step, buffer, near, keep, sems, copies):
    kept = [pltpu.make_async_copy(buffer.at[at], keep.at[at - 2], sems.at[at - 2]) for at in (2, 3)]
    for at in range(QUARTERS):

        @pl.when(step == at)
        def leave():
            (copies[at] if at < 2 else kept[at - 2]).start()

    @pl.when(step == QUARTERS - 1)
    def finish():
        for copy in list(copies) + kept:
            copy.wait()


def affine_row(gain, bias, norm):
    return gain[0, norm : norm + 1, :].astype(F32), bias[0, norm : norm + 1, :].astype(F32)


def leave_blocks(ref, row, value):
    size = value.shape[0]
    for b in range(value.shape[1] // BLOCK):
        ref[row + b * size : row + (b + 1) * size, :] = value[:, b * BLOCK : (b + 1) * BLOCK]


MESH = pl.DeviceIdType.MESH


def partners():
    t = lax.axis_index("tensor")
    return {"tensor": lax.bitwise_xor(t, 1)}, {"tensor": lax.bitwise_xor(t, 2)}, {"stream": lax.bitwise_xor(lax.axis_index("stream"), 1)}


def greet(*others):
    barrier = pltpu.get_barrier_semaphore()
    for other in others:
        pl.semaphore_signal(barrier, inc=1, device_id=other, device_id_type=MESH)
    pl.semaphore_wait(barrier, len(others))


def sender(send_sems, recv_sems):
    def copy(number, source, target, to):
        return pltpu.make_async_remote_copy(
            src_ref=source,
            dst_ref=target,
            send_sem=send_sems.at[number],
            recv_sem=recv_sems.at[number],
            device_id=to,
            device_id_type=MESH,
        )

    return copy


def pack(pieces, places, rest, ids):
    total = sum(m.size for m in pieces) // BLOCK
    cut, share = total - rest, rest // places

    def kernel(ids, *refs):
        sources, (own, first, mine) = refs[: len(pieces)], refs[len(pieces) :]
        row = 0
        for ref in sources:
            leave_blocks(own, row, ref[...])
            row += ref.size // BLOCK
        first[...] = own[0:cut, :]
        mine[...] = own[pl.ds(pl.multiple_of(cut + ids[1] * share, 16), share), :]

    return run(
        kernel,
        None,
        [s(ids)] + [w(m) for m in pieces],
        [w(shape(total, BLOCK)), w(shape(cut, BLOCK)), w(shape(share, BLOCK))],
        [],
        3,
    )


def cross_block(pairs, first, lengths, text, image, matrices, text_kept, image_kept, text_probs, image_probs, part):
    wq, wkv_text, wkv_image, wq_image, w_out, w_out_image = matrices
    text_low = text[...]
    image_low = image[...]
    text_kept[:, 0:256] = low(nn(text_low, wq[...]))
    text_kept[:, 256:768] = low(nn(text_low, wkv_text[...]))
    image_kept[:, 0:512] = low(nn(image_low, wkv_image[...]))
    image_kept[:, 512:768] = low(nn(image_low, wq_image[...]))

    image_mask = lax.broadcasted_iota(jnp.int32, (SLOTS, PADDED), 1) < REGIONS
    slots = lax.broadcasted_iota(jnp.int32, (PADDED, SLOTS), 1)
    units = [(p, h) for p in range(pairs) for h in range(2)]

    def text_part(at):
        return [text_kept[rows_of(p, SLOTS), at + h * HEAD : at + (h + 1) * HEAD] for p, h in units]

    def image_part(at):
        return [image_kept[rows_of(p, PADDED), at + h * HEAD : at + (h + 1) * HEAD] for p, h in units]

    scale = HEAD**-0.5
    probs, context = attend(text_part(0), image_part(0), image_part(256), scale, [image_mask] * len(units))
    for i, (p, h) in enumerate(units):
        text_probs[i] = probs[i]
        text_kept[rows_of(p, SLOTS), 768 + h * HEAD : 768 + (h + 1) * HEAD] = low(context[i])
    limits = [lengths[first + p] for p in range(pairs)]
    masks = [slots < limits[p] for p, h in units]
    probs, context = attend(image_part(512), text_part(256), text_part(512), scale, masks)
    for i, (p, h) in enumerate(units):
        image_probs[i] = probs[i]
        image_kept[rows_of(p, PADDED), 768 + h * HEAD : 768 + (h + 1) * HEAD] = low(context[i])
    leave_blocks(part, 0, low(nn(text_kept[:, 768:1024], w_out[...])))
    leave_blocks(part, 3 * text.shape[0], low(nn(image_kept[:, 768:1024], w_out_image[...])))


def cross_forward(pairs, lengths, text, image, *refs):
    matrices = refs[:6]
    text_pre, image_pre, image_own = refs[6:9]
    outs = refs[9:15]
    texts, images, text_kept, image_kept, text_probs, image_probs, parts, total, got, send_sems, recv_sems, out_sems = refs[15:]
    core, y, x = partners()
    copy = sender(send_sems, recv_sems)
    text_core = copy(0, text, texts.at[1], core)
    text_y = copy(1, text, texts.at[2], y)
    image_x = copy(2, image, images.at[0], x)
    image_core = copy(3, images.at[0], images.at[1], core)
    image_y = copy(4, images.at[0], images.at[2], y)
    text_corner = copy(5, texts.at[2], texts.at[3], core)
    image_corner = copy(6, images.at[2], images.at[3], core)
    near_part = copy(7, parts.at[1], got.at[0], core)
    corner_part = copy(8, parts.at[3], got.at[1], core)
    far_part = copy(9, total, got.at[2], y)

    greet(core, y, x)
    image_x.start()
    text_y.start()
    text_core.start()
    texts[0] = text[...]
    image_x.wait()
    image_y.start()
    image_core.start()

    def block(j, unused):
        @pl.when(j == 1)
        def near():
            text_core.wait()
            image_core.wait()

        @pl.when(j == 2)
        def far():
            text_y.wait()
            text_corner.start()
            image_y.wait()
            image_corner.start()

        @pl.when(j == 3)
        def corner():
            text_corner.wait()
            image_corner.wait()

        cross_block(
            pairs,
            lax.bitwise_xor(lax.axis_index("tensor"), j) * pairs,
            lengths,
            texts.at[j],
            images.at[j],
            matrices,
            text_kept.at[j],
            image_kept.at[j],
            text_probs.at[j],
            image_probs.at[j],
            parts.at[j],
        )

        @pl.when(j == 1)
        def near_done():
            near_part.start()

        return unused

    lax.fori_loop(0, QUARTERS, block, 0)
    corner_part.start()
    leaving = [
        pltpu.make_async_copy(source, out, out_sems.at[i])
        for i, (source, out) in enumerate(
            zip((texts, images, text_kept, image_kept, text_probs, image_probs), outs)
        )
    ]
    for leave in leaving:
        leave.start()
    corner_part.wait()
    total[...] = add(parts[2], got[1])
    far_part.start()
    near_part.wait()
    size, image_size = text.shape[0], image.shape[0]
    below = 3 * size
    image_own[...] = images[0]

    def summed(row, depth, count, start):
        for ref in (parts.at[0], got.at[0]):
            start = start + side(ref, row, depth, count).astype(F32)
        return start

    text_pre[...] = summed(0, size, 3, text[...].astype(F32))
    image_pre[...] = summed(below, image_size, 4, images[0].astype(F32))
    far_part.wait()
    text_pre[...] += side(got.at[2], 0, size, 3).astype(F32)
    image_pre[...] += side(got.at[2], below, image_size, 4).astype(F32)
    for leave in leaving:
        leave.wait()


def cross_block_back(pairs, grad, matrices, text_kept, image_kept, text_probs, image_probs, text_d, image_d, part):
    wq, wkv_text, wkv_image, wq_image, w_out, w_out_image = matrices
    text_rows, image_rows = text_kept.shape[0], image_kept.shape[0]
    text_dc = low(nt(side(grad, 0, text_rows, 3), w_out[...]))
    image_dc = low(nt(side(grad, 3 * text_rows, image_rows, 4), w_out_image[...]))
    units = [(p, h) for p in range(pairs) for h in range(2)]

    def text_part(at):
        return [text_kept[rows_of(p, SLOTS), at + h * HEAD : at + (h + 1) * HEAD] for p, h in units]

    def image_part(at):
        return [image_kept[rows_of(p, PADDED), at + h * HEAD : at + (h + 1) * HEAD] for p, h in units]

    scale = HEAD**-0.5
    outer = [text_dc[rows_of(p, SLOTS), h * HEAD : (h + 1) * HEAD] for p, h in units]
    probs = [text_probs[i] for i in range(len(units))]
    found = attend_back(text_part(0), image_part(0), image_part(256), probs, outer, scale)
    for i, (p, h) in enumerate(units):
        text_d[rows_of(p, SLOTS), h * HEAD : (h + 1) * HEAD] = found[0][i]
        image_d[rows_of(p, PADDED), h * HEAD : (h + 1) * HEAD] = found[1][i]
        image_d[rows_of(p, PADDED), 256 + h * HEAD : 256 + (h + 1) * HEAD] = found[2][i]
    outer = [image_dc[rows_of(p, PADDED), h * HEAD : (h + 1) * HEAD] for p, h in units]
    probs = [image_probs[i] for i in range(len(units))]
    found = attend_back(image_part(512), text_part(256), text_part(512), probs, outer, scale)
    for i, (p, h) in enumerate(units):
        image_d[rows_of(p, PADDED), 512 + h * HEAD : 512 + (h + 1) * HEAD] = found[0][i]
        text_d[rows_of(p, SLOTS), 256 + h * HEAD : 256 + (h + 1) * HEAD] = found[1][i]
        text_d[rows_of(p, SLOTS), 512 + h * HEAD : 512 + (h + 1) * HEAD] = found[2][i]
    text_dx = nt(text_d[:, 0:256], wq[...]) + nt(text_d[:, 256:768], wkv_text[...])
    image_dx = nt(image_d[:, 0:512], wkv_image[...]) + nt(image_d[:, 512:768], wq_image[...])
    leave_blocks(part, 0, low(text_dx))
    leave_blocks(part, 3 * text_rows, low(image_dx))


def cross_back(pairs, grad, vectors, text_kept, image_kept, text_probs, image_probs, *refs):
    matrices = refs[:6]
    grads_out, text_d_out, image_d_out, own_sum, total, vector_sum = refs[6:12]
    grads, text_d, image_d, parts, got, got_vectors, send_sems, recv_sems, out_sems = refs[12:]
    core, y, unused_x = partners()
    copy = sender(send_sems, recv_sems)
    to_core = copy(0, grad, grads.at[1], core)
    to_y = copy(1, grad, grads.at[2], y)
    corner = copy(2, grads.at[2], grads.at[3], core)
    near_part = copy(3, parts.at[1], got.at[0], core)
    corner_part = copy(4, parts.at[3], got.at[1], core)
    vectors_core = copy(5, vectors, got_vectors.at[0], core)
    vectors_y = copy(6, vector_sum, got_vectors.at[1], y)
    greet(core, y)
    vectors_core.start()
    to_y.start()
    to_core.start()
    grads[0] = grad[...]
    vectors_core.wait()
    vector_sum[...] = vectors[...] + got_vectors[0]
    vectors_y.start()

    def block(j, unused):
        @pl.when(j == 1)
        def near():
            to_core.wait()

        @pl.when(j == 2)
        def far():
            to_y.wait()
            corner.start()

        @pl.when(j == 3)
        def last():
            corner.wait()

        cross_block_back(
            pairs,
            grads.at[j],
            matrices,
            text_kept.at[j],
            image_kept.at[j],
            text_probs.at[j],
            image_probs.at[j],
            text_d.at[j],
            image_d.at[j],
            parts.at[j],
        )

        @pl.when(j == 1)
        def near_done():
            near_part.start()

        return unused

    lax.fori_loop(0, QUARTERS, block, 0)
    corner_part.start()
    leaving = [
        pltpu.make_async_copy(source, out, out_sems.at[i])
        for i, (source, out) in enumerate(((grads, grads_out), (text_d, text_d_out), (image_d, image_d_out)))
    ]
    for leave in leaving:
        leave.start()
    near_part.wait()
    own_sum[...] = parts[0].astype(F32) + got[0].astype(F32)
    vectors_y.wait()
    vector_sum[...] += got_vectors[1]
    corner_part.wait()
    total[...] = add(parts[2], got[1])
    for leave in leaving:
        leave.wait()


def cross_last(total, own_sum, vector_keep, vector_send, text_n, image_n, texts, images, grads, text_kept, image_kept, text_d, image_d, *refs):
    text_grad, image_grad, text_keep, text_send, image_keep, image_send = refs[:6]
    got, text_flip, text_g_flip, image_flip, image_g_flip, send_sems, recv_sems = refs[6:]
    unused_core, y, unused_x = partners()
    copy = sender(send_sems, recv_sems)
    far = copy(0, total, got, y)
    greet(y)
    far.start()
    size, image_size = texts.shape[1], images.shape[1]
    below = 3 * size
    for j in range(QUARTERS):
        text_flip[:, rows_of(j, size)] = texts[j].T
        image_flip[:, rows_of(j, image_size)] = images[j].T
        for b in range(3):
            text_g_flip[rows_of(b, BLOCK), rows_of(j, size)] = grads[j, rows_of(b, size), :].T
        for b in range(4):
            start = below + b * image_size
            image_g_flip[rows_of(b, BLOCK), rows_of(j, image_size)] = grads[j, start : start + image_size, :].T
    at = lax.axis_index("stream")
    for flip, g_flip, d, kept, keep, send in (
        (text_flip, text_g_flip, text_d, text_kept, text_keep, text_send),
        (image_flip, image_g_flip, image_d, image_kept, image_keep, image_send),
    ):
        dp = keep.shape[0]
        half = flip.shape[0] // 2
        depth = half // dp
        padded = -(-depth // 16) * 16
        rows = flip.shape[1]
        outer = d[...].reshape(rows, 768)
        context = kept[:, :, 768:1024].reshape(rows, 256)
        for out, apart in ((send, 1), (keep, 0)):
            start = pl.multiple_of(lax.bitwise_xor(at, apart) * half, 128)
            found = nn(flip[pl.ds(start, half), :], outer)
            last = nn(g_flip[pl.ds(start, half), :], context)
            for z in range(dp):
                taken = slice(z * depth, (z + 1) * depth)
                for b in range(3):
                    out[z, b * padded : b * padded + depth, :] = low(found[taken, b * BLOCK : (b + 1) * BLOCK])
                out[z, 3 * padded : 3 * padded + depth, :] = low(last[taken])
    for out, vector in ((text_keep, vector_keep), (text_send, vector_send)):
        below_all = out.shape[1] - vector.shape[1]
        for z in range(out.shape[0]):
            out[z, below_all:, :] = vector[z]
    far.wait()
    text_grad[...] = text_n[...] + side(own_sum, 0, size, 3) + side(got, 0, size, 3).astype(F32)
    image_grad[...] = low(image_n[...] + side(own_sum, below, image_size, 4) + side(got, below, image_size, 4).astype(F32))


def gate(hidden):
    half = 0.5 * (1.0 + lax.erf(hidden * (2.0**-0.5)))
    density = jnp.exp(-0.5 * hidden * hidden) * 0.3989422804014327
    return hidden * half, half + hidden * density


def mlp_forward(pairs, text_pre, image_pre, text_gain, text_bias, image_gain, image_bias, *refs):
    parts = refs[:6]
    text_low, image_low, text_next, image_next = refs[6:10]
    text_activ, text_slope, image_activ, image_slope = refs[10:14]
    weights, sems = refs[14:]
    step = pl.program_id(0)
    fetch(step, FORWARD, gathered(parts), weights, sems)

    @pl.when(step == 0)
    def begin():
        for pre, gain, bias, rounded, total in (
            (text_pre, text_gain, text_bias, text_low, text_next),
            (image_pre, image_gain, image_bias, image_low, image_next),
        ):
            g, b = affine_row(gain, bias, 0)
            one = normed(pre[...])[0] * g + b
            total[...] = one
            rounded[...] = low(one)

    w = weights.at[step]
    for b in range(3):
        activ, slope = gate(nn(text_low[...], w[b * 768 : (b + 1) * 768, :]))
        text_activ[0, :, b * 256 : (b + 1) * 256] = low(activ)
        text_slope[0, :, b * 256 : (b + 1) * 256] = low(slope)
    activ, slope = gate(nn(image_low[...], w[4608:5632, :]))
    image_activ[0] = low(activ)
    image_slope[0] = low(slope)
    text_next[...] += nn(text_activ[0], side(w, 2304, 768, 3))
    image_next[...] += nn(image_activ[0], side(w, 5632, 256, 4))


def lane_masks():
    lane = lax.broadcasted_iota(jnp.int32, (1, 2 * SELF_HEAD), 1)
    left = (lane < SELF_HEAD).astype(F32)
    return low(left), low(1.0 - left), lane < SELF_HEAD


def both_heads(tile, masks):
    return jnp.concatenate([tile * masks[0], tile * masks[1]], axis=0)


def one_tile(stacked, masks):
    return jnp.where(masks[2], stacked[:SLOTS], stacked[SLOTS:])


def self_forward(pairs, ids, lengths, text_pre, image_pre, text_gain, text_bias, image_gain, image_bias, text_cot, image_cot, *refs):
    parts = refs[:6]
    (
        text_out,
        image_out,
        text_grad,
        image_grad,
        text_vec,
        image_vec,
        rounded,
        text_q,
        text_k,
        text_v,
        text_c,
        text_probs,
        image_kept,
        image_probs,
    ) = refs[6:20]
    weights, text_sum, image_sum, text_low, image_low, sems = refs[20:]
    step = pl.program_id(0)
    fetch(step, FORWARD, gathered(parts), weights, sems)
    text_rows, image_rows = text_pre.shape[0], image_pre.shape[0]

    @pl.when(step == 0)
    def begin():
        for pre, gain, bias, total, lower, at in (
            (text_pre, text_gain, text_bias, text_sum, text_low, 0),
            (image_pre, image_gain, image_bias, image_sum, image_low, 6 * text_rows),
        ):
            g, b = affine_row(gain, bias, 1)
            two = normed(pre[...])[0] * g + b
            total[...] = two
            lower[...] = low(two)
            leave_blocks(rounded, at, low(two))

    w = weights.at[step]
    for n, out in enumerate((text_q, text_k, text_v)):
        wide = jnp.concatenate([w[b * 576 + n * 192 : b * 576 + (n + 1) * 192, :] for b in range(3)], axis=1)
        out[0] = low(nt(text_low[...], wide))
    for n in range(3):
        image_kept[0, :, n * 256 : (n + 1) * 256] = low(nn(image_low[...], w[2304 + n * 1024 : 3328 + n * 1024, :]))

    masks = lane_masks()
    slots = lax.broadcasted_iota(jnp.int32, (1, SLOTS), 1)
    base = ids[2]
    valid = [slots < lengths[base + p] for p in range(pairs)]
    first, last = slice(0, 128), slice(128, 192)
    queries, keys, values, limits = [], [], [], []
    for p in range(pairs):
        rows = rows_of(p, SLOTS)
        queries += [both_heads(text_q[0, rows, first], masks), text_q[0, rows, last]]
        keys += [text_k[0, rows, first], text_k[0, rows, last]]
        values += [text_v[0, rows, first], text_v[0, rows, last]]
        limits += [valid[p], valid[p]]
    probs, context = attend(queries, keys, values, SELF_HEAD**-0.5, limits)
    for p in range(pairs):
        rows = rows_of(p, SLOTS)
        text_probs[0, p, 0:256, :] = probs[2 * p]
        text_probs[0, p, 256:384, :] = probs[2 * p + 1]
        text_c[0, rows, first] = low(one_tile(context[2 * p], masks))
        text_c[0, rows, last] = low(context[2 * p + 1])

    image_mask = lax.broadcasted_iota(jnp.int32, (PADDED, PADDED), 1) < REGIONS
    units = [(p, h) for p in range(pairs) for h in range(2)]

    def image_part(at):
        return [image_kept[0, rows_of(p, PADDED), at + h * HEAD : at + (h + 1) * HEAD] for p, h in units]

    probs, context = attend(image_part(0), image_part(256), image_part(512), HEAD**-0.5, [image_mask] * len(units))
    for i, (p, h) in enumerate(units):
        image_probs[0, i] = probs[i]
        image_kept[0, rows_of(p, PADDED), 768 + h * HEAD : 768 + (h + 1) * HEAD] = low(context[i])

    text_sum[...] += nn(text_c[0], side(w, 1728, 192, 3))
    image_sum[...] += nn(image_kept[0, :, 768:1024], side(w, 5376, 256, 4))

    @pl.when(step == QUARTERS - 1)
    def finish():
        for total, gain, bias, cot, out, grad, vec, at in (
            (text_sum, text_gain, text_bias, text_cot, text_out, text_grad, text_vec, 3 * text_rows),
            (image_sum, image_gain, image_bias, image_cot, image_out, image_grad, image_vec, 6 * text_rows + 4 * image_rows),
        ):
            g, b = affine_row(gain, bias, 2)
            unit, scale = normed(total[...])
            out[...] = (unit * g + b).astype(out.dtype)
            back = norm_back(unit, scale, g, cot[...].astype(F32), vec)
            grad[...] = back
            leave_blocks(rounded, at, low(back))


def self_back(pairs, text_g, image_g, text_pre, image_pre, text_gain, image_gain, *refs):
    text_q, text_k, text_v, text_c, text_probs, image_kept, image_probs = refs[:7]
    parts = refs[7:13]
    text_n, image_n, text_vec, image_vec, near, keep = refs[13:19]
    weights, found, text_sum, image_sum, text_g_low, image_g_low, text_d, image_d, sems, out_sems, send_sems, recv_sems = refs[19:]
    step = pl.program_id(0)
    fetch(step, BACKWARD, gathered(parts), weights, sems)
    core = partners()[0]
    copy = sender(send_sems, recv_sems)

    @pl.when(step == 0)
    def begin():
        greet(core)
        text_sum[...] = text_g[...]
        image_sum[...] = image_g[...]
        text_g_low[...] = low(text_g[...])
        image_g_low[...] = low(image_g[...])

    w = weights.at[step]
    masks = lane_masks()
    first, last = slice(0, 128), slice(128, 192)
    text_dc = low(nt(text_g_low[...], side(w, 1728, 192, 3)))
    queries, keys, values, probs, outer = [], [], [], [], []
    for p in range(pairs):
        rows = rows_of(p, SLOTS)
        queries += [both_heads(text_q[0, rows, first], masks), text_q[0, rows, last]]
        keys += [text_k[0, rows, first], text_k[0, rows, last]]
        values += [text_v[0, rows, first], text_v[0, rows, last]]
        probs += [text_probs[0, p, 0:256, :], text_probs[0, p, 256:384, :]]
        outer += [both_heads(text_dc[rows, first], masks), text_dc[rows, last]]
    grad_q, grad_k, grad_v = attend_back(queries, keys, values, probs, outer, SELF_HEAD**-0.5)
    size = text_g.shape[0]
    for p in range(pairs):
        rows = rows_of(p, SLOTS)
        text_d[0, rows, first] = one_tile(grad_q[2 * p], masks)
        text_d[0, rows, last] = grad_q[2 * p + 1]
        for n, grad in ((1, grad_k), (2, grad_v)):
            text_d[n, rows, first] = grad[2 * p]
            text_d[n, rows, last] = grad[2 * p + 1]

    image_dc = low(nt(image_g_low[...], side(w, 5376, 256, 4)))
    units = [(p, h) for p in range(pairs) for h in range(2)]

    def image_part(at):
        return [image_kept[0, rows_of(p, PADDED), at + h * HEAD : at + (h + 1) * HEAD] for p, h in units]

    outer = [image_dc[rows_of(p, PADDED), h * HEAD : (h + 1) * HEAD] for p, h in units]
    given = attend_back(
        image_part(0), image_part(256), image_part(512), [image_probs[0, i] for i in range(len(units))], outer, HEAD**-0.5
    )
    for n in range(3):
        for i, (p, h) in enumerate(units):
            image_d[rows_of(p, PADDED), n * 256 + h * HEAD : n * 256 + (h + 1) * HEAD] = given[n][i]

    gained = text_sum[...]
    for n in range(3):
        wide = jnp.concatenate([w[b * 576 + n * 192 : b * 576 + (n + 1) * 192, :] for b in range(3)], axis=1)
        gained = gained + nn(text_d[n], wide)
    text_sum[...] = gained
    image_sum[...] += nt(image_d[...], side(w, 2304, 1024, 3))

    slot = found.at[step]
    slot[0:size, 0:128] = text_d[0, :, first]
    slot[0:size, 128:256] = text_d[1, :, first]
    slot[size : 2 * size, 0:128] = text_d[2, :, first]
    slot[size : 2 * size, 128:256] = text_c[0, :, first]
    slot[2 * size : 3 * size, 0:128] = jnp.concatenate([text_d[0, :, last], text_d[1, :, last]], axis=1)
    slot[2 * size : 3 * size, 128:256] = jnp.concatenate([text_d[2, :, last], text_c[0, :, last]], axis=1)
    leave_blocks(slot, 3 * size, image_d[...])
    leave_blocks(slot, 3 * size + 3 * image_g.shape[0], image_kept[0, :, 768:1024])
    leave_quarter(step, found, near, keep, out_sems, [copy(n, found.at[n], near.at[n], core) for n in range(2)])

    @pl.when(step == QUARTERS - 1)
    def finish():
        leave_norm(1, text_sum, image_sum, text_pre, image_pre, text_gain, image_gain, text_n, image_n, text_vec, image_vec)


def leave_norm(norm, text_sum, image_sum, text_pre, image_pre, text_gain, image_gain, text_n, image_n, text_vec, image_vec):
    for total, pre, gain, out, vec in (
        (text_sum, text_pre, text_gain, text_n, text_vec),
        (image_sum, image_pre, image_gain, image_n, image_vec),
    ):
        unit, scale = normed(pre[...])
        out[...] = norm_back(unit, scale, gain[0, norm : norm + 1, :].astype(F32), total[...], vec)


def mlp_back(pairs, text_g, image_g, text_one, image_one, text_pre, image_pre, text_gain, image_gain, *refs):
    text_activ, text_slope, image_activ, image_slope = refs[:4]
    parts = refs[4:10]
    text_n, image_n, next_low, text_vec, image_vec, rounded, rounded_near, near, keep = refs[10:19]
    weights, found, text_sum, image_sum, text_g_low, image_g_low, text_d, sems, out_sems, send_sems, recv_sems = refs[19:]
    step = pl.program_id(0)
    fetch(step, BACKWARD, gathered(parts), weights, sems)
    size, image_size = text_g.shape[0], image_g.shape[0]
    core = partners()[0]
    copy = sender(send_sems, recv_sems)
    rounded_copy = copy(2, rounded, rounded_near, core)

    @pl.when(step == 0)
    def begin():
        text_sum[...] = text_g[...]
        image_sum[...] = image_g[...]
        text_g_low[...] = low(text_g[...])
        image_g_low[...] = low(image_g[...])
        leave_blocks(rounded, 0, text_one[...])
        leave_blocks(rounded, 3 * size, text_g_low[...])
        leave_blocks(rounded, 6 * size, image_one[...])
        leave_blocks(rounded, 6 * size + 4 * image_size, image_g_low[...])
        greet(core)
        rounded_copy.start()

    w = weights.at[step]
    slot = found.at[step]
    wide = side(w, 2304, 768, 3)
    for b in range(3):
        columns = slice(b * 256, (b + 1) * 256)
        back = nt(text_g_low[...], wide[columns])
        text_d[:, columns] = low(back * text_slope[0, :, columns].astype(F32))
    text_sum[...] += nt(text_d[...], side(w, 0, 768, 3))
    image_d = low(nt(image_g_low[...], side(w, 5632, 256, 4)) * image_slope[0].astype(F32))
    image_sum[...] += nt(image_d, w[4608:5632, :])
    leave_blocks(slot, 0, text_d[...])
    leave_blocks(slot, 3 * size, text_activ[0])
    leave_blocks(slot, 6 * size, image_d)
    leave_blocks(slot, 6 * size + image_size, image_activ[0])
    leave_quarter(step, found, near, keep, out_sems, [copy(n, found.at[n], near.at[n], core) for n in range(2)])

    @pl.when(step == QUARTERS - 1)
    def finish():
        rounded_copy.wait()
        leave_norm(0, text_sum, image_sum, text_pre, image_pre, text_gain, image_gain, text_n, image_n, text_vec, image_vec)
        leave_blocks(next_low, 0, low(text_n[...]))
        leave_blocks(next_low, 3 * size, low(image_n[...]))


def weight_grad(is_self, sizes, x_at, own, near, own_quarters, near_quarters, *refs):
    if is_self:
        to_x, own_top, to_z, text_flip, text_g_flip, image_flip, image_g_flip = refs
    else:
        to_y, own_top, to_x, own_bottom, text_flip, text_g_flip, image_flip, image_g_flip = refs
    size, image_size = sizes
    dp = own_top.shape[1]
    x = x_at[0]
    for at, source in ((0, own), (1, near)):
        rows, image_rows = rows_of(at, size), rows_of(at, image_size)
        for b in range(3):
            text_flip[rows_of(b, BLOCK), rows] = source[rows_of(b, size), :].T
            text_g_flip[rows_of(b, BLOCK), rows] = source[rows_of(3 + b, size), :].T
        for b in range(4):
            start = 6 * size
            image_flip[rows_of(b, BLOCK), image_rows] = source[start + b * image_size : start + (b + 1) * image_size, :].T
            start = 6 * size + 4 * image_size
            image_g_flip[rows_of(b, BLOCK), image_rows] = source[start + b * image_size : start + (b + 1) * image_size, :].T

    text_depth, image_depth = DT // (2 * dp), DV // (2 * dp)
    padded = -(-text_depth // 16) * 16

    def write(ref, at, row, depth, value):
        for z in range(dp):
            ref[at, z, row : row + depth, :] = low(value[z * depth : (z + 1) * depth])

    lane = lax.broadcasted_iota(jnp.int32, (1, HEAD), 1) < SELF_HEAD
    for slot in (1, 0):

        def text_block(b):
            return jnp.concatenate([q[slot, rows_of(b, size), :] for q in (own_quarters, near_quarters)], axis=0)

        def image_block(b, text_blocks):
            start = text_blocks * size + b * image_size
            return jnp.concatenate([q[slot, start : start + image_size, :] for q in (own_quarters, near_quarters)], axis=0)

        for apart in range(2):
            half = lax.bitwise_xor(x, apart)
            text_rows = pl.ds(pl.multiple_of(half * (DT // 2), 128), DT // 2)
            image_rows = pl.ds(pl.multiple_of(half * (DV // 2), 128), DV // 2)
            if is_self:
                top, top_at = (to_x, slot) if apart else (own_top, slot)
            else:
                top, top_at = (to_y, apart) if slot else (own_top, apart)
                bottom, bottom_at = (to_x, slot) if apart else (own_bottom, slot)
            text_lhs, image_lhs = text_flip[text_rows, :], image_flip[image_rows, :]
            text_g_lhs, image_g_lhs = text_g_flip[text_rows, :], image_g_flip[image_rows, :]
            if is_self:
                one, two, three = text_block(0), text_block(1), text_block(2)
                write(top, top_at, 0, text_depth, nn(text_lhs, one))
                mixed = jnp.concatenate([nn(text_lhs, two[:, :HEAD]), nn(text_g_lhs, two[:, HEAD:])], axis=1)
                write(top, top_at, padded, text_depth, mixed)
                from_x = nn(text_lhs, three)
                from_g = nn(text_g_lhs, three[:, HEAD:])
                mixed = jnp.concatenate([from_x[:, :HEAD], jnp.where(lane, from_x[:, HEAD:], from_g)], axis=1)
                write(top, top_at, 2 * padded, text_depth, mixed)
                write(top, top_at, 3 * padded, image_depth, nn(image_lhs, image_block(0, 3)))
                for b in range(3):
                    found = nn(image_g_lhs if b == 2 else image_lhs, image_block(1 + b, 3))
                    row = ((2 * slot + apart) * 3 + b) * image_depth
                    for z in range(dp):
                        to_z[z, row : row + image_depth, :] = low(found[z * image_depth : (z + 1) * image_depth])
            else:
                for b in range(3):
                    write(top, top_at, b * padded, text_depth, nn(text_lhs, text_block(b)))
                    write(bottom, bottom_at, b * padded, text_depth, nn(text_g_lhs, text_block(3 + b)))
                write(top, top_at, 3 * padded, image_depth, nn(image_lhs, image_block(0, 6)))
                write(bottom, bottom_at, 3 * padded, image_depth, nn(image_g_lhs, image_block(1, 6)))


def gathered(parts):
    own, near, far, far_rest, corner, corner_rest = parts
    cut = far.shape[0]
    return ((0, 0, own), (1, 0, near), (2, 0, far), (2, cut, far_rest), (3, 0, corner), (3, cut, corner_rest))


ANY = pl.BlockSpec(memory_space=pl.ANY)
SCALARS = pl.BlockSpec(memory_space=pltpu.SMEM)


def whole(array):
    zeros = (0,) * len(array.shape)
    return pl.BlockSpec(array.shape, lambda *s: zeros)


def quarter(array, order):
    tail = (0,) * (len(array.shape) - 1)
    if order is FORWARD:
        return pl.BlockSpec((1,) + array.shape[1:], lambda s: (s,) + tail)
    return pl.BlockSpec((1,) + array.shape[1:], lambda s: (lax.rem(2 * s + 1 - lax.div(s, 2), 4),) + tail)


def shape(*dims, of=BF):
    return jax.ShapeDtypeStruct(dims, of)


def run(kernel, order, operands, outs, scratch, us, meeting=None):
    def spec(kind, array):
        return {"s": lambda: SCALARS, "w": lambda: whole(array), "q": lambda: quarter(array, order), "a": lambda: ANY}[kind]()

    return pl.pallas_call(
        kernel,
        grid=(QUARTERS,) if order else (1,),
        in_specs=[spec(*entry) for entry in operands],
        out_specs=[spec(*entry) for entry in outs],
        out_shape=[array for unused, array in outs],
        scratch_shapes=scratch,
        compiler_params=pltpu.CompilerParams(
            dimension_semantics=("arbitrary",),
            vmem_limit_bytes=60 * 2**20,
            collective_id=meeting,
            has_side_effects=meeting is not None,
        ),
        cost_estimate=pl.CostEstimate(flops=int(us * 1.1e9), bytes_accessed=1024, transcendentals=0),
    )(*[array for unused, array in operands])


def swap(value, axis, apart):
    return lax.ppermute(value, axis, [(i, i ^ apart) for i in range(lax.axis_size(axis))])


def after(value, *earlier):
    return lax.optimization_barrier((value,) + earlier)[0]


class Line:
    def __init__(self):
        self.last = ()

    def take(self, value):
        return after(value, *self.last)

    def leave(self, *values):
        self.last = values


def spread(packed, share):
    own, first, unused = packed
    far_rest = lax.all_gather(share, ("stream", "dp"), axis=0, tiled=True)
    return own, swap(own, "tensor", 1), swap(first, "tensor", 2), far_rest


def spread_on(line, own, near, far, far_rest):
    far, far_rest = line.take((far, far_rest))
    return own, near, far, far_rest, swap(far, "tensor", 1), swap(far_rest, "tensor", 1)


def add(left, right):
    return low(left.astype(F32) + right.astype(F32))


def fold_first(to_y, own_top, to_x, own_bottom):
    return swap(to_y, "tensor", 2), swap(to_x, "stream", 1), own_top, own_bottom


def fold_second(by_y, by_x, own_top, own_bottom):
    return add(own_top[1], by_y[1]), add(own_bottom[1], by_x[1])


def fold_third(first, second):
    by_y, by_x, own_top, own_bottom = first
    then_x, then_y = second

    def three(own, one, two):
        return low(own.astype(F32) + one.astype(F32) + two.astype(F32))

    return jnp.concatenate([three(own_top[0], by_y[0], then_x), three(own_bottom[0], by_x[0], then_y)], axis=1)


def fold_last(total):
    return lax.psum_scatter(total, "dp", scatter_dimension=0, tiled=True)[0]


def s(value):
    return ("s", value)


def w(value):
    return ("w", value)


def q(value):
    return ("q", value)


def a(value):
    return ("a", value)


def local(
    text_in,
    image_in,
    lengths,
    text_cot,
    image_cot,
    text_cross_q,
    text_cross_kv,
    text_cross_out,
    text_up,
    text_down,
    text_self_qkv,
    text_self_out,
    text_gain,
    text_bias,
    image_cross_q,
    image_cross_kv,
    image_cross_out,
    image_up,
    image_down,
    image_self_qkv,
    image_self_out,
    image_gain,
    image_bias,
):
    dp = lax.axis_size("dp")
    places = 2 * dp
    x_at = lax.axis_index("stream")
    t_at = lax.axis_index("tensor")
    size = text_in.shape[0]
    pairs = size // SLOTS
    image_size = pairs * PADDED
    units = 2 * pairs
    ids = jnp.stack([x_at, x_at * dp + lax.axis_index("dp")] + [(t_at ^ j) * pairs for j in range(QUARTERS)]).astype(jnp.int32)

    def spaced(rows):
        apart = jnp.pad(rows.reshape(pairs, REGIONS, DV), ((0, 0), (0, PADDED - REGIONS), (0, 0)))
        return apart.reshape(image_size, DV)

    def leave(rows):
        return swap(rows.reshape(pairs, PADDED, DV)[:, :REGIONS].reshape(pairs * REGIONS, DV), "stream", 1).astype(F32)

    line = Line()
    mlp_packed = pack([text_up[0], text_down[0], image_up[0], image_down[0]], places, 5120, ids)
    cross_w = (
        text_cross_q[0],
        image_cross_kv[0].reshape(DT, -1),
        text_cross_kv[0].reshape(DV, -1),
        image_cross_q[0],
        text_cross_out[0],
        image_cross_out[0],
    )
    self_packed = pack(
        [
            text_self_qkv[0].transpose(1, 2, 0).reshape(-1, DT),
            text_self_out[0],
            image_self_qkv[0].reshape(DV, -1),
            image_self_out[0],
        ],
        places,
        4608,
        after(ids, mlp_packed[0]),
    )
    line.leave(self_packed[0], cross_w[1], cross_w[2])
    mlp_share = line.take(swap(mlp_packed[2], "tensor", 2))
    self_share = line.take(swap(self_packed[2], "tensor", 2))
    line.leave(mlp_share, self_share)
    mlp_w = spread(mlp_packed, mlp_share)
    self_w = spread(self_packed, after(self_share, mlp_share))
    image_cot_here = swap(spaced(image_cot), "stream", 1)

    text_wide, image_wide = shape(size, DT, of=F32), shape(image_size, DV, of=F32)
    text_f32, image_f32 = pltpu.VMEM((size, DT), F32), pltpu.VMEM((image_size, DV), F32)
    text_bf, image_bf = pltpu.VMEM((size, DT), BF), pltpu.VMEM((image_size, DV), BF)
    in_sems, out_sems = pltpu.SemaphoreType.DMA((6,)), pltpu.SemaphoreType.DMA((2,))
    text_affine = [w(text_gain), w(text_bias)]
    image_affine = [w(image_gain), w(image_bias)]
    vector_outs = [w(shape(2, DT, of=F32)), w(shape(2, DV, of=F32))]
    part_rows = 3 * size + 4 * image_size

    def buffer(weights):
        return pltpu.VMEM((QUARTERS, weights[0].shape[0], BLOCK), BF)

    in_four = [
        (QUARTERS, size, DT),
        (QUARTERS, image_size, DV),
        (QUARTERS, size, 1024),
        (QUARTERS, image_size, 1024),
        (QUARTERS, units, SLOTS, PADDED),
        (QUARTERS, units, PADDED, SLOTS),
    ]

    def links(count):
        return [pltpu.SemaphoreType.DMA((count,)), pltpu.SemaphoreType.DMA((count,))]

    text_pre1, image_pre1, image, texts, images, *cross_kept = run(
        functools.partial(cross_forward, pairs),
        None,
        [s(lengths), w(line.take(text_in)), w(spaced(image_in))] + [w(m) for m in cross_w],
        [w(text_wide), w(image_wide), w(shape(image_size, DV))] + [a(shape(*dims)) for dims in in_four],
        [pltpu.VMEM(dims, BF) for dims in in_four]
        + [pltpu.VMEM((QUARTERS, part_rows, BLOCK), BF), pltpu.VMEM((part_rows, BLOCK), BF), pltpu.VMEM((3, part_rows, BLOCK), BF)]
        + links(10)
        + [pltpu.SemaphoreType.DMA((6,))],
        70,
        1,
    )
    line.leave(text_pre1, image_cot_here)
    mlp_w = spread_on(line, *mlp_w)
    (
        text_one,
        image_one,
        text_pre2,
        image_pre2,
        text_activ,
        text_slope,
        image_activ,
        image_slope,
    ) = run(
        functools.partial(mlp_forward, pairs),
        FORWARD,
        [w(text_pre1), w(image_pre1)] + text_affine + image_affine + [a(m) for m in mlp_w],
        [
            w(shape(size, DT)),
            w(shape(image_size, DV)),
            w(text_wide),
            w(image_wide),
            q(shape(QUARTERS, size, 768)),
            q(shape(QUARTERS, size, 768)),
            q(shape(QUARTERS, image_size, 256)),
            q(shape(QUARTERS, image_size, 256)),
        ],
        [buffer(mlp_w), in_sems],
        15,
    )
    line.leave(text_pre2)
    self_w = spread_on(line, *self_w)
    (
        text_out,
        image_out,
        text_n3,
        image_n3,
        text_vec3,
        image_vec3,
        self_rounded,
        self_q,
        self_k,
        self_v,
        self_c,
        self_probs,
        self_kept,
        self_image_probs,
    ) = run(
        functools.partial(self_forward, pairs),
        FORWARD,
        [s(ids), s(lengths), w(text_pre2), w(image_pre2)]
        + text_affine
        + image_affine
        + [w(text_cot), w(image_cot_here)]
        + [a(m) for m in self_w],
        [w(text_wide), w(shape(image_size, DV)), w(text_wide), w(image_wide)]
        + vector_outs
        + [
            w(shape(2 * part_rows, BLOCK)),
            q(shape(QUARTERS, size, 192)),
            q(shape(QUARTERS, size, 192)),
            q(shape(QUARTERS, size, 192)),
            q(shape(QUARTERS, size, 192)),
            q(shape(QUARTERS, pairs, 384, SLOTS)),
            q(shape(QUARTERS, image_size, 1024)),
            q(shape(QUARTERS, units, PADDED, PADDED)),
        ],
        [buffer(self_w), text_f32, image_f32, text_bf, image_bf, in_sems],
        19,
    )
    image_out = leave(image_out)

    text_depth, image_depth = DT // places, DV // places
    padded = -(-text_depth // 16) * 16

    def back_scratch(weights, rows):
        return [
            buffer(weights),
            pltpu.VMEM((QUARTERS, rows, BLOCK), BF),
            text_f32,
            image_f32,
            text_bf,
            image_bf,
        ]

    def weight_grads(is_self, turn, rounded, rounded_near, kept, kept_near):
        top = 3 * padded + image_depth
        if is_self:
            outs = [w(shape(2, dp, top, BLOCK)), w(shape(2, dp, top, BLOCK)), w(shape(dp, 12 * image_depth, BLOCK))]
        else:
            outs = [w(shape(2, dp, top, BLOCK))] * 4
        return run(
            functools.partial(weight_grad, is_self, (size, image_size)),
            None,
            [s(turn), w(rounded), w(rounded_near), w(kept), w(kept_near)],
            outs,
            [
                pltpu.VMEM((DT, 2 * size), BF),
                pltpu.VMEM((DT, 2 * size), BF),
                pltpu.VMEM((DV, 2 * image_size), BF),
                pltpu.VMEM((DV, 2 * image_size), BF),
            ],
            12,
        )

    self_rows = 3 * size + 4 * image_size
    self_rounded_near = swap(self_rounded, "tensor", 1)
    text_n2, image_n2, text_vec2, image_vec2, self_near, self_keep = run(
        functools.partial(self_back, pairs),
        BACKWARD,
        [
            w(text_n3),
            w(image_n3),
            w(text_pre2),
            w(image_pre2),
            w(text_gain),
            w(image_gain),
            q(self_q),
            q(self_k),
            q(self_v),
            q(self_c),
            q(self_probs),
            q(self_kept),
            q(self_image_probs),
        ]
        + [a(m) for m in self_w],
        [w(text_wide), w(image_wide)] + vector_outs + [a(shape(2, self_rows, BLOCK)), a(shape(2, self_rows, BLOCK))],
        back_scratch(self_w, self_rows)
        + [pltpu.VMEM((3, size, 192), BF), pltpu.VMEM((image_size, 768), BF), in_sems, out_sems]
        + links(2),
        23,
        2,
    )
    to_x, self_top, to_z = weight_grads(True, ids, self_rounded, self_rounded_near, self_keep, self_near)
    self_by_x = swap(to_x, "stream", 1)
    self_bottom = fold_last(to_z)
    line.leave(self_top)
    mlp_rows = 6 * size + 2 * image_size
    text_n1, image_n1, grad_low, text_vec1, image_vec1, mlp_rounded, mlp_rounded_near, mlp_near, mlp_keep = run(
        functools.partial(mlp_back, pairs),
        BACKWARD,
        [
            w(text_n2),
            w(image_n2),
            w(text_one),
            w(image_one),
            w(text_pre1),
            w(image_pre1),
            w(line.take(text_gain)),
            w(image_gain),
            q(text_activ),
            q(text_slope),
            q(image_activ),
            q(image_slope),
        ]
        + [a(m) for m in mlp_w],
        [w(text_wide), w(image_wide), w(shape(part_rows, BLOCK))]
        + vector_outs
        + [
            w(shape(2 * part_rows, BLOCK)),
            a(shape(2 * part_rows, BLOCK)),
            a(shape(2, mlp_rows, BLOCK)),
            a(shape(2, mlp_rows, BLOCK)),
        ],
        back_scratch(mlp_w, mlp_rows) + [text_bf, in_sems, out_sems] + links(3),
        20,
        3,
    )
    line.leave(grad_low)
    mlp_first = fold_first(
        *weight_grads(False, line.take(ids), mlp_rounded, mlp_rounded_near, mlp_keep, mlp_near)
    )
    line.leave(mlp_first[2])
    self_top, self_by_x = line.take((self_top, self_by_x))
    self_top, to_y = add(self_top[0], self_by_x[0]), add(self_top[1], self_by_x[1])
    self_then_y = swap(to_y, "tensor", 2)
    line.leave(self_top, to_y)
    d_dims = [(QUARTERS, part_rows, BLOCK), (QUARTERS, size, 768), (QUARTERS, image_size, 768)]
    vectors = jnp.concatenate(
        [jnp.pad(v, ((0, 0), (0, DV - DT))) for v in (text_vec1, text_vec2, text_vec3)]
        + [image_vec1, image_vec2, image_vec3, jnp.zeros((4, DV), F32)],
        axis=0,
    )
    grads, text_d, image_d, own_sum, total, vectors = run(
        functools.partial(cross_back, pairs),
        None,
        [w(line.take(grad_low)), w(vectors)] + [w(k) for k in cross_kept] + [w(m) for m in cross_w],
        [a(shape(*dims)) for dims in d_dims]
        + [w(shape(part_rows, BLOCK, of=F32)), w(shape(part_rows, BLOCK)), w(shape(16, DV, of=F32))],
        [pltpu.VMEM(dims, BF) for dims in d_dims]
        + [pltpu.VMEM((QUARTERS, part_rows, BLOCK), BF), pltpu.VMEM((2, part_rows, BLOCK), BF), pltpu.VMEM((2, 16, DV), F32)]
        + links(7)
        + [pltpu.SemaphoreType.DMA((3,))],
        48,
        4,
    )
    line.leave(total)
    self_top = add(self_top, line.take(self_then_y))
    self_bottom = line.take(self_bottom).reshape(2, 2, 3 * image_depth, BLOCK)
    self_bottom_x = swap(self_bottom[:, 1], "stream", 1)
    line.leave(self_top)
    text_only, image_only = 4 * padded + 16, 4 * image_depth
    text_vector = jnp.pad(vectors[:6, :DT].reshape(6, places, text_depth), ((0, 0), (0, 0), (0, BLOCK - text_depth)))
    image_vector = jnp.pad(vectors[6:].reshape(10, places, image_depth), ((0, 0), (0, 0), (0, BLOCK - image_depth)))
    vectors = low(jnp.concatenate([text_vector, image_vector], axis=0).transpose(1, 0, 2))
    vector_keep = lax.dynamic_slice_in_dim(vectors, x_at * dp, dp, 0)
    vector_send = lax.dynamic_slice_in_dim(vectors, (1 - x_at) * dp, dp, 0)
    text_grad, image_grad, text_keep, text_send, image_keep, image_send = run(
        cross_last,
        None,
        [
            w(line.take(total)),
            w(own_sum),
            w(vector_keep),
            w(vector_send),
            w(text_n1),
            w(image_n1),
            w(texts),
            w(images),
            w(grads),
            w(cross_kept[0]),
            w(cross_kept[1]),
            w(text_d),
            w(image_d),
        ],
        [
            w(text_wide),
            w(shape(image_size, DV)),
            w(shape(dp, text_only, BLOCK)),
            w(shape(dp, text_only, BLOCK)),
            w(shape(dp, image_only, BLOCK)),
            w(shape(dp, image_only, BLOCK)),
        ],
        [
            pltpu.VMEM((part_rows, BLOCK), BF),
            pltpu.VMEM((DT, QUARTERS * size), BF),
            pltpu.VMEM((DT, QUARTERS * size), BF),
            pltpu.VMEM((DV, QUARTERS * image_size), BF),
            pltpu.VMEM((DV, QUARTERS * image_size), BF),
        ]
        + links(1),
        30,
        5,
    )
    line.leave(text_grad)
    self_top = fold_last(self_top)
    sums = fold_second(*line.take(mlp_first))
    line.leave(*sums)
    mlp_second = swap(sums[0], "stream", 1), swap(sums[1], "tensor", 2)
    self_bottom = add(self_bottom[:, 0], line.take(self_bottom_x))
    self_bottom = add(self_bottom[0], swap(self_bottom[1], "tensor", 2))
    mlp_total = fold_third(mlp_first, line.take(mlp_second))
    line.leave(mlp_total, self_bottom)
    mlp_grads = fold_last(after(mlp_total, self_top))
    cross_text = add(text_keep, line.take(swap(text_send, "stream", 1)))
    line.leave(cross_text)
    cross_text = fold_last(after(cross_text, mlp_grads))
    cross_image = add(image_keep, line.take(swap(image_send, "stream", 1)))
    line.leave(cross_image)
    cross_image = fold_last(after(cross_image, cross_text))
    self_grads = jnp.concatenate([self_top, self_bottom], axis=0)
    image_grad = leave(image_grad)

    def pick(packed, first, count, depth, stride):
        rows = [packed[first + b * stride : first + b * stride + depth] for b in range(count)]
        return jnp.concatenate(rows, axis=1).astype(F32)

    def text_pick(packed, first, count):
        return pick(packed, first, count, text_depth, padded)

    def image_pick(packed, first, count):
        return pick(packed, first, count, image_depth, image_depth)

    sums = cross_text[4 * padded :].astype(F32)
    text_vectors, image_vectors = sums[:6, :text_depth], sums[6:12, :image_depth]

    self_text = text_pick(self_grads, 0, 3)

    def heads(at):
        return jnp.concatenate([self_text[:, at * 128 : (at + 1) * 128], self_text[:, 512 + at * 64 : 576 + at * 64]], axis=1)

    below = 3 * padded
    return (
        text_out,
        image_out,
        text_grad,
        image_grad,
        text_pick(cross_text, 0, 1)[None],
        image_pick(cross_image, 0, 2).reshape(1, image_depth, 2, 256),
        text_pick(cross_text, 3 * padded, 1).T[None],
        text_pick(mlp_grads, 0, 3)[None],
        text_pick(mlp_grads, below + image_depth, 3).T[None],
        jnp.stack([heads(n) for n in range(3)], axis=1)[None],
        heads(3).T[None],
        text_vectors[0::2][None],
        text_vectors[1::2][None],
        image_pick(cross_image, 2 * image_depth, 1)[None],
        text_pick(cross_text, padded, 2).reshape(1, text_depth, 2, 256),
        image_pick(cross_image, 3 * image_depth, 1).T[None],
        image_pick(mlp_grads, below, 1)[None],
        image_pick(mlp_grads, 2 * below + image_depth, 1).T[None],
        image_pick(self_grads, below, 3).reshape(1, image_depth, 3, 256),
        image_pick(self_grads, below + 3 * image_depth, 1).T[None],
        image_vectors[0::2][None],
        image_vectors[1::2][None],
    )


def solution(mesh):
    rows = P(("stream", "dp", "tensor"), None)
    wide_in = P(None, None, "tensor")
    group_in = P(None, None, None, "tensor")
    wide_out = P(None, "tensor", None)
    grad_in = P(None, ("stream", "dp"), "tensor")
    grad_group = P(None, ("stream", "dp"), None, "tensor")
    grad_out = P(None, "tensor", ("stream", "dp"))
    vector = P(None, None, ("stream", "dp"))
    weights = (wide_in, group_in, wide_out, wide_in, wide_out, group_in, wide_out, P(), P())
    grads = (grad_in, grad_group, grad_out, grad_in, grad_out, grad_group, grad_out, vector, vector)
    return jax.shard_map(
        local,
        mesh=mesh,
        in_specs=(rows, rows, P(("stream", "dp")), rows, rows) + weights + weights,
        out_specs=(rows, rows, rows, rows) + grads + grads,
        check_vma=False,
    )
```

```python
import functools

import jax
import jax.numpy as jnp
from jax import lax
from jax.experimental import pallas as pl
from jax.experimental.pallas import tpu as pltpu
from jax.sharding import PartitionSpec as P

DT = 768
DV = 1024
HEAD = 128
SELF_HEAD = 64
SLOTS = 128
REGIONS = 37
PADDED = 48
QUARTERS = 4
BLOCK = 256

norm_eps = 1e-05
masked_score = -1e30

BF = jnp.bfloat16
F32 = jnp.float32
FORWARD = (0, 1, 2, 3)
BACKWARD = (1, 3, 0, 2)


def nn(left, right):
    return lax.dot_general(left, right, (((1,), (0,)), ((), ())), preferred_element_type=F32)


def nt(left, right):
    return lax.dot_general(left, right, (((1,), (1,)), ((), ())), preferred_element_type=F32)


def tn(left, right):
    return lax.dot_general(left, right, (((0,), (0,)), ((), ())), preferred_element_type=F32)


def low(value):
    return value.astype(BF)


def normed(inputs):
    centered = inputs - jnp.mean(inputs, axis=-1, keepdims=True)
    scale = lax.rsqrt(jnp.mean(centered * centered, axis=-1, keepdims=True) + norm_eps)
    return centered * scale, scale


def norm_back(unit, scale, gain, grad, vec):
    vec[0:1] = jnp.sum(grad * unit, axis=0, keepdims=True)
    vec[1:2] = jnp.sum(grad, axis=0, keepdims=True)
    inner = grad * gain
    shift = jnp.mean(inner, axis=-1, keepdims=True)
    slope = jnp.mean(inner * unit, axis=-1, keepdims=True)
    return scale * (inner - shift - unit * slope)


def softmax_all(scores):
    tops = [jnp.max(s, axis=-1, keepdims=True) for s in scores]
    powers = [jnp.exp(s - t) for s, t in zip(scores, tops)]
    sums = [jnp.sum(e, axis=-1, keepdims=True) for e in powers]
    return [low(e / total) for e, total in zip(powers, sums)]


def attend(queries, keys, values, scale, masks):
    scores = [nt(q, k) * scale for q, k in zip(queries, keys)]
    scores = [s if m is None else jnp.where(m, s, masked_score) for s, m in zip(scores, masks)]
    probs = softmax_all(scores)
    return probs, [nn(p, v) for p, v in zip(probs, values)]


def attend_back(queries, keys, values, probs, grads, scale):
    grad_probs = [nt(g, v) for g, v in zip(grads, values)]
    grad_values = [low(tn(p, g)) for p, g in zip(probs, grads)]
    wide = [p.astype(F32) for p in probs]
    inner = [jnp.sum(p * g, axis=-1, keepdims=True) for p, g in zip(wide, grad_probs)]
    grad_scores = [low(p * (g - i)) for p, g, i in zip(wide, grad_probs, inner)]
    grad_queries = [low(nn(g, k) * scale) for g, k in zip(grad_scores, keys)]
    grad_keys = [low(tn(g, q) * scale) for g, q in zip(grad_scores, queries)]
    return grad_queries, grad_keys, grad_values


def side(ref, row, width, count):
    return jnp.concatenate([ref[row + b * width : row + (b + 1) * width, :] for b in range(count)], axis=1)


def rows_of(pair, size):
    return slice(pair * size, (pair + 1) * size)


def fetch(step, order, parts, buffer, sems):
    copies = [
        (order.index(quarter), pltpu.make_async_copy(ref, buffer.at[order.index(quarter), pl.ds(row, ref.shape[0])], sems.at[i]))
        for i, (quarter, row, ref) in enumerate(parts)
    ]
    copies.sort(key=lambda entry: entry[0])

    @pl.when(step == 0)
    def begin():
        for unused, copy in copies:
            copy.start()

    for at in range(QUARTERS):

        @pl.when(step == at)
        def arrive():
            for slot, copy in copies:
                if slot == at:
                    copy.wait()


def leave_quarter(step, buffer, near, keep, sems, copies):
    kept = [pltpu.make_async_copy(buffer.at[at], keep.at[at - 2], sems.at[at - 2]) for at in (2, 3)]
    for at in range(QUARTERS):

        @pl.when(step == at)
        def leave():
            (copies[at] if at < 2 else kept[at - 2]).start()

    @pl.when(step == QUARTERS - 1)
    def finish():
        for copy in list(copies) + kept:
            copy.wait()


def affine_row(gain, bias, norm):
    return gain[0, norm : norm + 1, :].astype(F32), bias[0, norm : norm + 1, :].astype(F32)


def leave_blocks(ref, row, value):
    size = value.shape[0]
    for b in range(value.shape[1] // BLOCK):
        ref[row + b * size : row + (b + 1) * size, :] = value[:, b * BLOCK : (b + 1) * BLOCK]


MESH = pl.DeviceIdType.MESH


def partners():
    t = lax.axis_index("tensor")
    return {"tensor": lax.bitwise_xor(t, 1)}, {"tensor": lax.bitwise_xor(t, 2)}, {"stream": lax.bitwise_xor(lax.axis_index("stream"), 1)}


def greet(*others):
    barrier = pltpu.get_barrier_semaphore()
    for other in others:
        pl.semaphore_signal(barrier, inc=1, device_id=other, device_id_type=MESH)
    pl.semaphore_wait(barrier, len(others))


def sender(send_sems, recv_sems):
    def copy(number, source, target, to):
        return pltpu.make_async_remote_copy(
            src_ref=source,
            dst_ref=target,
            send_sem=send_sems.at[number],
            recv_sem=recv_sems.at[number],
            device_id=to,
            device_id_type=MESH,
        )

    return copy


def pack(pieces, places, rest, ids):
    total = sum(m.size for m in pieces) // BLOCK
    cut, share = total - rest, rest // places

    def kernel(ids, *refs):
        sources, (own, first, mine) = refs[: len(pieces)], refs[len(pieces) :]
        row = 0
        for ref in sources:
            leave_blocks(own, row, ref[...])
            row += ref.size // BLOCK
        first[...] = own[0:cut, :]
        mine[...] = own[pl.ds(pl.multiple_of(cut + ids[1] * share, 16), share), :]

    return run(
        kernel,
        None,
        [s(ids)] + [w(m) for m in pieces],
        [w(shape(total, BLOCK)), w(shape(cut, BLOCK)), w(shape(share, BLOCK))],
        [],
        3,
    )


def cross_block(pairs, first, lengths, text, image, matrices, text_kept, image_kept, text_probs, image_probs, part):
    wq, wkv_text, wkv_image, wq_image, w_out, w_out_image = matrices
    text_low = text[...]
    image_low = image[...]
    text_kept[:, 0:256] = low(nn(text_low, wq[...]))
    text_kept[:, 256:768] = low(nn(text_low, wkv_text[...]))
    image_kept[:, 0:512] = low(nn(image_low, wkv_image[...]))
    image_kept[:, 512:768] = low(nn(image_low, wq_image[...]))

    image_mask = lax.broadcasted_iota(jnp.int32, (SLOTS, PADDED), 1) < REGIONS
    slots = lax.broadcasted_iota(jnp.int32, (PADDED, SLOTS), 1)
    units = [(p, h) for p in range(pairs) for h in range(2)]

    def text_part(at):
        return [text_kept[rows_of(p, SLOTS), at + h * HEAD : at + (h + 1) * HEAD] for p, h in units]

    def image_part(at):
        return [image_kept[rows_of(p, PADDED), at + h * HEAD : at + (h + 1) * HEAD] for p, h in units]

    scale = HEAD**-0.5
    probs, context = attend(text_part(0), image_part(0), image_part(256), scale, [image_mask] * len(units))
    for i, (p, h) in enumerate(units):
        text_probs[i] = probs[i]
        text_kept[rows_of(p, SLOTS), 768 + h * HEAD : 768 + (h + 1) * HEAD] = low(context[i])
    limits = [lengths[first + p] for p in range(pairs)]
    masks = [slots < limits[p] for p, h in units]
    probs, context = attend(image_part(512), text_part(256), text_part(512), scale, masks)
    for i, (p, h) in enumerate(units):
        image_probs[i] = probs[i]
        image_kept[rows_of(p, PADDED), 768 + h * HEAD : 768 + (h + 1) * HEAD] = low(context[i])
    leave_blocks(part, 0, low(nn(text_kept[:, 768:1024], w_out[...])))
    leave_blocks(part, 3 * text.shape[0], low(nn(image_kept[:, 768:1024], w_out_image[...])))


def cross_forward(pairs, lengths, text, image, *refs):
    matrices = refs[:6]
    text_pre, image_pre, image_own = refs[6:9]
    outs = refs[9:15]
    texts, images, text_kept, image_kept, text_probs, image_probs, parts, total, got, send_sems, recv_sems, out_sems = refs[15:]
    core, y, x = partners()
    copy = sender(send_sems, recv_sems)
    text_core = copy(0, text, texts.at[1], core)
    text_y = copy(1, text, texts.at[2], y)
    image_x = copy(2, image, images.at[0], x)
    image_core = copy(3, images.at[0], images.at[1], core)
    image_y = copy(4, images.at[0], images.at[2], y)
    text_corner = copy(5, texts.at[2], texts.at[3], core)
    image_corner = copy(6, images.at[2], images.at[3], core)
    near_part = copy(7, parts.at[1], got.at[0], core)
    corner_part = copy(8, parts.at[3], got.at[1], core)
    far_part = copy(9, total, got.at[2], y)

    greet(core, y, x)
    image_x.start()
    text_y.start()
    text_core.start()
    texts[0] = text[...]
    image_x.wait()
    image_y.start()
    image_core.start()

    def block(j, unused):
        @pl.when(j == 1)
        def near():
            text_core.wait()
            image_core.wait()

        @pl.when(j == 2)
        def far():
            text_y.wait()
            text_corner.start()
            image_y.wait()
            image_corner.start()

        @pl.when(j == 3)
        def corner():
            text_corner.wait()
            image_corner.wait()

        cross_block(
            pairs,
            lax.bitwise_xor(lax.axis_index("tensor"), j) * pairs,
            lengths,
            texts.at[j],
            images.at[j],
            matrices,
            text_kept.at[j],
            image_kept.at[j],
            text_probs.at[j],
            image_probs.at[j],
            parts.at[j],
        )

        @pl.when(j == 1)
        def near_done():
            near_part.start()

        return unused

    lax.fori_loop(0, QUARTERS, block, 0)
    corner_part.start()
    leaving = [
        pltpu.make_async_copy(source, out, out_sems.at[i])
        for i, (source, out) in enumerate(
            zip((texts, images, text_kept, image_kept, text_probs, image_probs), outs)
        )
    ]
    for leave in leaving:
        leave.start()
    corner_part.wait()
    total[...] = add(parts[2], got[1])
    far_part.start()
    near_part.wait()
    size, image_size = text.shape[0], image.shape[0]
    below = 3 * size
    image_own[...] = images[0]

    def summed(row, depth, count, start):
        for ref in (parts.at[0], got.at[0]):
            start = start + side(ref, row, depth, count).astype(F32)
        return start

    text_pre[...] = summed(0, size, 3, text[...].astype(F32))
    image_pre[...] = summed(below, image_size, 4, images[0].astype(F32))
    far_part.wait()
    text_pre[...] += side(got.at[2], 0, size, 3).astype(F32)
    image_pre[...] += side(got.at[2], below, image_size, 4).astype(F32)
    for leave in leaving:
        leave.wait()


def cross_block_back(pairs, grad, matrices, text_kept, image_kept, text_probs, image_probs, text_d, image_d, part):
    wq, wkv_text, wkv_image, wq_image, w_out, w_out_image = matrices
    text_rows, image_rows = text_kept.shape[0], image_kept.shape[0]
    text_dc = low(nt(side(grad, 0, text_rows, 3), w_out[...]))
    image_dc = low(nt(side(grad, 3 * text_rows, image_rows, 4), w_out_image[...]))
    units = [(p, h) for p in range(pairs) for h in range(2)]

    def text_part(at):
        return [text_kept[rows_of(p, SLOTS), at + h * HEAD : at + (h + 1) * HEAD] for p, h in units]

    def image_part(at):
        return [image_kept[rows_of(p, PADDED), at + h * HEAD : at + (h + 1) * HEAD] for p, h in units]

    scale = HEAD**-0.5
    outer = [text_dc[rows_of(p, SLOTS), h * HEAD : (h + 1) * HEAD] for p, h in units]
    probs = [text_probs[i] for i in range(len(units))]
    found = attend_back(text_part(0), image_part(0), image_part(256), probs, outer, scale)
    for i, (p, h) in enumerate(units):
        text_d[rows_of(p, SLOTS), h * HEAD : (h + 1) * HEAD] = found[0][i]
        image_d[rows_of(p, PADDED), h * HEAD : (h + 1) * HEAD] = found[1][i]
        image_d[rows_of(p, PADDED), 256 + h * HEAD : 256 + (h + 1) * HEAD] = found[2][i]
    outer = [image_dc[rows_of(p, PADDED), h * HEAD : (h + 1) * HEAD] for p, h in units]
    probs = [image_probs[i] for i in range(len(units))]
    found = attend_back(image_part(512), text_part(256), text_part(512), probs, outer, scale)
    for i, (p, h) in enumerate(units):
        image_d[rows_of(p, PADDED), 512 + h * HEAD : 512 + (h + 1) * HEAD] = found[0][i]
        text_d[rows_of(p, SLOTS), 256 + h * HEAD : 256 + (h + 1) * HEAD] = found[1][i]
        text_d[rows_of(p, SLOTS), 512 + h * HEAD : 512 + (h + 1) * HEAD] = found[2][i]
    text_dx = nt(text_d[:, 0:256], wq[...]) + nt(text_d[:, 256:768], wkv_text[...])
    image_dx = nt(image_d[:, 0:512], wkv_image[...]) + nt(image_d[:, 512:768], wq_image[...])
    leave_blocks(part, 0, low(text_dx))
    leave_blocks(part, 3 * text_rows, low(image_dx))


def cross_back(pairs, grad, vectors, text_kept, image_kept, text_probs, image_probs, *refs):
    matrices = refs[:6]
    grads_out, text_d_out, image_d_out, own_sum, total, vector_sum = refs[6:12]
    grads, text_d, image_d, parts, got, got_vectors, send_sems, recv_sems, out_sems = refs[12:]
    core, y, unused_x = partners()
    copy = sender(send_sems, recv_sems)
    to_core = copy(0, grad, grads.at[1], core)
    to_y = copy(1, grad, grads.at[2], y)
    corner = copy(2, grads.at[2], grads.at[3], core)
    near_part = copy(3, parts.at[1], got.at[0], core)
    corner_part = copy(4, parts.at[3], got.at[1], core)
    vectors_core = copy(5, vectors, got_vectors.at[0], core)
    vectors_y = copy(6, vector_sum, got_vectors.at[1], y)
    greet(core, y)
    vectors_core.start()
    to_y.start()
    to_core.start()
    grads[0] = grad[...]
    vectors_core.wait()
    vector_sum[...] = vectors[...] + got_vectors[0]
    vectors_y.start()

    def block(j, unused):
        @pl.when(j == 1)
        def near():
            to_core.wait()

        @pl.when(j == 2)
        def far():
            to_y.wait()
            corner.start()

        @pl.when(j == 3)
        def last():
            corner.wait()

        cross_block_back(
            pairs,
            grads.at[j],
            matrices,
            text_kept.at[j],
            image_kept.at[j],
            text_probs.at[j],
            image_probs.at[j],
            text_d.at[j],
            image_d.at[j],
            parts.at[j],
        )

        @pl.when(j == 1)
        def near_done():
            near_part.start()

        return unused

    lax.fori_loop(0, QUARTERS, block, 0)
    corner_part.start()
    leaving = [
        pltpu.make_async_copy(source, out, out_sems.at[i])
        for i, (source, out) in enumerate(((grads, grads_out), (text_d, text_d_out), (image_d, image_d_out)))
    ]
    for leave in leaving:
        leave.start()
    near_part.wait()
    own_sum[...] = parts[0].astype(F32) + got[0].astype(F32)
    vectors_y.wait()
    vector_sum[...] += got_vectors[1]
    corner_part.wait()
    total[...] = add(parts[2], got[1])
    for leave in leaving:
        leave.wait()


def cross_last(total, own_sum, vector_keep, vector_send, text_n, image_n, texts, images, grads, text_kept, image_kept, text_d, image_d, *refs):
    text_grad, image_grad, text_keep, image_keep, image_send = refs[:5]
    got, text_send, text_got, text_flip, text_g_flip, image_flip, image_g_flip, send_sems, recv_sems = refs[5:]
    unused_core, y, x = partners()
    copy = sender(send_sems, recv_sems)
    far = copy(0, total, got, y)
    text_x = copy(1, text_send, text_got, x)
    greet(y, x)
    far.start()
    size, image_size = texts.shape[1], images.shape[1]
    below = 3 * size
    for j in range(QUARTERS):
        text_flip[:, rows_of(j, size)] = texts[j].T
        image_flip[:, rows_of(j, image_size)] = images[j].T
        for b in range(3):
            text_g_flip[rows_of(b, BLOCK), rows_of(j, size)] = grads[j, rows_of(b, size), :].T
        for b in range(4):
            start = below + b * image_size
            image_g_flip[rows_of(b, BLOCK), rows_of(j, image_size)] = grads[j, start : start + image_size, :].T
    at = lax.axis_index("stream")
    for flip, g_flip, d, kept, keep, send in (
        (text_flip, text_g_flip, text_d, text_kept, text_keep, text_send),
        (image_flip, image_g_flip, image_d, image_kept, image_keep, image_send),
    ):
        dp = keep.shape[0]
        half = flip.shape[0] // 2
        depth = half // dp
        padded = -(-depth // 16) * 16
        rows = flip.shape[1]
        outer = d[...].reshape(rows, 768)
        context = kept[:, :, 768:1024].reshape(rows, 256)
        for out, apart in ((send, 1), (keep, 0)):
            start = pl.multiple_of(lax.bitwise_xor(at, apart) * half, 128)
            found = nn(flip[pl.ds(start, half), :], outer)
            last = nn(g_flip[pl.ds(start, half), :], context)
            for z in range(dp):
                taken = slice(z * depth, (z + 1) * depth)
                for b in range(3):
                    out[z, b * padded : b * padded + depth, :] = low(found[taken, b * BLOCK : (b + 1) * BLOCK])
                out[z, 3 * padded : 3 * padded + depth, :] = low(last[taken])
        if flip is text_flip:
            for out, vector in ((text_keep, vector_keep), (text_send, vector_send)):
                below_all = out.shape[1] - vector.shape[1]
                for z in range(dp):
                    out[z, below_all:, :] = vector[z]
            text_x.start()
    text_x.wait()
    text_keep[...] = add(text_keep[...], text_got[...])
    far.wait()
    text_grad[...] = text_n[...] + side(own_sum, 0, size, 3) + side(got, 0, size, 3).astype(F32)
    image_grad[...] = low(image_n[...] + side(own_sum, below, image_size, 4) + side(got, below, image_size, 4).astype(F32))


def gate(hidden):
    half = 0.5 * (1.0 + lax.erf(hidden * (2.0**-0.5)))
    density = jnp.exp(-0.5 * hidden * hidden) * 0.3989422804014327
    return hidden * half, half + hidden * density


def mlp_forward(pairs, text_pre, image_pre, text_gain, text_bias, image_gain, image_bias, *refs):
    parts = refs[:6]
    text_low, image_low, text_next, image_next = refs[6:10]
    text_activ, text_slope, image_activ, image_slope = refs[10:14]
    weights, sems = refs[14:]
    step = pl.program_id(0)
    fetch(step, FORWARD, gathered(parts), weights, sems)

    @pl.when(step == 0)
    def begin():
        for pre, gain, bias, rounded, total in (
            (text_pre, text_gain, text_bias, text_low, text_next),
            (image_pre, image_gain, image_bias, image_low, image_next),
        ):
            g, b = affine_row(gain, bias, 0)
            one = normed(pre[...])[0] * g + b
            total[...] = one
            rounded[...] = low(one)

    w = weights.at[step]
    for b in range(3):
        activ, slope = gate(nn(text_low[...], w[b * 768 : (b + 1) * 768, :]))
        text_activ[0, :, b * 256 : (b + 1) * 256] = low(activ)
        text_slope[0, :, b * 256 : (b + 1) * 256] = low(slope)
    activ, slope = gate(nn(image_low[...], w[4608:5632, :]))
    image_activ[0] = low(activ)
    image_slope[0] = low(slope)
    text_next[...] += nn(text_activ[0], side(w, 2304, 768, 3))
    image_next[...] += nn(image_activ[0], side(w, 5632, 256, 4))


def lane_masks():
    lane = lax.broadcasted_iota(jnp.int32, (1, 2 * SELF_HEAD), 1)
    left = (lane < SELF_HEAD).astype(F32)
    return low(left), low(1.0 - left), lane < SELF_HEAD


def both_heads(tile, masks):
    return jnp.concatenate([tile * masks[0], tile * masks[1]], axis=0)


def one_tile(stacked, masks):
    return jnp.where(masks[2], stacked[:SLOTS], stacked[SLOTS:])


def self_forward(pairs, ids, lengths, text_pre, image_pre, text_gain, text_bias, image_gain, image_bias, text_cot, image_cot, *refs):
    parts = refs[:6]
    (
        text_out,
        image_out,
        text_grad,
        image_grad,
        text_vec,
        image_vec,
        rounded,
        text_q,
        text_k,
        text_v,
        text_c,
        text_probs,
        image_kept,
        image_probs,
    ) = refs[6:20]
    weights, text_sum, image_sum, text_low, image_low, sems = refs[20:]
    step = pl.program_id(0)
    fetch(step, FORWARD, gathered(parts), weights, sems)
    text_rows, image_rows = text_pre.shape[0], image_pre.shape[0]

    @pl.when(step == 0)
    def begin():
        for pre, gain, bias, total, lower, at in (
            (text_pre, text_gain, text_bias, text_sum, text_low, 0),
            (image_pre, image_gain, image_bias, image_sum, image_low, 6 * text_rows),
        ):
            g, b = affine_row(gain, bias, 1)
            two = normed(pre[...])[0] * g + b
            total[...] = two
            lower[...] = low(two)
            leave_blocks(rounded, at, low(two))

    w = weights.at[step]
    for n, out in enumerate((text_q, text_k, text_v)):
        wide = jnp.concatenate([w[b * 576 + n * 192 : b * 576 + (n + 1) * 192, :] for b in range(3)], axis=1)
        out[0] = low(nt(text_low[...], wide))
    for n in range(3):
        image_kept[0, :, n * 256 : (n + 1) * 256] = low(nn(image_low[...], w[2304 + n * 1024 : 3328 + n * 1024, :]))

    masks = lane_masks()
    slots = lax.broadcasted_iota(jnp.int32, (1, SLOTS), 1)
    base = ids[2]
    valid = [slots < lengths[base + p] for p in range(pairs)]
    first, last = slice(0, 128), slice(128, 192)
    queries, keys, values, limits = [], [], [], []
    for p in range(pairs):
        rows = rows_of(p, SLOTS)
        queries += [both_heads(text_q[0, rows, first], masks), text_q[0, rows, last]]
        keys += [text_k[0, rows, first], text_k[0, rows, last]]
        values += [text_v[0, rows, first], text_v[0, rows, last]]
        limits += [valid[p], valid[p]]
    probs, context = attend(queries, keys, values, SELF_HEAD**-0.5, limits)
    for p in range(pairs):
        rows = rows_of(p, SLOTS)
        text_probs[0, p, 0:256, :] = probs[2 * p]
        text_probs[0, p, 256:384, :] = probs[2 * p + 1]
        text_c[0, rows, first] = low(one_tile(context[2 * p], masks))
        text_c[0, rows, last] = low(context[2 * p + 1])

    image_mask = lax.broadcasted_iota(jnp.int32, (PADDED, PADDED), 1) < REGIONS
    units = [(p, h) for p in range(pairs) for h in range(2)]

    def image_part(at):
        return [image_kept[0, rows_of(p, PADDED), at + h * HEAD : at + (h + 1) * HEAD] for p, h in units]

    probs, context = attend(image_part(0), image_part(256), image_part(512), HEAD**-0.5, [image_mask] * len(units))
    for i, (p, h) in enumerate(units):
        image_probs[0, i] = probs[i]
        image_kept[0, rows_of(p, PADDED), 768 + h * HEAD : 768 + (h + 1) * HEAD] = low(context[i])

    text_sum[...] += nn(text_c[0], side(w, 1728, 192, 3))
    image_sum[...] += nn(image_kept[0, :, 768:1024], side(w, 5376, 256, 4))

    @pl.when(step == QUARTERS - 1)
    def finish():
        for total, gain, bias, cot, out, grad, vec, at in (
            (text_sum, text_gain, text_bias, text_cot, text_out, text_grad, text_vec, 3 * text_rows),
            (image_sum, image_gain, image_bias, image_cot, image_out, image_grad, image_vec, 6 * text_rows + 4 * image_rows),
        ):
            g, b = affine_row(gain, bias, 2)
            unit, scale = normed(total[...])
            out[...] = (unit * g + b).astype(out.dtype)
            back = norm_back(unit, scale, g, cot[...].astype(F32), vec)
            grad[...] = back
            leave_blocks(rounded, at, low(back))


def self_back(pairs, text_g, image_g, text_pre, image_pre, text_gain, image_gain, *refs):
    text_q, text_k, text_v, text_c, text_probs, image_kept, image_probs = refs[:7]
    parts = refs[7:13]
    text_n, image_n, text_vec, image_vec, near, keep = refs[13:19]
    weights, found, text_sum, image_sum, text_g_low, image_g_low, text_d, image_d, sems, out_sems, send_sems, recv_sems = refs[19:]
    step = pl.program_id(0)
    fetch(step, BACKWARD, gathered(parts), weights, sems)
    core = partners()[0]
    copy = sender(send_sems, recv_sems)

    @pl.when(step == 0)
    def begin():
        greet(core)
        text_sum[...] = text_g[...]
        image_sum[...] = image_g[...]
        text_g_low[...] = low(text_g[...])
        image_g_low[...] = low(image_g[...])

    w = weights.at[step]
    masks = lane_masks()
    first, last = slice(0, 128), slice(128, 192)
    text_dc = low(nt(text_g_low[...], side(w, 1728, 192, 3)))
    queries, keys, values, probs, outer = [], [], [], [], []
    for p in range(pairs):
        rows = rows_of(p, SLOTS)
        queries += [both_heads(text_q[0, rows, first], masks), text_q[0, rows, last]]
        keys += [text_k[0, rows, first], text_k[0, rows, last]]
        values += [text_v[0, rows, first], text_v[0, rows, last]]
        probs += [text_probs[0, p, 0:256, :], text_probs[0, p, 256:384, :]]
        outer += [both_heads(text_dc[rows, first], masks), text_dc[rows, last]]
    grad_q, grad_k, grad_v = attend_back(queries, keys, values, probs, outer, SELF_HEAD**-0.5)
    size = text_g.shape[0]
    for p in range(pairs):
        rows = rows_of(p, SLOTS)
        text_d[0, rows, first] = one_tile(grad_q[2 * p], masks)
        text_d[0, rows, last] = grad_q[2 * p + 1]
        for n, grad in ((1, grad_k), (2, grad_v)):
            text_d[n, rows, first] = grad[2 * p]
            text_d[n, rows, last] = grad[2 * p + 1]

    image_dc = low(nt(image_g_low[...], side(w, 5376, 256, 4)))
    units = [(p, h) for p in range(pairs) for h in range(2)]

    def image_part(at):
        return [image_kept[0, rows_of(p, PADDED), at + h * HEAD : at + (h + 1) * HEAD] for p, h in units]

    outer = [image_dc[rows_of(p, PADDED), h * HEAD : (h + 1) * HEAD] for p, h in units]
    given = attend_back(
        image_part(0), image_part(256), image_part(512), [image_probs[0, i] for i in range(len(units))], outer, HEAD**-0.5
    )
    for n in range(3):
        for i, (p, h) in enumerate(units):
            image_d[rows_of(p, PADDED), n * 256 + h * HEAD : n * 256 + (h + 1) * HEAD] = given[n][i]

    gained = text_sum[...]
    for n in range(3):
        wide = jnp.concatenate([w[b * 576 + n * 192 : b * 576 + (n + 1) * 192, :] for b in range(3)], axis=1)
        gained = gained + nn(text_d[n], wide)
    text_sum[...] = gained
    image_sum[...] += nt(image_d[...], side(w, 2304, 1024, 3))

    slot = found.at[step]
    slot[0:size, 0:128] = text_d[0, :, first]
    slot[0:size, 128:256] = text_d[1, :, first]
    slot[size : 2 * size, 0:128] = text_d[2, :, first]
    slot[size : 2 * size, 128:256] = text_c[0, :, first]
    slot[2 * size : 3 * size, 0:128] = jnp.concatenate([text_d[0, :, last], text_d[1, :, last]], axis=1)
    slot[2 * size : 3 * size, 128:256] = jnp.concatenate([text_d[2, :, last], text_c[0, :, last]], axis=1)
    leave_blocks(slot, 3 * size, image_d[...])
    leave_blocks(slot, 3 * size + 3 * image_g.shape[0], image_kept[0, :, 768:1024])
    leave_quarter(step, found, near, keep, out_sems, [copy(n, found.at[n], near.at[n], core) for n in range(2)])

    @pl.when(step == QUARTERS - 1)
    def finish():
        leave_norm(1, text_sum, image_sum, text_pre, image_pre, text_gain, image_gain, text_n, image_n, text_vec, image_vec)


def leave_norm(norm, text_sum, image_sum, text_pre, image_pre, text_gain, image_gain, text_n, image_n, text_vec, image_vec):
    for total, pre, gain, out, vec in (
        (text_sum, text_pre, text_gain, text_n, text_vec),
        (image_sum, image_pre, image_gain, image_n, image_vec),
    ):
        unit, scale = normed(pre[...])
        out[...] = norm_back(unit, scale, gain[0, norm : norm + 1, :].astype(F32), total[...], vec)


def mlp_back(pairs, text_g, image_g, text_one, image_one, text_pre, image_pre, text_gain, image_gain, *refs):
    text_activ, text_slope, image_activ, image_slope = refs[:4]
    parts = refs[4:10]
    text_n, image_n, next_low, text_vec, image_vec, rounded, rounded_near, near, keep = refs[10:19]
    weights, found, text_sum, image_sum, text_g_low, image_g_low, text_d, sems, out_sems, send_sems, recv_sems = refs[19:]
    step = pl.program_id(0)
    fetch(step, BACKWARD, gathered(parts), weights, sems)
    size, image_size = text_g.shape[0], image_g.shape[0]
    core = partners()[0]
    copy = sender(send_sems, recv_sems)
    rounded_copy = copy(2, rounded, rounded_near, core)

    @pl.when(step == 0)
    def begin():
        text_sum[...] = text_g[...]
        image_sum[...] = image_g[...]
        text_g_low[...] = low(text_g[...])
        image_g_low[...] = low(image_g[...])
        leave_blocks(rounded, 0, text_one[...])
        leave_blocks(rounded, 3 * size, text_g_low[...])
        leave_blocks(rounded, 6 * size, image_one[...])
        leave_blocks(rounded, 6 * size + 4 * image_size, image_g_low[...])
        greet(core)
        rounded_copy.start()

    w = weights.at[step]
    slot = found.at[step]
    wide = side(w, 2304, 768, 3)
    for b in range(3):
        columns = slice(b * 256, (b + 1) * 256)
        back = nt(text_g_low[...], wide[columns])
        text_d[:, columns] = low(back * text_slope[0, :, columns].astype(F32))
    text_sum[...] += nt(text_d[...], side(w, 0, 768, 3))
    image_d = low(nt(image_g_low[...], side(w, 5632, 256, 4)) * image_slope[0].astype(F32))
    image_sum[...] += nt(image_d, w[4608:5632, :])
    leave_blocks(slot, 0, text_d[...])
    leave_blocks(slot, 3 * size, text_activ[0])
    leave_blocks(slot, 6 * size, image_d)
    leave_blocks(slot, 6 * size + image_size, image_activ[0])
    leave_quarter(step, found, near, keep, out_sems, [copy(n, found.at[n], near.at[n], core) for n in range(2)])

    @pl.when(step == QUARTERS - 1)
    def finish():
        rounded_copy.wait()
        leave_norm(0, text_sum, image_sum, text_pre, image_pre, text_gain, image_gain, text_n, image_n, text_vec, image_vec)
        leave_blocks(next_low, 0, low(text_n[...]))
        leave_blocks(next_low, 3 * size, low(image_n[...]))


def weight_grad(is_self, sizes, x_at, own, near, own_quarters, near_quarters, *refs):
    to_send, kept, to_z, text_flip, text_g_flip, image_flip, image_g_flip = refs
    size, image_size = sizes
    dp = kept.shape[1]
    x = x_at[0]
    for at, source in ((0, own), (1, near)):
        rows, image_rows = rows_of(at, size), rows_of(at, image_size)
        for b in range(3):
            text_flip[rows_of(b, BLOCK), rows] = source[rows_of(b, size), :].T
            text_g_flip[rows_of(b, BLOCK), rows] = source[rows_of(3 + b, size), :].T
        for b in range(4):
            start = 6 * size
            image_flip[rows_of(b, BLOCK), image_rows] = source[start + b * image_size : start + (b + 1) * image_size, :].T
            start = 6 * size + 4 * image_size
            image_g_flip[rows_of(b, BLOCK), image_rows] = source[start + b * image_size : start + (b + 1) * image_size, :].T

    text_depth, image_depth = DT // (2 * dp), DV // (2 * dp)
    padded = -(-text_depth // 16) * 16

    def write(ref, at, row, depth, value):
        for z in range(dp):
            ref[at, z, row : row + depth, :] = low(value[z * depth : (z + 1) * depth])

    lane = lax.broadcasted_iota(jnp.int32, (1, HEAD), 1) < SELF_HEAD
    for slot in (1, 0):

        def text_block(b):
            return jnp.concatenate([q[slot, rows_of(b, size), :] for q in (own_quarters, near_quarters)], axis=0)

        def image_block(b, text_blocks):
            start = text_blocks * size + b * image_size
            return jnp.concatenate([q[slot, start : start + image_size, :] for q in (own_quarters, near_quarters)], axis=0)

        for apart in range(2):
            half = lax.bitwise_xor(x, apart)
            text_rows = pl.ds(pl.multiple_of(half * (DT // 2), 128), DT // 2)
            image_rows = pl.ds(pl.multiple_of(half * (DV // 2), 128), DV // 2)
            text_lhs, image_lhs = text_flip[text_rows, :], image_flip[image_rows, :]
            text_g_lhs, image_g_lhs = text_g_flip[text_rows, :], image_g_flip[image_rows, :]

            def bottom(b, count, value):
                row = ((2 * slot + apart) * count + b) * image_depth
                for z in range(dp):
                    to_z[z, row : row + image_depth, :] = low(value[z * image_depth : (z + 1) * image_depth])

            if is_self:
                top, at = (to_send if slot else kept), apart
                one, two, three = text_block(0), text_block(1), text_block(2)
                write(top, at, 0, text_depth, nn(text_lhs, one))
                mixed = jnp.concatenate([nn(text_lhs, two[:, :HEAD]), nn(text_g_lhs, two[:, HEAD:])], axis=1)
                write(top, at, padded, text_depth, mixed)
                from_x = nn(text_lhs, three)
                from_g = nn(text_g_lhs, three[:, HEAD:])
                mixed = jnp.concatenate([from_x[:, :HEAD], jnp.where(lane, from_x[:, HEAD:], from_g)], axis=1)
                write(top, at, 2 * padded, text_depth, mixed)
                write(top, at, 3 * padded, image_depth, nn(image_lhs, image_block(0, 3)))
                for b in range(3):
                    bottom(b, 3, nn(image_g_lhs if b == 2 else image_lhs, image_block(1 + b, 3)))
            else:
                top, at = (to_send if apart else kept), slot
                for b in range(6):
                    write(top, at, b * padded, text_depth, nn(text_g_lhs if b > 2 else text_lhs, text_block(b)))
                for b in range(2):
                    bottom(b, 2, nn(image_g_lhs if b else image_lhs, image_block(b, 6)))


def gathered(parts):
    own, near, far, far_rest, corner, corner_rest = parts
    cut = far.shape[0]
    return ((0, 0, own), (1, 0, near), (2, 0, far), (2, cut, far_rest), (3, 0, corner), (3, cut, corner_rest))


ANY = pl.BlockSpec(memory_space=pl.ANY)
SCALARS = pl.BlockSpec(memory_space=pltpu.SMEM)


def whole(array):
    zeros = (0,) * len(array.shape)
    return pl.BlockSpec(array.shape, lambda *s: zeros)


def quarter(array, order):
    tail = (0,) * (len(array.shape) - 1)
    if order is FORWARD:
        return pl.BlockSpec((1,) + array.shape[1:], lambda s: (s,) + tail)
    return pl.BlockSpec((1,) + array.shape[1:], lambda s: (lax.rem(2 * s + 1 - lax.div(s, 2), 4),) + tail)


def shape(*dims, of=BF):
    return jax.ShapeDtypeStruct(dims, of)


def run(kernel, order, operands, outs, scratch, us, meeting=None):
    def spec(kind, array):
        return {"s": lambda: SCALARS, "w": lambda: whole(array), "q": lambda: quarter(array, order), "a": lambda: ANY}[kind]()

    return pl.pallas_call(
        kernel,
        grid=(QUARTERS,) if order else (1,),
        in_specs=[spec(*entry) for entry in operands],
        out_specs=[spec(*entry) for entry in outs],
        out_shape=[array for unused, array in outs],
        scratch_shapes=scratch,
        compiler_params=pltpu.CompilerParams(
            dimension_semantics=("arbitrary",),
            vmem_limit_bytes=60 * 2**20,
            collective_id=meeting,
            has_side_effects=meeting is not None,
        ),
        cost_estimate=pl.CostEstimate(flops=int(us * 1.1e9), bytes_accessed=1024, transcendentals=0),
    )(*[array for unused, array in operands])


def swap(value, axis, apart):
    return lax.ppermute(value, axis, [(i, i ^ apart) for i in range(lax.axis_size(axis))])


def after(value, *earlier):
    return lax.optimization_barrier((value,) + earlier)[0]


class Line:
    def __init__(self):
        self.last = ()

    def take(self, value):
        return after(value, *self.last)

    def leave(self, *values):
        self.last = values


def spread(packed, share):
    far_rest = lax.all_gather(share, ("stream", "dp"), axis=0, tiled=True)
    return packed[0], swap(packed[0], "tensor", 1), swap(packed[1], "tensor", 2), far_rest


def spread_on(line, own, near, far, far_rest):
    far, far_rest = line.take((far, far_rest))
    return own, near, far, far_rest, swap(far, "tensor", 1), swap(far_rest, "tensor", 1)


def add(left, right):
    return low(left.astype(F32) + right.astype(F32))


def fold_last(total):
    return lax.psum_scatter(total, "dp", scatter_dimension=0, tiled=True)[0]


def s(value):
    return ("s", value)


def w(value):
    return ("w", value)


def q(value):
    return ("q", value)


def a(value):
    return ("a", value)


def local(
    text_in,
    image_in,
    lengths,
    text_cot,
    image_cot,
    text_cross_q,
    text_cross_kv,
    text_cross_out,
    text_up,
    text_down,
    text_self_qkv,
    text_self_out,
    text_gain,
    text_bias,
    image_cross_q,
    image_cross_kv,
    image_cross_out,
    image_up,
    image_down,
    image_self_qkv,
    image_self_out,
    image_gain,
    image_bias,
):
    dp = lax.axis_size("dp")
    places = 2 * dp
    x_at = lax.axis_index("stream")
    t_at = lax.axis_index("tensor")
    size = text_in.shape[0]
    pairs = size // SLOTS
    image_size = pairs * PADDED
    units = 2 * pairs
    ids = jnp.stack([x_at, x_at * dp + lax.axis_index("dp")] + [(t_at ^ j) * pairs for j in range(QUARTERS)]).astype(jnp.int32)

    def spaced(rows):
        apart = jnp.pad(rows.reshape(pairs, REGIONS, DV), ((0, 0), (0, PADDED - REGIONS), (0, 0)))
        return apart.reshape(image_size, DV)

    def leave(rows):
        return swap(rows.reshape(pairs, PADDED, DV)[:, :REGIONS].reshape(pairs * REGIONS, DV), "stream", 1).astype(F32)

    line = Line()
    mlp_packed = pack([text_up[0], text_down[0], image_up[0], image_down[0]], places, 5120, ids)
    cross_w = (
        text_cross_q[0],
        image_cross_kv[0].reshape(DT, -1),
        text_cross_kv[0].reshape(DV, -1),
        image_cross_q[0],
        text_cross_out[0],
        image_cross_out[0],
    )
    self_packed = pack(
        [
            text_self_qkv[0].transpose(1, 2, 0).reshape(-1, DT),
            text_self_out[0],
            image_self_qkv[0].reshape(DV, -1),
            image_self_out[0],
        ],
        places,
        3584,
        after(ids, mlp_packed[0]),
    )
    line.leave(self_packed[0], cross_w[1], cross_w[2])
    mlp_share = line.take(swap(mlp_packed[2], "tensor", 2))
    self_share = line.take(swap(self_packed[2], "tensor", 2))
    line.leave(mlp_share, self_share)
    mlp_w = spread(mlp_packed, mlp_share)
    self_w = spread(self_packed, after(self_share, mlp_share))
    image_cot_here = swap(spaced(image_cot), "stream", 1)

    text_wide, image_wide = shape(size, DT, of=F32), shape(image_size, DV, of=F32)
    text_f32, image_f32 = pltpu.VMEM((size, DT), F32), pltpu.VMEM((image_size, DV), F32)
    text_bf, image_bf = pltpu.VMEM((size, DT), BF), pltpu.VMEM((image_size, DV), BF)
    in_sems, out_sems = pltpu.SemaphoreType.DMA((6,)), pltpu.SemaphoreType.DMA((2,))
    text_affine = [w(text_gain), w(text_bias)]
    image_affine = [w(image_gain), w(image_bias)]
    vector_outs = [w(shape(2, DT, of=F32)), w(shape(2, DV, of=F32))]
    part_rows = 3 * size + 4 * image_size

    def buffer(weights):
        return pltpu.VMEM((QUARTERS, weights[0].shape[0], BLOCK), BF)

    in_four = [
        (QUARTERS, size, DT),
        (QUARTERS, image_size, DV),
        (QUARTERS, size, 1024),
        (QUARTERS, image_size, 1024),
        (QUARTERS, units, SLOTS, PADDED),
        (QUARTERS, units, PADDED, SLOTS),
    ]

    def links(count):
        return [pltpu.SemaphoreType.DMA((count,)), pltpu.SemaphoreType.DMA((count,))]

    text_pre1, image_pre1, image, texts, images, *cross_kept = run(
        functools.partial(cross_forward, pairs),
        None,
        [s(lengths), w(line.take(text_in)), w(spaced(image_in))] + [w(m) for m in cross_w],
        [w(text_wide), w(image_wide), w(shape(image_size, DV))] + [a(shape(*dims)) for dims in in_four],
        [pltpu.VMEM(dims, BF) for dims in in_four]
        + [pltpu.VMEM((QUARTERS, part_rows, BLOCK), BF), pltpu.VMEM((part_rows, BLOCK), BF), pltpu.VMEM((3, part_rows, BLOCK), BF)]
        + links(10)
        + [pltpu.SemaphoreType.DMA((6,))],
        70,
        1,
    )
    line.leave(text_pre1, image_cot_here)
    mlp_w = spread_on(line, *mlp_w)
    self_w = (*self_w[:2], swap(line.take(self_packed[1]), "tensor", 2), self_w[3])
    (
        text_one,
        image_one,
        text_pre2,
        image_pre2,
        text_activ,
        text_slope,
        image_activ,
        image_slope,
    ) = run(
        functools.partial(mlp_forward, pairs),
        FORWARD,
        [w(text_pre1), w(image_pre1)] + text_affine + image_affine + [a(m) for m in mlp_w],
        [
            w(shape(size, DT)),
            w(shape(image_size, DV)),
            w(text_wide),
            w(image_wide),
            q(shape(QUARTERS, size, 768)),
            q(shape(QUARTERS, size, 768)),
            q(shape(QUARTERS, image_size, 256)),
            q(shape(QUARTERS, image_size, 256)),
        ],
        [buffer(mlp_w), in_sems],
        1,
    )
    line.leave(text_pre2)
    self_w = spread_on(line, *self_w)
    (
        text_out,
        image_out,
        text_n3,
        image_n3,
        text_vec3,
        image_vec3,
        self_rounded,
        self_q,
        self_k,
        self_v,
        self_c,
        self_probs,
        self_kept,
        self_image_probs,
    ) = run(
        functools.partial(self_forward, pairs),
        FORWARD,
        [s(ids), s(lengths), w(text_pre2), w(image_pre2)]
        + text_affine
        + image_affine
        + [w(text_cot), w(image_cot_here)]
        + [a(m) for m in self_w],
        [w(text_wide), w(shape(image_size, DV)), w(text_wide), w(image_wide)]
        + vector_outs
        + [
            w(shape(2 * part_rows, BLOCK)),
            q(shape(QUARTERS, size, 192)),
            q(shape(QUARTERS, size, 192)),
            q(shape(QUARTERS, size, 192)),
            q(shape(QUARTERS, size, 192)),
            q(shape(QUARTERS, pairs, 384, SLOTS)),
            q(shape(QUARTERS, image_size, 1024)),
            q(shape(QUARTERS, units, PADDED, PADDED)),
        ],
        [buffer(self_w), text_f32, image_f32, text_bf, image_bf, in_sems],
        19,
    )
    image_out = leave(image_out)

    text_depth, image_depth = DT // places, DV // places
    padded = -(-text_depth // 16) * 16

    def back_scratch(weights, rows):
        return [
            buffer(weights),
            pltpu.VMEM((QUARTERS, rows, BLOCK), BF),
            text_f32,
            image_f32,
            text_bf,
            image_bf,
        ]

    def weight_grads(is_self, turn, rounded, rounded_near, kept, kept_near):
        top = 3 * padded + image_depth if is_self else 6 * padded
        bottom = (3 if is_self else 2) * image_depth
        outs = [w(shape(2, dp, top, BLOCK)), w(shape(2, dp, top, BLOCK)), w(shape(dp, 4 * bottom, BLOCK))]
        return run(
            functools.partial(weight_grad, is_self, (size, image_size)),
            None,
            [s(turn), w(rounded), w(rounded_near), w(kept), w(kept_near)],
            outs,
            [
                pltpu.VMEM((DT, 2 * size), BF),
                pltpu.VMEM((DT, 2 * size), BF),
                pltpu.VMEM((DV, 2 * image_size), BF),
                pltpu.VMEM((DV, 2 * image_size), BF),
            ],
            12,
        )

    self_rows = 3 * size + 4 * image_size
    self_rounded_near = swap(self_rounded, "tensor", 1)
    text_n2, image_n2, text_vec2, image_vec2, self_near, self_keep = run(
        functools.partial(self_back, pairs),
        BACKWARD,
        [
            w(text_n3),
            w(image_n3),
            w(text_pre2),
            w(image_pre2),
            w(text_gain),
            w(image_gain),
            q(self_q),
            q(self_k),
            q(self_v),
            q(self_c),
            q(self_probs),
            q(self_kept),
            q(self_image_probs),
        ]
        + [a(m) for m in self_w],
        [w(text_wide), w(image_wide)] + vector_outs + [a(shape(2, self_rows, BLOCK)), a(shape(2, self_rows, BLOCK))],
        back_scratch(self_w, self_rows)
        + [pltpu.VMEM((3, size, 192), BF), pltpu.VMEM((image_size, 768), BF), in_sems, out_sems]
        + links(2),
        23,
        2,
    )
    to_y, self_top, to_z = weight_grads(True, ids, self_rounded, self_rounded_near, self_keep, self_near)
    self_by_y = swap(to_y, "tensor", 2)
    self_bottom = fold_last(to_z)
    line.leave(self_top)
    mlp_rows = 6 * size + 2 * image_size
    text_n1, image_n1, grad_low, text_vec1, image_vec1, mlp_rounded, mlp_rounded_near, mlp_near, mlp_keep = run(
        functools.partial(mlp_back, pairs),
        BACKWARD,
        [
            w(text_n2),
            w(image_n2),
            w(text_one),
            w(image_one),
            w(text_pre1),
            w(image_pre1),
            w(line.take(text_gain)),
            w(image_gain),
            q(text_activ),
            q(text_slope),
            q(image_activ),
            q(image_slope),
        ]
        + [a(m) for m in mlp_w],
        [w(text_wide), w(image_wide), w(shape(part_rows, BLOCK))]
        + vector_outs
        + [
            w(shape(2 * part_rows, BLOCK)),
            a(shape(2 * part_rows, BLOCK)),
            a(shape(2, mlp_rows, BLOCK)),
            a(shape(2, mlp_rows, BLOCK)),
        ],
        back_scratch(mlp_w, mlp_rows) + [text_bf, in_sems, out_sems] + links(3),
        20,
        3,
    )
    line.leave(grad_low)
    to_x, mlp_top, to_z = weight_grads(False, line.take(ids), mlp_rounded, mlp_rounded_near, mlp_keep, mlp_near)
    self_top, self_by_y, to_x, to_z = after((self_top, self_by_y, to_x, to_z), mlp_top)
    mlp_by_x = swap(to_x, "stream", 1)
    mlp_bottom = fold_last(to_z)
    self_top, to_x = add(self_top[0], self_by_y[0]), add(self_top[1], self_by_y[1])
    self_then_x = swap(to_x, "stream", 1)
    line.leave(self_top, to_x)
    d_dims = [(QUARTERS, part_rows, BLOCK), (QUARTERS, size, 768), (QUARTERS, image_size, 768)]
    vectors = jnp.concatenate(
        [jnp.pad(v, ((0, 0), (0, DV - DT))) for v in (text_vec1, text_vec2, text_vec3)]
        + [image_vec1, image_vec2, image_vec3, jnp.zeros((4, DV), F32)],
        axis=0,
    )
    grads, text_d, image_d, own_sum, total, vectors = run(
        functools.partial(cross_back, pairs),
        None,
        [w(line.take(grad_low)), w(vectors)] + [w(k) for k in cross_kept] + [w(m) for m in cross_w],
        [a(shape(*dims)) for dims in d_dims]
        + [w(shape(part_rows, BLOCK, of=F32)), w(shape(part_rows, BLOCK)), w(shape(16, DV, of=F32))],
        [pltpu.VMEM(dims, BF) for dims in d_dims]
        + [pltpu.VMEM((QUARTERS, part_rows, BLOCK), BF), pltpu.VMEM((2, part_rows, BLOCK), BF), pltpu.VMEM((2, 16, DV), F32)]
        + links(7)
        + [pltpu.SemaphoreType.DMA((3,))],
        48,
        4,
    )
    line.leave(total)
    text_only, image_only = 4 * padded + 16, 4 * image_depth
    text_vector = jnp.pad(vectors[:6, :DT].reshape(6, places, text_depth), ((0, 0), (0, 0), (0, BLOCK - text_depth)))
    image_vector = jnp.pad(vectors[6:].reshape(10, places, image_depth), ((0, 0), (0, 0), (0, BLOCK - image_depth)))
    vectors = low(jnp.concatenate([text_vector, image_vector], axis=0).transpose(1, 0, 2))
    vector_keep = lax.dynamic_slice_in_dim(vectors, x_at * dp, dp, 0)
    vector_send = lax.dynamic_slice_in_dim(vectors, (1 - x_at) * dp, dp, 0)
    text_grad, image_grad, cross_text, image_keep, image_send = run(
        cross_last,
        None,
        [
            w(line.take(total)),
            w(own_sum),
            w(vector_keep),
            w(vector_send),
            w(text_n1),
            w(image_n1),
            w(texts),
            w(images),
            w(grads),
            w(cross_kept[0]),
            w(cross_kept[1]),
            w(text_d),
            w(image_d),
        ],
        [
            w(text_wide),
            w(shape(image_size, DV)),
            w(shape(dp, text_only, BLOCK)),
            w(shape(dp, image_only, BLOCK)),
            w(shape(dp, image_only, BLOCK)),
        ],
        [
            pltpu.VMEM((part_rows, BLOCK), BF),
            pltpu.VMEM((dp, text_only, BLOCK), BF),
            pltpu.VMEM((dp, text_only, BLOCK), BF),
            pltpu.VMEM((DT, QUARTERS * size), BF),
            pltpu.VMEM((DT, QUARTERS * size), BF),
            pltpu.VMEM((DV, QUARTERS * image_size), BF),
            pltpu.VMEM((DV, QUARTERS * image_size), BF),
        ]
        + links(2),
        2,
        5,
    )
    line.leave(text_grad)
    self_top, self_then_x, mlp_top, mlp_by_x, self_bottom, cross_text, image_send = line.take(
        (self_top, self_then_x, mlp_top, mlp_by_x, self_bottom, cross_text, image_send)
    )
    cross_text = fold_last(cross_text)
    image_send = swap(image_send, "stream", 1)
    mlp_top, to_y = add(mlp_top[0], mlp_by_x[0]), add(mlp_top[1], mlp_by_x[1])
    mlp_then_y = swap(to_y, "tensor", 2)
    self_top = fold_last(add(self_top, self_then_x))
    line.leave(mlp_top, to_y)
    self_bottom = line.take(self_bottom).reshape(2, 2, 3 * image_depth, BLOCK)
    self_bottom_x = swap(self_bottom[:, 1], "stream", 1)
    cross_image = add(image_keep, line.take(image_send))
    line.leave(cross_image)
    cross_image = fold_last(cross_image)
    self_bottom = add(self_bottom[:, 0], line.take(self_bottom_x))
    self_bottom_y = swap(self_bottom[1], "tensor", 2)
    mlp_bottom = line.take(mlp_bottom).reshape(2, 2, 2 * image_depth, BLOCK)
    mlp_bottom_x = swap(mlp_bottom[:, 1], "stream", 1)
    mlp_top = add(mlp_top, line.take(mlp_then_y))
    line.leave(mlp_top)
    mlp_top = fold_last(mlp_top)
    mlp_bottom = add(mlp_bottom[:, 0], line.take(mlp_bottom_x))
    mlp_bottom = add(mlp_bottom[0], swap(mlp_bottom[1], "tensor", 2))
    self_bottom = add(self_bottom[0], self_bottom_y)
    self_grads = jnp.concatenate([self_top, self_bottom], axis=0)
    image_grad = leave(image_grad)

    def pick(packed, first, count, depth, stride):
        rows = [packed[first + b * stride : first + b * stride + depth] for b in range(count)]
        return jnp.concatenate(rows, axis=1).astype(F32)

    def text_pick(packed, first, count):
        return pick(packed, first, count, text_depth, padded)

    def image_pick(packed, first, count):
        return pick(packed, first, count, image_depth, image_depth)

    sums = cross_text[4 * padded :].astype(F32)
    text_vectors, image_vectors = sums[:6, :text_depth], sums[6:12, :image_depth]

    self_text = text_pick(self_grads, 0, 3)

    def heads(at):
        return jnp.concatenate([self_text[:, at * 128 : (at + 1) * 128], self_text[:, 512 + at * 64 : 576 + at * 64]], axis=1)

    below = 3 * padded
    return (
        text_out,
        image_out,
        text_grad,
        image_grad,
        text_pick(cross_text, 0, 1)[None],
        image_pick(cross_image, 0, 2).reshape(1, image_depth, 2, 256),
        text_pick(cross_text, 3 * padded, 1).T[None],
        text_pick(mlp_top, 0, 3)[None],
        text_pick(mlp_top, below, 3).T[None],
        jnp.stack([heads(n) for n in range(3)], axis=1)[None],
        heads(3).T[None],
        text_vectors[0::2][None],
        text_vectors[1::2][None],
        image_pick(cross_image, 2 * image_depth, 1)[None],
        text_pick(cross_text, padded, 2).reshape(1, text_depth, 2, 256),
        image_pick(cross_image, 3 * image_depth, 1).T[None],
        image_pick(mlp_bottom, 0, 1)[None],
        image_pick(mlp_bottom, image_depth, 1).T[None],
        image_pick(self_grads, below, 3).reshape(1, image_depth, 3, 256),
        image_pick(self_grads, below + 3 * image_depth, 1).T[None],
        image_vectors[0::2][None],
        image_vectors[1::2][None],
    )


def solution(mesh):
    rows = P(("stream", "dp", "tensor"), None)
    wide_in = P(None, None, "tensor")
    group_in = P(None, None, None, "tensor")
    wide_out = P(None, "tensor", None)
    grad_in = P(None, ("stream", "dp"), "tensor")
    grad_group = P(None, ("stream", "dp"), None, "tensor")
    grad_out = P(None, "tensor", ("stream", "dp"))
    vector = P(None, None, ("stream", "dp"))
    weights = (wide_in, group_in, wide_out, wide_in, wide_out, group_in, wide_out, P(), P())
    grads = (grad_in, grad_group, grad_out, grad_in, grad_out, grad_group, grad_out, vector, vector)
    return jax.shard_map(
        local,
        mesh=mesh,
        in_specs=(rows, rows, P(("stream", "dp")), rows, rows) + weights + weights,
        out_specs=(rows, rows, rows, rows) + grads + grads,
        check_vma=False,
    )
```

```python
import functools

import jax
import jax.numpy as jnp
from jax import lax
from jax.experimental import pallas as pl
from jax.experimental.pallas import tpu as pltpu
from jax.sharding import PartitionSpec as P

DT = 768
DV = 1024
HEAD = 128
SELF_HEAD = 64
SLOTS = 128
REGIONS = 37
PADDED = 48
QUARTERS = 4
BLOCK = 256

norm_eps = 1e-05
masked_score = -1e30

BF = jnp.bfloat16
F32 = jnp.float32
FORWARD = (0, 1, 2, 3)
BACKWARD = (1, 3, 0, 2)


def nn(left, right):
    return lax.dot_general(left, right, (((1,), (0,)), ((), ())), preferred_element_type=F32)


def nt(left, right):
    return lax.dot_general(left, right, (((1,), (1,)), ((), ())), preferred_element_type=F32)


def tn(left, right):
    return lax.dot_general(left, right, (((0,), (0,)), ((), ())), preferred_element_type=F32)


def low(value):
    return value.astype(BF)


def normed(inputs):
    centered = inputs - jnp.mean(inputs, axis=-1, keepdims=True)
    scale = lax.rsqrt(jnp.mean(centered * centered, axis=-1, keepdims=True) + norm_eps)
    return centered * scale, scale


def norm_back(unit, scale, gain, grad, vec):
    vec[0:1] = jnp.sum(grad * unit, axis=0, keepdims=True)
    vec[1:2] = jnp.sum(grad, axis=0, keepdims=True)
    inner = grad * gain
    shift = jnp.mean(inner, axis=-1, keepdims=True)
    slope = jnp.mean(inner * unit, axis=-1, keepdims=True)
    return scale * (inner - shift - unit * slope)


def softmax_all(scores):
    tops = [jnp.max(s, axis=-1, keepdims=True) for s in scores]
    powers = [jnp.exp(s - t) for s, t in zip(scores, tops)]
    sums = [jnp.sum(e, axis=-1, keepdims=True) for e in powers]
    return [low(e / total) for e, total in zip(powers, sums)]


def attend(queries, keys, values, scale, masks):
    scores = [nt(q, k) * scale for q, k in zip(queries, keys)]
    scores = [s if m is None else jnp.where(m, s, masked_score) for s, m in zip(scores, masks)]
    probs = softmax_all(scores)
    return probs, [nn(p, v) for p, v in zip(probs, values)]


def attend_back(queries, keys, values, probs, grads, scale):
    grad_probs = [nt(g, v) for g, v in zip(grads, values)]
    grad_values = [low(tn(p, g)) for p, g in zip(probs, grads)]
    wide = [p.astype(F32) for p in probs]
    inner = [jnp.sum(p * g, axis=-1, keepdims=True) for p, g in zip(wide, grad_probs)]
    grad_scores = [low(p * (g - i)) for p, g, i in zip(wide, grad_probs, inner)]
    grad_queries = [low(nn(g, k) * scale) for g, k in zip(grad_scores, keys)]
    grad_keys = [low(tn(g, q) * scale) for g, q in zip(grad_scores, queries)]
    return grad_queries, grad_keys, grad_values


def side(ref, row, width, count):
    return jnp.concatenate([ref[row + b * width : row + (b + 1) * width, :] for b in range(count)], axis=1)


def rows_of(pair, size):
    return slice(pair * size, (pair + 1) * size)


def fetch(step, order, own, near, far, far_rest, corner, buffer, sems):
    slots = [order.index(quarter) for quarter in range(QUARTERS)]
    cut, rest = far.shape[0], far_rest.shape[0]
    copies = [
        (slots[0], pltpu.make_async_copy(own, buffer.at[slots[0]], sems.at[0])),
        (slots[1], pltpu.make_async_copy(near, buffer.at[slots[1]], sems.at[1])),
        (slots[2], pltpu.make_async_copy(far, buffer.at[slots[2], pl.ds(0, cut)], sems.at[2])),
        (slots[2], pltpu.make_async_copy(far_rest, buffer.at[slots[2], pl.ds(cut, rest)], sems.at[3])),
    ]
    if corner is not None:
        copies.append((slots[3], pltpu.make_async_copy(corner, buffer.at[slots[3]], sems.at[4])))
    copies.sort(key=lambda entry: entry[0])

    @pl.when(step == 0)
    def begin():
        for unused, copy in copies:
            copy.start()

    for at in range(QUARTERS):

        @pl.when(step == at)
        def arrive():
            for slot, copy in copies:
                if slot == at:
                    copy.wait()


def fetch_round(step, own, near, far, far_rest, corner, buffer, sems, send_sems, recv_sems):
    core = partners()[0]
    copy = sender(send_sems, recv_sems)
    cut, rest = far.shape[0], far_rest.shape[0]
    over = copy(0, far, buffer.at[3, pl.ds(0, cut)], core), copy(1, far_rest, buffer.at[3, pl.ds(cut, rest)], core)
    leaving = pltpu.make_async_copy(buffer.at[3], corner, sems.at[4])
    fetch(step, FORWARD, own, near, far, far_rest, None, buffer, sems)

    @pl.when(step == 0)
    def begin():
        greet(core)
        for transfer in over:
            transfer.start()

    @pl.when(step == 3)
    def last():
        for transfer in over:
            transfer.wait()
        leaving.start()

    return leaving


def spacing(pairs):
    rows, columns = pairs * PADDED, pairs * REGIONS
    row = lax.broadcasted_iota(jnp.int32, (rows, columns), 0)
    column = lax.broadcasted_iota(jnp.int32, (rows, columns), 1)
    chosen = jnp.zeros((rows, columns), F32)
    for p in range(pairs):
        inside = (column >= p * REGIONS) & (column < (p + 1) * REGIONS)
        chosen = jnp.where(inside & (row - p * PADDED == column - p * REGIONS), 1.0, chosen)
    return low(chosen)


def leave_quarter(step, buffer, near, keep, sems, copies):
    kept = [pltpu.make_async_copy(buffer.at[at], keep.at[at - 2], sems.at[at - 2]) for at in (2, 3)]
    for at in range(QUARTERS):

        @pl.when(step == at)
        def leave():
            (copies[at] if at < 2 else kept[at - 2]).start()

    @pl.when(step == QUARTERS - 1)
    def finish():
        for copy in list(copies) + kept:
            copy.wait()


def affine_row(gain, bias, norm):
    return gain[0, norm : norm + 1, :].astype(F32), bias[0, norm : norm + 1, :].astype(F32)


def leave_blocks(ref, row, value):
    size = value.shape[0]
    for b in range(value.shape[1] // BLOCK):
        ref[row + b * size : row + (b + 1) * size, :] = value[:, b * BLOCK : (b + 1) * BLOCK]


MESH = pl.DeviceIdType.MESH


def partners():
    t = lax.axis_index("tensor")
    return {"tensor": lax.bitwise_xor(t, 1)}, {"tensor": lax.bitwise_xor(t, 2)}, {"stream": lax.bitwise_xor(lax.axis_index("stream"), 1)}


def greet(*others):
    barrier = pltpu.get_barrier_semaphore()
    for other in others:
        pl.semaphore_signal(barrier, inc=1, device_id=other, device_id_type=MESH)
    pl.semaphore_wait(barrier, len(others))


def sender(send_sems, recv_sems):
    def copy(number, source, target, to):
        return pltpu.make_async_remote_copy(
            src_ref=source,
            dst_ref=target,
            send_sem=send_sems.at[number],
            recv_sem=recv_sems.at[number],
            device_id=to,
            device_id_type=MESH,
        )

    return copy


def pack(pieces, places, rest, ids):
    total = sum(m.size for m in pieces) // BLOCK
    cut, share = total - rest, rest // places

    def kernel(ids, *refs):
        sources, (own, first, mine) = refs[: len(pieces)], refs[len(pieces) :]
        row = 0
        for ref in sources:
            leave_blocks(own, row, ref[...])
            row += ref.size // BLOCK
        first[...] = own[0:cut, :]
        mine[...] = own[pl.ds(pl.multiple_of(cut + ids[1] * share, 16), share), :]

    return run(
        kernel,
        None,
        [s(ids)] + [w(m) for m in pieces],
        [w(shape(total, BLOCK)), w(shape(cut, BLOCK)), w(shape(share, BLOCK))],
        [],
        3,
    )


def cross_block(pairs, first, lengths, text, image, matrices, text_kept, image_kept, text_probs, image_probs, part):
    wq, wkv_text, wkv_image, wq_image, w_out, w_out_image = matrices
    text_low = text[...]
    image_low = image[...]
    text_kept[:, 0:256] = low(nn(text_low, wq[...]))
    text_kept[:, 256:768] = low(nn(text_low, wkv_text[...]))
    image_kept[:, 0:512] = low(nn(image_low, wkv_image[...]))
    image_kept[:, 512:768] = low(nn(image_low, wq_image[...]))

    image_mask = lax.broadcasted_iota(jnp.int32, (SLOTS, PADDED), 1) < REGIONS
    slots = lax.broadcasted_iota(jnp.int32, (PADDED, SLOTS), 1)
    units = [(p, h) for p in range(pairs) for h in range(2)]

    def text_part(at):
        return [text_kept[rows_of(p, SLOTS), at + h * HEAD : at + (h + 1) * HEAD] for p, h in units]

    def image_part(at):
        return [image_kept[rows_of(p, PADDED), at + h * HEAD : at + (h + 1) * HEAD] for p, h in units]

    scale = HEAD**-0.5
    probs, context = attend(text_part(0), image_part(0), image_part(256), scale, [image_mask] * len(units))
    for i, (p, h) in enumerate(units):
        text_probs[i] = probs[i]
        text_kept[rows_of(p, SLOTS), 768 + h * HEAD : 768 + (h + 1) * HEAD] = low(context[i])
    limits = [lengths[first + p] for p in range(pairs)]
    masks = [slots < limits[p] for p, h in units]
    probs, context = attend(image_part(512), text_part(256), text_part(512), scale, masks)
    for i, (p, h) in enumerate(units):
        image_probs[i] = probs[i]
        image_kept[rows_of(p, PADDED), 768 + h * HEAD : 768 + (h + 1) * HEAD] = low(context[i])
    leave_blocks(part, 0, low(nn(text_kept[:, 768:1024], w_out[...])))
    leave_blocks(part, 3 * text.shape[0], low(nn(image_kept[:, 768:1024], w_out_image[...])))


def cross_forward(pairs, lengths, text, image, *refs):
    matrices = refs[:6]
    text_pre, image_pre = refs[6:8]
    outs = refs[8:14]
    texts, images, text_kept, image_kept, text_probs, image_probs, parts, total, got, image_apart = refs[14:24]
    send_sems, recv_sems, out_sems = refs[24:]
    core, y, x = partners()
    copy = sender(send_sems, recv_sems)
    text_core = copy(0, text, texts.at[1], core)
    text_y = copy(1, text, texts.at[2], y)
    image_x = copy(2, image_apart, images.at[0], x)
    image_core = copy(3, images.at[0], images.at[1], core)
    image_y = copy(4, images.at[0], images.at[2], y)
    text_corner = copy(5, texts.at[2], texts.at[3], core)
    image_corner = copy(6, images.at[2], images.at[3], core)
    near_part = copy(7, parts.at[1], got.at[0], core)
    corner_part = copy(8, parts.at[3], got.at[1], core)
    far_part = copy(9, total, got.at[2], y)

    image_apart[...] = low(nn(spacing(pairs), image[...]))
    greet(core, y, x)
    image_x.start()
    text_y.start()
    text_core.start()
    texts[0] = text[...]
    image_x.wait()
    image_y.start()
    image_core.start()

    def block(j, unused):
        @pl.when(j == 1)
        def near():
            text_core.wait()
            image_core.wait()

        @pl.when(j == 2)
        def far():
            text_y.wait()
            text_corner.start()
            image_y.wait()
            image_corner.start()

        @pl.when(j == 3)
        def corner():
            text_corner.wait()
            image_corner.wait()

        cross_block(
            pairs,
            lax.bitwise_xor(lax.axis_index("tensor"), j) * pairs,
            lengths,
            texts.at[j],
            images.at[j],
            matrices,
            text_kept.at[j],
            image_kept.at[j],
            text_probs.at[j],
            image_probs.at[j],
            parts.at[j],
        )

        @pl.when(j == 1)
        def near_done():
            near_part.start()

        return unused

    lax.fori_loop(0, QUARTERS, block, 0)
    corner_part.start()
    leaving = [
        pltpu.make_async_copy(source, out, out_sems.at[i])
        for i, (source, out) in enumerate(
            zip((texts, images, text_kept, image_kept, text_probs, image_probs), outs)
        )
    ]
    for leave in leaving:
        leave.start()
    corner_part.wait()
    total[...] = add(parts[2], got[1])
    far_part.start()
    near_part.wait()
    size, image_size = text.shape[0], image_apart.shape[0]
    below = 3 * size

    def summed(row, depth, count, start):
        for ref in (parts.at[0], got.at[0]):
            start = start + side(ref, row, depth, count).astype(F32)
        return start

    text_pre[...] = summed(0, size, 3, text[...].astype(F32))
    image_pre[...] = summed(below, image_size, 4, images[0].astype(F32))
    far_part.wait()
    text_pre[...] += side(got.at[2], 0, size, 3).astype(F32)
    image_pre[...] += side(got.at[2], below, image_size, 4).astype(F32)
    for leave in leaving:
        leave.wait()


def cross_block_back(pairs, grad, matrices, text_kept, image_kept, text_probs, image_probs, text_d, image_d, part):
    wq, wkv_text, wkv_image, wq_image, w_out, w_out_image = matrices
    text_rows, image_rows = text_kept.shape[0], image_kept.shape[0]
    text_dc = low(nt(side(grad, 0, text_rows, 3), w_out[...]))
    image_dc = low(nt(side(grad, 3 * text_rows, image_rows, 4), w_out_image[...]))
    units = [(p, h) for p in range(pairs) for h in range(2)]

    def text_part(at):
        return [text_kept[rows_of(p, SLOTS), at + h * HEAD : at + (h + 1) * HEAD] for p, h in units]

    def image_part(at):
        return [image_kept[rows_of(p, PADDED), at + h * HEAD : at + (h + 1) * HEAD] for p, h in units]

    scale = HEAD**-0.5
    outer = [text_dc[rows_of(p, SLOTS), h * HEAD : (h + 1) * HEAD] for p, h in units]
    probs = [text_probs[i] for i in range(len(units))]
    found = attend_back(text_part(0), image_part(0), image_part(256), probs, outer, scale)
    for i, (p, h) in enumerate(units):
        text_d[rows_of(p, SLOTS), h * HEAD : (h + 1) * HEAD] = found[0][i]
        image_d[rows_of(p, PADDED), h * HEAD : (h + 1) * HEAD] = found[1][i]
        image_d[rows_of(p, PADDED), 256 + h * HEAD : 256 + (h + 1) * HEAD] = found[2][i]
    outer = [image_dc[rows_of(p, PADDED), h * HEAD : (h + 1) * HEAD] for p, h in units]
    probs = [image_probs[i] for i in range(len(units))]
    found = attend_back(image_part(512), text_part(256), text_part(512), probs, outer, scale)
    for i, (p, h) in enumerate(units):
        image_d[rows_of(p, PADDED), 512 + h * HEAD : 512 + (h + 1) * HEAD] = found[0][i]
        text_d[rows_of(p, SLOTS), 256 + h * HEAD : 256 + (h + 1) * HEAD] = found[1][i]
        text_d[rows_of(p, SLOTS), 512 + h * HEAD : 512 + (h + 1) * HEAD] = found[2][i]
    text_dx = nt(text_d[:, 0:256], wq[...]) + nt(text_d[:, 256:768], wkv_text[...])
    image_dx = nt(image_d[:, 0:512], wkv_image[...]) + nt(image_d[:, 512:768], wq_image[...])
    leave_blocks(part, 0, low(text_dx))
    leave_blocks(part, 3 * text_rows, low(image_dx))


def cross_back(pairs, grad, vectors, text_kept, image_kept, text_probs, image_probs, *refs):
    matrices = refs[:6]
    grads_out, text_d_out, image_d_out, own_sum, total, vector_sum = refs[6:12]
    grads, text_d, image_d, parts, got, got_vectors, send_sems, recv_sems, out_sems = refs[12:]
    core, y, unused_x = partners()
    copy = sender(send_sems, recv_sems)
    to_core = copy(0, grad, grads.at[1], core)
    to_y = copy(1, grad, grads.at[2], y)
    corner = copy(2, grads.at[2], grads.at[3], core)
    near_part = copy(3, parts.at[1], got.at[0], core)
    corner_part = copy(4, parts.at[3], got.at[1], core)
    vectors_core = copy(5, vectors, got_vectors.at[0], core)
    vectors_y = copy(6, vector_sum, got_vectors.at[1], y)
    greet(core, y)
    vectors_core.start()
    to_y.start()
    to_core.start()
    grads[0] = grad[...]
    vectors_core.wait()
    vector_sum[...] = vectors[...] + got_vectors[0]
    vectors_y.start()

    def block(j, unused):
        @pl.when(j == 1)
        def near():
            to_core.wait()

        @pl.when(j == 2)
        def far():
            to_y.wait()
            corner.start()

        @pl.when(j == 3)
        def last():
            corner.wait()

        cross_block_back(
            pairs,
            grads.at[j],
            matrices,
            text_kept.at[j],
            image_kept.at[j],
            text_probs.at[j],
            image_probs.at[j],
            text_d.at[j],
            image_d.at[j],
            parts.at[j],
        )

        @pl.when(j == 1)
        def near_done():
            near_part.start()

        return unused

    lax.fori_loop(0, QUARTERS, block, 0)
    corner_part.start()
    leaving = [
        pltpu.make_async_copy(source, out, out_sems.at[i])
        for i, (source, out) in enumerate(((grads, grads_out), (text_d, text_d_out), (image_d, image_d_out)))
    ]
    for leave in leaving:
        leave.start()
    near_part.wait()
    own_sum[...] = parts[0].astype(F32) + got[0].astype(F32)
    vectors_y.wait()
    vector_sum[...] += got_vectors[1]
    corner_part.wait()
    total[...] = add(parts[2], got[1])
    for leave in leaving:
        leave.wait()


def cross_last(total, own_sum, vector_keep, vector_send, self_top, self_x, text_n, image_n, texts, images, grads, text_kept, image_kept, text_d, image_d, *refs):
    text_grad, image_grad, text_keep, image_keep, image_send, self_sum = refs[:6]
    got, text_send, text_got, self_all, self_got, text_flip, text_g_flip, image_flip, image_g_flip, send_sems, recv_sems = refs[6:]
    unused_core, y, x = partners()
    copy = sender(send_sems, recv_sems)
    far = copy(0, total, got, y)
    text_x = copy(1, text_send, text_got, x)
    dp = self_all.shape[0]
    z_at = lax.axis_index("dp")
    others = [lax.rem(z_at + k, dp) for k in range(1, dp)]
    along_z = [copy(2 + k, self_all.at[other], self_got.at[k], {"dp": other}) for k, other in enumerate(others)]
    greet(y, x, *[{"dp": other} for other in others])
    far.start()
    self_all[...] = add(self_top[...], self_x[...])
    for transfer in along_z:
        transfer.start()
    size, image_size = texts.shape[1], images.shape[1]
    below = 3 * size
    for j in range(QUARTERS):
        text_flip[:, rows_of(j, size)] = texts[j].T
        image_flip[:, rows_of(j, image_size)] = images[j].T
        for b in range(3):
            text_g_flip[rows_of(b, BLOCK), rows_of(j, size)] = grads[j, rows_of(b, size), :].T
        for b in range(4):
            start = below + b * image_size
            image_g_flip[rows_of(b, BLOCK), rows_of(j, image_size)] = grads[j, start : start + image_size, :].T
    at = lax.axis_index("stream")
    for flip, g_flip, d, kept, keep, send in (
        (text_flip, text_g_flip, text_d, text_kept, text_keep, text_send),
        (image_flip, image_g_flip, image_d, image_kept, image_keep, image_send),
    ):
        dp = keep.shape[0]
        half = flip.shape[0] // 2
        depth = half // dp
        padded = -(-depth // 16) * 16
        rows = flip.shape[1]
        outer = d[...].reshape(rows, 768)
        context = kept[:, :, 768:1024].reshape(rows, 256)
        for out, apart in ((send, 1), (keep, 0)):
            start = pl.multiple_of(lax.bitwise_xor(at, apart) * half, 128)
            found = nn(flip[pl.ds(start, half), :], outer)
            last = nn(g_flip[pl.ds(start, half), :], context)
            for z in range(dp):
                taken = slice(z * depth, (z + 1) * depth)
                for b in range(3):
                    out[z, b * padded : b * padded + depth, :] = low(found[taken, b * BLOCK : (b + 1) * BLOCK])
                out[z, 3 * padded : 3 * padded + depth, :] = low(last[taken])
        if flip is text_flip:
            for out, vector in ((text_keep, vector_keep), (text_send, vector_send)):
                below_all = out.shape[1] - vector.shape[1]
                for z in range(dp):
                    out[z, below_all:, :] = vector[z]
            text_x.start()
    summed = self_all[z_at].astype(F32)
    for k, transfer in enumerate(along_z):
        transfer.wait()
        summed = summed + self_got[k].astype(F32)
    self_sum[...] = low(summed)
    text_x.wait()
    text_keep[...] = add(text_keep[...], text_got[...])
    far.wait()
    text_grad[...] = text_n[...] + side(own_sum, 0, size, 3) + side(got, 0, size, 3).astype(F32)
    image_total = low(image_n[...] + side(own_sum, below, image_size, 4) + side(got, below, image_size, 4).astype(F32))
    image_grad[...] = low(tn(spacing(image_size // PADDED), image_total))


def gate(hidden):
    half = 0.5 * (1.0 + lax.erf(hidden * (2.0**-0.5)))
    density = jnp.exp(-0.5 * hidden * hidden) * 0.3989422804014327
    return hidden * half, half + hidden * density


def mlp_forward(pairs, text_pre, image_pre, text_gain, text_bias, image_gain, image_bias, *refs):
    parts = refs[:4]
    text_low, image_low, text_next, image_next = refs[4:8]
    text_activ, text_slope, image_activ, image_slope, corner = refs[8:13]
    weights, sems, send_sems, recv_sems = refs[13:]
    step = pl.program_id(0)
    leaving = fetch_round(step, *parts, corner, weights, sems, send_sems, recv_sems)

    @pl.when(step == 0)
    def begin():
        for pre, gain, bias, rounded, total in (
            (text_pre, text_gain, text_bias, text_low, text_next),
            (image_pre, image_gain, image_bias, image_low, image_next),
        ):
            g, b = affine_row(gain, bias, 0)
            one = normed(pre[...])[0] * g + b
            total[...] = one
            rounded[...] = low(one)

    w = weights.at[step]
    for b in range(3):
        activ, slope = gate(nn(text_low[...], w[b * 768 : (b + 1) * 768, :]))
        text_activ[0, :, b * 256 : (b + 1) * 256] = low(activ)
        text_slope[0, :, b * 256 : (b + 1) * 256] = low(slope)
    activ, slope = gate(nn(image_low[...], w[4608:5632, :]))
    image_activ[0] = low(activ)
    image_slope[0] = low(slope)
    text_next[...] += nn(text_activ[0], side(w, 2304, 768, 3))
    image_next[...] += nn(image_activ[0], side(w, 5632, 256, 4))

    @pl.when(step == QUARTERS - 1)
    def finish():
        leaving.wait()


def lane_masks():
    lane = lax.broadcasted_iota(jnp.int32, (1, 2 * SELF_HEAD), 1)
    left = (lane < SELF_HEAD).astype(F32)
    return low(left), low(1.0 - left), lane < SELF_HEAD


def both_heads(tile, masks):
    return jnp.concatenate([tile * masks[0], tile * masks[1]], axis=0)


def one_tile(stacked, masks):
    return jnp.where(masks[2], stacked[:SLOTS], stacked[SLOTS:])


def self_forward(pairs, ids, lengths, text_pre, image_pre, text_gain, text_bias, image_gain, image_bias, text_cot, image_cot, *refs):
    parts = refs[:4]
    (
        text_out,
        image_out,
        text_grad,
        image_grad,
        text_vec,
        image_vec,
        rounded,
        text_q,
        text_k,
        text_v,
        text_c,
        text_probs,
        image_kept,
        image_probs,
        corner,
    ) = refs[4:19]
    weights, text_sum, image_sum, text_low, image_low, sems, send_sems, recv_sems = refs[19:]
    step = pl.program_id(0)
    leaving = fetch_round(step, *parts, corner, weights, sems, send_sems, recv_sems)
    text_rows, image_rows = text_pre.shape[0], image_pre.shape[0]

    @pl.when(step == 0)
    def begin():
        for pre, gain, bias, total, lower, at in (
            (text_pre, text_gain, text_bias, text_sum, text_low, 0),
            (image_pre, image_gain, image_bias, image_sum, image_low, 6 * text_rows),
        ):
            g, b = affine_row(gain, bias, 1)
            two = normed(pre[...])[0] * g + b
            total[...] = two
            lower[...] = low(two)
            leave_blocks(rounded, at, low(two))

    w = weights.at[step]
    for n, out in enumerate((text_q, text_k, text_v)):
        wide = jnp.concatenate([w[b * 576 + n * 192 : b * 576 + (n + 1) * 192, :] for b in range(3)], axis=1)
        out[0] = low(nt(text_low[...], wide))
    for n in range(3):
        image_kept[0, :, n * 256 : (n + 1) * 256] = low(nn(image_low[...], w[2304 + n * 1024 : 3328 + n * 1024, :]))

    masks = lane_masks()
    slots = lax.broadcasted_iota(jnp.int32, (1, SLOTS), 1)
    base = ids[2]
    valid = [slots < lengths[base + p] for p in range(pairs)]
    first, last = slice(0, 128), slice(128, 192)
    queries, keys, values, limits = [], [], [], []
    for p in range(pairs):
        rows = rows_of(p, SLOTS)
        queries += [both_heads(text_q[0, rows, first], masks), text_q[0, rows, last]]
        keys += [text_k[0, rows, first], text_k[0, rows, last]]
        values += [text_v[0, rows, first], text_v[0, rows, last]]
        limits += [valid[p], valid[p]]
    probs, context = attend(queries, keys, values, SELF_HEAD**-0.5, limits)
    for p in range(pairs):
        rows = rows_of(p, SLOTS)
        text_probs[0, p, 0:256, :] = probs[2 * p]
        text_probs[0, p, 256:384, :] = probs[2 * p + 1]
        text_c[0, rows, first] = low(one_tile(context[2 * p], masks))
        text_c[0, rows, last] = low(context[2 * p + 1])

    image_mask = lax.broadcasted_iota(jnp.int32, (PADDED, PADDED), 1) < REGIONS
    units = [(p, h) for p in range(pairs) for h in range(2)]

    def image_part(at):
        return [image_kept[0, rows_of(p, PADDED), at + h * HEAD : at + (h + 1) * HEAD] for p, h in units]

    probs, context = attend(image_part(0), image_part(256), image_part(512), HEAD**-0.5, [image_mask] * len(units))
    for i, (p, h) in enumerate(units):
        image_probs[0, i] = probs[i]
        image_kept[0, rows_of(p, PADDED), 768 + h * HEAD : 768 + (h + 1) * HEAD] = low(context[i])

    text_sum[...] += nn(text_c[0], side(w, 1728, 192, 3))
    image_sum[...] += nn(image_kept[0, :, 768:1024], side(w, 5376, 256, 4))

    @pl.when(step == QUARTERS - 1)
    def finish():
        apart = spacing(pairs)
        image_cot_apart = nn(apart, image_cot[...])
        for total, gain, bias, cot, grad, vec, at in (
            (text_sum, text_gain, text_bias, text_cot[...].astype(F32), text_grad, text_vec, 3 * text_rows),
            (image_sum, image_gain, image_bias, image_cot_apart, image_grad, image_vec, 6 * text_rows + 4 * image_rows),
        ):
            g, b = affine_row(gain, bias, 2)
            unit, scale = normed(total[...])
            value = unit * g + b
            if total is text_sum:
                text_out[...] = value
            else:
                image_out[...] = low(tn(apart, low(value)))
            back = norm_back(unit, scale, g, cot, vec)
            grad[...] = back
            leave_blocks(rounded, at, low(back))
        leaving.wait()


def self_back(pairs, text_g, image_g, text_pre, image_pre, text_gain, image_gain, *refs):
    text_q, text_k, text_v, text_c, text_probs, image_kept, image_probs = refs[:7]
    parts = refs[7:12]
    text_n, image_n, text_vec, image_vec, near, keep = refs[12:18]
    weights, found, text_sum, image_sum, text_g_low, image_g_low, text_d, image_d, sems, out_sems, send_sems, recv_sems = refs[18:]
    step = pl.program_id(0)
    fetch(step, BACKWARD, *parts, weights, sems)
    core = partners()[0]
    copy = sender(send_sems, recv_sems)

    @pl.when(step == 0)
    def begin():
        greet(core)
        text_sum[...] = text_g[...]
        image_sum[...] = image_g[...]
        text_g_low[...] = low(text_g[...])
        image_g_low[...] = low(image_g[...])

    w = weights.at[step]
    masks = lane_masks()
    first, last = slice(0, 128), slice(128, 192)
    text_dc = low(nt(text_g_low[...], side(w, 1728, 192, 3)))
    queries, keys, values, probs, outer = [], [], [], [], []
    for p in range(pairs):
        rows = rows_of(p, SLOTS)
        queries += [both_heads(text_q[0, rows, first], masks), text_q[0, rows, last]]
        keys += [text_k[0, rows, first], text_k[0, rows, last]]
        values += [text_v[0, rows, first], text_v[0, rows, last]]
        probs += [text_probs[0, p, 0:256, :], text_probs[0, p, 256:384, :]]
        outer += [both_heads(text_dc[rows, first], masks), text_dc[rows, last]]
    grad_q, grad_k, grad_v = attend_back(queries, keys, values, probs, outer, SELF_HEAD**-0.5)
    size = text_g.shape[0]
    for p in range(pairs):
        rows = rows_of(p, SLOTS)
        text_d[0, rows, first] = one_tile(grad_q[2 * p], masks)
        text_d[0, rows, last] = grad_q[2 * p + 1]
        for n, grad in ((1, grad_k), (2, grad_v)):
            text_d[n, rows, first] = grad[2 * p]
            text_d[n, rows, last] = grad[2 * p + 1]

    image_dc = low(nt(image_g_low[...], side(w, 5376, 256, 4)))
    units = [(p, h) for p in range(pairs) for h in range(2)]

    def image_part(at):
        return [image_kept[0, rows_of(p, PADDED), at + h * HEAD : at + (h + 1) * HEAD] for p, h in units]

    outer = [image_dc[rows_of(p, PADDED), h * HEAD : (h + 1) * HEAD] for p, h in units]
    given = attend_back(
        image_part(0), image_part(256), image_part(512), [image_probs[0, i] for i in range(len(units))], outer, HEAD**-0.5
    )
    for n in range(3):
        for i, (p, h) in enumerate(units):
            image_d[rows_of(p, PADDED), n * 256 + h * HEAD : n * 256 + (h + 1) * HEAD] = given[n][i]

    gained = text_sum[...]
    for n in range(3):
        wide = jnp.concatenate([w[b * 576 + n * 192 : b * 576 + (n + 1) * 192, :] for b in range(3)], axis=1)
        gained = gained + nn(text_d[n], wide)
    text_sum[...] = gained
    image_sum[...] += nt(image_d[...], side(w, 2304, 1024, 3))

    slot = found.at[step]
    slot[0:size, 0:128] = text_d[0, :, first]
    slot[0:size, 128:256] = text_d[1, :, first]
    slot[size : 2 * size, 0:128] = text_d[2, :, first]
    slot[size : 2 * size, 128:256] = text_c[0, :, first]
    slot[2 * size : 3 * size, 0:128] = jnp.concatenate([text_d[0, :, last], text_d[1, :, last]], axis=1)
    slot[2 * size : 3 * size, 128:256] = jnp.concatenate([text_d[2, :, last], text_c[0, :, last]], axis=1)
    leave_blocks(slot, 3 * size, image_d[...])
    leave_blocks(slot, 3 * size + 3 * image_g.shape[0], image_kept[0, :, 768:1024])
    leave_quarter(step, found, near, keep, out_sems, [copy(n, found.at[n], near.at[n], core) for n in range(2)])

    @pl.when(step == QUARTERS - 1)
    def finish():
        leave_norm(1, text_sum, image_sum, text_pre, image_pre, text_gain, image_gain, text_n, image_n, text_vec, image_vec)


def leave_norm(norm, text_sum, image_sum, text_pre, image_pre, text_gain, image_gain, text_n, image_n, text_vec, image_vec):
    for total, pre, gain, out, vec in (
        (text_sum, text_pre, text_gain, text_n, text_vec),
        (image_sum, image_pre, image_gain, image_n, image_vec),
    ):
        unit, scale = normed(pre[...])
        out[...] = norm_back(unit, scale, gain[0, norm : norm + 1, :].astype(F32), total[...], vec)


def mlp_back(pairs, text_g, image_g, text_one, image_one, text_pre, image_pre, text_gain, image_gain, *refs):
    text_activ, text_slope, image_activ, image_slope = refs[:4]
    parts = refs[4:9]
    text_n, image_n, next_low, text_vec, image_vec, rounded, rounded_near, near, keep = refs[9:18]
    weights, found, text_sum, image_sum, text_g_low, image_g_low, text_d, sems, out_sems, send_sems, recv_sems = refs[18:]
    step = pl.program_id(0)
    fetch(step, BACKWARD, *parts, weights, sems)
    size, image_size = text_g.shape[0], image_g.shape[0]
    core = partners()[0]
    copy = sender(send_sems, recv_sems)
    rounded_copy = copy(2, rounded, rounded_near, core)

    @pl.when(step == 0)
    def begin():
        text_sum[...] = text_g[...]
        image_sum[...] = image_g[...]
        text_g_low[...] = low(text_g[...])
        image_g_low[...] = low(image_g[...])
        leave_blocks(rounded, 0, text_one[...])
        leave_blocks(rounded, 3 * size, text_g_low[...])
        leave_blocks(rounded, 6 * size, image_one[...])
        leave_blocks(rounded, 6 * size + 4 * image_size, image_g_low[...])
        greet(core)
        rounded_copy.start()

    w = weights.at[step]
    slot = found.at[step]
    wide = side(w, 2304, 768, 3)
    for b in range(3):
        columns = slice(b * 256, (b + 1) * 256)
        back = nt(text_g_low[...], wide[columns])
        text_d[:, columns] = low(back * text_slope[0, :, columns].astype(F32))
    text_sum[...] += nt(text_d[...], side(w, 0, 768, 3))
    image_d = low(nt(image_g_low[...], side(w, 5632, 256, 4)) * image_slope[0].astype(F32))
    image_sum[...] += nt(image_d, w[4608:5632, :])
    leave_blocks(slot, 0, text_d[...])
    leave_blocks(slot, 3 * size, text_activ[0])
    leave_blocks(slot, 6 * size, image_d)
    leave_blocks(slot, 6 * size + image_size, image_activ[0])
    leave_quarter(step, found, near, keep, out_sems, [copy(n, found.at[n], near.at[n], core) for n in range(2)])

    @pl.when(step == QUARTERS - 1)
    def finish():
        rounded_copy.wait()
        leave_norm(0, text_sum, image_sum, text_pre, image_pre, text_gain, image_gain, text_n, image_n, text_vec, image_vec)
        leave_blocks(next_low, 0, low(text_n[...]))
        leave_blocks(next_low, 3 * size, low(image_n[...]))


def weight_grad(is_self, sizes, x_at, own, near, own_quarters, near_quarters, *refs):
    to_send, kept, to_z, text_flip, text_g_flip, image_flip, image_g_flip = refs
    size, image_size = sizes
    dp = kept.shape[1]
    x = x_at[0]
    for at, source in ((0, own), (1, near)):
        rows, image_rows = rows_of(at, size), rows_of(at, image_size)
        for b in range(3):
            text_flip[rows_of(b, BLOCK), rows] = source[rows_of(b, size), :].T
            text_g_flip[rows_of(b, BLOCK), rows] = source[rows_of(3 + b, size), :].T
        for b in range(4):
            start = 6 * size
            image_flip[rows_of(b, BLOCK), image_rows] = source[start + b * image_size : start + (b + 1) * image_size, :].T
            start = 6 * size + 4 * image_size
            image_g_flip[rows_of(b, BLOCK), image_rows] = source[start + b * image_size : start + (b + 1) * image_size, :].T

    text_depth, image_depth = DT // (2 * dp), DV // (2 * dp)
    padded = -(-text_depth // 16) * 16

    def write(ref, at, row, depth, value):
        for z in range(dp):
            ref[at, z, row : row + depth, :] = low(value[z * depth : (z + 1) * depth])

    lane = lax.broadcasted_iota(jnp.int32, (1, HEAD), 1) < SELF_HEAD
    for slot in (1, 0):

        def text_block(b):
            return jnp.concatenate([q[slot, rows_of(b, size), :] for q in (own_quarters, near_quarters)], axis=0)

        def image_block(b, text_blocks):
            start = text_blocks * size + b * image_size
            return jnp.concatenate([q[slot, start : start + image_size, :] for q in (own_quarters, near_quarters)], axis=0)

        for apart in range(2):
            half = lax.bitwise_xor(x, apart)
            text_rows = pl.ds(pl.multiple_of(half * (DT // 2), 128), DT // 2)
            image_rows = pl.ds(pl.multiple_of(half * (DV // 2), 128), DV // 2)
            text_lhs, image_lhs = text_flip[text_rows, :], image_flip[image_rows, :]
            text_g_lhs, image_g_lhs = text_g_flip[text_rows, :], image_g_flip[image_rows, :]

            def bottom(b, count, value):
                row = ((2 * slot + apart) * count + b) * image_depth
                for z in range(dp):
                    to_z[z, row : row + image_depth, :] = low(value[z * image_depth : (z + 1) * image_depth])

            if is_self:
                top, at = (to_send if slot else kept), apart
                one, two, three = text_block(0), text_block(1), text_block(2)
                write(top, at, 0, text_depth, nn(text_lhs, one))
                mixed = jnp.concatenate([nn(text_lhs, two[:, :HEAD]), nn(text_g_lhs, two[:, HEAD:])], axis=1)
                write(top, at, padded, text_depth, mixed)
                from_x = nn(text_lhs, three)
                from_g = nn(text_g_lhs, three[:, HEAD:])
                mixed = jnp.concatenate([from_x[:, :HEAD], jnp.where(lane, from_x[:, HEAD:], from_g)], axis=1)
                write(top, at, 2 * padded, text_depth, mixed)
                write(top, at, 3 * padded, image_depth, nn(image_lhs, image_block(0, 3)))
                for b in range(3):
                    bottom(b, 3, nn(image_g_lhs if b == 2 else image_lhs, image_block(1 + b, 3)))
            else:
                top, at = (to_send if apart else kept), slot
                for b in range(6):
                    write(top, at, b * padded, text_depth, nn(text_g_lhs if b > 2 else text_lhs, text_block(b)))
                for b in range(2):
                    bottom(b, 2, nn(image_g_lhs if b else image_lhs, image_block(b, 6)))


ANY = pl.BlockSpec(memory_space=pl.ANY)
SCALARS = pl.BlockSpec(memory_space=pltpu.SMEM)


def whole(array):
    zeros = (0,) * len(array.shape)
    return pl.BlockSpec(array.shape, lambda *s: zeros)


def quarter(array, order):
    tail = (0,) * (len(array.shape) - 1)
    if order is FORWARD:
        return pl.BlockSpec((1,) + array.shape[1:], lambda s: (s,) + tail)
    return pl.BlockSpec((1,) + array.shape[1:], lambda s: (lax.rem(2 * s + 1 - lax.div(s, 2), 4),) + tail)


def shape(*dims, of=BF):
    return jax.ShapeDtypeStruct(dims, of)


def run(kernel, order, operands, outs, scratch, us, meeting=None):
    def spec(kind, array):
        return {"s": lambda: SCALARS, "w": lambda: whole(array), "q": lambda: quarter(array, order), "a": lambda: ANY}[kind]()

    return pl.pallas_call(
        kernel,
        grid=(QUARTERS,) if order else (1,),
        in_specs=[spec(*entry) for entry in operands],
        out_specs=[spec(*entry) for entry in outs],
        out_shape=[array for unused, array in outs],
        scratch_shapes=scratch,
        compiler_params=pltpu.CompilerParams(
            dimension_semantics=("arbitrary",),
            vmem_limit_bytes=60 * 2**20,
            collective_id=meeting,
            has_side_effects=meeting is not None,
        ),
        cost_estimate=pl.CostEstimate(flops=int(us * 1.1e9), bytes_accessed=1024, transcendentals=0),
    )(*[array for unused, array in operands])


def swap(value, axis, apart):
    return lax.ppermute(value, axis, [(i, i ^ apart) for i in range(lax.axis_size(axis))])


def after(value, *earlier):
    return lax.optimization_barrier((value,) + earlier)[0]


class Line:
    def __init__(self):
        self.last = ()

    def take(self, value):
        return after(value, *self.last)

    def leave(self, *values):
        self.last = values


def add(left, right):
    return low(left.astype(F32) + right.astype(F32))


def fold_last(total):
    return lax.psum_scatter(total, "dp", scatter_dimension=0, tiled=True)[0]


def s(value):
    return ("s", value)


def w(value):
    return ("w", value)


def q(value):
    return ("q", value)


def a(value):
    return ("a", value)


def local(
    text_in,
    image_in,
    lengths,
    text_cot,
    image_cot,
    text_cross_q,
    text_cross_kv,
    text_cross_out,
    text_up,
    text_down,
    text_self_qkv,
    text_self_out,
    text_gain,
    text_bias,
    image_cross_q,
    image_cross_kv,
    image_cross_out,
    image_up,
    image_down,
    image_self_qkv,
    image_self_out,
    image_gain,
    image_bias,
):
    dp = lax.axis_size("dp")
    places = 2 * dp
    x_at = lax.axis_index("stream")
    t_at = lax.axis_index("tensor")
    size = text_in.shape[0]
    pairs = size // SLOTS
    image_size = pairs * PADDED
    units = 2 * pairs
    ids = jnp.stack([x_at, x_at * dp + lax.axis_index("dp")] + [(t_at ^ j) * pairs for j in range(QUARTERS)]).astype(jnp.int32)

    def leave(rows):
        return swap(rows, "stream", 1).astype(F32)

    line = Line()
    mlp_own, mlp_first, mlp_mine = pack([text_up[0], text_down[0], image_up[0], image_down[0]], places, 5120, ids)
    mlp_share = swap(mlp_mine, "tensor", 2)
    self_own, self_first, self_mine = pack(
        [
            text_self_qkv[0].transpose(1, 2, 0).reshape(-1, DT),
            text_self_out[0],
            image_self_qkv[0].reshape(DV, -1),
            image_self_out[0],
        ],
        places,
        4096,
        after(ids, mlp_own),
    )
    cross_w = (
        text_cross_q[0],
        image_cross_kv[0].reshape(DT, -1),
        text_cross_kv[0].reshape(DV, -1),
        image_cross_q[0],
        text_cross_out[0],
        image_cross_out[0],
    )
    line.leave(self_own)
    mlp_share = line.take(mlp_share)
    line.leave(mlp_share, cross_w[1], cross_w[2])
    self_share = line.take(swap(self_mine, "tensor", 2))
    line.leave(self_share)
    mlp_rest = lax.all_gather(mlp_share, ("stream", "dp"), axis=0, tiled=True)
    self_rest = lax.all_gather(self_share, ("stream", "dp"), axis=0, tiled=True)
    self_near = swap(self_own, "tensor", 1)
    mlp_near_w = swap(mlp_own, "tensor", 1)
    image_cot_here = swap(image_cot, "stream", 1)
    mlp_far = swap(mlp_first, "tensor", 2)

    text_wide, image_wide = shape(size, DT, of=F32), shape(image_size, DV, of=F32)
    text_f32, image_f32 = pltpu.VMEM((size, DT), F32), pltpu.VMEM((image_size, DV), F32)
    text_bf, image_bf = pltpu.VMEM((size, DT), BF), pltpu.VMEM((image_size, DV), BF)
    in_sems, out_sems = pltpu.SemaphoreType.DMA((5,)), pltpu.SemaphoreType.DMA((2,))
    text_affine = [w(text_gain), w(text_bias)]
    image_affine = [w(image_gain), w(image_bias)]
    vector_outs = [w(shape(2, DT, of=F32)), w(shape(2, DV, of=F32))]
    part_rows = 3 * size + 4 * image_size

    def buffer(weights):
        return pltpu.VMEM((QUARTERS,) + weights.shape, BF)

    in_four = [
        (QUARTERS, size, DT),
        (QUARTERS, image_size, DV),
        (QUARTERS, size, 1024),
        (QUARTERS, image_size, 1024),
        (QUARTERS, units, SLOTS, PADDED),
        (QUARTERS, units, PADDED, SLOTS),
    ]

    def links(count):
        return [pltpu.SemaphoreType.DMA((count,)), pltpu.SemaphoreType.DMA((count,))]

    text_pre1, image_pre1, texts, images, *cross_kept = run(
        functools.partial(cross_forward, pairs),
        None,
        [s(lengths), w(line.take(text_in)), w(image_in)] + [w(m) for m in cross_w],
        [w(text_wide), w(image_wide)] + [a(shape(*dims)) for dims in in_four],
        [pltpu.VMEM(dims, BF) for dims in in_four]
        + [pltpu.VMEM((QUARTERS, part_rows, BLOCK), BF), pltpu.VMEM((part_rows, BLOCK), BF), pltpu.VMEM((3, part_rows, BLOCK), BF)]
        + [image_bf]
        + links(10)
        + [pltpu.SemaphoreType.DMA((6,))],
        70,
        1,
    )
    line.leave(text_pre1, image_cot_here)
    mlp_far, mlp_rest = line.take((mlp_far, mlp_rest))
    self_far = swap(after(self_first, mlp_far), "tensor", 2)
    (
        text_one,
        image_one,
        text_pre2,
        image_pre2,
        text_activ,
        text_slope,
        image_activ,
        image_slope,
        mlp_corner,
    ) = run(
        functools.partial(mlp_forward, pairs),
        FORWARD,
        [w(text_pre1), w(image_pre1)] + text_affine + image_affine + [a(m) for m in (mlp_own, mlp_near_w, mlp_far, mlp_rest)],
        [
            w(shape(size, DT)),
            w(shape(image_size, DV)),
            w(text_wide),
            w(image_wide),
            q(shape(QUARTERS, size, 768)),
            q(shape(QUARTERS, size, 768)),
            q(shape(QUARTERS, image_size, 256)),
            q(shape(QUARTERS, image_size, 256)),
            a(mlp_own),
        ],
        [buffer(mlp_own), in_sems] + links(2),
        1,
        7,
    )
    mlp_w = mlp_own, mlp_near_w, mlp_far, mlp_rest, mlp_corner
    line.leave(text_pre2)
    self_far, self_rest = line.take((self_far, self_rest))
    (
        text_out,
        image_out,
        text_n3,
        image_n3,
        text_vec3,
        image_vec3,
        self_rounded,
        self_q,
        self_k,
        self_v,
        self_c,
        self_probs,
        self_kept,
        self_image_probs,
        self_corner,
    ) = run(
        functools.partial(self_forward, pairs),
        FORWARD,
        [s(ids), s(lengths), w(text_pre2), w(image_pre2)]
        + text_affine
        + image_affine
        + [w(text_cot), w(image_cot_here)]
        + [a(m) for m in (self_own, self_near, self_far, self_rest)],
        [w(text_wide), w(image_cot), w(text_wide), w(image_wide)]
        + vector_outs
        + [
            w(shape(2 * part_rows, BLOCK)),
            q(shape(QUARTERS, size, 192)),
            q(shape(QUARTERS, size, 192)),
            q(shape(QUARTERS, size, 192)),
            q(shape(QUARTERS, size, 192)),
            q(shape(QUARTERS, pairs, 384, SLOTS)),
            q(shape(QUARTERS, image_size, 1024)),
            q(shape(QUARTERS, units, PADDED, PADDED)),
            a(self_own),
        ],
        [buffer(self_own), text_f32, image_f32, text_bf, image_bf, in_sems] + links(2),
        19,
        8,
    )
    self_w = self_own, self_near, self_far, self_rest, self_corner
    image_out = swap(image_out, "stream", 1)

    text_depth, image_depth = DT // places, DV // places
    padded = -(-text_depth // 16) * 16

    def back_scratch(weights, rows):
        return [
            buffer(weights[0]),
            pltpu.VMEM((QUARTERS, rows, BLOCK), BF),
            text_f32,
            image_f32,
            text_bf,
            image_bf,
        ]

    def weight_grads(is_self, turn, rounded, rounded_near, kept, kept_near):
        top = 3 * padded + image_depth if is_self else 6 * padded
        bottom = (3 if is_self else 2) * image_depth
        outs = [w(shape(2, dp, top, BLOCK)), w(shape(2, dp, top, BLOCK)), w(shape(dp, 4 * bottom, BLOCK))]
        return run(
            functools.partial(weight_grad, is_self, (size, image_size)),
            None,
            [s(turn), w(rounded), w(rounded_near), w(kept), w(kept_near)],
            outs,
            [
                pltpu.VMEM((DT, 2 * size), BF),
                pltpu.VMEM((DT, 2 * size), BF),
                pltpu.VMEM((DV, 2 * image_size), BF),
                pltpu.VMEM((DV, 2 * image_size), BF),
            ],
            12,
        )

    self_rows = 3 * size + 4 * image_size
    self_rounded_near = swap(self_rounded, "tensor", 1)
    text_n2, image_n2, text_vec2, image_vec2, self_other, self_keep = run(
        functools.partial(self_back, pairs),
        BACKWARD,
        [
            w(text_n3),
            w(image_n3),
            w(text_pre2),
            w(image_pre2),
            w(text_gain),
            w(image_gain),
            q(self_q),
            q(self_k),
            q(self_v),
            q(self_c),
            q(self_probs),
            q(self_kept),
            q(self_image_probs),
        ]
        + [a(m) for m in self_w],
        [w(text_wide), w(image_wide)] + vector_outs + [a(shape(2, self_rows, BLOCK)), a(shape(2, self_rows, BLOCK))],
        back_scratch(self_w, self_rows)
        + [pltpu.VMEM((3, size, 192), BF), pltpu.VMEM((image_size, 768), BF), in_sems, out_sems]
        + links(2),
        23,
        2,
    )
    to_y, self_top, to_z = weight_grads(True, ids, self_rounded, self_rounded_near, self_keep, self_other)
    self_by_y = swap(to_y, "tensor", 2)
    self_bottom = fold_last(to_z)
    line.leave(self_top)
    mlp_rows = 6 * size + 2 * image_size
    text_n1, image_n1, grad_low, text_vec1, image_vec1, mlp_rounded, mlp_rounded_near, mlp_near, mlp_keep = run(
        functools.partial(mlp_back, pairs),
        BACKWARD,
        [
            w(text_n2),
            w(image_n2),
            w(text_one),
            w(image_one),
            w(text_pre1),
            w(image_pre1),
            w(line.take(text_gain)),
            w(image_gain),
            q(text_activ),
            q(text_slope),
            q(image_activ),
            q(image_slope),
        ]
        + [a(m) for m in mlp_w],
        [w(text_wide), w(image_wide), w(shape(part_rows, BLOCK))]
        + vector_outs
        + [
            w(shape(2 * part_rows, BLOCK)),
            a(shape(2 * part_rows, BLOCK)),
            a(shape(2, mlp_rows, BLOCK)),
            a(shape(2, mlp_rows, BLOCK)),
        ],
        back_scratch(mlp_w, mlp_rows) + [text_bf, in_sems, out_sems] + links(3),
        20,
        3,
    )
    line.leave(grad_low)
    to_x, mlp_top, to_z = weight_grads(False, line.take(ids), mlp_rounded, mlp_rounded_near, mlp_keep, mlp_near)
    self_top, self_by_y, to_x, to_z, image_out = after((self_top, self_by_y, to_x, to_z, image_out), mlp_top)
    mlp_by_x = swap(to_x, "stream", 1)
    mlp_bottom = fold_last(to_z)
    self_top, to_x = add(self_top[0], self_by_y[0]), add(self_top[1], self_by_y[1])
    self_then_x = swap(to_x, "stream", 1)
    line.leave(self_top, to_x)
    d_dims = [(QUARTERS, part_rows, BLOCK), (QUARTERS, size, 768), (QUARTERS, image_size, 768)]
    vectors = jnp.concatenate(
        [jnp.pad(v, ((0, 0), (0, DV - DT))) for v in (text_vec1, text_vec2, text_vec3)]
        + [image_vec1, image_vec2, image_vec3, jnp.zeros((4, DV), F32)],
        axis=0,
    )
    grads, text_d, image_d, own_sum, total, vectors = run(
        functools.partial(cross_back, pairs),
        None,
        [w(line.take(grad_low)), w(vectors)] + [w(k) for k in cross_kept] + [w(m) for m in cross_w],
        [a(shape(*dims)) for dims in d_dims]
        + [w(shape(part_rows, BLOCK, of=F32)), w(shape(part_rows, BLOCK)), w(shape(16, DV, of=F32))],
        [pltpu.VMEM(dims, BF) for dims in d_dims]
        + [pltpu.VMEM((QUARTERS, part_rows, BLOCK), BF), pltpu.VMEM((2, part_rows, BLOCK), BF), pltpu.VMEM((2, 16, DV), F32)]
        + links(7)
        + [pltpu.SemaphoreType.DMA((3,))],
        48,
        4,
    )
    line.leave(total)
    text_only, image_only = 4 * padded + 16, 4 * image_depth
    text_vector = jnp.pad(vectors[:6, :DT].reshape(6, places, text_depth), ((0, 0), (0, 0), (0, BLOCK - text_depth)))
    image_vector = jnp.pad(vectors[6:].reshape(10, places, image_depth), ((0, 0), (0, 0), (0, BLOCK - image_depth)))
    vectors = low(jnp.concatenate([text_vector, image_vector], axis=0).transpose(1, 0, 2))
    vector_keep = lax.dynamic_slice_in_dim(vectors, x_at * dp, dp, 0)
    vector_send = lax.dynamic_slice_in_dim(vectors, (1 - x_at) * dp, dp, 0)
    text_grad, image_grad, cross_text, image_keep, image_send, self_top = run(
        cross_last,
        None,
        [
            w(line.take(total)),
            w(own_sum),
            w(vector_keep),
            w(vector_send),
            w(self_top),
            w(self_then_x),
            w(text_n1),
            w(image_n1),
            w(texts),
            w(images),
            w(grads),
            w(cross_kept[0]),
            w(cross_kept[1]),
            w(text_d),
            w(image_d),
        ],
        [
            w(text_wide),
            w(image_cot),
            w(shape(dp, text_only, BLOCK)),
            w(shape(dp, image_only, BLOCK)),
            w(shape(dp, image_only, BLOCK)),
            w(shape(*self_top.shape[1:])),
        ],
        [
            pltpu.VMEM((part_rows, BLOCK), BF),
            pltpu.VMEM((dp, text_only, BLOCK), BF),
            pltpu.VMEM((dp, text_only, BLOCK), BF),
            pltpu.VMEM(self_top.shape, BF),
            pltpu.VMEM((dp - 1, *self_top.shape[1:]), BF),
            pltpu.VMEM((DT, QUARTERS * size), BF),
            pltpu.VMEM((DT, QUARTERS * size), BF),
            pltpu.VMEM((DV, QUARTERS * image_size), BF),
            pltpu.VMEM((DV, QUARTERS * image_size), BF),
        ]
        + links(1 + dp),
        2,
        5,
    )
    line.leave(text_grad)
    mlp_top, mlp_by_x, self_bottom, cross_text, image_send = line.take(
        (mlp_top, mlp_by_x, self_bottom, cross_text, image_send)
    )
    cross_text = fold_last(cross_text)
    image_send = swap(image_send, "stream", 1)
    mlp_top, to_y = add(mlp_top[0], mlp_by_x[0]), add(mlp_top[1], mlp_by_x[1])
    mlp_then_y = swap(to_y, "tensor", 2)
    line.leave(mlp_top, to_y)
    self_bottom = line.take(self_bottom).reshape(2, 2, 3 * image_depth, BLOCK)
    self_bottom_x = swap(self_bottom[:, 1], "stream", 1)
    cross_image = add(image_keep, line.take(image_send))
    line.leave(cross_image)
    cross_image = fold_last(cross_image)
    self_bottom = add(self_bottom[:, 0], line.take(self_bottom_x))
    self_bottom_y = swap(self_bottom[1], "tensor", 2)
    mlp_bottom = line.take(mlp_bottom).reshape(2, 2, 2 * image_depth, BLOCK)
    mlp_bottom_x = swap(mlp_bottom[:, 1], "stream", 1)
    mlp_top = add(mlp_top, line.take(mlp_then_y))
    line.leave(mlp_top)
    mlp_top = fold_last(mlp_top)
    mlp_bottom = add(mlp_bottom[:, 0], line.take(mlp_bottom_x))
    mlp_bottom = add(mlp_bottom[0], swap(mlp_bottom[1], "tensor", 2))
    self_bottom = add(self_bottom[0], self_bottom_y)
    self_grads = jnp.concatenate([self_top, self_bottom], axis=0)
    image_grad = leave(image_grad)

    def pick(packed, first, count, depth, stride):
        rows = [packed[first + b * stride : first + b * stride + depth] for b in range(count)]
        return jnp.concatenate(rows, axis=1).astype(F32)

    def text_pick(packed, first, count):
        return pick(packed, first, count, text_depth, padded)

    def image_pick(packed, first, count):
        return pick(packed, first, count, image_depth, image_depth)

    sums = cross_text[4 * padded :].astype(F32)
    text_vectors, image_vectors = sums[:6, :text_depth], sums[6:12, :image_depth]

    self_text = text_pick(self_grads, 0, 3)

    def heads(at):
        return jnp.concatenate([self_text[:, at * 128 : (at + 1) * 128], self_text[:, 512 + at * 64 : 576 + at * 64]], axis=1)

    below = 3 * padded
    return (
        text_out,
        image_out.astype(F32),
        text_grad,
        image_grad,
        text_pick(cross_text, 0, 1)[None],
        image_pick(cross_image, 0, 2).reshape(1, image_depth, 2, 256),
        text_pick(cross_text, 3 * padded, 1).T[None],
        text_pick(mlp_top, 0, 3)[None],
        text_pick(mlp_top, below, 3).T[None],
        jnp.stack([heads(n) for n in range(3)], axis=1)[None],
        heads(3).T[None],
        text_vectors[0::2][None],
        text_vectors[1::2][None],
        image_pick(cross_image, 2 * image_depth, 1)[None],
        text_pick(cross_text, padded, 2).reshape(1, text_depth, 2, 256),
        image_pick(cross_image, 3 * image_depth, 1).T[None],
        image_pick(mlp_bottom, 0, 1)[None],
        image_pick(mlp_bottom, image_depth, 1).T[None],
        image_pick(self_grads, below, 3).reshape(1, image_depth, 3, 256),
        image_pick(self_grads, below + 3 * image_depth, 1).T[None],
        image_vectors[0::2][None],
        image_vectors[1::2][None],
    )


def solution(mesh):
    rows = P(("stream", "dp", "tensor"), None)
    wide_in = P(None, None, "tensor")
    group_in = P(None, None, None, "tensor")
    wide_out = P(None, "tensor", None)
    grad_in = P(None, ("stream", "dp"), "tensor")
    grad_group = P(None, ("stream", "dp"), None, "tensor")
    grad_out = P(None, "tensor", ("stream", "dp"))
    vector = P(None, None, ("stream", "dp"))
    weights = (wide_in, group_in, wide_out, wide_in, wide_out, group_in, wide_out, P(), P())
    grads = (grad_in, grad_group, grad_out, grad_in, grad_out, grad_group, grad_out, vector, vector)
    return jax.shard_map(
        local,
        mesh=mesh,
        in_specs=(rows, rows, P(("stream", "dp")), rows, rows) + weights + weights,
        out_specs=(rows, rows, rows, rows) + grads + grads,
        check_vma=False,
    )
```

```python
import functools

import jax
import jax.numpy as jnp
from jax import lax
from jax.experimental import pallas as pl
from jax.experimental.pallas import tpu as pltpu
from jax.sharding import PartitionSpec as P

DT = 768
DV = 1024
HEAD = 128
SELF_HEAD = 64
SLOTS = 128
REGIONS = 37
PADDED = 48
QUARTERS = 4
BLOCK = 256

norm_eps = 1e-05
masked_score = -1e30

BF = jnp.bfloat16
F32 = jnp.float32
FORWARD = (0, 1, 2, 3)
BACKWARD = (1, 3, 0, 2)


def nn(left, right):
    return lax.dot_general(left, right, (((1,), (0,)), ((), ())), preferred_element_type=F32)


def nt(left, right):
    return lax.dot_general(left, right, (((1,), (1,)), ((), ())), preferred_element_type=F32)


def tn(left, right):
    return lax.dot_general(left, right, (((0,), (0,)), ((), ())), preferred_element_type=F32)


def low(value):
    return value.astype(BF)


def normed(inputs):
    centered = inputs - jnp.mean(inputs, axis=-1, keepdims=True)
    scale = lax.rsqrt(jnp.mean(centered * centered, axis=-1, keepdims=True) + norm_eps)
    return centered * scale, scale


def norm_back(unit, scale, gain, grad, vec):
    vec[0:1] = jnp.sum(grad * unit, axis=0, keepdims=True)
    vec[1:2] = jnp.sum(grad, axis=0, keepdims=True)
    inner = grad * gain
    shift = jnp.mean(inner, axis=-1, keepdims=True)
    slope = jnp.mean(inner * unit, axis=-1, keepdims=True)
    return scale * (inner - shift - unit * slope)


def softmax_all(scores):
    tops = [jnp.max(s, axis=-1, keepdims=True) for s in scores]
    powers = [jnp.exp(s - t) for s, t in zip(scores, tops)]
    sums = [jnp.sum(e, axis=-1, keepdims=True) for e in powers]
    return [low(e / total) for e, total in zip(powers, sums)]


def attend(queries, keys, values, scale, masks):
    scores = [nt(q, k) * scale for q, k in zip(queries, keys)]
    scores = [s if m is None else jnp.where(m, s, masked_score) for s, m in zip(scores, masks)]
    probs = softmax_all(scores)
    return probs, [nn(p, v) for p, v in zip(probs, values)]


def attend_back(queries, keys, values, probs, grads, scale):
    grad_probs = [nt(g, v) for g, v in zip(grads, values)]
    grad_values = [low(tn(p, g)) for p, g in zip(probs, grads)]
    wide = [p.astype(F32) for p in probs]
    inner = [jnp.sum(p * g, axis=-1, keepdims=True) for p, g in zip(wide, grad_probs)]
    grad_scores = [low(p * (g - i)) for p, g, i in zip(wide, grad_probs, inner)]
    grad_queries = [low(nn(g, k) * scale) for g, k in zip(grad_scores, keys)]
    grad_keys = [low(tn(g, q) * scale) for g, q in zip(grad_scores, queries)]
    return grad_queries, grad_keys, grad_values


def side(ref, row, width, count):
    return jnp.concatenate([ref[row + b * width : row + (b + 1) * width, :] for b in range(count)], axis=1)


def rows_of(pair, size):
    return slice(pair * size, (pair + 1) * size)


def fetch(step, order, own, near, far, far_rest, corner, buffer, sems):
    slots = [order.index(quarter) for quarter in range(QUARTERS)]
    cut, rest = far.shape[0], far_rest.shape[0]
    copies = [
        (slots[0], pltpu.make_async_copy(own, buffer.at[slots[0]], sems.at[0])),
        (slots[1], pltpu.make_async_copy(near, buffer.at[slots[1]], sems.at[1])),
        (slots[2], pltpu.make_async_copy(far, buffer.at[slots[2], pl.ds(0, cut)], sems.at[2])),
        (slots[2], pltpu.make_async_copy(far_rest, buffer.at[slots[2], pl.ds(cut, rest)], sems.at[3])),
    ]
    if corner is not None:
        copies.append((slots[3], pltpu.make_async_copy(corner, buffer.at[slots[3]], sems.at[4])))
    copies.sort(key=lambda entry: entry[0])

    @pl.when(step == 0)
    def begin():
        for slot, copy in copies:
            if slot == 0:
                copy.start()

    for at in range(QUARTERS):

        @pl.when(step == at)
        def arrive():
            for slot, copy in copies:
                if slot == at:
                    copy.wait()

    @pl.when(step == 0)
    def others():
        for slot, copy in copies:
            if slot > 0:
                copy.start()


def fetch_round(step, own, near, far, far_rest, corner, buffer, sems, send_sems, recv_sems):
    core = partners()[0]
    copy = sender(send_sems, recv_sems)
    cut, rest = far.shape[0], far_rest.shape[0]
    over = copy(0, far, buffer.at[3, pl.ds(0, cut)], core), copy(1, far_rest, buffer.at[3, pl.ds(cut, rest)], core)
    leaving = pltpu.make_async_copy(buffer.at[3], corner, sems.at[4])
    fetch(step, FORWARD, own, near, far, far_rest, None, buffer, sems)

    @pl.when(step == 0)
    def begin():
        greet(core)
        for transfer in over:
            transfer.start()

    @pl.when(step == 3)
    def last():
        for transfer in over:
            transfer.wait()
        leaving.start()

    return leaving


def spacing(pairs):
    rows, columns = pairs * PADDED, pairs * REGIONS
    row = lax.broadcasted_iota(jnp.int32, (rows, columns), 0)
    column = lax.broadcasted_iota(jnp.int32, (rows, columns), 1)
    chosen = jnp.zeros((rows, columns), F32)
    for p in range(pairs):
        inside = (column >= p * REGIONS) & (column < (p + 1) * REGIONS)
        chosen = jnp.where(inside & (row - p * PADDED == column - p * REGIONS), 1.0, chosen)
    return low(chosen)


def send_quarter(step, copies):
    for at, copy in enumerate(copies):

        @pl.when(step == at)
        def leave():
            copy.start()


def affine_row(gain, bias, norm):
    return gain[0, norm : norm + 1, :].astype(F32), bias[0, norm : norm + 1, :].astype(F32)


def leave_blocks(ref, row, value):
    size = value.shape[0]
    for b in range(value.shape[1] // BLOCK):
        ref[row + b * size : row + (b + 1) * size, :] = value[:, b * BLOCK : (b + 1) * BLOCK]


MESH = pl.DeviceIdType.MESH


def partners():
    t = lax.axis_index("tensor")
    return {"tensor": lax.bitwise_xor(t, 1)}, {"tensor": lax.bitwise_xor(t, 2)}, {"stream": lax.bitwise_xor(lax.axis_index("stream"), 1)}


def greet(*others):
    barrier = pltpu.get_barrier_semaphore()
    for other in others:
        pl.semaphore_signal(barrier, inc=1, device_id=other, device_id_type=MESH)
    pl.semaphore_wait(barrier, len(others))


def sender(send_sems, recv_sems):
    def copy(number, source, target, to):
        return pltpu.make_async_remote_copy(
            src_ref=source,
            dst_ref=target,
            send_sem=send_sems.at[number],
            recv_sem=recv_sems.at[number],
            device_id=to,
            device_id_type=MESH,
        )

    return copy


def pack(pieces, places, rest, ids):
    total = sum(m.size for m in pieces) // BLOCK
    cut, share = total - rest, rest // places

    def kernel(ids, *refs):
        sources, (own, first, mine) = refs[: len(pieces)], refs[len(pieces) :]
        row = 0
        for ref in sources:
            leave_blocks(own, row, ref[...])
            row += ref.size // BLOCK
        first[...] = own[0:cut, :]
        mine[...] = own[pl.ds(pl.multiple_of(cut + ids[1] * share, 16), share), :]

    return run(
        kernel,
        None,
        [s(ids)] + [w(m) for m in pieces],
        [w(shape(total, BLOCK)), w(shape(cut, BLOCK)), w(shape(share, BLOCK))],
        [],
        3,
    )


def cross_block(pairs, first, lengths, text, image, matrices, text_kept, image_kept, text_probs, image_probs, part):
    wq, wkv_text, wkv_image, wq_image, w_out, w_out_image = matrices
    text_low = text[...]
    image_low = image[...]
    text_kept[:, 0:256] = low(nn(text_low, wq[...]))
    text_kept[:, 256:768] = low(nn(text_low, wkv_text[...]))
    image_kept[:, 0:512] = low(nn(image_low, wkv_image[...]))
    image_kept[:, 512:768] = low(nn(image_low, wq_image[...]))

    image_mask = lax.broadcasted_iota(jnp.int32, (SLOTS, PADDED), 1) < REGIONS
    slots = lax.broadcasted_iota(jnp.int32, (PADDED, SLOTS), 1)
    units = [(p, h) for p in range(pairs) for h in range(2)]

    def text_part(at):
        return [text_kept[rows_of(p, SLOTS), at + h * HEAD : at + (h + 1) * HEAD] for p, h in units]

    def image_part(at):
        return [image_kept[rows_of(p, PADDED), at + h * HEAD : at + (h + 1) * HEAD] for p, h in units]

    scale = HEAD**-0.5
    probs, context = attend(text_part(0), image_part(0), image_part(256), scale, [image_mask] * len(units))
    for i, (p, h) in enumerate(units):
        text_probs[i] = probs[i]
        text_kept[rows_of(p, SLOTS), 768 + h * HEAD : 768 + (h + 1) * HEAD] = low(context[i])
    limits = [lengths[first + p] for p in range(pairs)]
    masks = [slots < limits[p] for p, h in units]
    probs, context = attend(image_part(512), text_part(256), text_part(512), scale, masks)
    for i, (p, h) in enumerate(units):
        image_probs[i] = probs[i]
        image_kept[rows_of(p, PADDED), 768 + h * HEAD : 768 + (h + 1) * HEAD] = low(context[i])
    leave_blocks(part, 0, low(nn(text_kept[:, 768:1024], w_out[...])))
    leave_blocks(part, 3 * text.shape[0], low(nn(image_kept[:, 768:1024], w_out_image[...])))


def cross_forward(pairs, lengths, text, image, *refs):
    matrices = refs[:6]
    text_pre, image_pre = refs[6:8]
    outs = refs[8:14]
    texts, images, text_kept, image_kept, text_probs, image_probs, parts, total, got, image_apart = refs[14:24]
    send_sems, recv_sems, out_sems = refs[24:]
    core, y, x = partners()
    copy = sender(send_sems, recv_sems)
    text_core = copy(0, text, texts.at[1], core)
    text_y = copy(1, text, texts.at[2], y)
    image_x = copy(2, image_apart, images.at[0], x)
    image_core = copy(3, images.at[0], images.at[1], core)
    image_y = copy(4, images.at[0], images.at[2], y)
    text_corner = copy(5, texts.at[2], texts.at[3], core)
    image_corner = copy(6, images.at[2], images.at[3], core)
    near_part = copy(7, parts.at[1], got.at[0], core)
    corner_part = copy(8, parts.at[3], got.at[1], core)
    far_part = copy(9, total, got.at[2], y)

    image_apart[...] = low(nn(spacing(pairs), image[...]))
    greet(core, y, x)
    image_x.start()
    text_y.start()
    text_core.start()
    texts[0] = text[...]
    image_x.wait()
    image_y.start()
    image_core.start()

    def block(j, unused):
        @pl.when(j == 1)
        def near():
            text_core.wait()
            image_core.wait()

        @pl.when(j == 2)
        def far():
            text_y.wait()
            text_corner.start()
            image_y.wait()
            image_corner.start()

        @pl.when(j == 3)
        def corner():
            text_corner.wait()
            image_corner.wait()

        cross_block(
            pairs,
            lax.bitwise_xor(lax.axis_index("tensor"), j) * pairs,
            lengths,
            texts.at[j],
            images.at[j],
            matrices,
            text_kept.at[j],
            image_kept.at[j],
            text_probs.at[j],
            image_probs.at[j],
            parts.at[j],
        )

        @pl.when(j == 1)
        def near_done():
            near_part.start()

        return unused

    lax.fori_loop(0, QUARTERS, block, 0)
    corner_part.start()
    leaving = [
        pltpu.make_async_copy(source, out, out_sems.at[i])
        for i, (source, out) in enumerate(
            zip((texts, images, text_kept, image_kept, text_probs, image_probs), outs)
        )
    ]
    for leave in leaving:
        leave.start()
    corner_part.wait()
    total[...] = add(parts[2], got[1])
    far_part.start()
    near_part.wait()
    size, image_size = text.shape[0], image_apart.shape[0]
    below = 3 * size

    def summed(row, depth, count, start):
        for ref in (parts.at[0], got.at[0]):
            start = start + side(ref, row, depth, count).astype(F32)
        return start

    text_pre[...] = summed(0, size, 3, text[...].astype(F32))
    image_pre[...] = summed(below, image_size, 4, images[0].astype(F32))
    far_part.wait()
    text_pre[...] += side(got.at[2], 0, size, 3).astype(F32)
    image_pre[...] += side(got.at[2], below, image_size, 4).astype(F32)
    for leave in leaving:
        leave.wait()


def cross_block_back(pairs, grad, matrices, text_kept, image_kept, text_probs, image_probs, text_d, image_d, part):
    wq, wkv_text, wkv_image, wq_image, w_out, w_out_image = matrices
    text_rows, image_rows = text_kept.shape[0], image_kept.shape[0]
    text_dc = low(nt(side(grad, 0, text_rows, 3), w_out[...]))
    image_dc = low(nt(side(grad, 3 * text_rows, image_rows, 4), w_out_image[...]))
    units = [(p, h) for p in range(pairs) for h in range(2)]

    def text_part(at):
        return [text_kept[rows_of(p, SLOTS), at + h * HEAD : at + (h + 1) * HEAD] for p, h in units]

    def image_part(at):
        return [image_kept[rows_of(p, PADDED), at + h * HEAD : at + (h + 1) * HEAD] for p, h in units]

    scale = HEAD**-0.5
    outer = [text_dc[rows_of(p, SLOTS), h * HEAD : (h + 1) * HEAD] for p, h in units]
    probs = [text_probs[i] for i in range(len(units))]
    found = attend_back(text_part(0), image_part(0), image_part(256), probs, outer, scale)
    for i, (p, h) in enumerate(units):
        text_d[rows_of(p, SLOTS), h * HEAD : (h + 1) * HEAD] = found[0][i]
        image_d[rows_of(p, PADDED), h * HEAD : (h + 1) * HEAD] = found[1][i]
        image_d[rows_of(p, PADDED), 256 + h * HEAD : 256 + (h + 1) * HEAD] = found[2][i]
    outer = [image_dc[rows_of(p, PADDED), h * HEAD : (h + 1) * HEAD] for p, h in units]
    probs = [image_probs[i] for i in range(len(units))]
    found = attend_back(image_part(512), text_part(256), text_part(512), probs, outer, scale)
    for i, (p, h) in enumerate(units):
        image_d[rows_of(p, PADDED), 512 + h * HEAD : 512 + (h + 1) * HEAD] = found[0][i]
        text_d[rows_of(p, SLOTS), 256 + h * HEAD : 256 + (h + 1) * HEAD] = found[1][i]
        text_d[rows_of(p, SLOTS), 512 + h * HEAD : 512 + (h + 1) * HEAD] = found[2][i]
    text_dx = nt(text_d[:, 0:256], wq[...]) + nt(text_d[:, 256:768], wkv_text[...])
    image_dx = nt(image_d[:, 0:512], wkv_image[...]) + nt(image_d[:, 512:768], wq_image[...])
    leave_blocks(part, 0, low(text_dx))
    leave_blocks(part, 3 * text_rows, low(image_dx))


def cross_back(pairs, grad, vectors, text_kept, image_kept, text_probs, image_probs, *refs):
    matrices = refs[:6]
    grads_out, text_d_out, image_d_out, own_sum, total, vector_sum = refs[6:12]
    grads, text_d, image_d, parts, got, got_vectors, *kept = refs[12:-4]
    send_sems, recv_sems, out_sems, in_sems = refs[-4:]
    core, y, unused_x = partners()
    copy = sender(send_sems, recv_sems)
    loads = [
        [
            pltpu.make_async_copy(source.at[j], ref.at[j], in_sems.at[j, n])
            for n, (source, ref) in enumerate(zip((text_kept, image_kept, text_probs, image_probs), kept))
        ]
        for j in range(QUARTERS)
    ]
    text_kept, image_kept, text_probs, image_probs = kept
    to_core = copy(0, grad, grads.at[1], core)
    to_y = copy(1, grad, grads.at[2], y)
    corner = copy(2, grads.at[2], grads.at[3], core)
    near_part = copy(3, parts.at[1], got.at[0], core)
    corner_part = copy(4, parts.at[3], got.at[1], core)
    vectors_core = copy(5, vectors, got_vectors.at[0], core)
    vectors_y = copy(6, vector_sum, got_vectors.at[1], y)
    for load in loads[0]:
        load.start()
    greet(core, y)
    vectors_core.start()
    to_y.start()
    to_core.start()
    for load in sum(loads[1:], []):
        load.start()
    grads[0] = grad[...]
    vectors_core.wait()
    vector_sum[...] = vectors[...] + got_vectors[0]
    vectors_y.start()

    def block(j, unused):
        @pl.when(j == 1)
        def near():
            to_core.wait()

        @pl.when(j == 2)
        def far():
            to_y.wait()
            corner.start()

        @pl.when(j == 3)
        def last():
            corner.wait()

        for at in range(QUARTERS):

            @pl.when(j == at)
            def loaded():
                for load in loads[at]:
                    load.wait()

        cross_block_back(
            pairs,
            grads.at[j],
            matrices,
            text_kept.at[j],
            image_kept.at[j],
            text_probs.at[j],
            image_probs.at[j],
            text_d.at[j],
            image_d.at[j],
            parts.at[j],
        )

        @pl.when(j == 1)
        def near_done():
            near_part.start()

        return unused

    lax.fori_loop(0, QUARTERS, block, 0)
    corner_part.start()
    leaving = [
        pltpu.make_async_copy(source, out, out_sems.at[i])
        for i, (source, out) in enumerate(((grads, grads_out), (text_d, text_d_out), (image_d, image_d_out)))
    ]
    for leave in leaving:
        leave.start()
    near_part.wait()
    own_sum[...] = parts[0].astype(F32) + got[0].astype(F32)
    vectors_y.wait()
    vector_sum[...] += got_vectors[1]
    corner_part.wait()
    total[...] = add(parts[2], got[1])
    for leave in leaving:
        leave.wait()


def halves(flip, values, x):
    half = flip.shape[0] // 2
    starts = [pl.multiple_of(lax.bitwise_xor(x, apart) * half, HEAD) for apart in range(2)]
    return [nn(flip[pl.ds(start, half), :], values) for start in starts]


def cross_last(total, vector_keep, vector_send, *refs):
    sources, loaded = refs[:12], refs[18:30]
    text_grad, image_grad, text_keep, image_keep_out, image_send_out, self_sum = refs[12:18]
    got, image_keep, image_send, text_send, text_got, self_got, text_flip, text_g_flip, image_flip, image_g_flip = refs[30:40]
    send_sems, recv_sems, in_sems, out_sems = refs[40:]
    self_all, self_x, texts, grads, text_d, text_c, images, image_d, image_c, own_sum, text_n, image_n = loaded
    loads = []
    for n, (source, ref) in enumerate(zip(sources, loaded)):
        if source.shape != ref.shape:
            source = source.at[:, :, pl.ds(768, BLOCK)]
        loads.append(pltpu.make_async_copy(source, ref, in_sems.at[n]))
    for load in loads:
        load.start()
    unused_core, y, x = partners()
    copy = sender(send_sems, recv_sems)
    far = copy(0, total, got, y)
    text_x = copy(1, text_send, text_got, x)
    dp = self_all.shape[0]
    z_at = lax.axis_index("dp")
    others = [lax.rem(z_at + k, dp) for k in range(1, dp)]
    along_z = [copy(2 + k, self_all.at[other], self_got.at[k], {"dp": other}) for k, other in enumerate(others)]
    greet(y, x, *[{"dp": other} for other in others])
    far.start()
    loads[0].wait()
    loads[1].wait()
    self_all[...] = add(self_all[...], self_x[...])
    for transfer in along_z:
        transfer.start()
    size, image_size = texts.shape[1], images.shape[1]
    below = 3 * size
    at = lax.axis_index("stream")
    leaving = []
    for first, rows, count, flip, g_flip, keep, send, number in (
        (0, size, 3, text_flip, text_g_flip, text_keep, text_send, (2, 3, 4, 5)),
        (below, image_size, 4, image_flip, image_g_flip, image_keep, image_send, (6, 3, 7, 8)),
    ):
        values, unused, outer, context = (loaded[n] for n in number)
        for n in number[:1] if count == 4 else number[:2]:
            loads[n].wait()
        for j in range(QUARTERS):
            columns = rows_of(j, rows)
            for b in range(count):
                flip[rows_of(b, BLOCK), columns] = values[j, :, b * BLOCK : (b + 1) * BLOCK].T
                g_flip[rows_of(b, BLOCK), columns] = grads[j, first + b * rows : first + (b + 1) * rows, :].T
        loads[number[2]].wait()
        loads[number[3]].wait()
        depth = flip.shape[0] // (2 * dp)
        padded = -(-depth // 16) * 16
        found_halves = halves(flip, outer[...].reshape(QUARTERS * rows, 768), at)
        last_halves = halves(g_flip, context[...].reshape(QUARTERS * rows, BLOCK), at)
        for out, found, last in zip((keep, send), found_halves, last_halves):
            for z in range(dp):
                taken = slice(z * depth, (z + 1) * depth)
                for b in range(3):
                    out[z, b * padded : b * padded + depth, :] = low(found[taken, b * BLOCK : (b + 1) * BLOCK])
                out[z, 3 * padded : 3 * padded + depth, :] = low(last[taken])
        if count == 3:
            for out, vector in ((text_keep, vector_keep), (text_send, vector_send)):
                below_all = out.shape[1] - vector.shape[1]
                for z in range(dp):
                    out[z, below_all:, :] = vector[z]
            text_x.start()
        else:
            leaving = [
                pltpu.make_async_copy(image_keep, image_keep_out, out_sems.at[0]),
                pltpu.make_async_copy(image_send, image_send_out, out_sems.at[1]),
            ]
            for leave in leaving:
                leave.start()
    summed = self_all[z_at].astype(F32)
    for k, transfer in enumerate(along_z):
        transfer.wait()
        summed = summed + self_got[k].astype(F32)
    self_sum[...] = low(summed)
    for load in loads[9:]:
        load.wait()
    far.wait()
    text_grad[...] = text_n[...] + side(own_sum, 0, size, 3) + side(got, 0, size, 3).astype(F32)
    image_total = low(image_n[...] + side(own_sum, below, image_size, 4) + side(got, below, image_size, 4).astype(F32))
    image_grad[...] = low(tn(spacing(image_size // PADDED), image_total))
    text_x.wait()
    text_keep[...] = add(text_keep[...], text_got[...])
    for leave in leaving:
        leave.wait()


def gate(hidden):
    half = 0.5 * (1.0 + lax.erf(hidden * (2.0**-0.5)))
    density = jnp.exp(-0.5 * hidden * hidden) * 0.3989422804014327
    return hidden * half, half + hidden * density


def mlp_forward(pairs, text_pre, image_pre, text_gain, text_bias, image_gain, image_bias, *refs):
    parts = refs[:4]
    text_low, image_low, text_next, image_next = refs[4:8]
    text_activ, text_slope, image_activ, image_slope, corner = refs[8:13]
    weights, sems, send_sems, recv_sems = refs[13:]
    step = pl.program_id(0)
    leaving = fetch_round(step, *parts, corner, weights, sems, send_sems, recv_sems)

    @pl.when(step == 0)
    def begin():
        for pre, gain, bias, rounded, total in (
            (text_pre, text_gain, text_bias, text_low, text_next),
            (image_pre, image_gain, image_bias, image_low, image_next),
        ):
            g, b = affine_row(gain, bias, 0)
            one = normed(pre[...])[0] * g + b
            total[...] = one
            rounded[...] = low(one)

    w = weights.at[step]
    for b in range(3):
        activ, slope = gate(nn(text_low[...], w[b * 768 : (b + 1) * 768, :]))
        text_activ[0, :, b * 256 : (b + 1) * 256] = low(activ)
        text_slope[0, :, b * 256 : (b + 1) * 256] = low(slope)
    activ, slope = gate(nn(image_low[...], w[4608:5632, :]))
    image_activ[0] = low(activ)
    image_slope[0] = low(slope)
    text_next[...] += nn(text_activ[0], side(w, 2304, 768, 3))
    image_next[...] += nn(image_activ[0], side(w, 5632, 256, 4))

    @pl.when(step == QUARTERS - 1)
    def finish():
        leaving.wait()


def lane_masks():
    lane = lax.broadcasted_iota(jnp.int32, (1, 2 * SELF_HEAD), 1)
    left = (lane < SELF_HEAD).astype(F32)
    return low(left), low(1.0 - left), lane < SELF_HEAD


def both_heads(tile, masks):
    return jnp.concatenate([tile * masks[0], tile * masks[1]], axis=0)


def one_tile(stacked, masks):
    return jnp.where(masks[2], stacked[:SLOTS], stacked[SLOTS:])


def self_forward(pairs, ids, lengths, text_pre, image_pre, text_gain, text_bias, image_gain, image_bias, text_cot, image_cot, *refs):
    parts = refs[:4]
    (
        text_out,
        image_out,
        text_grad,
        image_grad,
        text_vec,
        image_vec,
        rounded,
        text_q,
        text_k,
        text_v,
        text_c,
        text_probs,
        image_kept,
        image_probs,
        corner,
    ) = refs[4:19]
    weights, text_sum, image_sum, text_low, image_low, sems, send_sems, recv_sems = refs[19:]
    step = pl.program_id(0)
    leaving = fetch_round(step, *parts, corner, weights, sems, send_sems, recv_sems)
    text_rows, image_rows = text_pre.shape[0], image_pre.shape[0]

    @pl.when(step == 0)
    def begin():
        for pre, gain, bias, total, lower, at in (
            (text_pre, text_gain, text_bias, text_sum, text_low, 0),
            (image_pre, image_gain, image_bias, image_sum, image_low, 6 * text_rows),
        ):
            g, b = affine_row(gain, bias, 1)
            two = normed(pre[...])[0] * g + b
            total[...] = two
            lower[...] = low(two)
            leave_blocks(rounded, at, low(two))

    w = weights.at[step]
    for n, out in enumerate((text_q, text_k, text_v)):
        wide = jnp.concatenate([w[b * 576 + n * 192 : b * 576 + (n + 1) * 192, :] for b in range(3)], axis=1)
        out[0] = low(nt(text_low[...], wide))
    for n in range(3):
        image_kept[0, :, n * 256 : (n + 1) * 256] = low(nn(image_low[...], w[2304 + n * 1024 : 3328 + n * 1024, :]))

    masks = lane_masks()
    slots = lax.broadcasted_iota(jnp.int32, (1, SLOTS), 1)
    base = ids[2]
    valid = [slots < lengths[base + p] for p in range(pairs)]
    first, last = slice(0, 128), slice(128, 192)
    queries, keys, values, limits = [], [], [], []
    for p in range(pairs):
        rows = rows_of(p, SLOTS)
        queries += [both_heads(text_q[0, rows, first], masks), text_q[0, rows, last]]
        keys += [text_k[0, rows, first], text_k[0, rows, last]]
        values += [text_v[0, rows, first], text_v[0, rows, last]]
        limits += [valid[p], valid[p]]
    probs, context = attend(queries, keys, values, SELF_HEAD**-0.5, limits)
    for p in range(pairs):
        rows = rows_of(p, SLOTS)
        text_probs[0, p, 0:256, :] = probs[2 * p]
        text_probs[0, p, 256:384, :] = probs[2 * p + 1]
        text_c[0, rows, first] = low(one_tile(context[2 * p], masks))
        text_c[0, rows, last] = low(context[2 * p + 1])

    image_mask = lax.broadcasted_iota(jnp.int32, (PADDED, PADDED), 1) < REGIONS
    units = [(p, h) for p in range(pairs) for h in range(2)]

    def image_part(at):
        return [image_kept[0, rows_of(p, PADDED), at + h * HEAD : at + (h + 1) * HEAD] for p, h in units]

    probs, context = attend(image_part(0), image_part(256), image_part(512), HEAD**-0.5, [image_mask] * len(units))
    for i, (p, h) in enumerate(units):
        image_probs[0, i] = probs[i]
        image_kept[0, rows_of(p, PADDED), 768 + h * HEAD : 768 + (h + 1) * HEAD] = low(context[i])

    text_sum[...] += nn(text_c[0], side(w, 1728, 192, 3))
    image_sum[...] += nn(image_kept[0, :, 768:1024], side(w, 5376, 256, 4))

    @pl.when(step == QUARTERS - 1)
    def finish():
        apart = spacing(pairs)
        image_cot_apart = nn(apart, image_cot[...])
        for total, gain, bias, cot, grad, vec, at in (
            (text_sum, text_gain, text_bias, text_cot[...].astype(F32), text_grad, text_vec, 3 * text_rows),
            (image_sum, image_gain, image_bias, image_cot_apart, image_grad, image_vec, 6 * text_rows + 4 * image_rows),
        ):
            g, b = affine_row(gain, bias, 2)
            unit, scale = normed(total[...])
            value = unit * g + b
            if total is text_sum:
                text_out[...] = value
            else:
                image_out[...] = low(tn(apart, low(value)))
            back = norm_back(unit, scale, g, cot, vec)
            grad[...] = back
            leave_blocks(rounded, at, low(back))
        leaving.wait()


def self_back(pairs, dp, text_g, image_g, text_pre, image_pre, text_gain, image_gain, rounded, *refs):
    text_q, text_k, text_v, text_c, text_probs, image_kept, image_probs = refs[:7]
    parts = refs[7:12]
    text_n, image_n, text_vec, image_vec = refs[12:16]
    outs = refs[16:19]
    weights, found, text_sum, image_sum, text_g_low, image_g_low, near, rounded_near = refs[19:27]
    flips, (text_d, image_d, sems, out_sems, send_sems, recv_sems) = refs[27:31], refs[31:]
    step = pl.program_id(0)
    fetch(step, BACKWARD, *parts, weights, sems)
    core = partners()[0]
    copy = sender(send_sems, recv_sems)
    copies = [copy(n, found.at[n], near.at[n], core) for n in range(2)]
    rounded_copy = copy(2, rounded, rounded_near, core)

    @pl.when(step == 0)
    def begin():
        greet(core)
        rounded_copy.start()
        text_sum[...] = text_g[...]
        image_sum[...] = image_g[...]
        text_g_low[...] = low(text_g[...])
        image_g_low[...] = low(image_g[...])

    w = weights.at[step]
    masks = lane_masks()
    first, last = slice(0, 128), slice(128, 192)
    text_dc = low(nt(text_g_low[...], side(w, 1728, 192, 3)))
    queries, keys, values, probs, outer = [], [], [], [], []
    for p in range(pairs):
        rows = rows_of(p, SLOTS)
        queries += [both_heads(text_q[0, rows, first], masks), text_q[0, rows, last]]
        keys += [text_k[0, rows, first], text_k[0, rows, last]]
        values += [text_v[0, rows, first], text_v[0, rows, last]]
        probs += [text_probs[0, p, 0:256, :], text_probs[0, p, 256:384, :]]
        outer += [both_heads(text_dc[rows, first], masks), text_dc[rows, last]]
    grad_q, grad_k, grad_v = attend_back(queries, keys, values, probs, outer, SELF_HEAD**-0.5)
    size = text_g.shape[0]
    for p in range(pairs):
        rows = rows_of(p, SLOTS)
        text_d[0, rows, first] = one_tile(grad_q[2 * p], masks)
        text_d[0, rows, last] = grad_q[2 * p + 1]
        for n, grad in ((1, grad_k), (2, grad_v)):
            text_d[n, rows, first] = grad[2 * p]
            text_d[n, rows, last] = grad[2 * p + 1]

    image_dc = low(nt(image_g_low[...], side(w, 5376, 256, 4)))
    units = [(p, h) for p in range(pairs) for h in range(2)]

    def image_part(at):
        return [image_kept[0, rows_of(p, PADDED), at + h * HEAD : at + (h + 1) * HEAD] for p, h in units]

    outer = [image_dc[rows_of(p, PADDED), h * HEAD : (h + 1) * HEAD] for p, h in units]
    given = attend_back(
        image_part(0), image_part(256), image_part(512), [image_probs[0, i] for i in range(len(units))], outer, HEAD**-0.5
    )
    for n in range(3):
        for i, (p, h) in enumerate(units):
            image_d[rows_of(p, PADDED), n * 256 + h * HEAD : n * 256 + (h + 1) * HEAD] = given[n][i]

    gained = text_sum[...]
    for n in range(3):
        wide = jnp.concatenate([w[b * 576 + n * 192 : b * 576 + (n + 1) * 192, :] for b in range(3)], axis=1)
        gained = gained + nn(text_d[n], wide)
    text_sum[...] = gained
    image_sum[...] += nt(image_d[...], side(w, 2304, 1024, 3))

    slot = found.at[step]
    slot[0:size, 0:128] = text_d[0, :, first]
    slot[0:size, 128:256] = text_d[1, :, first]
    slot[size : 2 * size, 0:128] = text_d[2, :, first]
    slot[size : 2 * size, 128:256] = text_c[0, :, first]
    slot[2 * size : 3 * size, 0:128] = jnp.concatenate([text_d[0, :, last], text_d[1, :, last]], axis=1)
    slot[2 * size : 3 * size, 128:256] = jnp.concatenate([text_d[2, :, last], text_c[0, :, last]], axis=1)
    leave_blocks(slot, 3 * size, image_d[...])
    leave_blocks(slot, 3 * size + 3 * image_g.shape[0], image_kept[0, :, 768:1024])
    send_quarter(step, copies)

    @pl.when(step == QUARTERS - 1)
    def finish():
        leave_norm(1, text_sum, image_sum, text_pre, image_pre, text_gain, image_gain, text_n, image_n, text_vec, image_vec)
        rounded_copy.wait()
        for transfer in copies:
            transfer.wait()
        weight_grad(True, dp, (size, image_g.shape[0]), (rounded, rounded_near), found, near, weights, outs, flips, out_sems)


def leave_norm(norm, text_sum, image_sum, text_pre, image_pre, text_gain, image_gain, text_n, image_n, text_vec, image_vec):
    for total, pre, gain, out, vec in (
        (text_sum, text_pre, text_gain, text_n, text_vec),
        (image_sum, image_pre, image_gain, image_n, image_vec),
    ):
        unit, scale = normed(pre[...])
        out[...] = norm_back(unit, scale, gain[0, norm : norm + 1, :].astype(F32), total[...], vec)


def mlp_back(pairs, dp, text_g, image_g, text_one, image_one, text_pre, image_pre, text_gain, image_gain, *refs):
    text_activ, text_slope, image_activ, image_slope = refs[:4]
    parts = refs[4:9]
    text_n, image_n, next_low, text_vec, image_vec = refs[9:14]
    outs = refs[14:17]
    weights, found, text_sum, image_sum, text_g_low, image_g_low, near, rounded_near = refs[17:25]
    flips, (rounded, text_d, sems, out_sems, send_sems, recv_sems) = refs[25:29], refs[29:]
    step = pl.program_id(0)
    fetch(step, BACKWARD, *parts, weights, sems)
    size, image_size = text_g.shape[0], image_g.shape[0]
    core = partners()[0]
    copy = sender(send_sems, recv_sems)
    rounded_copy = copy(2, rounded, rounded_near, core)
    copies = [copy(n, found.at[n], near.at[n], core) for n in range(2)]

    @pl.when(step == 0)
    def begin():
        text_sum[...] = text_g[...]
        image_sum[...] = image_g[...]
        text_g_low[...] = low(text_g[...])
        image_g_low[...] = low(image_g[...])
        leave_blocks(rounded, 0, text_one[...])
        leave_blocks(rounded, 3 * size, text_g_low[...])
        leave_blocks(rounded, 6 * size, image_one[...])
        leave_blocks(rounded, 6 * size + 4 * image_size, image_g_low[...])
        greet(core)
        rounded_copy.start()

    w = weights.at[step]
    slot = found.at[step]
    wide = side(w, 2304, 768, 3)
    for b in range(3):
        columns = slice(b * 256, (b + 1) * 256)
        back = nt(text_g_low[...], wide[columns])
        text_d[:, columns] = low(back * text_slope[0, :, columns].astype(F32))
    text_sum[...] += nt(text_d[...], side(w, 0, 768, 3))
    image_d = low(nt(image_g_low[...], side(w, 5632, 256, 4)) * image_slope[0].astype(F32))
    image_sum[...] += nt(image_d, w[4608:5632, :])
    leave_blocks(slot, 0, text_d[...])
    leave_blocks(slot, 3 * size, text_activ[0])
    leave_blocks(slot, 6 * size, image_d)
    leave_blocks(slot, 6 * size + image_size, image_activ[0])
    send_quarter(step, copies)

    @pl.when(step == QUARTERS - 1)
    def finish():
        leave_norm(0, text_sum, image_sum, text_pre, image_pre, text_gain, image_gain, text_n, image_n, text_vec, image_vec)
        leave_blocks(next_low, 0, low(text_n[...]))
        leave_blocks(next_low, 3 * size, low(image_n[...]))
        rounded_copy.wait()
        for transfer in copies:
            transfer.wait()
        weight_grad(False, dp, (size, image_size), (rounded, rounded_near), found, near, weights, outs, flips, out_sems)


def weight_grad(is_self, dp, sizes, rounded, found, near, spare, outs, flips, out_sems):
    text_flip, text_g_flip, image_flip, image_g_flip = flips
    to_send, kept, to_z = (spare.at[n] for n in range(3))
    size, image_size = sizes
    x = lax.axis_index("stream")
    for at in range(2):
        for b in range(3):
            text_flip[rows_of(b, BLOCK), rows_of(at, size)] = rounded[at][rows_of(b, size), :].T
            text_g_flip[rows_of(b, BLOCK), rows_of(at, size)] = rounded[at][rows_of(3 + b, size), :].T
        for b in range(8):
            start = 6 * size + b * image_size
            flip = image_g_flip if b > 3 else image_flip
            flip[rows_of(b % 4, BLOCK), rows_of(at, image_size)] = rounded[at][start : start + image_size, :].T

    text_depth, image_depth = DT // (2 * dp), DV // (2 * dp)
    padded = -(-text_depth // 16) * 16
    lane = lax.broadcasted_iota(jnp.int32, (1, HEAD), 1) < SELF_HEAD
    top = 3 * padded + image_depth if is_self else 6 * padded
    count = 3 if is_self else 2
    leaving = []

    def leave(source, target):
        leaving.append(pltpu.make_async_copy(source.at[pl.ds(0, target.shape[0])], target, out_sems.at[len(leaving)]))
        leaving[-1].start()

    for slot in (1, 0):

        def block(start, rows):
            return jnp.concatenate([found[2 + slot, start : start + rows, :], near[slot, start : start + rows, :]], axis=0)

        def text_block(b):
            return block(b * size, size)

        def image_block(b, text_blocks):
            return block(text_blocks * size + b * image_size, image_size)

        def write(row, depth, value):
            for apart in range(2):
                ref, at = ((to_send if slot else kept), apart) if is_self else ((to_send if apart else kept), slot)
                for z in range(dp):
                    to = (at * dp + z) * top + row
                    ref[to : to + depth, :] = low(value[apart][z * depth : (z + 1) * depth])

        def bottom(b, value):
            for apart in range(2):
                for z in range(dp):
                    to = ((z * 4 + 2 * slot + apart) * count + b) * image_depth
                    to_z[to : to + image_depth, :] = low(value[apart][z * image_depth : (z + 1) * image_depth])

        if is_self:
            one, two, three = text_block(0), text_block(1), text_block(2)
            write(0, text_depth, halves(text_flip, one, x))
            pairs = zip(halves(text_flip, two[:, :HEAD], x), halves(text_g_flip, two[:, HEAD:], x))
            write(padded, text_depth, [jnp.concatenate(pair, axis=1) for pair in pairs])
            pairs = zip(halves(text_flip, three, x), halves(text_g_flip, three[:, HEAD:], x))
            mixed = [jnp.concatenate([a[:, :HEAD], jnp.where(lane, a[:, HEAD:], b)], axis=1) for a, b in pairs]
            write(2 * padded, text_depth, mixed)
            write(3 * padded, image_depth, halves(image_flip, image_block(0, 3), x))
            leave(*((to_send, outs[0]) if slot else (kept, outs[1])))
            for b in range(3):
                bottom(b, halves(image_g_flip if b == 2 else image_flip, image_block(1 + b, 3), x))
        else:
            for b in range(6):
                write(b * padded, text_depth, halves(text_g_flip if b > 2 else text_flip, text_block(b), x))
            for b in range(2):
                bottom(b, halves(image_g_flip if b else image_flip, image_block(b, 6), x))
    if not is_self:
        leave(to_send, outs[0])
        leave(kept, outs[1])
    leave(to_z, outs[2])
    for copy in leaving:
        copy.wait()


ANY = pl.BlockSpec(memory_space=pl.ANY)
SCALARS = pl.BlockSpec(memory_space=pltpu.SMEM)


def whole(array, buffers=None):
    zeros = (0,) * len(array.shape)
    mode = {} if buffers is None else {"pipeline_mode": pl.Buffered(buffers)}
    return pl.BlockSpec(array.shape, lambda *s: zeros, **mode)


def quarter(array, order):
    tail = (0,) * (len(array.shape) - 1)
    if order is FORWARD:
        return pl.BlockSpec((1,) + array.shape[1:], lambda s: (s,) + tail)
    return pl.BlockSpec((1,) + array.shape[1:], lambda s: (lax.rem(2 * s + 1 - lax.div(s, 2), 4),) + tail)


def shape(*dims, of=BF):
    return jax.ShapeDtypeStruct(dims, of)


def run(kernel, order, operands, outs, scratch, us, meeting=None):
    def spec(kind, array, given=False):
        if kind == "w" and given and order:
            return whole(array, 1)
        return {"s": lambda: SCALARS, "w": lambda: whole(array), "q": lambda: quarter(array, order), "a": lambda: ANY}[kind]()

    return pl.pallas_call(
        kernel,
        grid=(QUARTERS,) if order else (1,),
        in_specs=[spec(*entry, given=True) for entry in operands],
        out_specs=[spec(*entry) for entry in outs],
        out_shape=[array for unused, array in outs],
        scratch_shapes=scratch,
        compiler_params=pltpu.CompilerParams(
            dimension_semantics=("arbitrary",),
            vmem_limit_bytes=60 * 2**20,
            collective_id=meeting,
            has_side_effects=meeting is not None,
        ),
        cost_estimate=pl.CostEstimate(flops=int(us * 1.1e9), bytes_accessed=1024, transcendentals=0),
    )(*[array for unused, array in operands])


def swap(value, axis, apart):
    return lax.ppermute(value, axis, [(i, i ^ apart) for i in range(lax.axis_size(axis))])


def after(value, *earlier):
    return lax.optimization_barrier((value,) + earlier)[0]


class Line:
    def __init__(self):
        self.last = ()

    def take(self, value):
        return after(value, *self.last)

    def leave(self, *values):
        self.last = values


def add(left, right):
    return low(left.astype(F32) + right.astype(F32))


def fold_last(total):
    return lax.psum_scatter(total, "dp", scatter_dimension=0, tiled=True)[0]


def s(value):
    return ("s", value)


def w(value):
    return ("w", value)


def q(value):
    return ("q", value)


def a(value):
    return ("a", value)


def local(
    text_in,
    image_in,
    lengths,
    text_cot,
    image_cot,
    text_cross_q,
    text_cross_kv,
    text_cross_out,
    text_up,
    text_down,
    text_self_qkv,
    text_self_out,
    text_gain,
    text_bias,
    image_cross_q,
    image_cross_kv,
    image_cross_out,
    image_up,
    image_down,
    image_self_qkv,
    image_self_out,
    image_gain,
    image_bias,
):
    dp = lax.axis_size("dp")
    places = 2 * dp
    x_at = lax.axis_index("stream")
    t_at = lax.axis_index("tensor")
    size = text_in.shape[0]
    pairs = size // SLOTS
    image_size = pairs * PADDED
    units = 2 * pairs
    ids = jnp.stack([x_at, x_at * dp + lax.axis_index("dp")] + [(t_at ^ j) * pairs for j in range(QUARTERS)]).astype(jnp.int32)

    def leave(rows):
        return swap(rows, "stream", 1).astype(F32)

    line = Line()
    mlp_own, mlp_first, mlp_mine = pack([text_up[0], text_down[0], image_up[0], image_down[0]], places, 5120, ids)
    mlp_share = swap(mlp_mine, "tensor", 2)
    self_own, self_first, self_mine = pack(
        [
            text_self_qkv[0].transpose(1, 2, 0).reshape(-1, DT),
            text_self_out[0],
            image_self_qkv[0].reshape(DV, -1),
            image_self_out[0],
        ],
        places,
        4096,
        after(ids, mlp_own),
    )
    cross_w = (
        text_cross_q[0],
        image_cross_kv[0].reshape(DT, -1),
        text_cross_kv[0].reshape(DV, -1),
        image_cross_q[0],
        text_cross_out[0],
        image_cross_out[0],
    )
    line.leave(self_own)
    mlp_share = line.take(mlp_share)
    line.leave(mlp_share, cross_w[1], cross_w[2])
    self_share = line.take(swap(self_mine, "tensor", 2))
    line.leave(self_share)
    mlp_rest = lax.all_gather(mlp_share, ("stream", "dp"), axis=0, tiled=True)
    self_rest = lax.all_gather(self_share, ("stream", "dp"), axis=0, tiled=True)
    self_near = swap(self_own, "tensor", 1)
    mlp_near_w = swap(mlp_own, "tensor", 1)
    image_cot_here = swap(image_cot, "stream", 1)
    mlp_far = swap(mlp_first, "tensor", 2)

    text_wide, image_wide = shape(size, DT, of=F32), shape(image_size, DV, of=F32)
    text_f32, image_f32 = pltpu.VMEM((size, DT), F32), pltpu.VMEM((image_size, DV), F32)
    text_bf, image_bf = pltpu.VMEM((size, DT), BF), pltpu.VMEM((image_size, DV), BF)
    in_sems, out_sems = pltpu.SemaphoreType.DMA((5,)), pltpu.SemaphoreType.DMA((3,))
    text_affine = [w(text_gain), w(text_bias)]
    image_affine = [w(image_gain), w(image_bias)]
    vector_outs = [w(shape(2, DT, of=F32)), w(shape(2, DV, of=F32))]
    part_rows = 3 * size + 4 * image_size

    def buffer(weights):
        return pltpu.VMEM((QUARTERS,) + weights.shape, BF)

    in_four = [
        (QUARTERS, size, DT),
        (QUARTERS, image_size, DV),
        (QUARTERS, size, 1024),
        (QUARTERS, image_size, 1024),
        (QUARTERS, units, SLOTS, PADDED),
        (QUARTERS, units, PADDED, SLOTS),
    ]

    def links(count):
        return [pltpu.SemaphoreType.DMA((count,)), pltpu.SemaphoreType.DMA((count,))]

    text_pre1, image_pre1, texts, images, *cross_kept = run(
        functools.partial(cross_forward, pairs),
        None,
        [s(lengths), w(line.take(text_in)), w(image_in)] + [w(m) for m in cross_w],
        [w(text_wide), w(image_wide)] + [a(shape(*dims)) for dims in in_four],
        [pltpu.VMEM(dims, BF) for dims in in_four]
        + [pltpu.VMEM((QUARTERS, part_rows, BLOCK), BF), pltpu.VMEM((part_rows, BLOCK), BF), pltpu.VMEM((3, part_rows, BLOCK), BF)]
        + [image_bf]
        + links(10)
        + [pltpu.SemaphoreType.DMA((6,))],
        70,
        1,
    )
    line.leave(text_pre1, image_cot_here)
    mlp_far, mlp_rest = line.take((mlp_far, mlp_rest))
    self_far = swap(after(self_first, mlp_far), "tensor", 2)
    (
        text_one,
        image_one,
        text_pre2,
        image_pre2,
        text_activ,
        text_slope,
        image_activ,
        image_slope,
        mlp_corner,
    ) = run(
        functools.partial(mlp_forward, pairs),
        FORWARD,
        [w(text_pre1), w(image_pre1)] + text_affine + image_affine + [a(m) for m in (mlp_own, mlp_near_w, mlp_far, mlp_rest)],
        [
            w(shape(size, DT)),
            w(shape(image_size, DV)),
            w(text_wide),
            w(image_wide),
            q(shape(QUARTERS, size, 768)),
            q(shape(QUARTERS, size, 768)),
            q(shape(QUARTERS, image_size, 256)),
            q(shape(QUARTERS, image_size, 256)),
            a(mlp_own),
        ],
        [buffer(mlp_own), in_sems] + links(2),
        1,
        7,
    )
    mlp_w = mlp_own, mlp_near_w, mlp_far, mlp_rest, mlp_corner
    line.leave(text_pre2)
    self_far, self_rest = line.take((self_far, self_rest))
    (
        text_out,
        image_out,
        text_n3,
        image_n3,
        text_vec3,
        image_vec3,
        self_rounded,
        self_q,
        self_k,
        self_v,
        self_c,
        self_probs,
        self_kept,
        self_image_probs,
        self_corner,
    ) = run(
        functools.partial(self_forward, pairs),
        FORWARD,
        [s(ids), s(lengths), w(text_pre2), w(image_pre2)]
        + text_affine
        + image_affine
        + [w(text_cot), w(image_cot_here)]
        + [a(m) for m in (self_own, self_near, self_far, self_rest)],
        [w(text_wide), w(image_cot), w(text_wide), w(image_wide)]
        + vector_outs
        + [
            w(shape(2 * part_rows, BLOCK)),
            q(shape(QUARTERS, size, 192)),
            q(shape(QUARTERS, size, 192)),
            q(shape(QUARTERS, size, 192)),
            q(shape(QUARTERS, size, 192)),
            q(shape(QUARTERS, pairs, 384, SLOTS)),
            q(shape(QUARTERS, image_size, 1024)),
            q(shape(QUARTERS, units, PADDED, PADDED)),
            a(self_own),
        ],
        [buffer(self_own), text_f32, image_f32, text_bf, image_bf, in_sems] + links(2),
        19,
        8,
    )
    self_w = self_own, self_near, self_far, self_rest, self_corner
    image_out = swap(image_out, "stream", 1)

    text_depth, image_depth = DT // places, DV // places
    padded = -(-text_depth // 16) * 16

    def back_scratch(weights, rows):
        return [
            buffer(weights[0]),
            pltpu.VMEM((QUARTERS, rows, BLOCK), BF),
            text_f32,
            image_f32,
            text_bf,
            image_bf,
            pltpu.VMEM((2, rows, BLOCK), BF),
            pltpu.VMEM((2 * part_rows, BLOCK), BF),
            pltpu.VMEM((DT, 2 * size), BF),
            pltpu.VMEM((DT, 2 * size), BF),
            pltpu.VMEM((DV, 2 * image_size), BF),
            pltpu.VMEM((DV, 2 * image_size), BF),
        ]

    def grad_shapes(is_self):
        top = 3 * padded + image_depth if is_self else 6 * padded
        bottom = (3 if is_self else 2) * image_depth
        return (2, dp, top, BLOCK), (dp, 4 * bottom, BLOCK)

    def grad_outs(is_self):
        first, last = grad_shapes(is_self)
        return [a(shape(2 * dp * first[2], BLOCK))] * 2 + [a(shape(dp * last[1], BLOCK))]

    def grad_arrays(is_self, to_send, kept, to_z):
        first, last = grad_shapes(is_self)
        return to_send.reshape(first), kept.reshape(first), to_z.reshape(last)

    self_rows = 3 * size + 4 * image_size
    text_n2, image_n2, text_vec2, image_vec2, *self_found = run(
        functools.partial(self_back, pairs, dp),
        BACKWARD,
        [
            w(text_n3),
            w(image_n3),
            w(text_pre2),
            w(image_pre2),
            w(text_gain),
            w(image_gain),
            w(self_rounded),
            q(self_q),
            q(self_k),
            q(self_v),
            q(self_c),
            q(self_probs),
            q(self_kept),
            q(self_image_probs),
        ]
        + [a(m) for m in self_w],
        [w(text_wide), w(image_wide)] + vector_outs + grad_outs(True),
        back_scratch(self_w, self_rows)
        + [pltpu.VMEM((3, size, 192), BF), pltpu.VMEM((image_size, 768), BF), in_sems, out_sems]
        + links(3),
        32,
        2,
    )
    to_y, self_top, to_z = grad_arrays(True, *self_found)
    self_by_y = swap(to_y, "tensor", 2)
    self_bottom = fold_last(to_z)
    line.leave(self_top)
    mlp_rows = 6 * size + 2 * image_size
    text_n1, image_n1, grad_low, text_vec1, image_vec1, *mlp_found = run(
        functools.partial(mlp_back, pairs, dp),
        BACKWARD,
        [
            w(text_n2),
            w(image_n2),
            w(text_one),
            w(image_one),
            w(text_pre1),
            w(image_pre1),
            w(line.take(text_gain)),
            w(image_gain),
            q(text_activ),
            q(text_slope),
            q(image_activ),
            q(image_slope),
        ]
        + [a(m) for m in mlp_w],
        [w(text_wide), w(image_wide), w(shape(part_rows, BLOCK))]
        + vector_outs
        + grad_outs(False),
        back_scratch(mlp_w, mlp_rows)
        + [pltpu.VMEM((2 * part_rows, BLOCK), BF), text_bf, in_sems, out_sems]
        + links(3),
        28,
        3,
    )
    line.leave(grad_low)
    to_x, mlp_top, to_z = grad_arrays(False, *mlp_found)
    self_top, self_by_y, to_x, to_z, image_out = after((self_top, self_by_y, to_x, to_z, image_out), mlp_top)
    mlp_by_x = swap(to_x, "stream", 1)
    mlp_bottom = fold_last(to_z)
    self_top, to_x = add(self_top[0], self_by_y[0]), add(self_top[1], self_by_y[1])
    self_then_x = swap(to_x, "stream", 1)
    line.leave(self_top, to_x)
    d_dims = [(QUARTERS, part_rows, BLOCK), (QUARTERS, size, 768), (QUARTERS, image_size, 768)]
    vectors = jnp.concatenate(
        [jnp.pad(v, ((0, 0), (0, DV - DT))) for v in (text_vec1, text_vec2, text_vec3)]
        + [image_vec1, image_vec2, image_vec3, jnp.zeros((4, DV), F32)],
        axis=0,
    )
    grads, text_d, image_d, own_sum, total, vectors = run(
        functools.partial(cross_back, pairs),
        None,
        [w(line.take(grad_low)), w(vectors)] + [a(k) for k in cross_kept] + [w(m) for m in cross_w],
        [a(shape(*dims)) for dims in d_dims]
        + [w(shape(part_rows, BLOCK, of=F32)), w(shape(part_rows, BLOCK)), w(shape(16, DV, of=F32))],
        [pltpu.VMEM(dims, BF) for dims in d_dims]
        + [pltpu.VMEM((QUARTERS, part_rows, BLOCK), BF), pltpu.VMEM((2, part_rows, BLOCK), BF), pltpu.VMEM((2, 16, DV), F32)]
        + [pltpu.VMEM(k.shape, BF) for k in cross_kept]
        + links(7)
        + [pltpu.SemaphoreType.DMA((3,)), pltpu.SemaphoreType.DMA((QUARTERS, 4))],
        48,
        4,
    )
    line.leave(total)
    text_only, image_only = 4 * padded + 16, 4 * image_depth
    text_vector = jnp.pad(vectors[:6, :DT].reshape(6, places, text_depth), ((0, 0), (0, 0), (0, BLOCK - text_depth)))
    image_vector = jnp.pad(vectors[6:].reshape(10, places, image_depth), ((0, 0), (0, 0), (0, BLOCK - image_depth)))
    vectors = low(jnp.concatenate([text_vector, image_vector], axis=0).transpose(1, 0, 2))
    vector_keep = lax.dynamic_slice_in_dim(vectors, x_at * dp, dp, 0)
    vector_send = lax.dynamic_slice_in_dim(vectors, (1 - x_at) * dp, dp, 0)
    last_inputs = [
        self_top,
        self_then_x,
        texts,
        grads,
        text_d,
        cross_kept[0],
        images,
        image_d,
        cross_kept[1],
        own_sum,
        text_n1,
        image_n1,
    ]
    last_scratch = [pltpu.VMEM(m.shape, m.dtype) for m in last_inputs]
    last_scratch[5], last_scratch[8] = pltpu.VMEM((QUARTERS, size, BLOCK), BF), pltpu.VMEM((QUARTERS, image_size, BLOCK), BF)
    text_grad, image_grad, cross_text, image_keep, image_send, self_top = run(
        cross_last,
        None,
        [w(line.take(total)), w(vector_keep), w(vector_send)] + [a(m) for m in last_inputs],
        [
            w(text_wide),
            w(image_cot),
            w(shape(dp, text_only, BLOCK)),
            a(shape(dp, image_only, BLOCK)),
            a(shape(dp, image_only, BLOCK)),
            w(shape(*self_top.shape[1:])),
        ],
        last_scratch
        + [
            pltpu.VMEM((part_rows, BLOCK), BF),
            pltpu.VMEM((dp, image_only, BLOCK), BF),
            pltpu.VMEM((dp, image_only, BLOCK), BF),
            pltpu.VMEM((dp, text_only, BLOCK), BF),
            pltpu.VMEM((dp, text_only, BLOCK), BF),
            pltpu.VMEM((dp - 1, *self_top.shape[1:]), BF),
            pltpu.VMEM((DT, QUARTERS * size), BF),
            pltpu.VMEM((DT, QUARTERS * size), BF),
            pltpu.VMEM((DV, QUARTERS * image_size), BF),
            pltpu.VMEM((DV, QUARTERS * image_size), BF),
        ]
        + links(1 + dp)
        + [pltpu.SemaphoreType.DMA((12,)), pltpu.SemaphoreType.DMA((2,))],
        2,
        5,
    )
    line.leave(text_grad)
    mlp_top, mlp_by_x, self_bottom, cross_text, image_send = line.take(
        (mlp_top, mlp_by_x, self_bottom, cross_text, image_send)
    )
    cross_text = fold_last(cross_text)
    image_send = swap(image_send, "stream", 1)
    mlp_top, to_y = add(mlp_top[0], mlp_by_x[0]), add(mlp_top[1], mlp_by_x[1])
    mlp_then_y = swap(to_y, "tensor", 2)
    line.leave(mlp_top, to_y)
    self_bottom = line.take(self_bottom).reshape(2, 2, 3 * image_depth, BLOCK)
    self_bottom_x = swap(self_bottom[:, 1], "stream", 1)
    cross_image = add(image_keep, line.take(image_send))
    line.leave(cross_image)
    cross_image = fold_last(cross_image)
    self_bottom = add(self_bottom[:, 0], line.take(self_bottom_x))
    self_bottom_y = swap(self_bottom[1], "tensor", 2)
    mlp_bottom = line.take(mlp_bottom).reshape(2, 2, 2 * image_depth, BLOCK)
    mlp_bottom_x = swap(mlp_bottom[:, 1], "stream", 1)
    mlp_top = add(mlp_top, line.take(mlp_then_y))
    line.leave(mlp_top)
    mlp_top = fold_last(mlp_top)
    mlp_bottom = add(mlp_bottom[:, 0], line.take(mlp_bottom_x))
    mlp_bottom = add(mlp_bottom[0], swap(mlp_bottom[1], "tensor", 2))
    self_bottom = add(self_bottom[0], self_bottom_y)
    self_grads = jnp.concatenate([self_top, self_bottom], axis=0)
    image_grad = leave(image_grad)

    def pick(packed, first, count, depth, stride):
        rows = [packed[first + b * stride : first + b * stride + depth] for b in range(count)]
        return jnp.concatenate(rows, axis=1).astype(F32)

    def text_pick(packed, first, count):
        return pick(packed, first, count, text_depth, padded)

    def image_pick(packed, first, count):
        return pick(packed, first, count, image_depth, image_depth)

    sums = cross_text[4 * padded :].astype(F32)
    text_vectors, image_vectors = sums[:6, :text_depth], sums[6:12, :image_depth]

    self_text = text_pick(self_grads, 0, 3)

    def heads(at):
        return jnp.concatenate([self_text[:, at * 128 : (at + 1) * 128], self_text[:, 512 + at * 64 : 576 + at * 64]], axis=1)

    below = 3 * padded
    return (
        text_out,
        image_out.astype(F32),
        text_grad,
        image_grad,
        text_pick(cross_text, 0, 1)[None],
        image_pick(cross_image, 0, 2).reshape(1, image_depth, 2, 256),
        text_pick(cross_text, 3 * padded, 1).T[None],
        text_pick(mlp_top, 0, 3)[None],
        text_pick(mlp_top, below, 3).T[None],
        jnp.stack([heads(n) for n in range(3)], axis=1)[None],
        heads(3).T[None],
        text_vectors[0::2][None],
        text_vectors[1::2][None],
        image_pick(cross_image, 2 * image_depth, 1)[None],
        text_pick(cross_text, padded, 2).reshape(1, text_depth, 2, 256),
        image_pick(cross_image, 3 * image_depth, 1).T[None],
        image_pick(mlp_bottom, 0, 1)[None],
        image_pick(mlp_bottom, image_depth, 1).T[None],
        image_pick(self_grads, below, 3).reshape(1, image_depth, 3, 256),
        image_pick(self_grads, below + 3 * image_depth, 1).T[None],
        image_vectors[0::2][None],
        image_vectors[1::2][None],
    )


def solution(mesh):
    rows = P(("stream", "dp", "tensor"), None)
    wide_in = P(None, None, "tensor")
    group_in = P(None, None, None, "tensor")
    wide_out = P(None, "tensor", None)
    grad_in = P(None, ("stream", "dp"), "tensor")
    grad_group = P(None, ("stream", "dp"), None, "tensor")
    grad_out = P(None, "tensor", ("stream", "dp"))
    vector = P(None, None, ("stream", "dp"))
    weights = (wide_in, group_in, wide_out, wide_in, wide_out, group_in, wide_out, P(), P())
    grads = (grad_in, grad_group, grad_out, grad_in, grad_out, grad_group, grad_out, vector, vector)
    return jax.shard_map(
        local,
        mesh=mesh,
        in_specs=(rows, rows, P(("stream", "dp")), rows, rows) + weights + weights,
        out_specs=(rows, rows, rows, rows) + grads + grads,
        check_vma=False,
    )
```

```python
import functools
import math

import jax
import jax.numpy as jnp
from jax import lax
from jax.experimental import pallas as pl
from jax.experimental.pallas import tpu as pltpu
from jax.sharding import PartitionSpec as P

DT = 768
DV = 1024
HEAD = 128
SELF_HEAD = 64
SLOTS = 128
REGIONS = 37
PADDED = 48
QUARTERS = 4
BLOCK = 256

norm_eps = 1e-05
masked_score = -1e30

BF = jnp.bfloat16
F32 = jnp.float32
FORWARD = (0, 1, 2, 3)
BACKWARD = (1, 3, 0, 2)


def nn(left, right):
    return lax.dot_general(left, right, (((1,), (0,)), ((), ())), preferred_element_type=F32)


def nt(left, right):
    return lax.dot_general(left, right, (((1,), (1,)), ((), ())), preferred_element_type=F32)


def tn(left, right):
    return lax.dot_general(left, right, (((0,), (0,)), ((), ())), preferred_element_type=F32)


def low(value):
    return value.astype(BF)


def normed(inputs):
    centered = inputs - jnp.mean(inputs, axis=-1, keepdims=True)
    scale = lax.rsqrt(jnp.mean(centered * centered, axis=-1, keepdims=True) + norm_eps)
    return centered * scale, scale


def norm_back(unit, scale, gain, grad, vec):
    vec[0:1] = jnp.sum(grad * unit, axis=0, keepdims=True)
    vec[1:2] = jnp.sum(grad, axis=0, keepdims=True)
    inner = grad * gain
    shift = jnp.mean(inner, axis=-1, keepdims=True)
    slope = jnp.mean(inner * unit, axis=-1, keepdims=True)
    return scale * (inner - shift - unit * slope)


def softmax_all(scores):
    tops = [jnp.max(s, axis=-1, keepdims=True) for s in scores]
    powers = [jnp.exp(s - t) for s, t in zip(scores, tops)]
    sums = [jnp.sum(e, axis=-1, keepdims=True) for e in powers]
    return [low(e / total) for e, total in zip(powers, sums)]


def attend(queries, keys, values, scale, masks):
    scores = [nt(q, k) * scale for q, k in zip(queries, keys)]
    scores = [s if m is None else jnp.where(m, s, masked_score) for s, m in zip(scores, masks)]
    probs = softmax_all(scores)
    return probs, [nn(p, v) for p, v in zip(probs, values)]


def attend_back(queries, keys, values, probs, grads, scale):
    grad_probs = [nt(g, v) for g, v in zip(grads, values)]
    grad_values = [low(tn(p, g)) for p, g in zip(probs, grads)]
    wide = [p.astype(F32) for p in probs]
    inner = [jnp.sum(p * g, axis=-1, keepdims=True) for p, g in zip(wide, grad_probs)]
    grad_scores = [low(p * (g - i)) for p, g, i in zip(wide, grad_probs, inner)]
    grad_queries = [low(nn(g, k) * scale) for g, k in zip(grad_scores, keys)]
    grad_keys = [low(tn(g, q) * scale) for g, q in zip(grad_scores, queries)]
    return grad_queries, grad_keys, grad_values


def side(ref, row, width, count):
    return jnp.concatenate([ref[row + b * width : row + (b + 1) * width, :] for b in range(count)], axis=1)


def rows_of(pair, size):
    return slice(pair * size, (pair + 1) * size)


def fetch(step, order, own, near, far, far_rest, corner, buffer, sems):
    slots = [order.index(quarter) for quarter in range(QUARTERS)]
    cut, rest = far.shape[0], far_rest.shape[0]
    copies = [
        (slots[0], pltpu.make_async_copy(own, buffer.at[slots[0]], sems.at[0])),
        (slots[1], pltpu.make_async_copy(near, buffer.at[slots[1]], sems.at[1])),
        (slots[2], pltpu.make_async_copy(far, buffer.at[slots[2], pl.ds(0, cut)], sems.at[2])),
        (slots[2], pltpu.make_async_copy(far_rest, buffer.at[slots[2], pl.ds(cut, rest)], sems.at[3])),
    ]
    if corner is not None:
        copies.append((slots[3], pltpu.make_async_copy(corner, buffer.at[slots[3]], sems.at[4])))
    copies.sort(key=lambda entry: entry[0])

    @pl.when(step == 0)
    def begin():
        for slot, copy in copies:
            if slot == 0:
                copy.start()

    for at in range(QUARTERS):

        @pl.when(step == at)
        def arrive():
            for slot, copy in copies:
                if slot == at:
                    copy.wait()

    @pl.when(step == 0)
    def others():
        for slot, copy in copies:
            if slot > 0:
                copy.start()


def fetch_round(step, own, near, far, far_rest, corner, buffer, sems, send_sems, recv_sems):
    core = partners()[0]
    copy = sender(send_sems, recv_sems)
    cut, rest = far.shape[0], far_rest.shape[0]
    over = copy(0, far, buffer.at[3, pl.ds(0, cut)], core), copy(1, far_rest, buffer.at[3, pl.ds(cut, rest)], core)
    leaving = pltpu.make_async_copy(buffer.at[3], corner, sems.at[4])
    fetch(step, FORWARD, own, near, far, far_rest, None, buffer, sems)

    @pl.when(step == 0)
    def begin():
        greet(core)
        for transfer in over:
            transfer.start()

    @pl.when(step == 3)
    def last():
        for transfer in over:
            transfer.wait()
        leaving.start()

    return leaving


def spacing(pairs):
    rows, columns = pairs * PADDED, pairs * REGIONS
    row = lax.broadcasted_iota(jnp.int32, (rows, columns), 0)
    column = lax.broadcasted_iota(jnp.int32, (rows, columns), 1)
    chosen = jnp.zeros((rows, columns), F32)
    for p in range(pairs):
        inside = (column >= p * REGIONS) & (column < (p + 1) * REGIONS)
        chosen = jnp.where(inside & (row - p * PADDED == column - p * REGIONS), 1.0, chosen)
    return low(chosen)


def send_quarter(step, copies):
    for at, copy in enumerate(copies):

        @pl.when(step == at)
        def leave():
            copy.start()


def affine_row(gain, bias, norm):
    return gain[0, norm : norm + 1, :].astype(F32), bias[0, norm : norm + 1, :].astype(F32)


def leave_blocks(ref, row, value):
    size = value.shape[0]
    for b in range(value.shape[1] // BLOCK):
        ref[row + b * size : row + (b + 1) * size, :] = value[:, b * BLOCK : (b + 1) * BLOCK]


MESH = pl.DeviceIdType.MESH


def partners():
    t = lax.axis_index("tensor")
    return {"tensor": lax.bitwise_xor(t, 1)}, {"tensor": lax.bitwise_xor(t, 2)}, {"stream": lax.bitwise_xor(lax.axis_index("stream"), 1)}


def greet(*others):
    barrier = pltpu.get_barrier_semaphore()
    for other in others:
        pl.semaphore_signal(barrier, inc=1, device_id=other, device_id_type=MESH)
    pl.semaphore_wait(barrier, len(others))


def sender(send_sems, recv_sems):
    def copy(number, source, target, to):
        return pltpu.make_async_remote_copy(
            src_ref=source,
            dst_ref=target,
            send_sem=send_sems.at[number],
            recv_sem=recv_sems.at[number],
            device_id=to,
            device_id_type=MESH,
        )

    return copy


def pack(pieces, places, rest, ids):
    total = sum(m.size for m in pieces) // BLOCK
    cut, share = total - rest, rest // places

    def kernel(ids, *refs):
        sources, (own, first, mine) = refs[: len(pieces)], refs[len(pieces) :]
        row = 0
        for ref in sources:
            leave_blocks(own, row, ref[...])
            row += ref.size // BLOCK
        first[...] = own[0:cut, :]
        mine[...] = own[pl.ds(pl.multiple_of(cut + ids[1] * share, 16), share), :]

    return run(
        kernel,
        None,
        [s(ids)] + [w(m) for m in pieces],
        [w(shape(total, BLOCK)), w(shape(cut, BLOCK)), w(shape(share, BLOCK))],
        [],
        3,
    )


def cross_block(pairs, first, lengths, text, image, matrices, text_kept, image_kept, text_probs, image_probs, part):
    wq, wkv_text, wkv_image, wq_image, w_out, w_out_image = matrices
    text_low = text[...]
    image_low = image[...]
    text_kept[:, 0:256] = low(nn(text_low, wq[...]))
    text_kept[:, 256:768] = low(nn(text_low, wkv_text[...]))
    image_kept[:, 0:512] = low(nn(image_low, wkv_image[...]))
    image_kept[:, 512:768] = low(nn(image_low, wq_image[...]))

    image_mask = lax.broadcasted_iota(jnp.int32, (SLOTS, PADDED), 1) < REGIONS
    slots = lax.broadcasted_iota(jnp.int32, (PADDED, SLOTS), 1)
    units = [(p, h) for p in range(pairs) for h in range(2)]

    def text_part(at):
        return [text_kept[rows_of(p, SLOTS), at + h * HEAD : at + (h + 1) * HEAD] for p, h in units]

    def image_part(at):
        return [image_kept[rows_of(p, PADDED), at + h * HEAD : at + (h + 1) * HEAD] for p, h in units]

    scale = HEAD**-0.5
    probs, context = attend(text_part(0), image_part(0), image_part(256), scale, [image_mask] * len(units))
    for i, (p, h) in enumerate(units):
        text_probs[i] = probs[i]
        text_kept[rows_of(p, SLOTS), 768 + h * HEAD : 768 + (h + 1) * HEAD] = low(context[i])
    limits = [lengths[first + p] for p in range(pairs)]
    masks = [slots < limits[p] for p, h in units]
    probs, context = attend(image_part(512), text_part(256), text_part(512), scale, masks)
    for i, (p, h) in enumerate(units):
        image_probs[i] = probs[i]
        image_kept[rows_of(p, PADDED), 768 + h * HEAD : 768 + (h + 1) * HEAD] = low(context[i])
    leave_blocks(part, 0, low(nn(text_kept[:, 768:1024], w_out[...])))
    leave_blocks(part, 3 * text.shape[0], low(nn(image_kept[:, 768:1024], w_out_image[...])))


def cross_forward(pairs, lengths, text, image, *refs):
    matrices = refs[:6]
    text_pre, image_pre = refs[6:8]
    outs = refs[8:14]
    texts, images, text_kept, image_kept, text_probs, image_probs, parts, total, got, image_apart = refs[14:24]
    send_sems, recv_sems, out_sems = refs[24:]
    core, y, x = partners()
    copy = sender(send_sems, recv_sems)
    text_core = copy(0, text, texts.at[1], core)
    text_y = copy(1, text, texts.at[2], y)
    image_x = copy(2, image_apart, images.at[0], x)
    image_core = copy(3, images.at[0], images.at[1], core)
    image_y = copy(4, images.at[0], images.at[2], y)
    text_corner = copy(5, texts.at[2], texts.at[3], core)
    image_corner = copy(6, images.at[2], images.at[3], core)
    near_part = copy(7, parts.at[1], got.at[0], core)
    corner_part = copy(8, parts.at[3], got.at[1], core)
    far_part = copy(9, total, got.at[2], y)

    image_apart[...] = low(nn(spacing(pairs), image[...]))
    greet(core, y, x)
    image_x.start()
    text_y.start()
    text_core.start()
    texts[0] = text[...]
    image_x.wait()
    image_y.start()
    image_core.start()

    def block(j, unused):
        @pl.when(j == 1)
        def near():
            text_core.wait()
            image_core.wait()

        @pl.when(j == 2)
        def far():
            text_y.wait()
            text_corner.start()
            image_y.wait()
            image_corner.start()

        @pl.when(j == 3)
        def corner():
            text_corner.wait()
            image_corner.wait()

        cross_block(
            pairs,
            lax.bitwise_xor(lax.axis_index("tensor"), j) * pairs,
            lengths,
            texts.at[j],
            images.at[j],
            matrices,
            text_kept.at[j],
            image_kept.at[j],
            text_probs.at[j],
            image_probs.at[j],
            parts.at[j],
        )

        @pl.when(j == 1)
        def near_done():
            near_part.start()

        return unused

    lax.fori_loop(0, QUARTERS, block, 0)
    corner_part.start()
    leaving = [
        pltpu.make_async_copy(source, out, out_sems.at[i])
        for i, (source, out) in enumerate(
            zip((texts, images, text_kept, image_kept, text_probs, image_probs), outs)
        )
    ]
    for leave in leaving:
        leave.start()
    corner_part.wait()
    total[...] = add(parts[2], got[1])
    far_part.start()
    near_part.wait()
    size, image_size = text.shape[0], image_apart.shape[0]
    below = 3 * size

    def summed(row, depth, count, start):
        for ref in (parts.at[0], got.at[0]):
            start = start + side(ref, row, depth, count).astype(F32)
        return start

    text_pre[...] = summed(0, size, 3, text[...].astype(F32))
    image_pre[...] = summed(below, image_size, 4, images[0].astype(F32))
    far_part.wait()
    text_pre[...] += side(got.at[2], 0, size, 3).astype(F32)
    image_pre[...] += side(got.at[2], below, image_size, 4).astype(F32)
    for leave in leaving:
        leave.wait()


def cross_block_back(pairs, grad, matrices, text_kept, image_kept, text_probs, image_probs, text_d, image_d, part):
    wq, wkv_text, wkv_image, wq_image, w_out, w_out_image = matrices
    text_rows, image_rows = text_kept.shape[0], image_kept.shape[0]
    text_dc = low(nt(side(grad, 0, text_rows, 3), w_out[...]))
    image_dc = low(nt(side(grad, 3 * text_rows, image_rows, 4), w_out_image[...]))
    units = [(p, h) for p in range(pairs) for h in range(2)]

    def text_part(at):
        return [text_kept[rows_of(p, SLOTS), at + h * HEAD : at + (h + 1) * HEAD] for p, h in units]

    def image_part(at):
        return [image_kept[rows_of(p, PADDED), at + h * HEAD : at + (h + 1) * HEAD] for p, h in units]

    scale = HEAD**-0.5
    outer = [text_dc[rows_of(p, SLOTS), h * HEAD : (h + 1) * HEAD] for p, h in units]
    probs = [text_probs[i] for i in range(len(units))]
    found = attend_back(text_part(0), image_part(0), image_part(256), probs, outer, scale)
    for i, (p, h) in enumerate(units):
        text_d[rows_of(p, SLOTS), h * HEAD : (h + 1) * HEAD] = found[0][i]
        image_d[rows_of(p, PADDED), h * HEAD : (h + 1) * HEAD] = found[1][i]
        image_d[rows_of(p, PADDED), 256 + h * HEAD : 256 + (h + 1) * HEAD] = found[2][i]
    outer = [image_dc[rows_of(p, PADDED), h * HEAD : (h + 1) * HEAD] for p, h in units]
    probs = [image_probs[i] for i in range(len(units))]
    found = attend_back(image_part(512), text_part(256), text_part(512), probs, outer, scale)
    for i, (p, h) in enumerate(units):
        image_d[rows_of(p, PADDED), 512 + h * HEAD : 512 + (h + 1) * HEAD] = found[0][i]
        text_d[rows_of(p, SLOTS), 256 + h * HEAD : 256 + (h + 1) * HEAD] = found[1][i]
        text_d[rows_of(p, SLOTS), 512 + h * HEAD : 512 + (h + 1) * HEAD] = found[2][i]
    text_dx = nt(text_d[:, 0:256], wq[...]) + nt(text_d[:, 256:768], wkv_text[...])
    image_dx = nt(image_d[:, 0:512], wkv_image[...]) + nt(image_d[:, 512:768], wq_image[...])
    leave_blocks(part, 0, low(text_dx))
    leave_blocks(part, 3 * text_rows, low(image_dx))


def cross_back(pairs, grad, *refs):
    given, (text_kept, image_kept, text_probs, image_probs), matrices = refs[:6], refs[6:10], refs[10:16]
    grads_out, text_d_out, image_d_out, own_sum, total, vector_sum = refs[16:22]
    grads, text_d, image_d, parts, got, got_vectors, vectors, *kept = refs[22:-4]
    send_sems, recv_sems, out_sems, in_sems = refs[-4:]
    core, y, unused_x = partners()
    copy = sender(send_sems, recv_sems)
    loads = [
        [
            pltpu.make_async_copy(source.at[j], ref.at[j], in_sems.at[j, n])
            for n, (source, ref) in enumerate(zip((text_kept, image_kept, text_probs, image_probs), kept))
        ]
        for j in range(QUARTERS)
    ]
    text_kept, image_kept, text_probs, image_probs = kept
    to_core = copy(0, grad, grads.at[1], core)
    to_y = copy(1, grad, grads.at[2], y)
    corner = copy(2, grads.at[2], grads.at[3], core)
    near_part = copy(3, parts.at[1], got.at[0], core)
    corner_part = copy(4, parts.at[3], got.at[1], core)
    vectors_core = copy(5, vectors, got_vectors.at[0], core)
    vectors_y = copy(6, vector_sum, got_vectors.at[1], y)
    for load in loads[0]:
        load.start()
    vectors[...] = jnp.zeros_like(vectors)
    for n, vector in enumerate(given):
        vectors[2 * n : 2 * n + 2, 0 : vector.shape[1]] = vector[...]
    greet(core, y)
    vectors_core.start()
    to_y.start()
    to_core.start()
    for load in sum(loads[1:], []):
        load.start()
    grads[0] = grad[...]
    vectors_core.wait()
    vector_sum[...] = vectors[...] + got_vectors[0]
    vectors_y.start()

    def block(j, unused):
        @pl.when(j == 1)
        def near():
            to_core.wait()

        @pl.when(j == 2)
        def far():
            to_y.wait()
            corner.start()

        @pl.when(j == 3)
        def last():
            corner.wait()

        for at in range(QUARTERS):

            @pl.when(j == at)
            def loaded():
                for load in loads[at]:
                    load.wait()

        cross_block_back(
            pairs,
            grads.at[j],
            matrices,
            text_kept.at[j],
            image_kept.at[j],
            text_probs.at[j],
            image_probs.at[j],
            text_d.at[j],
            image_d.at[j],
            parts.at[j],
        )

        @pl.when(j == 1)
        def near_done():
            near_part.start()

        return unused

    lax.fori_loop(0, QUARTERS, block, 0)
    corner_part.start()
    leaving = [
        pltpu.make_async_copy(source, out, out_sems.at[i])
        for i, (source, out) in enumerate(((grads, grads_out), (text_d, text_d_out), (image_d, image_d_out)))
    ]
    for leave in leaving:
        leave.start()
    near_part.wait()
    own_sum[...] = parts[0].astype(F32) + got[0].astype(F32)
    vectors_y.wait()
    vector_sum[...] += got_vectors[1]
    corner_part.wait()
    total[...] = add(parts[2], got[1])
    for leave in leaving:
        leave.wait()


def halves(flip, values, x):
    half = flip.shape[0] // 2
    starts = [pl.multiple_of(lax.bitwise_xor(x, apart) * half, HEAD) for apart in range(2)]
    return [nn(flip[pl.ds(start, half), :], values) for start in starts]


def pick_columns(values, start, depth):
    row = lax.broadcasted_iota(jnp.int32, (values.shape[1], BLOCK), 0)
    column = lax.broadcasted_iota(jnp.int32, (values.shape[1], BLOCK), 1)
    chosen = (row == column + start) & (column < depth)
    return nn(values, low(jnp.where(chosen, 1.0, 0.0)))


def cross_last(total, vectors, *refs):
    sources, loaded = refs[:14], refs[21:33]
    grad_left, grad_right, image_grad, text_keep, image_keep_out, image_send_out, self_sum = refs[14:21]
    got, image_keep, image_send, text_send, text_got, self_got, text_flip, text_g_flip, image_flip, image_g_flip = refs[33:43]
    send_sems, recv_sems, in_sems, out_sems = refs[43:]
    self_all, self_more, texts, grads, text_d, text_c, images, image_d, image_c, own_sum, text_n, image_n = loaded
    self_loads = []
    for n, (target, first) in enumerate(((self_all, 0), (self_all, 1), (self_more, 0), (self_more, 1))):
        depth = sources[n].shape[1]
        target = target.at[:, pl.ds(first * sources[n - 1].shape[1], depth)]
        self_loads.append(pltpu.make_async_copy(sources[n], target, in_sems.at[n]))
    loads = [None, None]
    for n, (source, ref) in enumerate(zip(sources[4:], loaded[2:])):
        if source.shape != ref.shape:
            source = source.at[:, :, pl.ds(768, BLOCK)]
        loads.append(pltpu.make_async_copy(source, ref, in_sems.at[4 + n]))
    for load in self_loads + loads[2:]:
        load.start()
    unused_core, y, x = partners()
    copy = sender(send_sems, recv_sems)
    far = copy(0, total, got, y)
    text_x = copy(1, text_send, text_got, x)
    dp = self_all.shape[0]
    z_at = lax.axis_index("dp")
    others = [lax.rem(z_at + k, dp) for k in range(1, dp)]
    along_z = [copy(2 + k, self_all.at[other], self_got.at[k], {"dp": other}) for k, other in enumerate(others)]
    greet(y, x, *[{"dp": other} for other in others])
    far.start()
    for load in self_loads:
        load.wait()
    self_all[...] = add(self_all[...], self_more[...])
    for transfer in along_z:
        transfer.start()
    size, image_size = texts.shape[1], images.shape[1]
    below = 3 * size
    at = lax.axis_index("stream")
    leaving = []
    for first, rows, count, flip, g_flip, keep, send, number in (
        (0, size, 3, text_flip, text_g_flip, text_keep, text_send, (2, 3, 4, 5)),
        (below, image_size, 4, image_flip, image_g_flip, image_keep, image_send, (6, 3, 7, 8)),
    ):
        values, unused, outer, context = (loaded[n] for n in number)
        for n in number[:1] if count == 4 else number[:2]:
            loads[n].wait()
        for j in range(QUARTERS):
            columns = rows_of(j, rows)
            for b in range(count):
                flip[rows_of(b, BLOCK), columns] = values[j, :, b * BLOCK : (b + 1) * BLOCK].T
                g_flip[rows_of(b, BLOCK), columns] = grads[j, first + b * rows : first + (b + 1) * rows, :].T
        loads[number[2]].wait()
        loads[number[3]].wait()
        depth = flip.shape[0] // (2 * dp)
        padded = -(-depth // 16) * 16
        found_halves = halves(flip, outer[...].reshape(QUARTERS * rows, 768), at)
        last_halves = halves(g_flip, context[...].reshape(QUARTERS * rows, BLOCK), at)
        for out, found, last in zip((keep, send), found_halves, last_halves):
            for z in range(dp):
                taken = slice(z * depth, (z + 1) * depth)
                for b in range(3):
                    out[z, b * padded : b * padded + depth, :] = low(found[taken, b * BLOCK : (b + 1) * BLOCK])
                out[z, 3 * padded : 3 * padded + depth, :] = low(last[taken])
        if count == 3:
            rounded = low(vectors[...])
            is_text = lax.broadcasted_iota(jnp.int32, (rounded.shape[0], BLOCK), 0) < 6
            for apart, out in enumerate((text_keep, text_send)):
                for z in range(dp):
                    place = lax.bitwise_xor(at, apart) * dp + z
                    text_part = pick_columns(rounded[:, :DT], place * depth, depth)
                    image_depth = DV // (2 * dp)
                    image_part = pick_columns(rounded, place * image_depth, image_depth)
                    out[z, 4 * padded :, :] = low(jnp.where(is_text, text_part, image_part))
            text_x.start()
        else:
            leaving = [
                pltpu.make_async_copy(image_keep, image_keep_out, out_sems.at[0]),
                pltpu.make_async_copy(image_send, image_send_out, out_sems.at[1]),
            ]
            for leave in leaving:
                leave.start()
    summed = self_all[z_at].astype(F32)
    for k, transfer in enumerate(along_z):
        transfer.wait()
        summed = summed + self_got[k].astype(F32)
    self_sum[...] = low(summed)
    for load in loads[9:]:
        load.wait()
    far.wait()
    text_total = text_n[...] + side(own_sum, 0, size, 3) + side(got, 0, size, 3).astype(F32)
    grad_left[...] = text_total[:, : DT // 2]
    grad_right[...] = text_total[:, DT // 2 :]
    image_total = low(image_n[...] + side(own_sum, below, image_size, 4) + side(got, below, image_size, 4).astype(F32))
    image_grad[...] = low(tn(spacing(image_size // PADDED), image_total))
    text_x.wait()
    text_keep[...] = add(text_keep[...], text_got[...])
    for leave in leaving:
        leave.wait()


def gate(hidden):
    half = 0.5 * (1.0 + lax.erf(hidden * (2.0**-0.5)))
    density = jnp.exp(-0.5 * hidden * hidden) * 0.3989422804014327
    return hidden * half, half + hidden * density


def mlp_forward(pairs, text_pre, image_pre, text_gain, text_bias, image_gain, image_bias, *refs):
    parts = refs[:4]
    text_low, image_low, text_next, image_next = refs[4:8]
    text_activ, text_slope, image_activ, image_slope, corner = refs[8:13]
    weights, sems, send_sems, recv_sems = refs[13:]
    step = pl.program_id(0)
    leaving = fetch_round(step, *parts, corner, weights, sems, send_sems, recv_sems)

    @pl.when(step == 0)
    def begin():
        for pre, gain, bias, rounded, total in (
            (text_pre, text_gain, text_bias, text_low, text_next),
            (image_pre, image_gain, image_bias, image_low, image_next),
        ):
            g, b = affine_row(gain, bias, 0)
            one = normed(pre[...])[0] * g + b
            total[...] = one
            rounded[...] = low(one)

    w = weights.at[step]
    for b in range(3):
        activ, slope = gate(nn(text_low[...], w[b * 768 : (b + 1) * 768, :]))
        text_activ[0, :, b * 256 : (b + 1) * 256] = low(activ)
        text_slope[0, :, b * 256 : (b + 1) * 256] = low(slope)
    activ, slope = gate(nn(image_low[...], w[4608:5632, :]))
    image_activ[0] = low(activ)
    image_slope[0] = low(slope)
    text_next[...] += nn(text_activ[0], side(w, 2304, 768, 3))
    image_next[...] += nn(image_activ[0], side(w, 5632, 256, 4))

    @pl.when(step == QUARTERS - 1)
    def finish():
        leaving.wait()


def lane_masks():
    lane = lax.broadcasted_iota(jnp.int32, (1, 2 * SELF_HEAD), 1)
    left = (lane < SELF_HEAD).astype(F32)
    return low(left), low(1.0 - left), lane < SELF_HEAD


def both_heads(tile, masks):
    return jnp.concatenate([tile * masks[0], tile * masks[1]], axis=0)


def one_tile(stacked, masks):
    return jnp.where(masks[2], stacked[:SLOTS], stacked[SLOTS:])


def self_forward(pairs, ids, lengths, text_pre, image_pre, text_gain, text_bias, image_gain, image_bias, text_cot, image_cot, *refs):
    parts = refs[:4]
    (
        text_left,
        text_right,
        image_out,
        text_grad,
        image_grad,
        text_vec,
        image_vec,
        rounded,
        text_q,
        text_k,
        text_v,
        text_c,
        text_probs,
        image_kept,
        image_probs,
        corner,
    ) = refs[4:20]
    weights, text_sum, image_sum, text_low, image_low, sems, send_sems, recv_sems = refs[20:]
    step = pl.program_id(0)
    leaving = fetch_round(step, *parts, corner, weights, sems, send_sems, recv_sems)
    text_rows, image_rows = text_pre.shape[0], image_pre.shape[0]

    @pl.when(step == 0)
    def begin():
        for pre, gain, bias, total, lower, at in (
            (text_pre, text_gain, text_bias, text_sum, text_low, 0),
            (image_pre, image_gain, image_bias, image_sum, image_low, 6 * text_rows),
        ):
            g, b = affine_row(gain, bias, 1)
            two = normed(pre[...])[0] * g + b
            total[...] = two
            lower[...] = low(two)
            leave_blocks(rounded, at, low(two))

    w = weights.at[step]
    for n, out in enumerate((text_q, text_k, text_v)):
        wide = jnp.concatenate([w[b * 576 + n * 192 : b * 576 + (n + 1) * 192, :] for b in range(3)], axis=1)
        out[0] = low(nt(text_low[...], wide))
    for n in range(3):
        image_kept[0, :, n * 256 : (n + 1) * 256] = low(nn(image_low[...], w[2304 + n * 1024 : 3328 + n * 1024, :]))

    masks = lane_masks()
    slots = lax.broadcasted_iota(jnp.int32, (1, SLOTS), 1)
    base = ids[2]
    valid = [slots < lengths[base + p] for p in range(pairs)]
    first, last = slice(0, 128), slice(128, 192)
    queries, keys, values, limits = [], [], [], []
    for p in range(pairs):
        rows = rows_of(p, SLOTS)
        queries += [both_heads(text_q[0, rows, first], masks), text_q[0, rows, last]]
        keys += [text_k[0, rows, first], text_k[0, rows, last]]
        values += [text_v[0, rows, first], text_v[0, rows, last]]
        limits += [valid[p], valid[p]]
    probs, context = attend(queries, keys, values, SELF_HEAD**-0.5, limits)
    for p in range(pairs):
        rows = rows_of(p, SLOTS)
        text_probs[0, p, 0:256, :] = probs[2 * p]
        text_probs[0, p, 256:384, :] = probs[2 * p + 1]
        text_c[0, rows, first] = low(one_tile(context[2 * p], masks))
        text_c[0, rows, last] = low(context[2 * p + 1])

    image_mask = lax.broadcasted_iota(jnp.int32, (PADDED, PADDED), 1) < REGIONS
    units = [(p, h) for p in range(pairs) for h in range(2)]

    def image_part(at):
        return [image_kept[0, rows_of(p, PADDED), at + h * HEAD : at + (h + 1) * HEAD] for p, h in units]

    probs, context = attend(image_part(0), image_part(256), image_part(512), HEAD**-0.5, [image_mask] * len(units))
    for i, (p, h) in enumerate(units):
        image_probs[0, i] = probs[i]
        image_kept[0, rows_of(p, PADDED), 768 + h * HEAD : 768 + (h + 1) * HEAD] = low(context[i])

    text_sum[...] += nn(text_c[0], side(w, 1728, 192, 3))
    image_sum[...] += nn(image_kept[0, :, 768:1024], side(w, 5376, 256, 4))

    @pl.when(step == QUARTERS - 1)
    def finish():
        apart = spacing(pairs)
        image_cot_apart = nn(apart, image_cot[...])
        for total, gain, bias, cot, grad, vec, at in (
            (text_sum, text_gain, text_bias, text_cot[...].astype(F32), text_grad, text_vec, 3 * text_rows),
            (image_sum, image_gain, image_bias, image_cot_apart, image_grad, image_vec, 6 * text_rows + 4 * image_rows),
        ):
            g, b = affine_row(gain, bias, 2)
            unit, scale = normed(total[...])
            value = unit * g + b
            if total is text_sum:
                text_left[...] = value[:, : DT // 2]
                text_right[...] = value[:, DT // 2 :]
            else:
                image_out[...] = low(tn(apart, low(value)))
            back = norm_back(unit, scale, g, cot, vec)
            grad[...] = back
            leave_blocks(rounded, at, low(back))
        leaving.wait()


def self_back(pairs, dp, text_g, image_g, text_pre, image_pre, text_gain, image_gain, rounded, *refs):
    text_q, text_k, text_v, text_c, text_probs, image_kept, image_probs = refs[:7]
    parts = refs[7:12]
    text_n, image_n, text_vec, image_vec = refs[12:16]
    outs = refs[16:21]
    weights, found, text_sum, image_sum, text_g_low, image_g_low, near, rounded_near = refs[21:29]
    flips, (text_d, image_d, sems, out_sems, send_sems, recv_sems) = refs[29:33], refs[33:]
    step = pl.program_id(0)
    fetch(step, BACKWARD, *parts, weights, sems)
    core = partners()[0]
    copy = sender(send_sems, recv_sems)
    copies = [copy(n, found.at[n], near.at[n], core) for n in range(2)]
    rounded_copy = copy(2, rounded, rounded_near, core)

    @pl.when(step == 0)
    def begin():
        greet(core)
        rounded_copy.start()
        text_sum[...] = text_g[...]
        image_sum[...] = image_g[...]
        text_g_low[...] = low(text_g[...])
        image_g_low[...] = low(image_g[...])

    w = weights.at[step]
    masks = lane_masks()
    first, last = slice(0, 128), slice(128, 192)
    text_dc = low(nt(text_g_low[...], side(w, 1728, 192, 3)))
    queries, keys, values, probs, outer = [], [], [], [], []
    for p in range(pairs):
        rows = rows_of(p, SLOTS)
        queries += [both_heads(text_q[0, rows, first], masks), text_q[0, rows, last]]
        keys += [text_k[0, rows, first], text_k[0, rows, last]]
        values += [text_v[0, rows, first], text_v[0, rows, last]]
        probs += [text_probs[0, p, 0:256, :], text_probs[0, p, 256:384, :]]
        outer += [both_heads(text_dc[rows, first], masks), text_dc[rows, last]]
    grad_q, grad_k, grad_v = attend_back(queries, keys, values, probs, outer, SELF_HEAD**-0.5)
    size = text_g.shape[0]
    for p in range(pairs):
        rows = rows_of(p, SLOTS)
        text_d[0, rows, first] = one_tile(grad_q[2 * p], masks)
        text_d[0, rows, last] = grad_q[2 * p + 1]
        for n, grad in ((1, grad_k), (2, grad_v)):
            text_d[n, rows, first] = grad[2 * p]
            text_d[n, rows, last] = grad[2 * p + 1]

    image_dc = low(nt(image_g_low[...], side(w, 5376, 256, 4)))
    units = [(p, h) for p in range(pairs) for h in range(2)]

    def image_part(at):
        return [image_kept[0, rows_of(p, PADDED), at + h * HEAD : at + (h + 1) * HEAD] for p, h in units]

    outer = [image_dc[rows_of(p, PADDED), h * HEAD : (h + 1) * HEAD] for p, h in units]
    given = attend_back(
        image_part(0), image_part(256), image_part(512), [image_probs[0, i] for i in range(len(units))], outer, HEAD**-0.5
    )
    for n in range(3):
        for i, (p, h) in enumerate(units):
            image_d[rows_of(p, PADDED), n * 256 + h * HEAD : n * 256 + (h + 1) * HEAD] = given[n][i]

    gained = text_sum[...]
    for n in range(3):
        wide = jnp.concatenate([w[b * 576 + n * 192 : b * 576 + (n + 1) * 192, :] for b in range(3)], axis=1)
        gained = gained + nn(text_d[n], wide)
    text_sum[...] = gained
    image_sum[...] += nt(image_d[...], side(w, 2304, 1024, 3))

    slot = found.at[step]
    slot[0:size, 0:128] = text_d[0, :, first]
    slot[0:size, 128:256] = text_d[1, :, first]
    slot[size : 2 * size, 0:128] = text_d[2, :, first]
    slot[size : 2 * size, 128:256] = text_c[0, :, first]
    slot[2 * size : 3 * size, 0:128] = jnp.concatenate([text_d[0, :, last], text_d[1, :, last]], axis=1)
    slot[2 * size : 3 * size, 128:256] = jnp.concatenate([text_d[2, :, last], text_c[0, :, last]], axis=1)
    leave_blocks(slot, 3 * size, image_d[...])
    leave_blocks(slot, 3 * size + 3 * image_g.shape[0], image_kept[0, :, 768:1024])
    send_quarter(step, copies)

    @pl.when(step == QUARTERS - 1)
    def finish():
        leave_norm(1, text_sum, image_sum, text_pre, image_pre, text_gain, image_gain, text_n, image_n, text_vec, image_vec)
        rounded_copy.wait()
        for transfer in copies:
            transfer.wait()
        weight_grad(True, dp, (size, image_g.shape[0]), (rounded, rounded_near), found, near, weights, outs, flips, out_sems)


def leave_norm(norm, text_sum, image_sum, text_pre, image_pre, text_gain, image_gain, text_n, image_n, text_vec, image_vec):
    for total, pre, gain, out, vec in (
        (text_sum, text_pre, text_gain, text_n, text_vec),
        (image_sum, image_pre, image_gain, image_n, image_vec),
    ):
        unit, scale = normed(pre[...])
        out[...] = norm_back(unit, scale, gain[0, norm : norm + 1, :].astype(F32), total[...], vec)


def mlp_back(pairs, dp, text_g, image_g, text_one, image_one, text_pre, image_pre, text_gain, image_gain, *refs):
    text_activ, text_slope, image_activ, image_slope = refs[:4]
    parts = refs[4:9]
    text_n, image_n, next_low, text_vec, image_vec = refs[9:14]
    outs = refs[14:17]
    weights, found, text_sum, image_sum, text_g_low, image_g_low, near, rounded_near = refs[17:25]
    flips, (rounded, text_d, sems, out_sems, send_sems, recv_sems) = refs[25:29], refs[29:]
    step = pl.program_id(0)
    fetch(step, BACKWARD, *parts, weights, sems)
    size, image_size = text_g.shape[0], image_g.shape[0]
    core = partners()[0]
    copy = sender(send_sems, recv_sems)
    rounded_copy = copy(2, rounded, rounded_near, core)
    copies = [copy(n, found.at[n], near.at[n], core) for n in range(2)]

    @pl.when(step == 0)
    def begin():
        text_sum[...] = text_g[...]
        image_sum[...] = image_g[...]
        text_g_low[...] = low(text_g[...])
        image_g_low[...] = low(image_g[...])
        leave_blocks(rounded, 0, text_one[...])
        leave_blocks(rounded, 3 * size, text_g_low[...])
        leave_blocks(rounded, 6 * size, image_one[...])
        leave_blocks(rounded, 6 * size + 4 * image_size, image_g_low[...])
        greet(core)
        rounded_copy.start()

    w = weights.at[step]
    slot = found.at[step]
    wide = side(w, 2304, 768, 3)
    for b in range(3):
        columns = slice(b * 256, (b + 1) * 256)
        back = nt(text_g_low[...], wide[columns])
        text_d[:, columns] = low(back * text_slope[0, :, columns].astype(F32))
    text_sum[...] += nt(text_d[...], side(w, 0, 768, 3))
    image_d = low(nt(image_g_low[...], side(w, 5632, 256, 4)) * image_slope[0].astype(F32))
    image_sum[...] += nt(image_d, w[4608:5632, :])
    leave_blocks(slot, 0, text_d[...])
    leave_blocks(slot, 3 * size, text_activ[0])
    leave_blocks(slot, 6 * size, image_d)
    leave_blocks(slot, 6 * size + image_size, image_activ[0])
    send_quarter(step, copies)

    @pl.when(step == QUARTERS - 1)
    def finish():
        leave_norm(0, text_sum, image_sum, text_pre, image_pre, text_gain, image_gain, text_n, image_n, text_vec, image_vec)
        leave_blocks(next_low, 0, low(text_n[...]))
        leave_blocks(next_low, 3 * size, low(image_n[...]))
        rounded_copy.wait()
        for transfer in copies:
            transfer.wait()
        weight_grad(False, dp, (size, image_size), (rounded, rounded_near), found, near, weights, outs, flips, out_sems)


def weight_grad(is_self, dp, sizes, rounded, found, near, spare, outs, flips, out_sems):
    text_flip, text_g_flip, image_flip, image_g_flip = flips
    to_send, kept, to_z, by_image = (spare.at[n] for n in range(QUARTERS))
    size, image_size = sizes
    x = lax.axis_index("stream")
    for at in range(2):
        for b in range(3):
            text_flip[rows_of(b, BLOCK), rows_of(at, size)] = rounded[at][rows_of(b, size), :].T
            text_g_flip[rows_of(b, BLOCK), rows_of(at, size)] = rounded[at][rows_of(3 + b, size), :].T
        for b in range(8):
            start = 6 * size + b * image_size
            flip = image_g_flip if b > 3 else image_flip
            flip[rows_of(b % 4, BLOCK), rows_of(at, image_size)] = rounded[at][start : start + image_size, :].T

    text_depth, image_depth = DT // (2 * dp), DV // (2 * dp)
    padded = -(-text_depth // 16) * 16
    lane = lax.broadcasted_iota(jnp.int32, (1, HEAD), 1) < SELF_HEAD
    top = 3 * padded if is_self else 5 * padded
    below = 2 * image_depth if is_self else 2 * image_depth + padded
    leaving = []

    def leave(source, target, first=0):
        leaving.append(pltpu.make_async_copy(source.at[pl.ds(first, target.shape[0])], target, out_sems.at[len(leaving)]))
        leaving[-1].start()

    for slot in (1, 0):

        def block(start, rows):
            return jnp.concatenate([found[2 + slot, start : start + rows, :], near[slot, start : start + rows, :]], axis=0)

        def text_block(b):
            return block(b * size, size)

        def image_block(b, text_blocks):
            return block(text_blocks * size + b * image_size, image_size)

        def write(row, depth, value):
            for apart in range(2):
                ref, at = ((to_send if slot else kept), apart) if is_self else ((to_send if apart else kept), slot)
                for z in range(dp):
                    to = (at * dp + z) * top + row
                    ref[to : to + depth, :] = low(value[apart][z * depth : (z + 1) * depth])

        def bottom(row, depth, value):
            for apart in range(2):
                for z in range(dp):
                    to = (z * 4 + 2 * slot + apart) * below + row
                    to_z[to : to + depth, :] = low(value[apart][z * depth : (z + 1) * depth])

        if is_self:
            one, two, three = text_block(0), text_block(1), text_block(2)
            write(0, text_depth, halves(text_flip, one, x))
            pairs = zip(halves(text_flip, two[:, :HEAD], x), halves(text_g_flip, two[:, HEAD:], x))
            write(padded, text_depth, [jnp.concatenate(pair, axis=1) for pair in pairs])
            pairs = zip(halves(text_flip, three, x), halves(text_g_flip, three[:, HEAD:], x))
            mixed = [jnp.concatenate([a[:, :HEAD], jnp.where(lane, a[:, HEAD:], b)], axis=1) for a, b in pairs]
            write(2 * padded, text_depth, mixed)
            for b in range(2):
                for apart, value in enumerate(halves(image_flip, image_block(b, 3), x)):
                    for z in range(dp):
                        to = (((2 * (1 - apart) + slot) * dp + z) * 2 + b) * image_depth
                        by_image[to : to + image_depth, :] = low(value[z * image_depth : (z + 1) * image_depth])
            leave(*((to_send, outs[0]) if slot else (kept, outs[1])))
            for b, flip in enumerate((image_flip, image_g_flip)):
                bottom(b * image_depth, image_depth, halves(flip, image_block(2 + b, 3), x))
        else:
            for b in range(5):
                write(b * padded, text_depth, halves(text_g_flip if b > 2 else text_flip, text_block(b), x))
            bottom(2 * image_depth, text_depth, halves(text_g_flip, text_block(5), x))
            for b, flip in enumerate((image_flip, image_g_flip)):
                bottom(b * image_depth, image_depth, halves(flip, image_block(b, 6), x))
    if not is_self:
        leave(to_send, outs[0])
        leave(kept, outs[1])
    leave(to_z, outs[2])
    for number, out in enumerate(outs[3:]):
        leave(by_image, out, number * out.shape[0])
    for copy in leaving:
        copy.wait()


ANY = pl.BlockSpec(memory_space=pl.ANY)
SCALARS = pl.BlockSpec(memory_space=pltpu.SMEM)


def whole(array, buffers=None):
    zeros = (0,) * len(array.shape)
    mode = {} if buffers is None else {"pipeline_mode": pl.Buffered(buffers)}
    return pl.BlockSpec(array.shape, lambda *s: zeros, **mode)


def quarter(array, order):
    tail = (0,) * (len(array.shape) - 1)
    if order is FORWARD:
        return pl.BlockSpec((1,) + array.shape[1:], lambda s: (s,) + tail)
    return pl.BlockSpec((1,) + array.shape[1:], lambda s: (lax.rem(2 * s + 1 - lax.div(s, 2), 4),) + tail)


def shape(*dims, of=BF):
    return jax.ShapeDtypeStruct(dims, of)


def run(kernel, order, operands, outs, scratch, us, meeting=None):
    def spec(kind, array, given=False):
        if kind == "w" and given and order:
            return whole(array, 1)
        return {"s": lambda: SCALARS, "w": lambda: whole(array), "q": lambda: quarter(array, order), "a": lambda: ANY}[kind]()

    return pl.pallas_call(
        kernel,
        grid=(QUARTERS,) if order else (1,),
        in_specs=[spec(*entry, given=True) for entry in operands],
        out_specs=[spec(*entry) for entry in outs],
        out_shape=[array for unused, array in outs],
        scratch_shapes=scratch,
        compiler_params=pltpu.CompilerParams(
            dimension_semantics=("arbitrary",),
            vmem_limit_bytes=60 * 2**20,
            collective_id=meeting,
            has_side_effects=meeting is not None,
        ),
        cost_estimate=pl.CostEstimate(flops=int(us * 1.1e9), bytes_accessed=1024, transcendentals=0),
    )(*[array for unused, array in operands])


def swap(value, axis, apart):
    return lax.ppermute(value, axis, [(i, i ^ apart) for i in range(lax.axis_size(axis))])


def after(value, *earlier):
    return lax.optimization_barrier((value,) + earlier)[0]


class Line:
    def __init__(self):
        self.last = ()

    def take(self, value):
        return after(value, *self.last)

    def leave(self, *values):
        self.last = values


def add(left, right):
    return low(left.astype(F32) + right.astype(F32))


def fold_last(total):
    return lax.psum_scatter(total, "dp", scatter_dimension=0, tiled=True)[0]


def s(value):
    return ("s", value)


def w(value):
    return ("w", value)


def q(value):
    return ("q", value)


def a(value):
    return ("a", value)


def local(
    text_in,
    image_in,
    lengths,
    text_cot,
    image_cot,
    text_cross_q,
    text_cross_kv,
    text_cross_out,
    text_up,
    text_down,
    text_self_qkv,
    text_self_out,
    text_gain,
    text_bias,
    image_cross_q,
    image_cross_kv,
    image_cross_out,
    image_up,
    image_down,
    image_self_qkv,
    image_self_out,
    image_gain,
    image_bias,
):
    dp = lax.axis_size("dp")
    places = 2 * dp
    x_at = lax.axis_index("stream")
    t_at = lax.axis_index("tensor")
    size = text_in.shape[0]
    pairs = size // SLOTS
    image_size = pairs * PADDED
    units = 2 * pairs
    ids = jnp.stack([x_at, x_at * dp + lax.axis_index("dp")] + [(t_at ^ j) * pairs for j in range(QUARTERS)]).astype(jnp.int32)

    def leave(rows):
        return swap(rows, "stream", 1).astype(F32)

    line = Line()
    mlp_own, mlp_first, mlp_mine = pack([text_up[0], text_down[0], image_up[0], image_down[0]], places, 5120, ids)
    mlp_share = swap(mlp_mine, "tensor", 2)
    self_own, self_first, self_mine = pack(
        [
            text_self_qkv[0].transpose(1, 2, 0).reshape(-1, DT),
            text_self_out[0],
            image_self_qkv[0].reshape(DV, -1),
            image_self_out[0],
        ],
        places,
        4096,
        after(ids, mlp_own),
    )
    cross_w = (
        text_cross_q[0],
        image_cross_kv[0].reshape(DT, -1),
        text_cross_kv[0].reshape(DV, -1),
        image_cross_q[0],
        text_cross_out[0],
        image_cross_out[0],
    )
    line.leave(self_own)
    mlp_share = line.take(mlp_share)
    line.leave(mlp_share, cross_w[1], cross_w[2])
    self_share = line.take(swap(self_mine, "tensor", 2))
    line.leave(self_share)
    mlp_rest = lax.all_gather(mlp_share, ("stream", "dp"), axis=0, tiled=True)
    self_rest = lax.all_gather(self_share, ("stream", "dp"), axis=0, tiled=True)
    self_near = swap(self_own, "tensor", 1)
    mlp_near_w = swap(mlp_own, "tensor", 1)
    image_cot_here = swap(image_cot, "stream", 1)
    mlp_far = swap(mlp_first, "tensor", 2)

    text_wide, image_wide = shape(size, DT, of=F32), shape(image_size, DV, of=F32)
    text_half = shape(size, DT // 2, of=F32)
    text_f32, image_f32 = pltpu.VMEM((size, DT), F32), pltpu.VMEM((image_size, DV), F32)
    text_bf, image_bf = pltpu.VMEM((size, DT), BF), pltpu.VMEM((image_size, DV), BF)
    in_sems, out_sems = pltpu.SemaphoreType.DMA((5,)), pltpu.SemaphoreType.DMA((5,))
    text_affine = [w(text_gain), w(text_bias)]
    image_affine = [w(image_gain), w(image_bias)]
    vector_outs = [w(shape(2, DT, of=F32)), w(shape(2, DV, of=F32))]
    part_rows = 3 * size + 4 * image_size

    def buffer(weights):
        return pltpu.VMEM((QUARTERS,) + weights.shape, BF)

    in_four = [
        (QUARTERS, size, DT),
        (QUARTERS, image_size, DV),
        (QUARTERS, size, 1024),
        (QUARTERS, image_size, 1024),
        (QUARTERS, units, SLOTS, PADDED),
        (QUARTERS, units, PADDED, SLOTS),
    ]

    def links(count):
        return [pltpu.SemaphoreType.DMA((count,)), pltpu.SemaphoreType.DMA((count,))]

    text_pre1, image_pre1, texts, images, *cross_kept = run(
        functools.partial(cross_forward, pairs),
        None,
        [s(lengths), w(line.take(text_in)), w(image_in)] + [w(m) for m in cross_w],
        [w(text_wide), w(image_wide)] + [a(shape(*dims)) for dims in in_four],
        [pltpu.VMEM(dims, BF) for dims in in_four]
        + [pltpu.VMEM((QUARTERS, part_rows, BLOCK), BF), pltpu.VMEM((part_rows, BLOCK), BF), pltpu.VMEM((3, part_rows, BLOCK), BF)]
        + [image_bf]
        + links(10)
        + [pltpu.SemaphoreType.DMA((6,))],
        70,
        1,
    )
    line.leave(text_pre1, image_cot_here)
    mlp_far, mlp_rest = line.take((mlp_far, mlp_rest))
    self_far = swap(after(self_first, mlp_far), "tensor", 2)
    (
        text_one,
        image_one,
        text_pre2,
        image_pre2,
        text_activ,
        text_slope,
        image_activ,
        image_slope,
        mlp_corner,
    ) = run(
        functools.partial(mlp_forward, pairs),
        FORWARD,
        [w(text_pre1), w(image_pre1)] + text_affine + image_affine + [a(m) for m in (mlp_own, mlp_near_w, mlp_far, mlp_rest)],
        [
            w(shape(size, DT)),
            w(shape(image_size, DV)),
            w(text_wide),
            w(image_wide),
            q(shape(QUARTERS, size, 768)),
            q(shape(QUARTERS, size, 768)),
            q(shape(QUARTERS, image_size, 256)),
            q(shape(QUARTERS, image_size, 256)),
            a(mlp_own),
        ],
        [buffer(mlp_own), in_sems] + links(2),
        1,
        7,
    )
    mlp_w = mlp_own, mlp_near_w, mlp_far, mlp_rest, mlp_corner
    line.leave(text_pre2)
    self_far, self_rest = line.take((self_far, self_rest))
    (
        text_left,
        text_right,
        image_out,
        text_n3,
        image_n3,
        text_vec3,
        image_vec3,
        self_rounded,
        self_q,
        self_k,
        self_v,
        self_c,
        self_probs,
        self_kept,
        self_image_probs,
        self_corner,
    ) = run(
        functools.partial(self_forward, pairs),
        FORWARD,
        [s(ids), s(lengths), w(text_pre2), w(image_pre2)]
        + text_affine
        + image_affine
        + [w(text_cot), w(image_cot_here)]
        + [a(m) for m in (self_own, self_near, self_far, self_rest)],
        [w(text_half), w(text_half), w(image_cot), w(text_wide), w(image_wide)]
        + vector_outs
        + [
            w(shape(2 * part_rows, BLOCK)),
            q(shape(QUARTERS, size, 192)),
            q(shape(QUARTERS, size, 192)),
            q(shape(QUARTERS, size, 192)),
            q(shape(QUARTERS, size, 192)),
            q(shape(QUARTERS, pairs, 384, SLOTS)),
            q(shape(QUARTERS, image_size, 1024)),
            q(shape(QUARTERS, units, PADDED, PADDED)),
            a(self_own),
        ],
        [buffer(self_own), text_f32, image_f32, text_bf, image_bf, in_sems] + links(2),
        19,
        8,
    )
    self_w = self_own, self_near, self_far, self_rest, self_corner
    image_out = swap(image_out, "stream", 1)

    text_depth, image_depth = DT // places, DV // places
    padded = -(-text_depth // 16) * 16

    def back_scratch(weights, rows):
        return [
            buffer(weights[0]),
            pltpu.VMEM((QUARTERS, rows, BLOCK), BF),
            text_f32,
            image_f32,
            text_bf,
            image_bf,
            pltpu.VMEM((2, rows, BLOCK), BF),
            pltpu.VMEM((2 * part_rows, BLOCK), BF),
            pltpu.VMEM((DT, 2 * size), BF),
            pltpu.VMEM((DT, 2 * size), BF),
            pltpu.VMEM((DV, 2 * image_size), BF),
            pltpu.VMEM((DV, 2 * image_size), BF),
        ]

    def grad_shapes(is_self):
        first = (2, dp, (3 if is_self else 5) * padded, BLOCK)
        last = (dp, 4 * (2 * image_depth + (0 if is_self else padded)), BLOCK)
        return [first, first, last] + [(2, dp, 2 * image_depth, BLOCK)] * (2 if is_self else 0)

    def grad_outs(is_self):
        return [a(shape(math.prod(dims[:-1]), BLOCK)) for dims in grad_shapes(is_self)]

    def grad_arrays(is_self, *found):
        return [out.reshape(dims) for out, dims in zip(found, grad_shapes(is_self))]

    self_rows = 3 * size + 4 * image_size
    text_n2, image_n2, text_vec2, image_vec2, *self_found = run(
        functools.partial(self_back, pairs, dp),
        BACKWARD,
        [
            w(text_n3),
            w(image_n3),
            w(text_pre2),
            w(image_pre2),
            w(text_gain),
            w(image_gain),
            w(self_rounded),
            q(self_q),
            q(self_k),
            q(self_v),
            q(self_c),
            q(self_probs),
            q(self_kept),
            q(self_image_probs),
        ]
        + [a(m) for m in self_w],
        [w(text_wide), w(image_wide)] + vector_outs + grad_outs(True),
        back_scratch(self_w, self_rows)
        + [pltpu.VMEM((3, size, 192), BF), pltpu.VMEM((image_size, 768), BF), in_sems, out_sems]
        + links(3),
        32,
        2,
    )
    to_y, self_top, to_z, to_x, self_side = grad_arrays(True, *self_found)
    self_by_y = swap(to_y, "tensor", 2)
    self_by_x = swap(to_x, "stream", 1)
    self_bottom = fold_last(to_z)
    line.leave(self_top)
    mlp_rows = 6 * size + 2 * image_size
    text_n1, image_n1, grad_low, text_vec1, image_vec1, *mlp_found = run(
        functools.partial(mlp_back, pairs, dp),
        BACKWARD,
        [
            w(text_n2),
            w(image_n2),
            w(text_one),
            w(image_one),
            w(text_pre1),
            w(image_pre1),
            w(line.take(text_gain)),
            w(image_gain),
            q(text_activ),
            q(text_slope),
            q(image_activ),
            q(image_slope),
        ]
        + [a(m) for m in mlp_w],
        [w(text_wide), w(image_wide), w(shape(part_rows, BLOCK))]
        + vector_outs
        + grad_outs(False),
        back_scratch(mlp_w, mlp_rows)
        + [pltpu.VMEM((2 * part_rows, BLOCK), BF), text_bf, in_sems, out_sems]
        + links(3),
        28,
        3,
    )
    line.leave(grad_low)
    to_x, mlp_top, to_z = grad_arrays(False, *mlp_found)
    self_top, self_by_y, self_side, self_by_x, to_x, to_z, image_out = after(
        (self_top, self_by_y, self_side, self_by_x, to_x, to_z, image_out), mlp_top
    )
    mlp_by_x = swap(to_x, "stream", 1)
    mlp_bottom = fold_last(to_z)
    self_top, to_x = add(self_top[0], self_by_y[0]), add(self_top[1], self_by_y[1])
    self_then_x = swap(to_x, "stream", 1)
    self_side, to_y = add(self_side[0], self_by_x[0]), add(self_side[1], self_by_x[1])
    self_then_y = swap(to_y, "tensor", 2)
    line.leave(self_top, to_x, self_side, to_y)
    d_dims = [(QUARTERS, part_rows, BLOCK), (QUARTERS, size, 768), (QUARTERS, image_size, 768)]
    grads, text_d, image_d, own_sum, total, vectors = run(
        functools.partial(cross_back, pairs),
        None,
        [w(line.take(grad_low))]
        + [w(v) for v in (text_vec1, text_vec2, text_vec3, image_vec1, image_vec2, image_vec3)]
        + [a(k) for k in cross_kept] + [w(m) for m in cross_w],
        [a(shape(*dims)) for dims in d_dims]
        + [w(shape(part_rows, BLOCK, of=F32)), w(shape(part_rows, BLOCK)), w(shape(16, DV, of=F32))],
        [pltpu.VMEM(dims, BF) for dims in d_dims]
        + [pltpu.VMEM((QUARTERS, part_rows, BLOCK), BF), pltpu.VMEM((2, part_rows, BLOCK), BF), pltpu.VMEM((2, 16, DV), F32)]
        + [pltpu.VMEM((16, DV), F32)]
        + [pltpu.VMEM(k.shape, BF) for k in cross_kept]
        + links(7)
        + [pltpu.SemaphoreType.DMA((3,)), pltpu.SemaphoreType.DMA((QUARTERS, 4))],
        48,
        4,
    )
    line.leave(total)
    text_only, image_only = 4 * padded + 16, 4 * image_depth
    last_inputs = [
        self_top,
        self_side,
        self_then_x,
        self_then_y,
        texts,
        grads,
        text_d,
        cross_kept[0],
        images,
        image_d,
        cross_kept[1],
        own_sum,
        text_n1,
        image_n1,
    ]
    self_all = (dp, 3 * padded + 2 * image_depth, BLOCK)
    last_scratch = [pltpu.VMEM(self_all, BF)] * 2 + [pltpu.VMEM(m.shape, m.dtype) for m in last_inputs[4:]]
    last_scratch[5], last_scratch[8] = pltpu.VMEM((QUARTERS, size, BLOCK), BF), pltpu.VMEM((QUARTERS, image_size, BLOCK), BF)
    grad_left, grad_right, image_grad, cross_text, image_keep, image_send, self_top = run(
        cross_last,
        None,
        [w(line.take(total)), w(vectors)] + [a(m) for m in last_inputs],
        [
            w(text_half),
            w(text_half),
            w(image_cot),
            w(shape(dp, text_only, BLOCK)),
            a(shape(dp, image_only, BLOCK)),
            a(shape(dp, image_only, BLOCK)),
            w(shape(*self_all[1:])),
        ],
        last_scratch
        + [
            pltpu.VMEM((part_rows, BLOCK), BF),
            pltpu.VMEM((dp, image_only, BLOCK), BF),
            pltpu.VMEM((dp, image_only, BLOCK), BF),
            pltpu.VMEM((dp, text_only, BLOCK), BF),
            pltpu.VMEM((dp, text_only, BLOCK), BF),
            pltpu.VMEM((dp - 1, *self_all[1:]), BF),
            pltpu.VMEM((DT, QUARTERS * size), BF),
            pltpu.VMEM((DT, QUARTERS * size), BF),
            pltpu.VMEM((DV, QUARTERS * image_size), BF),
            pltpu.VMEM((DV, QUARTERS * image_size), BF),
        ]
        + links(1 + dp)
        + [pltpu.SemaphoreType.DMA((14,)), pltpu.SemaphoreType.DMA((2,))],
        2,
        5,
    )
    line.leave(grad_left)
    mlp_top, mlp_by_x, self_bottom, mlp_bottom, cross_text, image_send = line.take(
        (mlp_top, mlp_by_x, self_bottom, mlp_bottom, cross_text, image_send)
    )
    cross_text = fold_last(cross_text)
    image_send = swap(image_send, "stream", 1)
    mlp_top, to_y = add(mlp_top[0], mlp_by_x[0]), add(mlp_top[1], mlp_by_x[1])
    mlp_then_y = swap(to_y, "tensor", 2)
    line.leave(mlp_top, to_y)
    self_bottom = line.take(self_bottom).reshape(2, 2, 2 * image_depth, BLOCK)
    self_bottom_x = swap(self_bottom[:, 1], "stream", 1)
    cross_image = add(image_keep, line.take(image_send))
    line.leave(cross_image)
    cross_image = fold_last(cross_image)
    self_bottom = add(self_bottom[:, 0], line.take(self_bottom_x))
    self_bottom_y = swap(self_bottom[1], "tensor", 2)
    mlp_bottom = line.take(mlp_bottom).reshape(2, 2, 2 * image_depth + padded, BLOCK)
    mlp_bottom_x = swap(mlp_bottom[:, 1], "stream", 1)
    mlp_top = add(mlp_top, line.take(mlp_then_y))
    line.leave(mlp_top)
    mlp_top = fold_last(mlp_top)
    mlp_bottom = add(mlp_bottom[:, 0], line.take(mlp_bottom_x))
    mlp_bottom = add(mlp_bottom[0], swap(mlp_bottom[1], "tensor", 2))
    self_bottom = add(self_bottom[0], self_bottom_y)
    self_grads = jnp.concatenate([self_top, self_bottom], axis=0)
    image_grad = leave(image_grad)

    def pick(packed, first, count, depth, stride):
        rows = [packed[first + b * stride : first + b * stride + depth] for b in range(count)]
        return jnp.concatenate(rows, axis=1).astype(F32)

    def text_pick(packed, first, count):
        return pick(packed, first, count, text_depth, padded)

    def image_pick(packed, first, count):
        return pick(packed, first, count, image_depth, image_depth)

    sums = cross_text[4 * padded :].astype(F32)
    text_vectors, image_vectors = sums[:6, :text_depth], sums[6:12, :image_depth]

    self_text = text_pick(self_grads, 0, 3)

    def heads(at):
        return jnp.concatenate([self_text[:, at * 128 : (at + 1) * 128], self_text[:, 512 + at * 64 : 576 + at * 64]], axis=1)

    below = 3 * padded
    return (
        jnp.concatenate([text_left, text_right], axis=1),
        image_out.astype(F32),
        jnp.concatenate([grad_left, grad_right], axis=1),
        image_grad,
        text_pick(cross_text, 0, 1)[None],
        image_pick(cross_image, 0, 2).reshape(1, image_depth, 2, 256),
        text_pick(cross_text, 3 * padded, 1).T[None],
        text_pick(mlp_top, 0, 3)[None],
        jnp.concatenate([text_pick(mlp_top, below, 2), text_pick(mlp_bottom, 2 * image_depth, 1)], axis=1).T[None],
        jnp.stack([heads(n) for n in range(3)], axis=1)[None],
        heads(3).T[None],
        text_vectors[0::2][None],
        text_vectors[1::2][None],
        image_pick(cross_image, 2 * image_depth, 1)[None],
        text_pick(cross_text, padded, 2).reshape(1, text_depth, 2, 256),
        image_pick(cross_image, 3 * image_depth, 1).T[None],
        image_pick(mlp_bottom, 0, 1)[None],
        image_pick(mlp_bottom, image_depth, 1).T[None],
        image_pick(self_grads, below, 3).reshape(1, image_depth, 3, 256),
        image_pick(self_grads, below + 3 * image_depth, 1).T[None],
        image_vectors[0::2][None],
        image_vectors[1::2][None],
    )


def solution(mesh):
    rows = P(("stream", "dp", "tensor"), None)
    wide_in = P(None, None, "tensor")
    group_in = P(None, None, None, "tensor")
    wide_out = P(None, "tensor", None)
    grad_in = P(None, ("stream", "dp"), "tensor")
    grad_group = P(None, ("stream", "dp"), None, "tensor")
    grad_out = P(None, "tensor", ("stream", "dp"))
    vector = P(None, None, ("stream", "dp"))
    weights = (wide_in, group_in, wide_out, wide_in, wide_out, group_in, wide_out, P(), P())
    grads = (grad_in, grad_group, grad_out, grad_in, grad_out, grad_group, grad_out, vector, vector)
    return jax.shard_map(
        local,
        mesh=mesh,
        in_specs=(rows, rows, P(("stream", "dp")), rows, rows) + weights + weights,
        out_specs=(rows, rows, rows, rows) + grads + grads,
        check_vma=False,
    )
```

```python
import functools
import math

import jax
import jax.numpy as jnp
from jax import lax
from jax.experimental import pallas as pl
from jax.experimental.pallas import tpu as pltpu
from jax.sharding import PartitionSpec as P

DT = 768
DV = 1024
HEAD = 128
SELF_HEAD = 64
SLOTS = 128
REGIONS = 37
PADDED = 48
QUARTERS = 4
BLOCK = 256

norm_eps = 1e-05
masked_score = -1e30

BF = jnp.bfloat16
F32 = jnp.float32
FORWARD = (0, 1, 2, 3)
BACKWARD = (1, 3, 0, 2)


def nn(left, right):
    return lax.dot_general(left, right, (((1,), (0,)), ((), ())), preferred_element_type=F32)


def nt(left, right):
    return lax.dot_general(left, right, (((1,), (1,)), ((), ())), preferred_element_type=F32)


def tn(left, right):
    return lax.dot_general(left, right, (((0,), (0,)), ((), ())), preferred_element_type=F32)


def low(value):
    return value.astype(BF)


def normed(inputs):
    centered = inputs - jnp.mean(inputs, axis=-1, keepdims=True)
    scale = lax.rsqrt(jnp.mean(centered * centered, axis=-1, keepdims=True) + norm_eps)
    return centered * scale, scale


def norm_back(unit, scale, gain, grad, vec):
    vec[0:1] = jnp.sum(grad * unit, axis=0, keepdims=True)
    vec[1:2] = jnp.sum(grad, axis=0, keepdims=True)
    inner = grad * gain
    shift = jnp.mean(inner, axis=-1, keepdims=True)
    slope = jnp.mean(inner * unit, axis=-1, keepdims=True)
    return scale * (inner - shift - unit * slope)


def softmax_all(scores):
    tops = [jnp.max(s, axis=-1, keepdims=True) for s in scores]
    powers = [jnp.exp(s - t) for s, t in zip(scores, tops)]
    sums = [jnp.sum(e, axis=-1, keepdims=True) for e in powers]
    return [low(e / total) for e, total in zip(powers, sums)]


def attend(queries, keys, values, scale, masks):
    scores = [nt(q, k) * scale for q, k in zip(queries, keys)]
    scores = [s if m is None else jnp.where(m, s, masked_score) for s, m in zip(scores, masks)]
    probs = softmax_all(scores)
    return probs, [nn(p, v) for p, v in zip(probs, values)]


def attend_back(queries, keys, values, probs, grads, scale):
    grad_probs = [nt(g, v) for g, v in zip(grads, values)]
    grad_values = [low(tn(p, g)) for p, g in zip(probs, grads)]
    wide = [p.astype(F32) for p in probs]
    inner = [jnp.sum(p * g, axis=-1, keepdims=True) for p, g in zip(wide, grad_probs)]
    grad_scores = [low(p * (g - i)) for p, g, i in zip(wide, grad_probs, inner)]
    grad_queries = [low(nn(g, k) * scale) for g, k in zip(grad_scores, keys)]
    grad_keys = [low(tn(g, q) * scale) for g, q in zip(grad_scores, queries)]
    return grad_queries, grad_keys, grad_values


def side(ref, row, width, count):
    return jnp.concatenate([ref[row + b * width : row + (b + 1) * width, :] for b in range(count)], axis=1)


def rows_of(pair, size):
    return slice(pair * size, (pair + 1) * size)


def fetch(step, order, own, near, far, far_rest, corner, buffer, sems):
    slots = [order.index(quarter) for quarter in range(QUARTERS)]
    cut, rest = far.shape[0], far_rest.shape[0]
    copies = [
        (slots[0], pltpu.make_async_copy(own, buffer.at[slots[0]], sems.at[0])),
        (slots[1], pltpu.make_async_copy(near, buffer.at[slots[1]], sems.at[1])),
        (slots[2], pltpu.make_async_copy(far, buffer.at[slots[2], pl.ds(0, cut)], sems.at[2])),
        (slots[2], pltpu.make_async_copy(far_rest, buffer.at[slots[2], pl.ds(cut, rest)], sems.at[3])),
    ]
    if corner is not None:
        copies.append((slots[3], pltpu.make_async_copy(corner, buffer.at[slots[3]], sems.at[4])))
    copies.sort(key=lambda entry: entry[0])

    @pl.when(step == 0)
    def begin():
        for slot, copy in copies:
            if slot == 0:
                copy.start()

    for at in range(QUARTERS):

        @pl.when(step == at)
        def arrive():
            for slot, copy in copies:
                if slot == at:
                    copy.wait()

    @pl.when(step == 0)
    def others():
        for slot, copy in copies:
            if slot > 0:
                copy.start()


def fetch_round(step, own, near, far, far_rest, corner, buffer, sems, send_sems, recv_sems):
    core = partners()[0]
    copy = sender(send_sems, recv_sems)
    cut, rest = far.shape[0], far_rest.shape[0]
    over = copy(0, far, buffer.at[3, pl.ds(0, cut)], core), copy(1, far_rest, buffer.at[3, pl.ds(cut, rest)], core)
    leaving = pltpu.make_async_copy(buffer.at[3], corner, sems.at[4])
    fetch(step, FORWARD, own, near, far, far_rest, None, buffer, sems)

    @pl.when(step == 0)
    def begin():
        greet(core)
        for transfer in over:
            transfer.start()

    @pl.when(step == 3)
    def last():
        for transfer in over:
            transfer.wait()
        leaving.start()

    return leaving


def spacing(pairs):
    rows, columns = pairs * PADDED, pairs * REGIONS
    row = lax.broadcasted_iota(jnp.int32, (rows, columns), 0)
    column = lax.broadcasted_iota(jnp.int32, (rows, columns), 1)
    chosen = jnp.zeros((rows, columns), F32)
    for p in range(pairs):
        inside = (column >= p * REGIONS) & (column < (p + 1) * REGIONS)
        chosen = jnp.where(inside & (row - p * PADDED == column - p * REGIONS), 1.0, chosen)
    return low(chosen)


def send_quarter(step, copies):
    for at, copy in enumerate(copies):

        @pl.when(step == at)
        def leave():
            copy.start()


def affine_row(gain, bias, norm):
    return gain[0, norm : norm + 1, :].astype(F32), bias[0, norm : norm + 1, :].astype(F32)


def leave_blocks(ref, row, value):
    size = value.shape[0]
    for b in range(value.shape[1] // BLOCK):
        ref[row + b * size : row + (b + 1) * size, :] = value[:, b * BLOCK : (b + 1) * BLOCK]


MESH = pl.DeviceIdType.MESH


def partners():
    t = lax.axis_index("tensor")
    return {"tensor": lax.bitwise_xor(t, 1)}, {"tensor": lax.bitwise_xor(t, 2)}, {"stream": lax.bitwise_xor(lax.axis_index("stream"), 1)}


def greet(*others):
    barrier = pltpu.get_barrier_semaphore()
    for other in others:
        pl.semaphore_signal(barrier, inc=1, device_id=other, device_id_type=MESH)
    pl.semaphore_wait(barrier, len(others))


def sender(send_sems, recv_sems):
    def copy(number, source, target, to):
        return pltpu.make_async_remote_copy(
            src_ref=source,
            dst_ref=target,
            send_sem=send_sems.at[number],
            recv_sem=recv_sems.at[number],
            device_id=to,
            device_id_type=MESH,
        )

    return copy


def pack(pieces, places, rest, ids):
    total = sum(m.size for m in pieces) // BLOCK
    cut, share = total - rest, rest // places

    def kernel(ids, *refs):
        sources, (own, first, mine) = refs[: len(pieces)], refs[len(pieces) :]
        row = 0
        for ref in sources:
            leave_blocks(own, row, ref[...])
            row += ref.size // BLOCK
        first[...] = own[0:cut, :]
        mine[...] = own[pl.ds(pl.multiple_of(cut + ids[1] * share, 16), share), :]

    return run(
        kernel,
        None,
        [s(ids)] + [w(m) for m in pieces],
        [w(shape(total, BLOCK)), w(shape(cut, BLOCK)), w(shape(share, BLOCK))],
        [],
        3,
    )


def cross_block(pairs, first, lengths, text, image, matrices, text_kept, image_kept, text_probs, image_probs, part):
    wq, wkv_text, wkv_image, wq_image, w_out, w_out_image = matrices
    text_low = text[...]
    image_low = image[...]
    text_kept[:, 0:256] = low(nn(text_low, wq[...]))
    text_kept[:, 256:768] = low(nn(text_low, wkv_text[...]))
    image_kept[:, 0:512] = low(nn(image_low, wkv_image[...]))
    image_kept[:, 512:768] = low(nn(image_low, wq_image[...]))

    image_mask = lax.broadcasted_iota(jnp.int32, (SLOTS, PADDED), 1) < REGIONS
    slots = lax.broadcasted_iota(jnp.int32, (PADDED, SLOTS), 1)
    units = [(p, h) for p in range(pairs) for h in range(2)]

    def text_part(at):
        return [text_kept[rows_of(p, SLOTS), at + h * HEAD : at + (h + 1) * HEAD] for p, h in units]

    def image_part(at):
        return [image_kept[rows_of(p, PADDED), at + h * HEAD : at + (h + 1) * HEAD] for p, h in units]

    scale = HEAD**-0.5
    probs, context = attend(text_part(0), image_part(0), image_part(256), scale, [image_mask] * len(units))
    for i, (p, h) in enumerate(units):
        text_probs[i] = probs[i]
        text_kept[rows_of(p, SLOTS), 768 + h * HEAD : 768 + (h + 1) * HEAD] = low(context[i])
    limits = [lengths[first + p] for p in range(pairs)]
    masks = [slots < limits[p] for p, h in units]
    probs, context = attend(image_part(512), text_part(256), text_part(512), scale, masks)
    for i, (p, h) in enumerate(units):
        image_probs[i] = probs[i]
        image_kept[rows_of(p, PADDED), 768 + h * HEAD : 768 + (h + 1) * HEAD] = low(context[i])
    leave_blocks(part, 0, low(nn(text_kept[:, 768:1024], w_out[...])))
    leave_blocks(part, 3 * text.shape[0], low(nn(image_kept[:, 768:1024], w_out_image[...])))


def cross_forward(pairs, lengths, text, image, *refs):
    matrices = refs[:6]
    text_pre, image_pre = refs[6:8]
    outs = refs[8:14]
    texts, images, text_kept, image_kept, text_probs, image_probs, parts, total, got, image_apart = refs[14:24]
    send_sems, recv_sems, out_sems = refs[24:]
    core, y, x = partners()
    copy = sender(send_sems, recv_sems)
    text_core = copy(0, text, texts.at[1], core)
    text_y = copy(1, text, texts.at[2], y)
    image_x = copy(2, image_apart, images.at[0], x)
    image_core = copy(3, images.at[0], images.at[1], core)
    image_y = copy(4, images.at[0], images.at[2], y)
    text_corner = copy(5, texts.at[2], texts.at[3], core)
    image_corner = copy(6, images.at[2], images.at[3], core)
    near_part = copy(7, parts.at[1], got.at[0], core)
    corner_part = copy(8, parts.at[3], got.at[1], core)
    far_part = copy(9, total, got.at[2], y)

    image_apart[...] = low(nn(spacing(pairs), image[...]))
    greet(core, y, x)
    image_x.start()
    text_y.start()
    text_core.start()
    texts[0] = text[...]
    image_x.wait()
    image_y.start()
    image_core.start()

    def block(j, unused):
        @pl.when(j == 1)
        def near():
            text_core.wait()
            image_core.wait()

        @pl.when(j == 2)
        def far():
            text_y.wait()
            text_corner.start()
            image_y.wait()
            image_corner.start()

        @pl.when(j == 3)
        def corner():
            text_corner.wait()
            image_corner.wait()

        cross_block(
            pairs,
            lax.bitwise_xor(lax.axis_index("tensor"), j) * pairs,
            lengths,
            texts.at[j],
            images.at[j],
            matrices,
            text_kept.at[j],
            image_kept.at[j],
            text_probs.at[j],
            image_probs.at[j],
            parts.at[j],
        )

        @pl.when(j == 1)
        def near_done():
            near_part.start()

        return unused

    lax.fori_loop(0, QUARTERS, block, 0)
    corner_part.start()
    leaving = [
        pltpu.make_async_copy(source, out, out_sems.at[i])
        for i, (source, out) in enumerate(
            zip((texts, images, text_kept, image_kept, text_probs, image_probs), outs)
        )
    ]
    for leave in leaving:
        leave.start()
    corner_part.wait()
    total[...] = add(parts[2], got[1])
    far_part.start()
    near_part.wait()
    size, image_size = text.shape[0], image_apart.shape[0]
    below = 3 * size

    def summed(row, depth, count, start):
        for ref in (parts.at[0], got.at[0]):
            start = start + side(ref, row, depth, count).astype(F32)
        return start

    text_pre[...] = summed(0, size, 3, text[...].astype(F32))
    image_pre[...] = summed(below, image_size, 4, images[0].astype(F32))
    far_part.wait()
    text_pre[...] += side(got.at[2], 0, size, 3).astype(F32)
    image_pre[...] += side(got.at[2], below, image_size, 4).astype(F32)
    for leave in leaving:
        leave.wait()


def cross_block_back(pairs, grad, matrices, text_kept, image_kept, text_probs, image_probs, text_d, image_d, part):
    wq, wkv_text, wkv_image, wq_image, w_out, w_out_image = matrices
    text_rows, image_rows = text_kept.shape[0], image_kept.shape[0]
    text_dc = low(nt(side(grad, 0, text_rows, 3), w_out[...]))
    image_dc = low(nt(side(grad, 3 * text_rows, image_rows, 4), w_out_image[...]))
    units = [(p, h) for p in range(pairs) for h in range(2)]

    def text_part(at):
        return [text_kept[rows_of(p, SLOTS), at + h * HEAD : at + (h + 1) * HEAD] for p, h in units]

    def image_part(at):
        return [image_kept[rows_of(p, PADDED), at + h * HEAD : at + (h + 1) * HEAD] for p, h in units]

    scale = HEAD**-0.5
    outer = [text_dc[rows_of(p, SLOTS), h * HEAD : (h + 1) * HEAD] for p, h in units]
    probs = [text_probs[i] for i in range(len(units))]
    found = attend_back(text_part(0), image_part(0), image_part(256), probs, outer, scale)
    for i, (p, h) in enumerate(units):
        text_d[rows_of(p, SLOTS), h * HEAD : (h + 1) * HEAD] = found[0][i]
        image_d[rows_of(p, PADDED), h * HEAD : (h + 1) * HEAD] = found[1][i]
        image_d[rows_of(p, PADDED), 256 + h * HEAD : 256 + (h + 1) * HEAD] = found[2][i]
    outer = [image_dc[rows_of(p, PADDED), h * HEAD : (h + 1) * HEAD] for p, h in units]
    probs = [image_probs[i] for i in range(len(units))]
    found = attend_back(image_part(512), text_part(256), text_part(512), probs, outer, scale)
    for i, (p, h) in enumerate(units):
        image_d[rows_of(p, PADDED), 512 + h * HEAD : 512 + (h + 1) * HEAD] = found[0][i]
        text_d[rows_of(p, SLOTS), 256 + h * HEAD : 256 + (h + 1) * HEAD] = found[1][i]
        text_d[rows_of(p, SLOTS), 512 + h * HEAD : 512 + (h + 1) * HEAD] = found[2][i]
    text_dx = nt(text_d[:, 0:256], wq[...]) + nt(text_d[:, 256:768], wkv_text[...])
    image_dx = nt(image_d[:, 0:512], wkv_image[...]) + nt(image_d[:, 512:768], wq_image[...])
    leave_blocks(part, 0, low(text_dx))
    leave_blocks(part, 3 * text_rows, low(image_dx))


def cross_back(pairs, grad, *refs):
    given, (text_kept, image_kept, text_probs, image_probs), matrices = refs[:6], refs[6:10], refs[10:16]
    grads_out, text_d_out, image_d_out, own_sum, total, vector_sum = refs[16:22]
    grads, text_d, image_d, parts, got, got_vectors, vectors, *kept = refs[22:-4]
    send_sems, recv_sems, out_sems, in_sems = refs[-4:]
    core, y, unused_x = partners()
    copy = sender(send_sems, recv_sems)
    loads = [
        [
            pltpu.make_async_copy(source.at[j], ref.at[j], in_sems.at[j, n])
            for n, (source, ref) in enumerate(zip((text_kept, image_kept, text_probs, image_probs), kept))
        ]
        for j in range(QUARTERS)
    ]
    text_kept, image_kept, text_probs, image_probs = kept
    to_core = copy(0, grad, grads.at[1], core)
    to_y = copy(1, grad, grads.at[2], y)
    corner = copy(2, grads.at[2], grads.at[3], core)
    near_part = copy(3, parts.at[1], got.at[0], core)
    corner_part = copy(4, parts.at[3], got.at[1], core)
    vectors_core = copy(5, vectors, got_vectors.at[0], core)
    vectors_y = copy(6, vector_sum, got_vectors.at[1], y)
    for load in loads[0]:
        load.start()
    vectors[...] = jnp.zeros_like(vectors)
    for n, vector in enumerate(given):
        vectors[2 * n : 2 * n + 2, 0 : vector.shape[1]] = vector[...]
    greet(core, y)
    vectors_core.start()
    to_y.start()
    to_core.start()
    for load in sum(loads[1:], []):
        load.start()
    grads[0] = grad[...]
    vectors_core.wait()
    vector_sum[...] = vectors[...] + got_vectors[0]
    vectors_y.start()

    def block(j, unused):
        @pl.when(j == 1)
        def near():
            to_core.wait()

        @pl.when(j == 2)
        def far():
            to_y.wait()
            corner.start()

        @pl.when(j == 3)
        def last():
            corner.wait()

        for at in range(QUARTERS):

            @pl.when(j == at)
            def loaded():
                for load in loads[at]:
                    load.wait()

        cross_block_back(
            pairs,
            grads.at[j],
            matrices,
            text_kept.at[j],
            image_kept.at[j],
            text_probs.at[j],
            image_probs.at[j],
            text_d.at[j],
            image_d.at[j],
            parts.at[j],
        )

        @pl.when(j == 1)
        def near_done():
            near_part.start()

        return unused

    lax.fori_loop(0, QUARTERS, block, 0)
    corner_part.start()
    leaving = [
        pltpu.make_async_copy(source, out, out_sems.at[i])
        for i, (source, out) in enumerate(((grads, grads_out), (text_d, text_d_out), (image_d, image_d_out)))
    ]
    for leave in leaving:
        leave.start()
    near_part.wait()
    own_sum[...] = parts[0].astype(F32) + got[0].astype(F32)
    vectors_y.wait()
    vector_sum[...] += got_vectors[1]
    corner_part.wait()
    total[...] = add(parts[2], got[1])
    for leave in leaving:
        leave.wait()


def halves(flip, values, x):
    half = flip.shape[0] // 2
    starts = [pl.multiple_of(lax.bitwise_xor(x, apart) * half, HEAD) for apart in range(2)]
    return [nn(flip[pl.ds(start, half), :], values) for start in starts]


def pick_columns(values, start, depth):
    row = lax.broadcasted_iota(jnp.int32, (values.shape[1], BLOCK), 0)
    column = lax.broadcasted_iota(jnp.int32, (values.shape[1], BLOCK), 1)
    chosen = (row == column + start) & (column < depth)
    return nn(values, low(jnp.where(chosen, 1.0, 0.0)))


def cross_last(total, vectors, *refs):
    sources, loaded = refs[:14], refs[21:33]
    grad_left, grad_right, image_grad, text_keep, image_keep_out, image_send_out, self_sum = refs[14:21]
    got, image_keep, image_send, text_send, text_got, self_got, text_flip, text_g_flip, image_flip, image_g_flip = refs[33:43]
    send_sems, recv_sems, in_sems, out_sems = refs[43:]
    self_all, self_more, texts, grads, text_d, text_c, images, image_d, image_c, own_sum, text_n, image_n = loaded
    self_loads = []
    for n, (target, first) in enumerate(((self_all, 0), (self_all, 1), (self_more, 0), (self_more, 1))):
        depth = sources[n].shape[1]
        target = target.at[:, pl.ds(first * sources[n - 1].shape[1], depth)]
        self_loads.append(pltpu.make_async_copy(sources[n], target, in_sems.at[n]))
    loads = [None, None]
    for n, (source, ref) in enumerate(zip(sources[4:], loaded[2:])):
        if source.shape != ref.shape:
            source = source.at[:, :, pl.ds(768, BLOCK)]
        loads.append(pltpu.make_async_copy(source, ref, in_sems.at[4 + n]))
    for load in self_loads + loads[2:]:
        load.start()
    unused_core, y, x = partners()
    copy = sender(send_sems, recv_sems)
    far = copy(0, total, got, y)
    text_x = copy(1, text_send, text_got, x)
    dp = self_all.shape[0]
    z_at = lax.axis_index("dp")
    others = [lax.rem(z_at + k, dp) for k in range(1, dp)]
    along_z = [copy(2 + k, self_all.at[other], self_got.at[k], {"dp": other}) for k, other in enumerate(others)]
    greet(y, x, *[{"dp": other} for other in others])
    far.start()
    for load in self_loads:
        load.wait()
    self_all[...] = add(self_all[...], self_more[...])
    for transfer in along_z:
        transfer.start()
    size, image_size = texts.shape[1], images.shape[1]
    below = 3 * size
    at = lax.axis_index("stream")
    leaving = []
    for first, rows, count, flip, g_flip, keep, send, number in (
        (0, size, 3, text_flip, text_g_flip, text_keep, text_send, (2, 3, 4, 5)),
        (below, image_size, 4, image_flip, image_g_flip, image_keep, image_send, (6, 3, 7, 8)),
    ):
        values, unused, outer, context = (loaded[n] for n in number)
        for n in number[:1] if count == 4 else number[:2]:
            loads[n].wait()
        for j in range(QUARTERS):
            columns = rows_of(j, rows)
            for b in range(count):
                flip[rows_of(b, BLOCK), columns] = values[j, :, b * BLOCK : (b + 1) * BLOCK].T
                g_flip[rows_of(b, BLOCK), columns] = grads[j, first + b * rows : first + (b + 1) * rows, :].T
        loads[number[2]].wait()
        loads[number[3]].wait()
        depth = flip.shape[0] // (2 * dp)
        padded = -(-depth // 16) * 16
        found_halves = halves(flip, outer[...].reshape(QUARTERS * rows, 768), at)
        last_halves = halves(g_flip, context[...].reshape(QUARTERS * rows, BLOCK), at)
        for out, found, last in zip((keep, send), found_halves, last_halves):
            for z in range(dp):
                taken = slice(z * depth, (z + 1) * depth)
                for b in range(3):
                    out[z, b * padded : b * padded + depth, :] = low(found[taken, b * BLOCK : (b + 1) * BLOCK])
                out[z, 3 * padded : 3 * padded + depth, :] = low(last[taken])
        if count == 3:
            rounded = low(vectors[...])
            is_text = lax.broadcasted_iota(jnp.int32, (rounded.shape[0], BLOCK), 0) < 6
            for apart, out in enumerate((text_keep, text_send)):
                for z in range(dp):
                    place = lax.bitwise_xor(at, apart) * dp + z
                    text_part = pick_columns(rounded[:, :DT], place * depth, depth)
                    image_depth = DV // (2 * dp)
                    image_part = pick_columns(rounded, place * image_depth, image_depth)
                    out[z, 4 * padded :, :] = low(jnp.where(is_text, text_part, image_part))
            text_x.start()
        else:
            leaving = [
                pltpu.make_async_copy(image_keep, image_keep_out, out_sems.at[0]),
                pltpu.make_async_copy(image_send, image_send_out, out_sems.at[1]),
            ]
            for leave in leaving:
                leave.start()
    summed = self_all[z_at].astype(F32)
    for k, transfer in enumerate(along_z):
        transfer.wait()
        summed = summed + self_got[k].astype(F32)
    self_sum[...] = low(summed)
    for load in loads[9:]:
        load.wait()
    far.wait()
    text_total = text_n[...] + side(own_sum, 0, size, 3) + side(got, 0, size, 3).astype(F32)
    grad_left[...] = text_total[:, : DT // 2]
    grad_right[...] = text_total[:, DT // 2 :]
    image_total = low(image_n[...] + side(own_sum, below, image_size, 4) + side(got, below, image_size, 4).astype(F32))
    image_grad[...] = low(tn(spacing(image_size // PADDED), image_total))
    text_x.wait()
    text_keep[...] = add(text_keep[...], text_got[...])
    for leave in leaving:
        leave.wait()


def gate(hidden):
    half = 0.5 * (1.0 + lax.erf(hidden * (2.0**-0.5)))
    density = jnp.exp(-0.5 * hidden * hidden) * 0.3989422804014327
    return hidden * half, half + hidden * density


def mlp_forward(pairs, text_pre, image_pre, text_gain, text_bias, image_gain, image_bias, *refs):
    parts = refs[:4]
    text_low, image_low, text_next, image_next = refs[4:8]
    text_activ, text_slope, image_activ, image_slope, corner = refs[8:13]
    weights, sems, send_sems, recv_sems = refs[13:]
    step = pl.program_id(0)
    leaving = fetch_round(step, *parts, corner, weights, sems, send_sems, recv_sems)

    @pl.when(step == 0)
    def begin():
        for pre, gain, bias, rounded, total in (
            (text_pre, text_gain, text_bias, text_low, text_next),
            (image_pre, image_gain, image_bias, image_low, image_next),
        ):
            g, b = affine_row(gain, bias, 0)
            one = normed(pre[...])[0] * g + b
            total[...] = one
            rounded[...] = low(one)

    w = weights.at[step]
    for b in range(3):
        activ, slope = gate(nn(text_low[...], w[b * 768 : (b + 1) * 768, :]))
        text_activ[0, :, b * 256 : (b + 1) * 256] = low(activ)
        text_slope[0, :, b * 256 : (b + 1) * 256] = low(slope)
    activ, slope = gate(nn(image_low[...], w[4608:5632, :]))
    image_activ[0] = low(activ)
    image_slope[0] = low(slope)
    text_next[...] += nn(text_activ[0], side(w, 2304, 768, 3))
    image_next[...] += nn(image_activ[0], side(w, 5632, 256, 4))

    @pl.when(step == QUARTERS - 1)
    def finish():
        leaving.wait()


def lane_masks():
    lane = lax.broadcasted_iota(jnp.int32, (1, 2 * SELF_HEAD), 1)
    left = (lane < SELF_HEAD).astype(F32)
    return low(left), low(1.0 - left), lane < SELF_HEAD


def both_heads(tile, masks):
    return jnp.concatenate([tile * masks[0], tile * masks[1]], axis=0)


def one_tile(stacked, masks):
    return jnp.where(masks[2], stacked[:SLOTS], stacked[SLOTS:])


def self_forward(pairs, ids, lengths, text_pre, image_pre, text_gain, text_bias, image_gain, image_bias, text_cot, image_cot, *refs):
    parts = refs[:4]
    (
        text_left,
        text_right,
        image_out,
        text_grad,
        image_grad,
        text_vec,
        image_vec,
        rounded,
        text_q,
        text_k,
        text_v,
        text_c,
        text_probs,
        image_kept,
        image_probs,
        corner,
    ) = refs[4:20]
    weights, text_sum, image_sum, text_low, image_low, sems, send_sems, recv_sems = refs[20:]
    step = pl.program_id(0)
    leaving = fetch_round(step, *parts, corner, weights, sems, send_sems, recv_sems)
    text_rows, image_rows = text_pre.shape[0], image_pre.shape[0]

    @pl.when(step == 0)
    def begin():
        for pre, gain, bias, total, lower, at in (
            (text_pre, text_gain, text_bias, text_sum, text_low, 0),
            (image_pre, image_gain, image_bias, image_sum, image_low, 6 * text_rows),
        ):
            g, b = affine_row(gain, bias, 1)
            two = normed(pre[...])[0] * g + b
            total[...] = two
            lower[...] = low(two)
            leave_blocks(rounded, at, low(two))

    w = weights.at[step]
    for n, out in enumerate((text_q, text_k, text_v)):
        wide = jnp.concatenate([w[b * 576 + n * 192 : b * 576 + (n + 1) * 192, :] for b in range(3)], axis=1)
        out[0] = low(nt(text_low[...], wide))
    for n in range(3):
        image_kept[0, :, n * 256 : (n + 1) * 256] = low(nn(image_low[...], w[2304 + n * 1024 : 3328 + n * 1024, :]))

    masks = lane_masks()
    slots = lax.broadcasted_iota(jnp.int32, (1, SLOTS), 1)
    base = ids[2]
    valid = [slots < lengths[base + p] for p in range(pairs)]
    first, last = slice(0, 128), slice(128, 192)
    queries, keys, values, limits = [], [], [], []
    for p in range(pairs):
        rows = rows_of(p, SLOTS)
        queries += [both_heads(text_q[0, rows, first], masks), text_q[0, rows, last]]
        keys += [text_k[0, rows, first], text_k[0, rows, last]]
        values += [text_v[0, rows, first], text_v[0, rows, last]]
        limits += [valid[p], valid[p]]
    probs, context = attend(queries, keys, values, SELF_HEAD**-0.5, limits)
    for p in range(pairs):
        rows = rows_of(p, SLOTS)
        text_probs[0, p, 0:256, :] = probs[2 * p]
        text_probs[0, p, 256:384, :] = probs[2 * p + 1]
        text_c[0, rows, first] = low(one_tile(context[2 * p], masks))
        text_c[0, rows, last] = low(context[2 * p + 1])

    image_mask = lax.broadcasted_iota(jnp.int32, (PADDED, PADDED), 1) < REGIONS
    units = [(p, h) for p in range(pairs) for h in range(2)]

    def image_part(at):
        return [image_kept[0, rows_of(p, PADDED), at + h * HEAD : at + (h + 1) * HEAD] for p, h in units]

    probs, context = attend(image_part(0), image_part(256), image_part(512), HEAD**-0.5, [image_mask] * len(units))
    for i, (p, h) in enumerate(units):
        image_probs[0, i] = probs[i]
        image_kept[0, rows_of(p, PADDED), 768 + h * HEAD : 768 + (h + 1) * HEAD] = low(context[i])

    text_sum[...] += nn(text_c[0], side(w, 1728, 192, 3))
    image_sum[...] += nn(image_kept[0, :, 768:1024], side(w, 5376, 256, 4))

    @pl.when(step == QUARTERS - 1)
    def finish():
        apart = spacing(pairs)
        image_cot_apart = nn(apart, image_cot[...])
        for total, gain, bias, cot, grad, vec, at in (
            (text_sum, text_gain, text_bias, text_cot[...].astype(F32), text_grad, text_vec, 3 * text_rows),
            (image_sum, image_gain, image_bias, image_cot_apart, image_grad, image_vec, 6 * text_rows + 4 * image_rows),
        ):
            g, b = affine_row(gain, bias, 2)
            unit, scale = normed(total[...])
            value = unit * g + b
            if total is text_sum:
                text_left[...] = value[:, : DT // 2]
                text_right[...] = value[:, DT // 2 :]
            else:
                image_out[...] = low(tn(apart, low(value)))
            back = norm_back(unit, scale, g, cot, vec)
            grad[...] = back
            leave_blocks(rounded, at, low(back))
        leaving.wait()


def self_back(pairs, dp, text_g, image_g, text_pre, image_pre, text_gain, image_gain, rounded, *refs):
    text_q, text_k, text_v, text_c, text_probs, image_kept, image_probs = refs[:7]
    parts = refs[7:12]
    text_n, image_n, text_vec, image_vec = refs[12:16]
    outs = refs[16:21]
    weights, found, text_sum, image_sum, text_g_low, image_g_low, near, rounded_near = refs[21:29]
    flips, (text_d, image_d, sems, out_sems, send_sems, recv_sems) = refs[29:33], refs[33:]
    step = pl.program_id(0)
    fetch(step, BACKWARD, *parts, weights, sems)
    core = partners()[0]
    copy = sender(send_sems, recv_sems)
    copies = [copy(n, found.at[n], near.at[n], core) for n in range(2)]
    rounded_copy = copy(2, rounded, rounded_near, core)

    @pl.when(step == 0)
    def begin():
        greet(core)
        rounded_copy.start()
        text_sum[...] = text_g[...]
        image_sum[...] = image_g[...]
        text_g_low[...] = low(text_g[...])
        image_g_low[...] = low(image_g[...])

    w = weights.at[step]
    masks = lane_masks()
    first, last = slice(0, 128), slice(128, 192)
    text_dc = low(nt(text_g_low[...], side(w, 1728, 192, 3)))
    queries, keys, values, probs, outer = [], [], [], [], []
    for p in range(pairs):
        rows = rows_of(p, SLOTS)
        queries += [both_heads(text_q[0, rows, first], masks), text_q[0, rows, last]]
        keys += [text_k[0, rows, first], text_k[0, rows, last]]
        values += [text_v[0, rows, first], text_v[0, rows, last]]
        probs += [text_probs[0, p, 0:256, :], text_probs[0, p, 256:384, :]]
        outer += [both_heads(text_dc[rows, first], masks), text_dc[rows, last]]
    grad_q, grad_k, grad_v = attend_back(queries, keys, values, probs, outer, SELF_HEAD**-0.5)
    size = text_g.shape[0]
    for p in range(pairs):
        rows = rows_of(p, SLOTS)
        text_d[0, rows, first] = one_tile(grad_q[2 * p], masks)
        text_d[0, rows, last] = grad_q[2 * p + 1]
        for n, grad in ((1, grad_k), (2, grad_v)):
            text_d[n, rows, first] = grad[2 * p]
            text_d[n, rows, last] = grad[2 * p + 1]

    image_dc = low(nt(image_g_low[...], side(w, 5376, 256, 4)))
    units = [(p, h) for p in range(pairs) for h in range(2)]

    def image_part(at):
        return [image_kept[0, rows_of(p, PADDED), at + h * HEAD : at + (h + 1) * HEAD] for p, h in units]

    outer = [image_dc[rows_of(p, PADDED), h * HEAD : (h + 1) * HEAD] for p, h in units]
    given = attend_back(
        image_part(0), image_part(256), image_part(512), [image_probs[0, i] for i in range(len(units))], outer, HEAD**-0.5
    )
    for n in range(3):
        for i, (p, h) in enumerate(units):
            image_d[rows_of(p, PADDED), n * 256 + h * HEAD : n * 256 + (h + 1) * HEAD] = given[n][i]

    gained = text_sum[...]
    for n in range(3):
        wide = jnp.concatenate([w[b * 576 + n * 192 : b * 576 + (n + 1) * 192, :] for b in range(3)], axis=1)
        gained = gained + nn(text_d[n], wide)
    text_sum[...] = gained
    image_sum[...] += nt(image_d[...], side(w, 2304, 1024, 3))

    slot = found.at[step]
    slot[0:size, 0:128] = text_d[0, :, first]
    slot[0:size, 128:256] = text_d[1, :, first]
    slot[size : 2 * size, 0:128] = text_d[2, :, first]
    slot[size : 2 * size, 128:256] = text_c[0, :, first]
    slot[2 * size : 3 * size, 0:128] = jnp.concatenate([text_d[0, :, last], text_d[1, :, last]], axis=1)
    slot[2 * size : 3 * size, 128:256] = jnp.concatenate([text_d[2, :, last], text_c[0, :, last]], axis=1)
    leave_blocks(slot, 3 * size, image_d[...])
    leave_blocks(slot, 3 * size + 3 * image_g.shape[0], image_kept[0, :, 768:1024])
    send_quarter(step, copies)

    @pl.when(step == QUARTERS - 1)
    def finish():
        leave_norm(1, text_sum, image_sum, text_pre, image_pre, text_gain, image_gain, text_n, image_n, text_vec, image_vec)
        rounded_copy.wait()
        for transfer in copies:
            transfer.wait()
        weight_grad(True, dp, (size, image_g.shape[0]), (rounded, rounded_near), found, near, weights, outs, flips, out_sems)


def leave_norm(norm, text_sum, image_sum, text_pre, image_pre, text_gain, image_gain, text_n, image_n, text_vec, image_vec):
    for total, pre, gain, out, vec in (
        (text_sum, text_pre, text_gain, text_n, text_vec),
        (image_sum, image_pre, image_gain, image_n, image_vec),
    ):
        unit, scale = normed(pre[...])
        out[...] = norm_back(unit, scale, gain[0, norm : norm + 1, :].astype(F32), total[...], vec)


def mlp_back(pairs, dp, text_g, image_g, text_one, image_one, text_pre, image_pre, text_gain, image_gain, *refs):
    text_activ, text_slope, image_activ, image_slope = refs[:4]
    parts = refs[4:9]
    text_n, image_n, next_low, text_vec, image_vec = refs[9:14]
    outs = refs[14:17]
    weights, found, text_sum, image_sum, text_g_low, image_g_low, near, rounded_near = refs[17:25]
    flips, (rounded, text_d, sems, out_sems, send_sems, recv_sems) = refs[25:29], refs[29:]
    step = pl.program_id(0)
    fetch(step, BACKWARD, *parts, weights, sems)
    size, image_size = text_g.shape[0], image_g.shape[0]
    core = partners()[0]
    copy = sender(send_sems, recv_sems)
    rounded_copy = copy(2, rounded, rounded_near, core)
    copies = [copy(n, found.at[n], near.at[n], core) for n in range(2)]

    @pl.when(step == 0)
    def begin():
        text_sum[...] = text_g[...]
        image_sum[...] = image_g[...]
        text_g_low[...] = low(text_g[...])
        image_g_low[...] = low(image_g[...])
        leave_blocks(rounded, 0, text_one[...])
        leave_blocks(rounded, 3 * size, text_g_low[...])
        leave_blocks(rounded, 6 * size, image_one[...])
        leave_blocks(rounded, 6 * size + 4 * image_size, image_g_low[...])
        greet(core)
        rounded_copy.start()

    w = weights.at[step]
    slot = found.at[step]
    wide = side(w, 2304, 768, 3)
    for b in range(3):
        columns = slice(b * 256, (b + 1) * 256)
        back = nt(text_g_low[...], wide[columns])
        text_d[:, columns] = low(back * text_slope[0, :, columns].astype(F32))
    text_sum[...] += nt(text_d[...], side(w, 0, 768, 3))
    image_d = low(nt(image_g_low[...], side(w, 5632, 256, 4)) * image_slope[0].astype(F32))
    image_sum[...] += nt(image_d, w[4608:5632, :])
    leave_blocks(slot, 0, text_d[...])
    leave_blocks(slot, 3 * size, text_activ[0])
    leave_blocks(slot, 6 * size, image_d)
    leave_blocks(slot, 6 * size + image_size, image_activ[0])
    send_quarter(step, copies)

    @pl.when(step == QUARTERS - 1)
    def finish():
        leave_norm(0, text_sum, image_sum, text_pre, image_pre, text_gain, image_gain, text_n, image_n, text_vec, image_vec)
        leave_blocks(next_low, 0, low(text_n[...]))
        leave_blocks(next_low, 3 * size, low(image_n[...]))
        rounded_copy.wait()
        for transfer in copies:
            transfer.wait()
        weight_grad(False, dp, (size, image_size), (rounded, rounded_near), found, near, weights, outs, flips, out_sems)


def weight_grad(is_self, dp, sizes, rounded, found, near, spare, outs, flips, out_sems):
    text_flip, text_g_flip, image_flip, image_g_flip = flips
    to_send, kept, to_z, by_image = (spare.at[n] for n in range(QUARTERS))
    size, image_size = sizes
    x = lax.axis_index("stream")
    for at in range(2):
        for b in range(3):
            text_flip[rows_of(b, BLOCK), rows_of(at, size)] = rounded[at][rows_of(b, size), :].T
            text_g_flip[rows_of(b, BLOCK), rows_of(at, size)] = rounded[at][rows_of(3 + b, size), :].T
        for b in range(8):
            start = 6 * size + b * image_size
            flip = image_g_flip if b > 3 else image_flip
            flip[rows_of(b % 4, BLOCK), rows_of(at, image_size)] = rounded[at][start : start + image_size, :].T

    text_depth, image_depth = DT // (2 * dp), DV // (2 * dp)
    padded = -(-text_depth // 16) * 16
    lane = lax.broadcasted_iota(jnp.int32, (1, HEAD), 1) < SELF_HEAD
    top = 3 * padded if is_self else 5 * padded
    below = 2 * image_depth if is_self else 2 * image_depth + padded
    leaving = []

    def leave(source, target, first=0):
        leaving.append(pltpu.make_async_copy(source.at[pl.ds(first, target.shape[0])], target, out_sems.at[len(leaving)]))
        leaving[-1].start()

    for slot in (1, 0):

        def block(start, rows):
            return jnp.concatenate([found[2 + slot, start : start + rows, :], near[slot, start : start + rows, :]], axis=0)

        def text_block(b):
            return block(b * size, size)

        def image_block(b, text_blocks):
            return block(text_blocks * size + b * image_size, image_size)

        def write(row, depth, value):
            for apart in range(2):
                ref, at = ((to_send if slot else kept), apart) if is_self else ((to_send if apart else kept), slot)
                for z in range(dp):
                    to = (at * dp + z) * top + row
                    ref[to : to + depth, :] = low(value[apart][z * depth : (z + 1) * depth])

        def bottom(row, depth, value):
            for apart in range(2):
                for z in range(dp):
                    to = (z * 4 + 2 * slot + apart) * below + row
                    to_z[to : to + depth, :] = low(value[apart][z * depth : (z + 1) * depth])

        if is_self:
            one, two, three = text_block(0), text_block(1), text_block(2)
            write(0, text_depth, halves(text_flip, one, x))
            pairs = zip(halves(text_flip, two[:, :HEAD], x), halves(text_g_flip, two[:, HEAD:], x))
            write(padded, text_depth, [jnp.concatenate(pair, axis=1) for pair in pairs])
            pairs = zip(halves(text_flip, three, x), halves(text_g_flip, three[:, HEAD:], x))
            mixed = [jnp.concatenate([a[:, :HEAD], jnp.where(lane, a[:, HEAD:], b)], axis=1) for a, b in pairs]
            write(2 * padded, text_depth, mixed)
            for b in range(2):
                for apart, value in enumerate(halves(image_flip, image_block(b, 3), x)):
                    for z in range(dp):
                        to = (((2 * (1 - apart) + slot) * dp + z) * 2 + b) * image_depth
                        by_image[to : to + image_depth, :] = low(value[z * image_depth : (z + 1) * image_depth])
            leave(*((to_send, outs[0]) if slot else (kept, outs[1])))
            for b, flip in enumerate((image_flip, image_g_flip)):
                bottom(b * image_depth, image_depth, halves(flip, image_block(2 + b, 3), x))
        else:
            for b in range(5):
                write(b * padded, text_depth, halves(text_g_flip if b > 2 else text_flip, text_block(b), x))
            bottom(2 * image_depth, text_depth, halves(text_g_flip, text_block(5), x))
            for b, flip in enumerate((image_flip, image_g_flip)):
                bottom(b * image_depth, image_depth, halves(flip, image_block(b, 6), x))
    if not is_self:
        leave(to_send, outs[0])
        leave(kept, outs[1])
    leave(to_z, outs[2])
    for number, out in enumerate(outs[3:]):
        leave(by_image, out, number * out.shape[0])
    for copy in leaving:
        copy.wait()


ANY = pl.BlockSpec(memory_space=pl.ANY)
SCALARS = pl.BlockSpec(memory_space=pltpu.SMEM)


def whole(array, buffers=None):
    zeros = (0,) * len(array.shape)
    mode = {} if buffers is None else {"pipeline_mode": pl.Buffered(buffers)}
    return pl.BlockSpec(array.shape, lambda *s: zeros, **mode)


def quarter(array, order):
    tail = (0,) * (len(array.shape) - 1)
    if order is FORWARD:
        return pl.BlockSpec((1,) + array.shape[1:], lambda s: (s,) + tail)
    return pl.BlockSpec((1,) + array.shape[1:], lambda s: (lax.rem(2 * s + 1 - lax.div(s, 2), 4),) + tail)


def shape(*dims, of=BF):
    return jax.ShapeDtypeStruct(dims, of)


def run(kernel, order, operands, outs, scratch, us, meeting=None):
    def spec(kind, array, given=False):
        if kind == "w" and given and order:
            return whole(array, 1)
        return {"s": lambda: SCALARS, "w": lambda: whole(array), "q": lambda: quarter(array, order), "a": lambda: ANY}[kind]()

    return pl.pallas_call(
        kernel,
        grid=(QUARTERS,) if order else (1,),
        in_specs=[spec(*entry, given=True) for entry in operands],
        out_specs=[spec(*entry) for entry in outs],
        out_shape=[array for unused, array in outs],
        scratch_shapes=scratch,
        compiler_params=pltpu.CompilerParams(
            dimension_semantics=("arbitrary",),
            vmem_limit_bytes=60 * 2**20,
            collective_id=meeting,
            has_side_effects=meeting is not None,
        ),
        cost_estimate=pl.CostEstimate(flops=int(us * 1.1e9), bytes_accessed=1024, transcendentals=0),
    )(*[array for unused, array in operands])


def swap(value, axis, apart):
    return lax.ppermute(value, axis, [(i, i ^ apart) for i in range(lax.axis_size(axis))])


def after(value, *earlier):
    return lax.optimization_barrier((value,) + earlier)[0]


class Line:
    def __init__(self):
        self.last = ()

    def take(self, value):
        return after(value, *self.last)

    def leave(self, *values):
        self.last = values


def add(left, right):
    return low(left.astype(F32) + right.astype(F32))


def fold_last(total):
    return lax.psum_scatter(total, "dp", scatter_dimension=0, tiled=True)[0]


def s(value):
    return ("s", value)


def w(value):
    return ("w", value)


def q(value):
    return ("q", value)


def a(value):
    return ("a", value)


def local(
    text_in,
    image_in,
    lengths,
    text_cot,
    image_cot,
    text_cross_q,
    text_cross_kv,
    text_cross_out,
    text_up,
    text_down,
    text_self_qkv,
    text_self_out,
    text_gain,
    text_bias,
    image_cross_q,
    image_cross_kv,
    image_cross_out,
    image_up,
    image_down,
    image_self_qkv,
    image_self_out,
    image_gain,
    image_bias,
):
    dp = lax.axis_size("dp")
    places = 2 * dp
    x_at = lax.axis_index("stream")
    t_at = lax.axis_index("tensor")
    size = text_in.shape[0]
    pairs = size // SLOTS
    image_size = pairs * PADDED
    units = 2 * pairs
    ids = jnp.stack([x_at, x_at * dp + lax.axis_index("dp")] + [(t_at ^ j) * pairs for j in range(QUARTERS)]).astype(jnp.int32)

    def leave(rows):
        return swap(rows, "stream", 1).astype(F32)

    line = Line()
    mlp_own, mlp_first, mlp_mine = pack([text_up[0], text_down[0], image_up[0], image_down[0]], places, 5120, ids)
    mlp_share = swap(mlp_mine, "tensor", 2)
    self_own, self_first, self_mine = pack(
        [
            text_self_qkv[0].transpose(1, 2, 0).reshape(-1, DT),
            text_self_out[0],
            image_self_qkv[0].reshape(DV, -1),
            image_self_out[0],
        ],
        places,
        4608,
        after(ids, mlp_own),
    )
    cross_w = (
        text_cross_q[0],
        image_cross_kv[0].reshape(DT, -1),
        text_cross_kv[0].reshape(DV, -1),
        image_cross_q[0],
        text_cross_out[0],
        image_cross_out[0],
    )
    line.leave(self_own)
    mlp_share = line.take(mlp_share)
    line.leave(mlp_share, cross_w[1], cross_w[2])
    self_share = line.take(swap(self_mine, "tensor", 2))
    line.leave(self_share)
    mlp_rest = lax.all_gather(mlp_share, ("stream", "dp"), axis=0, tiled=True)
    self_rest = lax.all_gather(self_share, ("stream", "dp"), axis=0, tiled=True)
    self_near = swap(self_own, "tensor", 1)
    mlp_near_w = swap(mlp_own, "tensor", 1)
    image_cot_here = swap(image_cot, "stream", 1)
    mlp_far = swap(mlp_first, "tensor", 2)

    text_wide, image_wide = shape(size, DT, of=F32), shape(image_size, DV, of=F32)
    text_half = shape(size, DT // 2, of=F32)
    text_f32, image_f32 = pltpu.VMEM((size, DT), F32), pltpu.VMEM((image_size, DV), F32)
    text_bf, image_bf = pltpu.VMEM((size, DT), BF), pltpu.VMEM((image_size, DV), BF)
    in_sems, out_sems = pltpu.SemaphoreType.DMA((5,)), pltpu.SemaphoreType.DMA((5,))
    text_affine = [w(text_gain), w(text_bias)]
    image_affine = [w(image_gain), w(image_bias)]
    vector_outs = [w(shape(2, DT, of=F32)), w(shape(2, DV, of=F32))]
    part_rows = 3 * size + 4 * image_size

    def buffer(weights):
        return pltpu.VMEM((QUARTERS,) + weights.shape, BF)

    in_four = [
        (QUARTERS, size, DT),
        (QUARTERS, image_size, DV),
        (QUARTERS, size, 1024),
        (QUARTERS, image_size, 1024),
        (QUARTERS, units, SLOTS, PADDED),
        (QUARTERS, units, PADDED, SLOTS),
    ]

    def links(count):
        return [pltpu.SemaphoreType.DMA((count,)), pltpu.SemaphoreType.DMA((count,))]

    text_pre1, image_pre1, texts, images, *cross_kept = run(
        functools.partial(cross_forward, pairs),
        None,
        [s(lengths), w(line.take(text_in)), w(image_in)] + [w(m) for m in cross_w],
        [w(text_wide), w(image_wide)] + [a(shape(*dims)) for dims in in_four],
        [pltpu.VMEM(dims, BF) for dims in in_four]
        + [pltpu.VMEM((QUARTERS, part_rows, BLOCK), BF), pltpu.VMEM((part_rows, BLOCK), BF), pltpu.VMEM((3, part_rows, BLOCK), BF)]
        + [image_bf]
        + links(10)
        + [pltpu.SemaphoreType.DMA((6,))],
        70,
        1,
    )
    line.leave(text_pre1, image_cot_here)
    mlp_far, mlp_rest = line.take((mlp_far, mlp_rest))
    self_far = swap(after(self_first, mlp_far), "tensor", 2)
    (
        text_one,
        image_one,
        text_pre2,
        image_pre2,
        text_activ,
        text_slope,
        image_activ,
        image_slope,
        mlp_corner,
    ) = run(
        functools.partial(mlp_forward, pairs),
        FORWARD,
        [w(text_pre1), w(image_pre1)] + text_affine + image_affine + [a(m) for m in (mlp_own, mlp_near_w, mlp_far, mlp_rest)],
        [
            w(shape(size, DT)),
            w(shape(image_size, DV)),
            w(text_wide),
            w(image_wide),
            q(shape(QUARTERS, size, 768)),
            q(shape(QUARTERS, size, 768)),
            q(shape(QUARTERS, image_size, 256)),
            q(shape(QUARTERS, image_size, 256)),
            a(mlp_own),
        ],
        [buffer(mlp_own), in_sems] + links(2),
        1,
        7,
    )
    mlp_w = mlp_own, mlp_near_w, mlp_far, mlp_rest, mlp_corner
    line.leave(text_pre2)
    self_far, self_rest = line.take((self_far, self_rest))
    (
        text_left,
        text_right,
        image_out,
        text_n3,
        image_n3,
        text_vec3,
        image_vec3,
        self_rounded,
        self_q,
        self_k,
        self_v,
        self_c,
        self_probs,
        self_kept,
        self_image_probs,
        self_corner,
    ) = run(
        functools.partial(self_forward, pairs),
        FORWARD,
        [s(ids), s(lengths), w(text_pre2), w(image_pre2)]
        + text_affine
        + image_affine
        + [w(text_cot), w(image_cot_here)]
        + [a(m) for m in (self_own, self_near, self_far, self_rest)],
        [w(text_half), w(text_half), w(image_cot), w(text_wide), w(image_wide)]
        + vector_outs
        + [
            w(shape(2 * part_rows, BLOCK)),
            q(shape(QUARTERS, size, 192)),
            q(shape(QUARTERS, size, 192)),
            q(shape(QUARTERS, size, 192)),
            q(shape(QUARTERS, size, 192)),
            q(shape(QUARTERS, pairs, 384, SLOTS)),
            q(shape(QUARTERS, image_size, 1024)),
            q(shape(QUARTERS, units, PADDED, PADDED)),
            a(self_own),
        ],
        [buffer(self_own), text_f32, image_f32, text_bf, image_bf, in_sems] + links(2),
        19,
        8,
    )
    self_w = self_own, self_near, self_far, self_rest, self_corner
    image_out = swap(image_out, "stream", 1)

    text_depth, image_depth = DT // places, DV // places
    padded = -(-text_depth // 16) * 16

    def back_scratch(weights, rows):
        return [
            buffer(weights[0]),
            pltpu.VMEM((QUARTERS, rows, BLOCK), BF),
            text_f32,
            image_f32,
            text_bf,
            image_bf,
            pltpu.VMEM((2, rows, BLOCK), BF),
            pltpu.VMEM((2 * part_rows, BLOCK), BF),
            pltpu.VMEM((DT, 2 * size), BF),
            pltpu.VMEM((DT, 2 * size), BF),
            pltpu.VMEM((DV, 2 * image_size), BF),
            pltpu.VMEM((DV, 2 * image_size), BF),
        ]

    def grad_shapes(is_self):
        first = (2, dp, (3 if is_self else 5) * padded, BLOCK)
        last = (dp, 4 * (2 * image_depth + (0 if is_self else padded)), BLOCK)
        return [first, first, last] + [(2, dp, 2 * image_depth, BLOCK)] * (2 if is_self else 0)

    def grad_outs(is_self):
        return [a(shape(math.prod(dims[:-1]), BLOCK)) for dims in grad_shapes(is_self)]

    def grad_arrays(is_self, *found):
        return [out.reshape(dims) for out, dims in zip(found, grad_shapes(is_self))]

    self_rows = 3 * size + 4 * image_size
    text_n2, image_n2, text_vec2, image_vec2, *self_found = run(
        functools.partial(self_back, pairs, dp),
        BACKWARD,
        [
            w(text_n3),
            w(image_n3),
            w(text_pre2),
            w(image_pre2),
            w(text_gain),
            w(image_gain),
            w(self_rounded),
            q(self_q),
            q(self_k),
            q(self_v),
            q(self_c),
            q(self_probs),
            q(self_kept),
            q(self_image_probs),
        ]
        + [a(m) for m in self_w],
        [w(text_wide), w(image_wide)] + vector_outs + grad_outs(True),
        back_scratch(self_w, self_rows)
        + [pltpu.VMEM((3, size, 192), BF), pltpu.VMEM((image_size, 768), BF), in_sems, out_sems]
        + links(3),
        32,
        2,
    )
    to_y, self_top, to_z, to_x, self_side = grad_arrays(True, *self_found)
    self_by_y = swap(to_y, "tensor", 2)
    self_by_x = swap(to_x, "stream", 1)
    self_bottom = fold_last(to_z)
    line.leave(self_top)
    mlp_rows = 6 * size + 2 * image_size
    text_n1, image_n1, grad_low, text_vec1, image_vec1, *mlp_found = run(
        functools.partial(mlp_back, pairs, dp),
        BACKWARD,
        [
            w(text_n2),
            w(image_n2),
            w(text_one),
            w(image_one),
            w(text_pre1),
            w(image_pre1),
            w(line.take(text_gain)),
            w(image_gain),
            q(text_activ),
            q(text_slope),
            q(image_activ),
            q(image_slope),
        ]
        + [a(m) for m in mlp_w],
        [w(text_wide), w(image_wide), w(shape(part_rows, BLOCK))]
        + vector_outs
        + grad_outs(False),
        back_scratch(mlp_w, mlp_rows)
        + [pltpu.VMEM((2 * part_rows, BLOCK), BF), text_bf, in_sems, out_sems]
        + links(3),
        28,
        3,
    )
    line.leave(grad_low)
    to_x, mlp_top, to_z = grad_arrays(False, *mlp_found)
    self_top, self_by_y, self_side, self_by_x, to_x, to_z, image_out = after(
        (self_top, self_by_y, self_side, self_by_x, to_x, to_z, image_out), mlp_top
    )
    mlp_by_x = swap(to_x, "stream", 1)
    mlp_bottom = fold_last(to_z)
    self_top, to_x = add(self_top[0], self_by_y[0]), add(self_top[1], self_by_y[1])
    self_then_x = swap(to_x, "stream", 1)
    self_side, to_y = add(self_side[0], self_by_x[0]), add(self_side[1], self_by_x[1])
    self_then_y = swap(to_y, "tensor", 2)
    line.leave(self_top, to_x, self_side, to_y)
    d_dims = [(QUARTERS, part_rows, BLOCK), (QUARTERS, size, 768), (QUARTERS, image_size, 768)]
    grads, text_d, image_d, own_sum, total, vectors = run(
        functools.partial(cross_back, pairs),
        None,
        [w(line.take(grad_low))]
        + [w(v) for v in (text_vec1, text_vec2, text_vec3, image_vec1, image_vec2, image_vec3)]
        + [a(k) for k in cross_kept] + [w(m) for m in cross_w],
        [a(shape(*dims)) for dims in d_dims]
        + [w(shape(part_rows, BLOCK, of=F32)), w(shape(part_rows, BLOCK)), w(shape(16, DV, of=F32))],
        [pltpu.VMEM(dims, BF) for dims in d_dims]
        + [pltpu.VMEM((QUARTERS, part_rows, BLOCK), BF), pltpu.VMEM((2, part_rows, BLOCK), BF), pltpu.VMEM((2, 16, DV), F32)]
        + [pltpu.VMEM((16, DV), F32)]
        + [pltpu.VMEM(k.shape, BF) for k in cross_kept]
        + links(7)
        + [pltpu.SemaphoreType.DMA((3,)), pltpu.SemaphoreType.DMA((QUARTERS, 4))],
        48,
        4,
    )
    line.leave(total)
    text_only, image_only = 4 * padded + 16, 4 * image_depth
    last_inputs = [
        self_top,
        self_side,
        self_then_x,
        self_then_y,
        texts,
        grads,
        text_d,
        cross_kept[0],
        images,
        image_d,
        cross_kept[1],
        own_sum,
        text_n1,
        image_n1,
    ]
    self_all = (dp, 3 * padded + 2 * image_depth, BLOCK)
    last_scratch = [pltpu.VMEM(self_all, BF)] * 2 + [pltpu.VMEM(m.shape, m.dtype) for m in last_inputs[4:]]
    last_scratch[5], last_scratch[8] = pltpu.VMEM((QUARTERS, size, BLOCK), BF), pltpu.VMEM((QUARTERS, image_size, BLOCK), BF)
    grad_left, grad_right, image_grad, cross_text, image_keep, image_send, self_top = run(
        cross_last,
        None,
        [w(line.take(total)), w(vectors)] + [a(m) for m in last_inputs],
        [
            w(text_half),
            w(text_half),
            w(image_cot),
            w(shape(dp, text_only, BLOCK)),
            a(shape(dp, image_only, BLOCK)),
            a(shape(dp, image_only, BLOCK)),
            w(shape(*self_all[1:])),
        ],
        last_scratch
        + [
            pltpu.VMEM((part_rows, BLOCK), BF),
            pltpu.VMEM((dp, image_only, BLOCK), BF),
            pltpu.VMEM((dp, image_only, BLOCK), BF),
            pltpu.VMEM((dp, text_only, BLOCK), BF),
            pltpu.VMEM((dp, text_only, BLOCK), BF),
            pltpu.VMEM((dp - 1, *self_all[1:]), BF),
            pltpu.VMEM((DT, QUARTERS * size), BF),
            pltpu.VMEM((DT, QUARTERS * size), BF),
            pltpu.VMEM((DV, QUARTERS * image_size), BF),
            pltpu.VMEM((DV, QUARTERS * image_size), BF),
        ]
        + links(1 + dp)
        + [pltpu.SemaphoreType.DMA((14,)), pltpu.SemaphoreType.DMA((2,))],
        2,
        5,
    )
    line.leave(grad_left)
    mlp_top, mlp_by_x, self_bottom, mlp_bottom, cross_text, image_send = line.take(
        (mlp_top, mlp_by_x, self_bottom, mlp_bottom, cross_text, image_send)
    )
    cross_text = fold_last(cross_text)
    image_send = swap(image_send, "stream", 1)
    mlp_top, to_y = add(mlp_top[0], mlp_by_x[0]), add(mlp_top[1], mlp_by_x[1])
    mlp_then_y = swap(to_y, "tensor", 2)
    line.leave(mlp_top, to_y)
    self_bottom = line.take(self_bottom).reshape(2, 2, 2 * image_depth, BLOCK)
    self_bottom_x = swap(self_bottom[:, 1], "stream", 1)
    cross_image = add(image_keep, line.take(image_send))
    line.leave(cross_image)
    cross_image = fold_last(cross_image)
    self_bottom = add(self_bottom[:, 0], line.take(self_bottom_x))
    self_bottom_y = swap(self_bottom[1], "tensor", 2)
    mlp_bottom = line.take(mlp_bottom).reshape(2, 2, 2 * image_depth + padded, BLOCK)
    mlp_bottom_x = swap(mlp_bottom[:, 1], "stream", 1)
    mlp_top = add(mlp_top, line.take(mlp_then_y))
    line.leave(mlp_top)
    mlp_top = fold_last(mlp_top)
    mlp_bottom = add(mlp_bottom[:, 0], line.take(mlp_bottom_x))
    mlp_bottom = add(mlp_bottom[0], swap(mlp_bottom[1], "tensor", 2))
    self_bottom = add(self_bottom[0], self_bottom_y)
    self_grads = jnp.concatenate([self_top, self_bottom], axis=0)
    image_grad = leave(image_grad)

    def pick(packed, first, count, depth, stride):
        rows = [packed[first + b * stride : first + b * stride + depth] for b in range(count)]
        return jnp.concatenate(rows, axis=1).astype(F32)

    def text_pick(packed, first, count):
        return pick(packed, first, count, text_depth, padded)

    def image_pick(packed, first, count):
        return pick(packed, first, count, image_depth, image_depth)

    sums = cross_text[4 * padded :].astype(F32)
    text_vectors, image_vectors = sums[:6, :text_depth], sums[6:12, :image_depth]

    self_text = text_pick(self_grads, 0, 3)

    def heads(at):
        return jnp.concatenate([self_text[:, at * 128 : (at + 1) * 128], self_text[:, 512 + at * 64 : 576 + at * 64]], axis=1)

    below = 3 * padded
    return (
        jnp.concatenate([text_left, text_right], axis=1),
        image_out.astype(F32),
        jnp.concatenate([grad_left, grad_right], axis=1),
        image_grad,
        text_pick(cross_text, 0, 1)[None],
        image_pick(cross_image, 0, 2).reshape(1, image_depth, 2, 256),
        text_pick(cross_text, 3 * padded, 1).T[None],
        text_pick(mlp_top, 0, 3)[None],
        jnp.concatenate([text_pick(mlp_top, below, 2), text_pick(mlp_bottom, 2 * image_depth, 1)], axis=1).T[None],
        jnp.stack([heads(n) for n in range(3)], axis=1)[None],
        heads(3).T[None],
        text_vectors[0::2][None],
        text_vectors[1::2][None],
        image_pick(cross_image, 2 * image_depth, 1)[None],
        text_pick(cross_text, padded, 2).reshape(1, text_depth, 2, 256),
        image_pick(cross_image, 3 * image_depth, 1).T[None],
        image_pick(mlp_bottom, 0, 1)[None],
        image_pick(mlp_bottom, image_depth, 1).T[None],
        image_pick(self_grads, below, 3).reshape(1, image_depth, 3, 256),
        image_pick(self_grads, below + 3 * image_depth, 1).T[None],
        image_vectors[0::2][None],
        image_vectors[1::2][None],
    )


def solution(mesh):
    rows = P(("stream", "dp", "tensor"), None)
    wide_in = P(None, None, "tensor")
    group_in = P(None, None, None, "tensor")
    wide_out = P(None, "tensor", None)
    grad_in = P(None, ("stream", "dp"), "tensor")
    grad_group = P(None, ("stream", "dp"), None, "tensor")
    grad_out = P(None, "tensor", ("stream", "dp"))
    vector = P(None, None, ("stream", "dp"))
    weights = (wide_in, group_in, wide_out, wide_in, wide_out, group_in, wide_out, P(), P())
    grads = (grad_in, grad_group, grad_out, grad_in, grad_out, grad_group, grad_out, vector, vector)
    return jax.shard_map(
        local,
        mesh=mesh,
        in_specs=(rows, rows, P(("stream", "dp")), rows, rows) + weights + weights,
        out_specs=(rows, rows, rows, rows) + grads + grads,
        check_vma=False,
    )
```

```python
import functools
import math

import jax
import jax.numpy as jnp
from jax import lax
from jax.experimental import pallas as pl
from jax.experimental.pallas import tpu as pltpu
from jax.sharding import PartitionSpec as P

DT = 768
DV = 1024
HEAD = 128
SELF_HEAD = 64
SLOTS = 128
REGIONS = 37
PADDED = 48
QUARTERS = 4
BLOCK = 256

norm_eps = 1e-05
masked_score = -1e30

BF = jnp.bfloat16
F32 = jnp.float32
FORWARD = (0, 1, 2, 3)
BACKWARD = (1, 3, 0, 2)


def nn(left, right):
    return lax.dot_general(left, right, (((1,), (0,)), ((), ())), preferred_element_type=F32)


def nt(left, right):
    return lax.dot_general(left, right, (((1,), (1,)), ((), ())), preferred_element_type=F32)


def tn(left, right):
    return lax.dot_general(left, right, (((0,), (0,)), ((), ())), preferred_element_type=F32)


def low(value):
    return value.astype(BF)


def normed(inputs):
    centered = inputs - jnp.mean(inputs, axis=-1, keepdims=True)
    scale = lax.rsqrt(jnp.mean(centered * centered, axis=-1, keepdims=True) + norm_eps)
    return centered * scale, scale


def norm_back(unit, scale, gain, grad, vec):
    vec[0:1] = jnp.sum(grad * unit, axis=0, keepdims=True)
    vec[1:2] = jnp.sum(grad, axis=0, keepdims=True)
    inner = grad * gain
    shift = jnp.mean(inner, axis=-1, keepdims=True)
    slope = jnp.mean(inner * unit, axis=-1, keepdims=True)
    return scale * (inner - shift - unit * slope)


def softmax_all(scores):
    tops = [jnp.max(s, axis=-1, keepdims=True) for s in scores]
    powers = [jnp.exp(s - t) for s, t in zip(scores, tops)]
    sums = [jnp.sum(e, axis=-1, keepdims=True) for e in powers]
    return [low(e * (1.0 / total)) for e, total in zip(powers, sums)]


def attend(queries, keys, values, scale, masks):
    scores = [nt(q, k) * scale for q, k in zip(queries, keys)]
    scores = [s if m is None else jnp.where(m, s, masked_score) for s, m in zip(scores, masks)]
    probs = softmax_all(scores)
    return probs, [nn(p, v) for p, v in zip(probs, values)]


def attend_back(queries, keys, values, probs, grads, scale):
    grad_probs = [nt(g, v) for g, v in zip(grads, values)]
    grad_values = [low(tn(p, g)) for p, g in zip(probs, grads)]
    wide = [p.astype(F32) for p in probs]
    inner = [jnp.sum(p * g, axis=-1, keepdims=True) for p, g in zip(wide, grad_probs)]
    grad_scores = [low(p * (g - i)) for p, g, i in zip(wide, grad_probs, inner)]
    grad_queries = [low(nn(g, k) * scale) for g, k in zip(grad_scores, keys)]
    grad_keys = [low(tn(g, q) * scale) for g, q in zip(grad_scores, queries)]
    return grad_queries, grad_keys, grad_values


def side(ref, row, width, count):
    return jnp.concatenate([ref[row + b * width : row + (b + 1) * width, :] for b in range(count)], axis=1)


def rows_of(pair, size):
    return slice(pair * size, (pair + 1) * size)


def fetch(step, order, own, near, far, far_rest, corner, buffer, sems):
    slots = [order.index(quarter) for quarter in range(QUARTERS)]
    cut, rest = far.shape[0], far_rest.shape[0]
    copies = [
        (slots[0], pltpu.make_async_copy(own, buffer.at[slots[0]], sems.at[0])),
        (slots[1], pltpu.make_async_copy(near, buffer.at[slots[1]], sems.at[1])),
        (slots[2], pltpu.make_async_copy(far, buffer.at[slots[2], pl.ds(0, cut)], sems.at[2])),
        (slots[2], pltpu.make_async_copy(far_rest, buffer.at[slots[2], pl.ds(cut, rest)], sems.at[3])),
    ]
    if corner is not None:
        copies.append((slots[3], pltpu.make_async_copy(corner, buffer.at[slots[3]], sems.at[4])))
    copies.sort(key=lambda entry: entry[0])

    @pl.when(step == 0)
    def begin():
        for slot, copy in copies:
            if slot == 0:
                copy.start()

    for at in range(QUARTERS):

        @pl.when(step == at)
        def arrive():
            for slot, copy in copies:
                if slot == at:
                    copy.wait()

    @pl.when(step == 0)
    def others():
        for slot, copy in copies:
            if slot > 0:
                copy.start()


def fetch_round(step, own, near, far, far_rest, corner, buffer, sems, send_sems, recv_sems):
    core = partners()[0]
    copy = sender(send_sems, recv_sems)
    cut, rest = far.shape[0], far_rest.shape[0]
    over = copy(0, far, buffer.at[3, pl.ds(0, cut)], core), copy(1, far_rest, buffer.at[3, pl.ds(cut, rest)], core)
    leaving = pltpu.make_async_copy(buffer.at[3], corner, sems.at[4])
    fetch(step, FORWARD, own, near, far, far_rest, None, buffer, sems)

    @pl.when(step == 0)
    def begin():
        greet(core)
        for transfer in over:
            transfer.start()

    @pl.when(step == 3)
    def last():
        for transfer in over:
            transfer.wait()
        leaving.start()

    return leaving


def spacing(pairs):
    rows, columns = pairs * PADDED, pairs * REGIONS
    row = lax.broadcasted_iota(jnp.int32, (rows, columns), 0)
    column = lax.broadcasted_iota(jnp.int32, (rows, columns), 1)
    chosen = jnp.zeros((rows, columns), F32)
    for p in range(pairs):
        inside = (column >= p * REGIONS) & (column < (p + 1) * REGIONS)
        chosen = jnp.where(inside & (row - p * PADDED == column - p * REGIONS), 1.0, chosen)
    return low(chosen)


def send_quarter(step, copies):
    for at, copy in enumerate(copies):

        @pl.when(step == at)
        def leave():
            copy.start()


def affine_row(gain, bias, norm):
    return gain[0, norm : norm + 1, :].astype(F32), bias[0, norm : norm + 1, :].astype(F32)


def leave_blocks(ref, row, value):
    size = value.shape[0]
    for b in range(value.shape[1] // BLOCK):
        ref[row + b * size : row + (b + 1) * size, :] = value[:, b * BLOCK : (b + 1) * BLOCK]


MESH = pl.DeviceIdType.MESH


def partners():
    t = lax.axis_index("tensor")
    return {"tensor": lax.bitwise_xor(t, 1)}, {"tensor": lax.bitwise_xor(t, 2)}, {"stream": lax.bitwise_xor(lax.axis_index("stream"), 1)}


def greet(*others):
    barrier = pltpu.get_barrier_semaphore()
    for other in others:
        pl.semaphore_signal(barrier, inc=1, device_id=other, device_id_type=MESH)
    pl.semaphore_wait(barrier, len(others))


def sender(send_sems, recv_sems):
    def copy(number, source, target, to):
        return pltpu.make_async_remote_copy(
            src_ref=source,
            dst_ref=target,
            send_sem=send_sems.at[number],
            recv_sem=recv_sems.at[number],
            device_id=to,
            device_id_type=MESH,
        )

    return copy


def pack(pieces, places, rest, ids):
    total = sum(m.size for m in pieces) // BLOCK
    cut, share = total - rest, rest // places

    def kernel(ids, *refs):
        sources, (own, first, mine) = refs[: len(pieces)], refs[len(pieces) :]
        row = 0
        for ref in sources:
            leave_blocks(own, row, ref[...])
            row += ref.size // BLOCK
        first[...] = own[0:cut, :]
        mine[...] = own[pl.ds(pl.multiple_of(cut + ids[1] * share, 16), share), :]

    return run(
        kernel,
        None,
        [s(ids)] + [w(m) for m in pieces],
        [w(shape(total, BLOCK)), w(shape(cut, BLOCK)), w(shape(share, BLOCK))],
        [],
        3,
    )


def cross_block(pairs, first, lengths, text, image, matrices, text_kept, image_kept, text_probs, image_probs, part):
    wq, wkv_text, wkv_image, wq_image, w_out, w_out_image = matrices
    text_low = text[...]
    image_low = image[...]
    text_kept[:, 0:256] = low(nn(text_low, wq[...]))
    text_kept[:, 256:768] = low(nn(text_low, wkv_text[...]))
    image_kept[:, 0:512] = low(nn(image_low, wkv_image[...]))
    image_kept[:, 512:768] = low(nn(image_low, wq_image[...]))

    image_mask = lax.broadcasted_iota(jnp.int32, (SLOTS, PADDED), 1) < REGIONS
    slots = lax.broadcasted_iota(jnp.int32, (PADDED, SLOTS), 1)
    units = [(p, h) for p in range(pairs) for h in range(2)]

    def text_part(at):
        return [text_kept[rows_of(p, SLOTS), at + h * HEAD : at + (h + 1) * HEAD] for p, h in units]

    def image_part(at):
        return [image_kept[rows_of(p, PADDED), at + h * HEAD : at + (h + 1) * HEAD] for p, h in units]

    scale = HEAD**-0.5
    probs, context = attend(text_part(0), image_part(0), image_part(256), scale, [image_mask] * len(units))
    for i, (p, h) in enumerate(units):
        text_probs[i] = probs[i]
        text_kept[rows_of(p, SLOTS), 768 + h * HEAD : 768 + (h + 1) * HEAD] = low(context[i])
    limits = [lengths[first + p] for p in range(pairs)]
    masks = [slots < limits[p] for p, h in units]
    probs, context = attend(image_part(512), text_part(256), text_part(512), scale, masks)
    for i, (p, h) in enumerate(units):
        image_probs[i] = probs[i]
        image_kept[rows_of(p, PADDED), 768 + h * HEAD : 768 + (h + 1) * HEAD] = low(context[i])
    leave_blocks(part, 0, low(nn(text_kept[:, 768:1024], w_out[...])))
    leave_blocks(part, 3 * text.shape[0], low(nn(image_kept[:, 768:1024], w_out_image[...])))


def cross_forward(pairs, lengths, text, image, *refs):
    matrices = refs[:6]
    text_pre, image_pre = refs[6:8]
    outs = refs[8:14]
    texts, images, text_kept, image_kept, text_probs, image_probs, parts, total, got, image_apart = refs[14:24]
    send_sems, recv_sems, out_sems = refs[24:]
    core, y, x = partners()
    copy = sender(send_sems, recv_sems)
    text_core = copy(0, text, texts.at[1], core)
    text_y = copy(1, text, texts.at[2], y)
    image_x = copy(2, image_apart, images.at[0], x)
    image_core = copy(3, images.at[0], images.at[1], core)
    image_y = copy(4, images.at[0], images.at[2], y)
    text_corner = copy(5, texts.at[2], texts.at[3], core)
    image_corner = copy(6, images.at[2], images.at[3], core)
    near_part = copy(7, parts.at[1], got.at[0], core)
    corner_part = copy(8, parts.at[3], got.at[1], core)
    far_part = copy(9, total, got.at[2], y)

    image_apart[...] = low(nn(spacing(pairs), image[...]))
    greet(core, y, x)
    image_x.start()
    text_y.start()
    text_core.start()
    texts[0] = text[...]
    image_x.wait()
    image_y.start()
    image_core.start()

    def block(j, unused):
        @pl.when(j == 1)
        def near():
            text_core.wait()
            image_core.wait()

        @pl.when(j == 2)
        def far():
            text_y.wait()
            text_corner.start()
            image_y.wait()
            image_corner.start()

        @pl.when(j == 3)
        def corner():
            text_corner.wait()
            image_corner.wait()

        cross_block(
            pairs,
            lax.bitwise_xor(lax.axis_index("tensor"), j) * pairs,
            lengths,
            texts.at[j],
            images.at[j],
            matrices,
            text_kept.at[j],
            image_kept.at[j],
            text_probs.at[j],
            image_probs.at[j],
            parts.at[j],
        )

        @pl.when(j == 1)
        def near_done():
            near_part.start()

        return unused

    lax.fori_loop(0, QUARTERS, block, 0)
    corner_part.start()
    leaving = [
        pltpu.make_async_copy(source, out, out_sems.at[i])
        for i, (source, out) in enumerate(
            zip((texts, images, text_kept, image_kept, text_probs, image_probs), outs)
        )
    ]
    for leave in leaving:
        leave.start()
    corner_part.wait()
    total[...] = add(parts[2], got[1])
    far_part.start()
    near_part.wait()
    size, image_size = text.shape[0], image_apart.shape[0]
    below = 3 * size

    def summed(row, depth, count, start):
        for ref in (parts.at[0], got.at[0]):
            start = start + side(ref, row, depth, count).astype(F32)
        return start

    text_pre[...] = summed(0, size, 3, text[...].astype(F32))
    image_pre[...] = summed(below, image_size, 4, images[0].astype(F32))
    far_part.wait()
    text_pre[...] += side(got.at[2], 0, size, 3).astype(F32)
    image_pre[...] += side(got.at[2], below, image_size, 4).astype(F32)
    for leave in leaving:
        leave.wait()


def cross_block_back(pairs, grad, matrices, text_kept, image_kept, text_probs, image_probs, text_d, image_d, part):
    wq, wkv_text, wkv_image, wq_image, w_out, w_out_image = matrices
    text_rows, image_rows = text_kept.shape[0], image_kept.shape[0]
    text_dc = low(nt(side(grad, 0, text_rows, 3), w_out[...]))
    image_dc = low(nt(side(grad, 3 * text_rows, image_rows, 4), w_out_image[...]))
    units = [(p, h) for p in range(pairs) for h in range(2)]

    def text_part(at):
        return [text_kept[rows_of(p, SLOTS), at + h * HEAD : at + (h + 1) * HEAD] for p, h in units]

    def image_part(at):
        return [image_kept[rows_of(p, PADDED), at + h * HEAD : at + (h + 1) * HEAD] for p, h in units]

    scale = HEAD**-0.5
    outer = [text_dc[rows_of(p, SLOTS), h * HEAD : (h + 1) * HEAD] for p, h in units]
    probs = [text_probs[i] for i in range(len(units))]
    found = attend_back(text_part(0), image_part(0), image_part(256), probs, outer, scale)
    for i, (p, h) in enumerate(units):
        text_d[rows_of(p, SLOTS), h * HEAD : (h + 1) * HEAD] = found[0][i]
        image_d[rows_of(p, PADDED), h * HEAD : (h + 1) * HEAD] = found[1][i]
        image_d[rows_of(p, PADDED), 256 + h * HEAD : 256 + (h + 1) * HEAD] = found[2][i]
    outer = [image_dc[rows_of(p, PADDED), h * HEAD : (h + 1) * HEAD] for p, h in units]
    probs = [image_probs[i] for i in range(len(units))]
    found = attend_back(image_part(512), text_part(256), text_part(512), probs, outer, scale)
    for i, (p, h) in enumerate(units):
        image_d[rows_of(p, PADDED), 512 + h * HEAD : 512 + (h + 1) * HEAD] = found[0][i]
        text_d[rows_of(p, SLOTS), 256 + h * HEAD : 256 + (h + 1) * HEAD] = found[1][i]
        text_d[rows_of(p, SLOTS), 512 + h * HEAD : 512 + (h + 1) * HEAD] = found[2][i]
    text_dx = nt(text_d[:, 0:256], wq[...]) + nt(text_d[:, 256:768], wkv_text[...])
    image_dx = nt(image_d[:, 0:512], wkv_image[...]) + nt(image_d[:, 512:768], wq_image[...])
    leave_blocks(part, 0, low(text_dx))
    leave_blocks(part, 3 * text_rows, low(image_dx))


def cross_back(pairs, grad, *refs):
    given, (text_kept, image_kept, text_probs, image_probs), matrices = refs[:6], refs[6:10], refs[10:16]
    grads_out, text_d_out, image_d_out, own_sum, total, vector_sum = refs[16:22]
    grads, text_d, image_d, parts, got, got_vectors, vectors, *kept = refs[22:-4]
    send_sems, recv_sems, out_sems, in_sems = refs[-4:]
    core, y, unused_x = partners()
    copy = sender(send_sems, recv_sems)
    loads = [
        [
            pltpu.make_async_copy(source.at[j], ref.at[j], in_sems.at[j, n])
            for n, (source, ref) in enumerate(zip((text_kept, image_kept, text_probs, image_probs), kept))
        ]
        for j in range(QUARTERS)
    ]
    text_kept, image_kept, text_probs, image_probs = kept
    to_core = copy(0, grad, grads.at[1], core)
    to_y = copy(1, grad, grads.at[2], y)
    corner = copy(2, grads.at[2], grads.at[3], core)
    near_part = copy(3, parts.at[1], got.at[0], core)
    corner_part = copy(4, parts.at[3], got.at[1], core)
    vectors_core = copy(5, vectors, got_vectors.at[0], core)
    vectors_y = copy(6, vector_sum, got_vectors.at[1], y)
    for load in loads[0]:
        load.start()
    vectors[...] = jnp.zeros_like(vectors)
    for n, vector in enumerate(given):
        vectors[2 * n : 2 * n + 2, 0 : vector.shape[1]] = vector[...]
    greet(core, y)
    vectors_core.start()
    to_y.start()
    to_core.start()
    for load in sum(loads[1:], []):
        load.start()
    grads[0] = grad[...]
    vectors_core.wait()
    vector_sum[...] = vectors[...] + got_vectors[0]
    vectors_y.start()

    def block(j, unused):
        @pl.when(j == 1)
        def near():
            to_core.wait()

        @pl.when(j == 2)
        def far():
            to_y.wait()
            corner.start()

        @pl.when(j == 3)
        def last():
            corner.wait()

        for at in range(QUARTERS):

            @pl.when(j == at)
            def loaded():
                for load in loads[at]:
                    load.wait()

        cross_block_back(
            pairs,
            grads.at[j],
            matrices,
            text_kept.at[j],
            image_kept.at[j],
            text_probs.at[j],
            image_probs.at[j],
            text_d.at[j],
            image_d.at[j],
            parts.at[j],
        )

        @pl.when(j == 1)
        def near_done():
            near_part.start()

        return unused

    lax.fori_loop(0, QUARTERS, block, 0)
    corner_part.start()
    leaving = [
        pltpu.make_async_copy(source, out, out_sems.at[i])
        for i, (source, out) in enumerate(((grads, grads_out), (text_d, text_d_out), (image_d, image_d_out)))
    ]
    for leave in leaving:
        leave.start()
    near_part.wait()
    own_sum[...] = parts[0].astype(F32) + got[0].astype(F32)
    vectors_y.wait()
    vector_sum[...] += got_vectors[1]
    corner_part.wait()
    total[...] = add(parts[2], got[1])
    for leave in leaving:
        leave.wait()


def halves(flip, values, x):
    half = flip.shape[0] // 2
    starts = [pl.multiple_of(lax.bitwise_xor(x, apart) * half, HEAD) for apart in range(2)]
    return [nn(flip[pl.ds(start, half), :], values) for start in starts]


def pick_columns(values, start, depth):
    row = lax.broadcasted_iota(jnp.int32, (values.shape[1], BLOCK), 0)
    column = lax.broadcasted_iota(jnp.int32, (values.shape[1], BLOCK), 1)
    chosen = (row == column + start) & (column < depth)
    return nn(values, low(jnp.where(chosen, 1.0, 0.0)))


def cross_last(total, vectors, *refs):
    sources, loaded = refs[:14], refs[21:33]
    grad_left, grad_right, image_grad, text_keep, image_keep_out, image_send_out, self_sum = refs[14:21]
    got, image_keep, image_send, text_send, text_got, self_got, text_flip, text_g_flip, image_flip, image_g_flip = refs[33:43]
    send_sems, recv_sems, in_sems, out_sems = refs[43:]
    self_all, self_more, texts, grads, text_d, text_c, images, image_d, image_c, own_sum, text_n, image_n = loaded
    self_loads = []
    for n, (target, first) in enumerate(((self_all, 0), (self_all, 1), (self_more, 0), (self_more, 1))):
        depth = sources[n].shape[1]
        target = target.at[:, pl.ds(first * sources[n - 1].shape[1], depth)]
        self_loads.append(pltpu.make_async_copy(sources[n], target, in_sems.at[n]))
    loads = [None, None]
    for n, (source, ref) in enumerate(zip(sources[4:], loaded[2:])):
        if source.shape != ref.shape:
            source = source.at[:, :, pl.ds(768, BLOCK)]
        loads.append(pltpu.make_async_copy(source, ref, in_sems.at[4 + n]))
    for load in self_loads + loads[2:]:
        load.start()
    unused_core, y, x = partners()
    copy = sender(send_sems, recv_sems)
    far = copy(0, total, got, y)
    text_x = copy(1, text_send, text_got, x)
    dp = self_all.shape[0]
    z_at = lax.axis_index("dp")
    others = [lax.rem(z_at + k, dp) for k in range(1, dp)]
    along_z = [copy(2 + k, self_all.at[other], self_got.at[k], {"dp": other}) for k, other in enumerate(others)]
    greet(y, x, *[{"dp": other} for other in others])
    far.start()
    for load in self_loads:
        load.wait()
    self_all[...] = add(self_all[...], self_more[...])
    for transfer in along_z:
        transfer.start()
    size, image_size = texts.shape[1], images.shape[1]
    below = 3 * size
    at = lax.axis_index("stream")
    leaving = []
    for first, rows, count, flip, g_flip, keep, send, number in (
        (0, size, 3, text_flip, text_g_flip, text_keep, text_send, (2, 3, 4, 5)),
        (below, image_size, 4, image_flip, image_g_flip, image_keep, image_send, (6, 3, 7, 8)),
    ):
        values, unused, outer, context = (loaded[n] for n in number)
        for n in number[:1] if count == 4 else number[:2]:
            loads[n].wait()
        for j in range(QUARTERS):
            columns = rows_of(j, rows)
            for b in range(count):
                flip[rows_of(b, BLOCK), columns] = values[j, :, b * BLOCK : (b + 1) * BLOCK].T
                g_flip[rows_of(b, BLOCK), columns] = grads[j, first + b * rows : first + (b + 1) * rows, :].T
        loads[number[2]].wait()
        loads[number[3]].wait()
        depth = flip.shape[0] // (2 * dp)
        padded = -(-depth // 16) * 16
        found_halves = halves(flip, outer[...].reshape(QUARTERS * rows, 768), at)
        last_halves = halves(g_flip, context[...].reshape(QUARTERS * rows, BLOCK), at)
        for out, found, last in zip((keep, send), found_halves, last_halves):
            for z in range(dp):
                taken = slice(z * depth, (z + 1) * depth)
                for b in range(3):
                    out[z, b * padded : b * padded + depth, :] = low(found[taken, b * BLOCK : (b + 1) * BLOCK])
                out[z, 3 * padded : 3 * padded + depth, :] = low(last[taken])
        if count == 3:
            rounded = low(vectors[...])
            is_text = lax.broadcasted_iota(jnp.int32, (rounded.shape[0], BLOCK), 0) < 6
            for apart, out in enumerate((text_keep, text_send)):
                for z in range(dp):
                    place = lax.bitwise_xor(at, apart) * dp + z
                    text_part = pick_columns(rounded[:, :DT], place * depth, depth)
                    image_depth = DV // (2 * dp)
                    image_part = pick_columns(rounded, place * image_depth, image_depth)
                    out[z, 4 * padded :, :] = low(jnp.where(is_text, text_part, image_part))
            text_x.start()
        else:
            leaving = [
                pltpu.make_async_copy(image_keep, image_keep_out, out_sems.at[0]),
                pltpu.make_async_copy(image_send, image_send_out, out_sems.at[1]),
            ]
            for leave in leaving:
                leave.start()
    summed = self_all[z_at].astype(F32)
    for k, transfer in enumerate(along_z):
        transfer.wait()
        summed = summed + self_got[k].astype(F32)
    self_sum[...] = low(summed)
    for load in loads[9:]:
        load.wait()
    far.wait()
    text_total = text_n[...] + side(own_sum, 0, size, 3) + side(got, 0, size, 3).astype(F32)
    grad_left[...] = text_total[:, : DT // 2]
    grad_right[...] = text_total[:, DT // 2 :]
    image_total = low(image_n[...] + side(own_sum, below, image_size, 4) + side(got, below, image_size, 4).astype(F32))
    image_grad[...] = low(tn(spacing(image_size // PADDED), image_total))
    text_x.wait()
    text_keep[...] = add(text_keep[...], text_got[...])
    for leave in leaving:
        leave.wait()


def gate(hidden):
    half = 0.5 * (1.0 + lax.erf(hidden * (2.0**-0.5)))
    density = jnp.exp(-0.5 * hidden * hidden) * 0.3989422804014327
    return hidden * half, half + hidden * density


def mlp_forward(pairs, text_pre, image_pre, text_gain, text_bias, image_gain, image_bias, *refs):
    parts = refs[:4]
    text_low, image_low, text_next, image_next = refs[4:8]
    text_activ, text_slope, image_activ, image_slope, corner = refs[8:13]
    weights, sems, send_sems, recv_sems = refs[13:]
    step = pl.program_id(0)
    leaving = fetch_round(step, *parts, corner, weights, sems, send_sems, recv_sems)

    @pl.when(step == 0)
    def begin():
        for pre, gain, bias, rounded, total in (
            (text_pre, text_gain, text_bias, text_low, text_next),
            (image_pre, image_gain, image_bias, image_low, image_next),
        ):
            g, b = affine_row(gain, bias, 0)
            one = normed(pre[...])[0] * g + b
            total[...] = one
            rounded[...] = low(one)

    w = weights.at[step]
    for b in range(3):
        activ, slope = gate(nn(text_low[...], w[b * 768 : (b + 1) * 768, :]))
        text_activ[0, :, b * 256 : (b + 1) * 256] = low(activ)
        text_slope[0, :, b * 256 : (b + 1) * 256] = low(slope)
    activ, slope = gate(nn(image_low[...], w[4608:5632, :]))
    image_activ[0] = low(activ)
    image_slope[0] = low(slope)
    text_next[...] += nn(text_activ[0], side(w, 2304, 768, 3))
    image_next[...] += nn(image_activ[0], side(w, 5632, 256, 4))

    @pl.when(step == QUARTERS - 1)
    def finish():
        leaving.wait()


def lane_masks():
    lane = lax.broadcasted_iota(jnp.int32, (1, 2 * SELF_HEAD), 1)
    left = (lane < SELF_HEAD).astype(F32)
    return low(left), low(1.0 - left), lane < SELF_HEAD


def both_heads(tile, masks):
    return jnp.concatenate([tile * masks[0], tile * masks[1]], axis=0)


def one_tile(stacked, masks):
    return jnp.where(masks[2], stacked[:SLOTS], stacked[SLOTS:])


def self_forward(pairs, ids, lengths, text_pre, image_pre, text_gain, text_bias, image_gain, image_bias, text_cot, image_cot, *refs):
    parts = refs[:4]
    (
        text_left,
        text_right,
        image_out,
        text_grad,
        image_grad,
        text_vec,
        image_vec,
        rounded,
        text_q,
        text_k,
        text_v,
        text_c,
        text_probs,
        image_kept,
        image_probs,
        corner,
    ) = refs[4:20]
    weights, text_sum, image_sum, text_low, image_low, sems, send_sems, recv_sems = refs[20:]
    step = pl.program_id(0)
    leaving = fetch_round(step, *parts, corner, weights, sems, send_sems, recv_sems)
    text_rows, image_rows = text_pre.shape[0], image_pre.shape[0]

    @pl.when(step == 0)
    def begin():
        for pre, gain, bias, total, lower, at in (
            (text_pre, text_gain, text_bias, text_sum, text_low, 0),
            (image_pre, image_gain, image_bias, image_sum, image_low, 6 * text_rows),
        ):
            g, b = affine_row(gain, bias, 1)
            two = normed(pre[...])[0] * g + b
            total[...] = two
            lower[...] = low(two)
            leave_blocks(rounded, at, low(two))

    w = weights.at[step]
    for n, out in enumerate((text_q, text_k, text_v)):
        wide = jnp.concatenate([w[b * 576 + n * 192 : b * 576 + (n + 1) * 192, :] for b in range(3)], axis=1)
        out[0] = low(nt(text_low[...], wide))
    for n in range(3):
        image_kept[0, :, n * 256 : (n + 1) * 256] = low(nn(image_low[...], w[2304 + n * 1024 : 3328 + n * 1024, :]))

    masks = lane_masks()
    slots = lax.broadcasted_iota(jnp.int32, (1, SLOTS), 1)
    base = ids[2]
    valid = [slots < lengths[base + p] for p in range(pairs)]
    first, last = slice(0, 128), slice(128, 192)
    queries, keys, values, limits = [], [], [], []
    for p in range(pairs):
        rows = rows_of(p, SLOTS)
        queries += [both_heads(text_q[0, rows, first], masks), text_q[0, rows, last]]
        keys += [text_k[0, rows, first], text_k[0, rows, last]]
        values += [text_v[0, rows, first], text_v[0, rows, last]]
        limits += [valid[p], valid[p]]
    probs, context = attend(queries, keys, values, SELF_HEAD**-0.5, limits)
    for p in range(pairs):
        rows = rows_of(p, SLOTS)
        text_probs[0, p, 0:256, :] = probs[2 * p]
        text_probs[0, p, 256:384, :] = probs[2 * p + 1]
        text_c[0, rows, first] = low(one_tile(context[2 * p], masks))
        text_c[0, rows, last] = low(context[2 * p + 1])

    image_mask = lax.broadcasted_iota(jnp.int32, (PADDED, PADDED), 1) < REGIONS
    units = [(p, h) for p in range(pairs) for h in range(2)]

    def image_part(at):
        return [image_kept[0, rows_of(p, PADDED), at + h * HEAD : at + (h + 1) * HEAD] for p, h in units]

    probs, context = attend(image_part(0), image_part(256), image_part(512), HEAD**-0.5, [image_mask] * len(units))
    for i, (p, h) in enumerate(units):
        image_probs[0, i] = probs[i]
        image_kept[0, rows_of(p, PADDED), 768 + h * HEAD : 768 + (h + 1) * HEAD] = low(context[i])

    text_sum[...] += nn(text_c[0], side(w, 1728, 192, 3))
    image_sum[...] += nn(image_kept[0, :, 768:1024], side(w, 5376, 256, 4))

    @pl.when(step == QUARTERS - 1)
    def finish():
        apart = spacing(pairs)
        image_cot_apart = nn(apart, image_cot[...])
        for total, gain, bias, cot, grad, vec, at in (
            (text_sum, text_gain, text_bias, text_cot[...].astype(F32), text_grad, text_vec, 3 * text_rows),
            (image_sum, image_gain, image_bias, image_cot_apart, image_grad, image_vec, 6 * text_rows + 4 * image_rows),
        ):
            g, b = affine_row(gain, bias, 2)
            unit, scale = normed(total[...])
            value = unit * g + b
            if total is text_sum:
                text_left[...] = value[:, : DT // 2]
                text_right[...] = value[:, DT // 2 :]
            else:
                image_out[...] = low(tn(apart, low(value)))
            back = norm_back(unit, scale, g, cot, vec)
            grad[...] = back
            leave_blocks(rounded, at, low(back))
        leaving.wait()


def self_back(pairs, dp, text_g, image_g, text_pre, image_pre, text_gain, image_gain, rounded, *refs):
    text_q, text_k, text_v, text_c, text_probs, image_kept, image_probs = refs[:7]
    parts = refs[7:12]
    text_n, image_n, text_vec, image_vec = refs[12:16]
    outs = refs[16:21]
    weights, found, text_sum, image_sum, text_g_low, image_g_low, near, rounded_near = refs[21:29]
    flips, (text_d, image_d, sems, out_sems, send_sems, recv_sems) = refs[29:33], refs[33:]
    step = pl.program_id(0)
    fetch(step, BACKWARD, *parts, weights, sems)
    core = partners()[0]
    copy = sender(send_sems, recv_sems)
    copies = [copy(n, found.at[n], near.at[n], core) for n in range(2)]
    rounded_copy = copy(2, rounded, rounded_near, core)

    @pl.when(step == 0)
    def begin():
        greet(core)
        rounded_copy.start()
        text_sum[...] = text_g[...]
        image_sum[...] = image_g[...]
        text_g_low[...] = low(text_g[...])
        image_g_low[...] = low(image_g[...])

    w = weights.at[step]
    masks = lane_masks()
    first, last = slice(0, 128), slice(128, 192)
    text_dc = low(nt(text_g_low[...], side(w, 1728, 192, 3)))
    queries, keys, values, probs, outer = [], [], [], [], []
    for p in range(pairs):
        rows = rows_of(p, SLOTS)
        queries += [both_heads(text_q[0, rows, first], masks), text_q[0, rows, last]]
        keys += [text_k[0, rows, first], text_k[0, rows, last]]
        values += [text_v[0, rows, first], text_v[0, rows, last]]
        probs += [text_probs[0, p, 0:256, :], text_probs[0, p, 256:384, :]]
        outer += [both_heads(text_dc[rows, first], masks), text_dc[rows, last]]
    grad_q, grad_k, grad_v = attend_back(queries, keys, values, probs, outer, SELF_HEAD**-0.5)
    size = text_g.shape[0]
    for p in range(pairs):
        rows = rows_of(p, SLOTS)
        text_d[0, rows, first] = one_tile(grad_q[2 * p], masks)
        text_d[0, rows, last] = grad_q[2 * p + 1]
        for n, grad in ((1, grad_k), (2, grad_v)):
            text_d[n, rows, first] = grad[2 * p]
            text_d[n, rows, last] = grad[2 * p + 1]

    image_dc = low(nt(image_g_low[...], side(w, 5376, 256, 4)))
    units = [(p, h) for p in range(pairs) for h in range(2)]

    def image_part(at):
        return [image_kept[0, rows_of(p, PADDED), at + h * HEAD : at + (h + 1) * HEAD] for p, h in units]

    outer = [image_dc[rows_of(p, PADDED), h * HEAD : (h + 1) * HEAD] for p, h in units]
    given = attend_back(
        image_part(0), image_part(256), image_part(512), [image_probs[0, i] for i in range(len(units))], outer, HEAD**-0.5
    )
    for n in range(3):
        for i, (p, h) in enumerate(units):
            image_d[rows_of(p, PADDED), n * 256 + h * HEAD : n * 256 + (h + 1) * HEAD] = given[n][i]

    gained = text_sum[...]
    for n in range(3):
        wide = jnp.concatenate([w[b * 576 + n * 192 : b * 576 + (n + 1) * 192, :] for b in range(3)], axis=1)
        gained = gained + nn(text_d[n], wide)
    text_sum[...] = gained
    image_sum[...] += nt(image_d[...], side(w, 2304, 1024, 3))

    slot = found.at[step]
    slot[0:size, 0:128] = text_d[0, :, first]
    slot[0:size, 128:256] = text_d[1, :, first]
    slot[size : 2 * size, 0:128] = text_d[2, :, first]
    slot[size : 2 * size, 128:256] = text_c[0, :, first]
    slot[2 * size : 3 * size, 0:128] = jnp.concatenate([text_d[0, :, last], text_d[1, :, last]], axis=1)
    slot[2 * size : 3 * size, 128:256] = jnp.concatenate([text_d[2, :, last], text_c[0, :, last]], axis=1)
    leave_blocks(slot, 3 * size, image_d[...])
    leave_blocks(slot, 3 * size + 3 * image_g.shape[0], image_kept[0, :, 768:1024])
    send_quarter(step, copies)

    @pl.when(step == QUARTERS - 1)
    def finish():
        leave_norm(1, text_sum, image_sum, text_pre, image_pre, text_gain, image_gain, text_n, image_n, text_vec, image_vec)
        rounded_copy.wait()
        for transfer in copies:
            transfer.wait()
        weight_grad(True, dp, (size, image_g.shape[0]), (rounded, rounded_near), found, near, weights, outs, flips, out_sems)


def leave_norm(norm, text_sum, image_sum, text_pre, image_pre, text_gain, image_gain, text_n, image_n, text_vec, image_vec):
    for total, pre, gain, out, vec in (
        (text_sum, text_pre, text_gain, text_n, text_vec),
        (image_sum, image_pre, image_gain, image_n, image_vec),
    ):
        unit, scale = normed(pre[...])
        out[...] = norm_back(unit, scale, gain[0, norm : norm + 1, :].astype(F32), total[...], vec)


def mlp_back(pairs, dp, text_g, image_g, text_one, image_one, text_pre, image_pre, text_gain, image_gain, *refs):
    text_activ, text_slope, image_activ, image_slope = refs[:4]
    parts = refs[4:9]
    text_n, image_n, next_low, text_vec, image_vec = refs[9:14]
    outs = refs[14:17]
    weights, found, text_sum, image_sum, text_g_low, image_g_low, near, rounded_near = refs[17:25]
    flips, (rounded, text_d, sems, out_sems, send_sems, recv_sems) = refs[25:29], refs[29:]
    step = pl.program_id(0)
    fetch(step, BACKWARD, *parts, weights, sems)
    size, image_size = text_g.shape[0], image_g.shape[0]
    core = partners()[0]
    copy = sender(send_sems, recv_sems)
    rounded_copy = copy(2, rounded, rounded_near, core)
    copies = [copy(n, found.at[n], near.at[n], core) for n in range(2)]

    @pl.when(step == 0)
    def begin():
        text_sum[...] = text_g[...]
        image_sum[...] = image_g[...]
        text_g_low[...] = low(text_g[...])
        image_g_low[...] = low(image_g[...])
        leave_blocks(rounded, 0, text_one[...])
        leave_blocks(rounded, 3 * size, text_g_low[...])
        leave_blocks(rounded, 6 * size, image_one[...])
        leave_blocks(rounded, 6 * size + 4 * image_size, image_g_low[...])
        greet(core)
        rounded_copy.start()

    w = weights.at[step]
    slot = found.at[step]
    wide = side(w, 2304, 768, 3)
    for b in range(3):
        columns = slice(b * 256, (b + 1) * 256)
        back = nt(text_g_low[...], wide[columns])
        text_d[:, columns] = low(back * text_slope[0, :, columns].astype(F32))
    text_sum[...] += nt(text_d[...], side(w, 0, 768, 3))
    image_d = low(nt(image_g_low[...], side(w, 5632, 256, 4)) * image_slope[0].astype(F32))
    image_sum[...] += nt(image_d, w[4608:5632, :])
    leave_blocks(slot, 0, text_d[...])
    leave_blocks(slot, 3 * size, text_activ[0])
    leave_blocks(slot, 6 * size, image_d)
    leave_blocks(slot, 6 * size + image_size, image_activ[0])
    send_quarter(step, copies)

    @pl.when(step == QUARTERS - 1)
    def finish():
        leave_norm(0, text_sum, image_sum, text_pre, image_pre, text_gain, image_gain, text_n, image_n, text_vec, image_vec)
        leave_blocks(next_low, 0, low(text_n[...]))
        leave_blocks(next_low, 3 * size, low(image_n[...]))
        rounded_copy.wait()
        for transfer in copies:
            transfer.wait()
        weight_grad(False, dp, (size, image_size), (rounded, rounded_near), found, near, weights, outs, flips, out_sems)


def weight_grad(is_self, dp, sizes, rounded, found, near, spare, outs, flips, out_sems):
    text_flip, text_g_flip, image_flip, image_g_flip = flips
    to_send, kept, to_z, by_image = (spare.at[n] for n in range(QUARTERS))
    size, image_size = sizes
    x = lax.axis_index("stream")
    for at in range(2):
        for b in range(3):
            text_flip[rows_of(b, BLOCK), rows_of(at, size)] = rounded[at][rows_of(b, size), :].T
            text_g_flip[rows_of(b, BLOCK), rows_of(at, size)] = rounded[at][rows_of(3 + b, size), :].T
        for b in range(8):
            start = 6 * size + b * image_size
            flip = image_g_flip if b > 3 else image_flip
            flip[rows_of(b % 4, BLOCK), rows_of(at, image_size)] = rounded[at][start : start + image_size, :].T

    text_depth, image_depth = DT // (2 * dp), DV // (2 * dp)
    padded = -(-text_depth // 16) * 16
    lane = lax.broadcasted_iota(jnp.int32, (1, HEAD), 1) < SELF_HEAD
    top = 3 * padded if is_self else 5 * padded
    below = 2 * image_depth if is_self else 2 * image_depth + padded
    leaving = []

    def leave(source, target, first=0):
        leaving.append(pltpu.make_async_copy(source.at[pl.ds(first, target.shape[0])], target, out_sems.at[len(leaving)]))
        leaving[-1].start()

    for slot in (1, 0):

        def block(start, rows):
            return jnp.concatenate([found[2 + slot, start : start + rows, :], near[slot, start : start + rows, :]], axis=0)

        def text_block(b):
            return block(b * size, size)

        def image_block(b, text_blocks):
            return block(text_blocks * size + b * image_size, image_size)

        def write(row, depth, value):
            for apart in range(2):
                ref, at = ((to_send if slot else kept), apart) if is_self else ((to_send if apart else kept), slot)
                for z in range(dp):
                    to = (at * dp + z) * top + row
                    ref[to : to + depth, :] = low(value[apart][z * depth : (z + 1) * depth])

        def bottom(row, depth, value):
            for apart in range(2):
                for z in range(dp):
                    to = (z * 4 + 2 * slot + apart) * below + row
                    to_z[to : to + depth, :] = low(value[apart][z * depth : (z + 1) * depth])

        if is_self:
            one, two, three = text_block(0), text_block(1), text_block(2)
            write(0, text_depth, halves(text_flip, one, x))
            pairs = zip(halves(text_flip, two[:, :HEAD], x), halves(text_g_flip, two[:, HEAD:], x))
            write(padded, text_depth, [jnp.concatenate(pair, axis=1) for pair in pairs])
            pairs = zip(halves(text_flip, three, x), halves(text_g_flip, three[:, HEAD:], x))
            mixed = [jnp.concatenate([a[:, :HEAD], jnp.where(lane, a[:, HEAD:], b)], axis=1) for a, b in pairs]
            write(2 * padded, text_depth, mixed)
            for b in range(2):
                for apart, value in enumerate(halves(image_flip, image_block(b, 3), x)):
                    for z in range(dp):
                        to = (((2 * (1 - apart) + slot) * dp + z) * 2 + b) * image_depth
                        by_image[to : to + image_depth, :] = low(value[z * image_depth : (z + 1) * image_depth])
            leave(*((to_send, outs[0]) if slot else (kept, outs[1])))
            for b, flip in enumerate((image_flip, image_g_flip)):
                bottom(b * image_depth, image_depth, halves(flip, image_block(2 + b, 3), x))
        else:
            for b in range(5):
                write(b * padded, text_depth, halves(text_g_flip if b > 2 else text_flip, text_block(b), x))
            bottom(2 * image_depth, text_depth, halves(text_g_flip, text_block(5), x))
            for b, flip in enumerate((image_flip, image_g_flip)):
                bottom(b * image_depth, image_depth, halves(flip, image_block(b, 6), x))
    if not is_self:
        leave(to_send, outs[0])
        leave(kept, outs[1])
    leave(to_z, outs[2])
    for number, out in enumerate(outs[3:]):
        leave(by_image, out, number * out.shape[0])
    for copy in leaving:
        copy.wait()


ANY = pl.BlockSpec(memory_space=pl.ANY)
SCALARS = pl.BlockSpec(memory_space=pltpu.SMEM)


def whole(array, buffers=None):
    zeros = (0,) * len(array.shape)
    mode = {} if buffers is None else {"pipeline_mode": pl.Buffered(buffers)}
    return pl.BlockSpec(array.shape, lambda *s: zeros, **mode)


def quarter(array, order):
    tail = (0,) * (len(array.shape) - 1)
    if order is FORWARD:
        return pl.BlockSpec((1,) + array.shape[1:], lambda s: (s,) + tail)
    return pl.BlockSpec((1,) + array.shape[1:], lambda s: (lax.rem(2 * s + 1 - lax.div(s, 2), 4),) + tail)


def shape(*dims, of=BF):
    return jax.ShapeDtypeStruct(dims, of)


def run(kernel, order, operands, outs, scratch, us, meeting=None):
    def spec(kind, array, given=False):
        if kind == "w" and given and order:
            return whole(array, 1)
        return {"s": lambda: SCALARS, "w": lambda: whole(array), "q": lambda: quarter(array, order), "a": lambda: ANY}[kind]()

    return pl.pallas_call(
        kernel,
        grid=(QUARTERS,) if order else (1,),
        in_specs=[spec(*entry, given=True) for entry in operands],
        out_specs=[spec(*entry) for entry in outs],
        out_shape=[array for unused, array in outs],
        scratch_shapes=scratch,
        compiler_params=pltpu.CompilerParams(
            dimension_semantics=("arbitrary",),
            vmem_limit_bytes=60 * 2**20,
            collective_id=meeting,
            has_side_effects=meeting is not None,
        ),
        cost_estimate=pl.CostEstimate(flops=int(us * 1.1e9), bytes_accessed=1024, transcendentals=0),
    )(*[array for unused, array in operands])


def swap(value, axis, apart):
    return lax.ppermute(value, axis, [(i, i ^ apart) for i in range(lax.axis_size(axis))])


def after(value, *earlier):
    return lax.optimization_barrier((value,) + earlier)[0]


class Line:
    def __init__(self):
        self.last = ()

    def take(self, value):
        return after(value, *self.last)

    def leave(self, *values):
        self.last = values


def add(left, right):
    return low(left.astype(F32) + right.astype(F32))


def fold_last(total):
    return lax.psum_scatter(total, "dp", scatter_dimension=0, tiled=True)[0]


def s(value):
    return ("s", value)


def w(value):
    return ("w", value)


def q(value):
    return ("q", value)


def a(value):
    return ("a", value)


def local(
    text_in,
    image_in,
    lengths,
    text_cot,
    image_cot,
    text_cross_q,
    text_cross_kv,
    text_cross_out,
    text_up,
    text_down,
    text_self_qkv,
    text_self_out,
    text_gain,
    text_bias,
    image_cross_q,
    image_cross_kv,
    image_cross_out,
    image_up,
    image_down,
    image_self_qkv,
    image_self_out,
    image_gain,
    image_bias,
):
    dp = lax.axis_size("dp")
    places = 2 * dp
    x_at = lax.axis_index("stream")
    t_at = lax.axis_index("tensor")
    size = text_in.shape[0]
    pairs = size // SLOTS
    image_size = pairs * PADDED
    units = 2 * pairs
    ids = jnp.stack([x_at, x_at * dp + lax.axis_index("dp")] + [(t_at ^ j) * pairs for j in range(QUARTERS)]).astype(jnp.int32)

    def leave(rows):
        return swap(rows, "stream", 1).astype(F32)

    line = Line()
    mlp_own, mlp_first, mlp_mine = pack([text_up[0], text_down[0], image_up[0], image_down[0]], places, 5120, ids)
    mlp_share = swap(mlp_mine, "tensor", 2)
    self_own, self_first, self_mine = pack(
        [
            text_self_qkv[0].transpose(1, 2, 0).reshape(-1, DT),
            text_self_out[0],
            image_self_qkv[0].reshape(DV, -1),
            image_self_out[0],
        ],
        places,
        4608,
        after(ids, mlp_own),
    )
    cross_w = (
        text_cross_q[0],
        image_cross_kv[0].reshape(DT, -1),
        text_cross_kv[0].reshape(DV, -1),
        image_cross_q[0],
        text_cross_out[0],
        image_cross_out[0],
    )
    line.leave(self_own)
    mlp_share = line.take(mlp_share)
    line.leave(mlp_share, cross_w[1], cross_w[2])
    self_share = line.take(swap(self_mine, "tensor", 2))
    line.leave(self_share)
    mlp_rest = lax.all_gather(mlp_share, ("stream", "dp"), axis=0, tiled=True)
    self_rest = lax.all_gather(self_share, ("stream", "dp"), axis=0, tiled=True)
    self_near = swap(self_own, "tensor", 1)
    mlp_near_w = swap(mlp_own, "tensor", 1)
    image_cot_here = swap(image_cot, "stream", 1)
    mlp_far = swap(mlp_first, "tensor", 2)

    text_wide, image_wide = shape(size, DT, of=F32), shape(image_size, DV, of=F32)
    text_half = shape(size, DT // 2, of=F32)
    text_f32, image_f32 = pltpu.VMEM((size, DT), F32), pltpu.VMEM((image_size, DV), F32)
    text_bf, image_bf = pltpu.VMEM((size, DT), BF), pltpu.VMEM((image_size, DV), BF)
    in_sems, out_sems = pltpu.SemaphoreType.DMA((5,)), pltpu.SemaphoreType.DMA((5,))
    text_affine = [w(text_gain), w(text_bias)]
    image_affine = [w(image_gain), w(image_bias)]
    vector_outs = [w(shape(2, DT, of=F32)), w(shape(2, DV, of=F32))]
    part_rows = 3 * size + 4 * image_size

    def buffer(weights):
        return pltpu.VMEM((QUARTERS,) + weights.shape, BF)

    in_four = [
        (QUARTERS, size, DT),
        (QUARTERS, image_size, DV),
        (QUARTERS, size, 1024),
        (QUARTERS, image_size, 1024),
        (QUARTERS, units, SLOTS, PADDED),
        (QUARTERS, units, PADDED, SLOTS),
    ]

    def links(count):
        return [pltpu.SemaphoreType.DMA((count,)), pltpu.SemaphoreType.DMA((count,))]

    text_pre1, image_pre1, texts, images, *cross_kept = run(
        functools.partial(cross_forward, pairs),
        None,
        [s(lengths), w(line.take(text_in)), w(image_in)] + [w(m) for m in cross_w],
        [w(text_wide), w(image_wide)] + [a(shape(*dims)) for dims in in_four],
        [pltpu.VMEM(dims, BF) for dims in in_four]
        + [pltpu.VMEM((QUARTERS, part_rows, BLOCK), BF), pltpu.VMEM((part_rows, BLOCK), BF), pltpu.VMEM((3, part_rows, BLOCK), BF)]
        + [image_bf]
        + links(10)
        + [pltpu.SemaphoreType.DMA((6,))],
        70,
        1,
    )
    line.leave(text_pre1, image_cot_here)
    mlp_far, mlp_rest = line.take((mlp_far, mlp_rest))
    self_far = swap(after(self_first, mlp_far), "tensor", 2)
    (
        text_one,
        image_one,
        text_pre2,
        image_pre2,
        text_activ,
        text_slope,
        image_activ,
        image_slope,
        mlp_corner,
    ) = run(
        functools.partial(mlp_forward, pairs),
        FORWARD,
        [w(text_pre1), w(image_pre1)] + text_affine + image_affine + [a(m) for m in (mlp_own, mlp_near_w, mlp_far, mlp_rest)],
        [
            w(shape(size, DT)),
            w(shape(image_size, DV)),
            w(text_wide),
            w(image_wide),
            q(shape(QUARTERS, size, 768)),
            q(shape(QUARTERS, size, 768)),
            q(shape(QUARTERS, image_size, 256)),
            q(shape(QUARTERS, image_size, 256)),
            a(mlp_own),
        ],
        [buffer(mlp_own), in_sems] + links(2),
        1,
        7,
    )
    mlp_w = mlp_own, mlp_near_w, mlp_far, mlp_rest, mlp_corner
    line.leave(text_pre2)
    self_far, self_rest = line.take((self_far, self_rest))
    (
        text_left,
        text_right,
        image_out,
        text_n3,
        image_n3,
        text_vec3,
        image_vec3,
        self_rounded,
        self_q,
        self_k,
        self_v,
        self_c,
        self_probs,
        self_kept,
        self_image_probs,
        self_corner,
    ) = run(
        functools.partial(self_forward, pairs),
        FORWARD,
        [s(ids), s(lengths), w(text_pre2), w(image_pre2)]
        + text_affine
        + image_affine
        + [w(text_cot), w(image_cot_here)]
        + [a(m) for m in (self_own, self_near, self_far, self_rest)],
        [w(text_half), w(text_half), w(image_cot), w(text_wide), w(image_wide)]
        + vector_outs
        + [
            w(shape(2 * part_rows, BLOCK)),
            q(shape(QUARTERS, size, 192)),
            q(shape(QUARTERS, size, 192)),
            q(shape(QUARTERS, size, 192)),
            q(shape(QUARTERS, size, 192)),
            q(shape(QUARTERS, pairs, 384, SLOTS)),
            q(shape(QUARTERS, image_size, 1024)),
            q(shape(QUARTERS, units, PADDED, PADDED)),
            a(self_own),
        ],
        [buffer(self_own), text_f32, image_f32, text_bf, image_bf, in_sems] + links(2),
        19,
        8,
    )
    self_w = self_own, self_near, self_far, self_rest, self_corner
    image_out = swap(image_out, "stream", 1)

    text_depth, image_depth = DT // places, DV // places
    padded = -(-text_depth // 16) * 16

    def back_scratch(weights, rows):
        return [
            buffer(weights[0]),
            pltpu.VMEM((QUARTERS, rows, BLOCK), BF),
            text_f32,
            image_f32,
            text_bf,
            image_bf,
            pltpu.VMEM((2, rows, BLOCK), BF),
            pltpu.VMEM((2 * part_rows, BLOCK), BF),
            pltpu.VMEM((DT, 2 * size), BF),
            pltpu.VMEM((DT, 2 * size), BF),
            pltpu.VMEM((DV, 2 * image_size), BF),
            pltpu.VMEM((DV, 2 * image_size), BF),
        ]

    def grad_shapes(is_self):
        first = (2, dp, (3 if is_self else 5) * padded, BLOCK)
        last = (dp, 4 * (2 * image_depth + (0 if is_self else padded)), BLOCK)
        return [first, first, last] + [(2, dp, 2 * image_depth, BLOCK)] * (2 if is_self else 0)

    def grad_outs(is_self):
        return [a(shape(math.prod(dims[:-1]), BLOCK)) for dims in grad_shapes(is_self)]

    def grad_arrays(is_self, *found):
        return [out.reshape(dims) for out, dims in zip(found, grad_shapes(is_self))]

    self_rows = 3 * size + 4 * image_size
    text_n2, image_n2, text_vec2, image_vec2, *self_found = run(
        functools.partial(self_back, pairs, dp),
        BACKWARD,
        [
            w(text_n3),
            w(image_n3),
            w(text_pre2),
            w(image_pre2),
            w(text_gain),
            w(image_gain),
            w(self_rounded),
            q(self_q),
            q(self_k),
            q(self_v),
            q(self_c),
            q(self_probs),
            q(self_kept),
            q(self_image_probs),
        ]
        + [a(m) for m in self_w],
        [w(text_wide), w(image_wide)] + vector_outs + grad_outs(True),
        back_scratch(self_w, self_rows)
        + [pltpu.VMEM((3, size, 192), BF), pltpu.VMEM((image_size, 768), BF), in_sems, out_sems]
        + links(3),
        32,
        2,
    )
    to_y, self_top, to_z, to_x, self_side = grad_arrays(True, *self_found)
    self_by_y = swap(to_y, "tensor", 2)
    self_by_x = swap(to_x, "stream", 1)
    self_bottom = fold_last(to_z)
    line.leave(self_top)
    mlp_rows = 6 * size + 2 * image_size
    text_n1, image_n1, grad_low, text_vec1, image_vec1, *mlp_found = run(
        functools.partial(mlp_back, pairs, dp),
        BACKWARD,
        [
            w(text_n2),
            w(image_n2),
            w(text_one),
            w(image_one),
            w(text_pre1),
            w(image_pre1),
            w(line.take(text_gain)),
            w(image_gain),
            q(text_activ),
            q(text_slope),
            q(image_activ),
            q(image_slope),
        ]
        + [a(m) for m in mlp_w],
        [w(text_wide), w(image_wide), w(shape(part_rows, BLOCK))]
        + vector_outs
        + grad_outs(False),
        back_scratch(mlp_w, mlp_rows)
        + [pltpu.VMEM((2 * part_rows, BLOCK), BF), text_bf, in_sems, out_sems]
        + links(3),
        28,
        3,
    )
    line.leave(grad_low)
    to_x, mlp_top, to_z = grad_arrays(False, *mlp_found)
    self_top, self_by_y, self_side, self_by_x, to_x, to_z, image_out = after(
        (self_top, self_by_y, self_side, self_by_x, to_x, to_z, image_out), mlp_top
    )
    mlp_by_x = swap(to_x, "stream", 1)
    mlp_bottom = fold_last(to_z)
    self_top, to_x = add(self_top[0], self_by_y[0]), add(self_top[1], self_by_y[1])
    self_then_x = swap(to_x, "stream", 1)
    self_side, to_y = add(self_side[0], self_by_x[0]), add(self_side[1], self_by_x[1])
    self_then_y = swap(to_y, "tensor", 2)
    line.leave(self_top, to_x, self_side, to_y)
    d_dims = [(QUARTERS, part_rows, BLOCK), (QUARTERS, size, 768), (QUARTERS, image_size, 768)]
    grads, text_d, image_d, own_sum, total, vectors = run(
        functools.partial(cross_back, pairs),
        None,
        [w(line.take(grad_low))]
        + [w(v) for v in (text_vec1, text_vec2, text_vec3, image_vec1, image_vec2, image_vec3)]
        + [a(k) for k in cross_kept] + [w(m) for m in cross_w],
        [a(shape(*dims)) for dims in d_dims]
        + [w(shape(part_rows, BLOCK, of=F32)), w(shape(part_rows, BLOCK)), w(shape(16, DV, of=F32))],
        [pltpu.VMEM(dims, BF) for dims in d_dims]
        + [pltpu.VMEM((QUARTERS, part_rows, BLOCK), BF), pltpu.VMEM((2, part_rows, BLOCK), BF), pltpu.VMEM((2, 16, DV), F32)]
        + [pltpu.VMEM((16, DV), F32)]
        + [pltpu.VMEM(k.shape, BF) for k in cross_kept]
        + links(7)
        + [pltpu.SemaphoreType.DMA((3,)), pltpu.SemaphoreType.DMA((QUARTERS, 4))],
        48,
        4,
    )
    line.leave(total)
    text_only, image_only = 4 * padded + 16, 4 * image_depth
    last_inputs = [
        self_top,
        self_side,
        self_then_x,
        self_then_y,
        texts,
        grads,
        text_d,
        cross_kept[0],
        images,
        image_d,
        cross_kept[1],
        own_sum,
        text_n1,
        image_n1,
    ]
    self_all = (dp, 3 * padded + 2 * image_depth, BLOCK)
    last_scratch = [pltpu.VMEM(self_all, BF)] * 2 + [pltpu.VMEM(m.shape, m.dtype) for m in last_inputs[4:]]
    last_scratch[5], last_scratch[8] = pltpu.VMEM((QUARTERS, size, BLOCK), BF), pltpu.VMEM((QUARTERS, image_size, BLOCK), BF)
    grad_left, grad_right, image_grad, cross_text, image_keep, image_send, self_top = run(
        cross_last,
        None,
        [w(line.take(total)), w(vectors)] + [a(m) for m in last_inputs],
        [
            w(text_half),
            w(text_half),
            w(image_cot),
            w(shape(dp, text_only, BLOCK)),
            a(shape(dp, image_only, BLOCK)),
            a(shape(dp, image_only, BLOCK)),
            w(shape(*self_all[1:])),
        ],
        last_scratch
        + [
            pltpu.VMEM((part_rows, BLOCK), BF),
            pltpu.VMEM((dp, image_only, BLOCK), BF),
            pltpu.VMEM((dp, image_only, BLOCK), BF),
            pltpu.VMEM((dp, text_only, BLOCK), BF),
            pltpu.VMEM((dp, text_only, BLOCK), BF),
            pltpu.VMEM((dp - 1, *self_all[1:]), BF),
            pltpu.VMEM((DT, QUARTERS * size), BF),
            pltpu.VMEM((DT, QUARTERS * size), BF),
            pltpu.VMEM((DV, QUARTERS * image_size), BF),
            pltpu.VMEM((DV, QUARTERS * image_size), BF),
        ]
        + links(1 + dp)
        + [pltpu.SemaphoreType.DMA((14,)), pltpu.SemaphoreType.DMA((2,))],
        2,
        5,
    )
    line.leave(grad_left)
    mlp_top, mlp_by_x, self_bottom, mlp_bottom, cross_text, image_send = line.take(
        (mlp_top, mlp_by_x, self_bottom, mlp_bottom, cross_text, image_send)
    )
    cross_text = fold_last(cross_text)
    image_send = swap(image_send, "stream", 1)
    mlp_top, to_y = add(mlp_top[0], mlp_by_x[0]), add(mlp_top[1], mlp_by_x[1])
    mlp_then_y = swap(to_y, "tensor", 2)
    line.leave(mlp_top, to_y)
    self_bottom = line.take(self_bottom).reshape(2, 2, 2 * image_depth, BLOCK)
    self_bottom_x = swap(self_bottom[:, 1], "stream", 1)
    cross_image = add(image_keep, line.take(image_send))
    line.leave(cross_image)
    cross_image = fold_last(cross_image)
    self_bottom = add(self_bottom[:, 0], line.take(self_bottom_x))
    self_bottom_y = swap(self_bottom[1], "tensor", 2)
    mlp_bottom = line.take(mlp_bottom).reshape(2, 2, 2 * image_depth + padded, BLOCK)
    mlp_bottom_x = swap(mlp_bottom[:, 1], "stream", 1)
    mlp_top = add(mlp_top, line.take(mlp_then_y))
    line.leave(mlp_top)
    mlp_top = fold_last(mlp_top)
    mlp_bottom = add(mlp_bottom[:, 0], line.take(mlp_bottom_x))
    mlp_bottom = add(mlp_bottom[0], swap(mlp_bottom[1], "tensor", 2))
    self_bottom = add(self_bottom[0], self_bottom_y)
    self_grads = jnp.concatenate([self_top, self_bottom], axis=0)
    image_grad = leave(image_grad)

    def pick(packed, first, count, depth, stride):
        rows = [packed[first + b * stride : first + b * stride + depth] for b in range(count)]
        return jnp.concatenate(rows, axis=1).astype(F32)

    def text_pick(packed, first, count):
        return pick(packed, first, count, text_depth, padded)

    def image_pick(packed, first, count):
        return pick(packed, first, count, image_depth, image_depth)

    sums = cross_text[4 * padded :].astype(F32)
    text_vectors, image_vectors = sums[:6, :text_depth], sums[6:12, :image_depth]

    self_text = text_pick(self_grads, 0, 3)

    def heads(at):
        return jnp.concatenate([self_text[:, at * 128 : (at + 1) * 128], self_text[:, 512 + at * 64 : 576 + at * 64]], axis=1)

    below = 3 * padded
    return (
        jnp.concatenate([text_left, text_right], axis=1),
        image_out.astype(F32),
        jnp.concatenate([grad_left, grad_right], axis=1),
        image_grad,
        text_pick(cross_text, 0, 1)[None],
        image_pick(cross_image, 0, 2).reshape(1, image_depth, 2, 256),
        text_pick(cross_text, 3 * padded, 1).T[None],
        text_pick(mlp_top, 0, 3)[None],
        jnp.concatenate([text_pick(mlp_top, below, 2), text_pick(mlp_bottom, 2 * image_depth, 1)], axis=1).T[None],
        jnp.stack([heads(n) for n in range(3)], axis=1)[None],
        heads(3).T[None],
        text_vectors[0::2][None],
        text_vectors[1::2][None],
        image_pick(cross_image, 2 * image_depth, 1)[None],
        text_pick(cross_text, padded, 2).reshape(1, text_depth, 2, 256),
        image_pick(cross_image, 3 * image_depth, 1).T[None],
        image_pick(mlp_bottom, 0, 1)[None],
        image_pick(mlp_bottom, image_depth, 1).T[None],
        image_pick(self_grads, below, 3).reshape(1, image_depth, 3, 256),
        image_pick(self_grads, below + 3 * image_depth, 1).T[None],
        image_vectors[0::2][None],
        image_vectors[1::2][None],
    )


def solution(mesh):
    rows = P(("stream", "dp", "tensor"), None)
    wide_in = P(None, None, "tensor")
    group_in = P(None, None, None, "tensor")
    wide_out = P(None, "tensor", None)
    grad_in = P(None, ("stream", "dp"), "tensor")
    grad_group = P(None, ("stream", "dp"), None, "tensor")
    grad_out = P(None, "tensor", ("stream", "dp"))
    vector = P(None, None, ("stream", "dp"))
    weights = (wide_in, group_in, wide_out, wide_in, wide_out, group_in, wide_out, P(), P())
    grads = (grad_in, grad_group, grad_out, grad_in, grad_out, grad_group, grad_out, vector, vector)
    return jax.shard_map(
        local,
        mesh=mesh,
        in_specs=(rows, rows, P(("stream", "dp")), rows, rows) + weights + weights,
        out_specs=(rows, rows, rows, rows) + grads + grads,
        check_vma=False,
    )
```
